32 devices in a mesh: win: 8 (over z, y), ch: 4 (over x, core).
Axes of the slice: x: 2, y: 2, z: 4, core: 2. Of those that a mesh axis runs over, the one named last changes fastest.
Arguments:
- tokens: bfloat16 [2, 64, 196, 384], P(None, ('win', 'ch')), may hold values from -6 to 6
- valid_rows: int32 [2, 64], P(None, ('win', 'ch')), may hold values from 7 to 14
- valid_cols: int32 [2, 64], P(None, ('win', 'ch')), may hold values from 7 to 14
- partner: int32 [2, 64], P(None, ('win', 'ch')), may hold values from 0 to 63
- mix_level: int32 [2, 64], P(None, ('win', 'ch')), may hold values from 1 to 15
- labels: int32 [2, 64], replicated, may hold values from 0 to 999
- w_qkv: float32 [2, 384, 1152], P(None, 'win', 'ch'), may hold values from -0.3125 to 0.3125
- m_qkv: float32 [2, 384, 1152], P(None, 'win', 'ch'), may hold values from -0.00036621094 to 0.00036621094
- v_qkv: float32 [2, 384, 1152], P(None, 'win', 'ch'), may hold values from 6.348181e-10 to 2.5392723e-09
- w_proj: float32 [2, 384, 384], P(None, 'win', 'ch'), may hold values from -0.875 to 0.875
- m_proj: float32 [2, 384, 384], P(None, 'win', 'ch'), may hold values from -0.00036621094 to 0.00036621094
- v_proj: float32 [2, 384, 384], P(None, 'win', 'ch'), may hold values from 6.348181e-10 to 2.5392723e-09
- w_fc1: float32 [2, 384, 1536], P(None, 'win', 'ch'), may hold values from -0.3125 to 0.3125
- m_fc1: float32 [2, 384, 1536], P(None, 'win', 'ch'), may hold values from -0.00036621094 to 0.00036621094
- v_fc1: float32 [2, 384, 1536], P(None, 'win', 'ch'), may hold values from 6.348181e-10 to 2.5392723e-09
- w_fc2: float32 [2, 1536, 384], P(None, 'ch', 'win'), may hold values from -0.15625 to 0.15625
- m_fc2: float32 [2, 1536, 384], P(None, 'ch', 'win'), may hold values from -0.00036621094 to 0.00036621094
- v_fc2: float32 [2, 1536, 384], P(None, 'ch', 'win'), may hold values from 6.348181e-10 to 2.5392723e-09
- w_head: float32 [384, 1000], P('win', 'ch'), may hold values from -0.3125 to 0.3125
- m_head: float32 [384, 1000], P('win', 'ch'), may hold values from -0.00036621094 to 0.00036621094
- v_head: float32 [384, 1000], P('win', 'ch'), may hold values from 6.348181e-10 to 2.5392723e-09
- vectors: float32 [29, 384], replicated, as said below
- m_vec: float32 [29, 384], replicated, may hold values from -0.00036621094 to 0.00036621094
- v_vec: float32 [29, 384], replicated, may hold values from 6.348181e-10 to 2.5392723e-09
- rel_table: float32 [2, 169, 12], replicated, may hold values from -3 to 3
- m_rel: float32 [2, 169, 12], replicated, may hold values from -2.2888184e-05 to 2.2888184e-05
- v_rel: float32 [2, 169, 12], replicated, may hold values from 1.015709e-12 to 4.062836e-12
Outputs:
- loss_total: float32 [], replicated
- grad_norm: float32 [], replicated
- qkv_first: float32 [2, 384, 1152], P(None, 'win', 'ch')
- qkv_second: float32 [2, 384, 1152], P(None, 'win', 'ch')
- qkv_weight: float32 [2, 384, 1152], P(None, 'win', 'ch')
- proj_first: float32 [2, 384, 384], P(None, 'win', 'ch')
- proj_second: float32 [2, 384, 384], P(None, 'win', 'ch')
- proj_weight: float32 [2, 384, 384], P(None, 'win', 'ch')
- expand_first: float32 [2, 384, 1536], P(None, 'win', 'ch')
- expand_second: float32 [2, 384, 1536], P(None, 'win', 'ch')
- expand_weight: float32 [2, 384, 1536], P(None, 'win', 'ch')
- reduce_first: float32 [2, 1536, 384], P(None, 'ch', 'win')
- reduce_second: float32 [2, 1536, 384], P(None, 'ch', 'win')
- reduce_weight: float32 [2, 1536, 384], P(None, 'ch', 'win')
- head_first: float32 [384, 1000], P('win', 'ch')
- head_second: float32 [384, 1000], P('win', 'ch')
- head_weight: float32 [384, 1000], P('win', 'ch')
- vector_first: float32 [29, 384], replicated
- vector_second: float32 [29, 384], replicated
- vector_weight: float32 [29, 384], replicated
- table_first: float32 [2, 169, 12], replicated
- table_second: float32 [2, 169, 12], replicated
- table_weight: float32 [2, 169, 12], replicated
The draws below stay inside these ranges and needn't reach their ends.
Inputs may be any that keep to these rules, and one draw needn't show every extreme that they name: `valid_rows`: padding rows are the image's last ones. `valid_cols`: padding columns are the image's last ones. `vectors`: gains lie near one, biases near zero.
All inputs are finite; a program needn't handle non-finite values.
Results may differ from the reference program's by a relative error of at most 0.024.
Values may be sent and summed in bfloat16 or wider, within the bound.
No kernel may reach another device: no remote copies, remote signals or barrier semaphores. Data moves between devices by JAX's collectives and lax.ppermute only.
A program may use at most 256 MiB of HBM per device.

```python
import math
import jax
import jax.numpy as jnp
from jax import lax

C = 384
HEADS = 12
HID = 1536
CLASSES = 1000
WSIDE = 7
GRID = 14
L = 2
MICRO = 2
STEP = 10
IMAGES = 64
RREL = 169
VROWS = 29
NPARAM = 3938136


def draw_vectors(key, part):
    key = jax.random.fold_in(key, 7)
    per_layer = 8 + HID // C
    index = jnp.arange(VROWS, dtype=jnp.int32)
    within = index % per_layer
    is_gain = (index < L * per_layer) & ((within == 0) | (within == 5)) | (index == L * per_layer)
    noise = jnp.clip(0.25 * jax.random.normal(key, (VROWS, C), jnp.float32), -0.6, 0.6)
    return jnp.where(is_gain[:, None], 1.0 + noise, noise)


def touch_ends(drawn, own_key, smallest, high):
    index_at = [jax.random.randint(jax.random.fold_in(own_key, axis), (), 0, length) for axis, length in enumerate(drawn.shape)]
    widest = drawn.shape.index(max(drawn.shape))
    next_to = index_at[:widest] + [(index_at[widest] + 1) % drawn.shape[widest]] + index_at[widest + 1:]
    return drawn.at[tuple(index_at)].set(smallest).at[tuple(next_to)].set(high)


def steps_of(own_key, extent, pieces, least, largest):
    def one(dim, shards_of):
        heights = jax.random.uniform(jax.random.fold_in(jax.random.fold_in(own_key, 6), dim), (shards_of,), jnp.float32, least / len(pieces), largest / len(pieces))
        return jnp.repeat(jnp.exp(heights), extent[dim] // shards_of).reshape((-1,) + (1,) * (len(extent) - dim - 1))

    level = one(*pieces[0])
    for cut in pieces[1:]:
        level = level * one(*cut)
    return level


def gaussian(key, dims, scale, reach, shards=(), kind=jnp.bfloat16):
    entries = jax.random.normal(key, dims, jnp.float32) * scale
    if len(shards) > 0:
        entries = steps_of(key, dims, shards, -0.22, 0.18) * entries
    return jnp.clip(entries, min=-reach, max=reach).astype(kind)


def setup_inputs(seed: int = 0) -> dict:
    key_of = jax.random.split(jax.random.key(seed), 28)
    tokens = gaussian(key_of[0], (MICRO, IMAGES, GRID * GRID, C), 1.0, 6.0, ((1, 32),))
    valid_rows = touch_ends(jax.random.randint(key_of[1], (MICRO, IMAGES), WSIDE, GRID + 1), jax.random.fold_in(key_of[1], 1), WSIDE, GRID).astype(jnp.int32)
    valid_cols = touch_ends(jax.random.randint(key_of[2], (MICRO, IMAGES), WSIDE, GRID + 1), jax.random.fold_in(key_of[2], 1), WSIDE, GRID).astype(jnp.int32)
    partner = touch_ends(jax.random.randint(key_of[3], (MICRO, IMAGES), 0, IMAGES), jax.random.fold_in(key_of[3], 1), 0, IMAGES - 1).astype(jnp.int32)
    mix_level = touch_ends(jax.random.randint(key_of[4], (MICRO, IMAGES), 1, 16), jax.random.fold_in(key_of[4], 1), 1, 15).astype(jnp.int32)
    labels = touch_ends(jax.random.randint(key_of[5], (MICRO, IMAGES), 0, CLASSES), jax.random.fold_in(key_of[5], 1), 0, CLASSES - 1).astype(jnp.int32)
    w_qkv = gaussian(key_of[6], (L, C, 3 * C), C ** -0.5, 0.3125, ((1, 8), (2, 4)), jnp.float32)
    m_qkv = gaussian(key_of[7], (L, C, 3 * C), (0.05 / NPARAM ** 0.5), 0.00036621094, ((1, 8), (2, 4)), jnp.float32)
    v_qkv = jnp.clip(jnp.exp(math.log(2.539272347945598e-09) - 1.3862944 * jax.random.uniform(key_of[8], (L, C, 3 * C), jnp.float32) ** steps_of(key_of[8], (L, C, 3 * C), ((1, 8), (2, 4)), -0.2, 0.2)), 6.348180869863995e-10, 2.539272347945598e-09)
    w_proj = gaussian(key_of[9], (L, C, C), (C // WSIDE) ** -0.5, 0.875, ((1, 8), (2, 4)), jnp.float32)
    m_proj = gaussian(key_of[10], (L, C, C), (0.05 / NPARAM ** 0.5), 0.00036621094, ((1, 8), (2, 4)), jnp.float32)
    v_proj = jnp.clip(jnp.exp(math.log(2.539272347945598e-09) - 1.3862944 * jax.random.uniform(key_of[11], (L, C, C), jnp.float32) ** steps_of(key_of[11], (L, C, C), ((1, 8), (2, 4)), -0.2, 0.2)), 6.348180869863995e-10, 2.539272347945598e-09)
    w_fc1 = gaussian(key_of[12], (L, C, HID), C ** -0.5, 0.3125, ((1, 8), (2, 4)), jnp.float32)
    m_fc1 = gaussian(key_of[13], (L, C, HID), (0.05 / NPARAM ** 0.5), 0.00036621094, ((1, 8), (2, 4)), jnp.float32)
    v_fc1 = jnp.clip(jnp.exp(math.log(2.539272347945598e-09) - 1.3862944 * jax.random.uniform(key_of[14], (L, C, HID), jnp.float32) ** steps_of(key_of[14], (L, C, HID), ((1, 8), (2, 4)), -0.2, 0.2)), 6.348180869863995e-10, 2.539272347945598e-09)
    w_fc2 = gaussian(key_of[15], (L, HID, C), HID ** -0.5, 0.15625, ((1, 4), (2, 8)), jnp.float32)
    m_fc2 = gaussian(key_of[16], (L, HID, C), (0.05 / NPARAM ** 0.5), 0.00036621094, ((1, 4), (2, 8)), jnp.float32)
    v_fc2 = jnp.clip(jnp.exp(math.log(2.539272347945598e-09) - 1.3862944 * jax.random.uniform(key_of[17], (L, HID, C), jnp.float32) ** steps_of(key_of[17], (L, HID, C), ((1, 4), (2, 8)), -0.2, 0.2)), 6.348180869863995e-10, 2.539272347945598e-09)
    w_head = gaussian(key_of[18], (C, CLASSES), C ** -0.5, 0.3125, ((0, 8), (1, 4)), jnp.float32)
    m_head = gaussian(key_of[19], (C, CLASSES), (0.05 / NPARAM ** 0.5), 0.00036621094, ((0, 8), (1, 4)), jnp.float32)
    v_head = jnp.clip(jnp.exp(math.log(2.539272347945598e-09) - 1.3862944 * jax.random.uniform(key_of[20], (C, CLASSES), jnp.float32) ** steps_of(key_of[20], (C, CLASSES), ((0, 8), (1, 4)), -0.2, 0.2)), 6.348180869863995e-10, 2.539272347945598e-09)
    vectors = draw_vectors(jax.random.fold_in(key_of[27], 71), 0)
    m_vec = gaussian(key_of[22], (VROWS, C), (0.05 / NPARAM ** 0.5), 0.00036621094, (), jnp.float32)
    v_vec = jnp.clip(jnp.exp(jax.random.uniform(key_of[23], (VROWS, C), jnp.float32, math.log(6.348180869863995e-10), math.log(2.539272347945598e-09))), 6.348180869863995e-10, 2.539272347945598e-09)
    rel_table = gaussian(key_of[24], (L, RREL, HEADS), 0.5, 3.0, (), jnp.float32)
    m_rel = gaussian(key_of[25], (L, RREL, HEADS), (0.003 / NPARAM ** 0.5), 2.288818359375e-05, (), jnp.float32)
    v_rel = jnp.clip(jnp.exp(jax.random.uniform(key_of[26], (L, RREL, HEADS), jnp.float32, math.log(1.0157090012813397e-12), math.log(4.062836005125359e-12))), 1.0157090012813397e-12, 4.062836005125359e-12)
    return dict(tokens=tokens, valid_rows=valid_rows, valid_cols=valid_cols, partner=partner, mix_level=mix_level, labels=labels, w_qkv=w_qkv, m_qkv=m_qkv, v_qkv=v_qkv, w_proj=w_proj, m_proj=m_proj, v_proj=v_proj, w_fc1=w_fc1, m_fc1=m_fc1, v_fc1=v_fc1, w_fc2=w_fc2, m_fc2=m_fc2, v_fc2=v_fc2, w_head=w_head, m_head=m_head, v_head=v_head, vectors=vectors, m_vec=m_vec, v_vec=v_vec, rel_table=rel_table, m_rel=m_rel, v_rel=v_rel)


HIGH = lax.Precision.HIGHEST
NORM_EPS = 1e-05
CLIP_NORM = 0.05
LEARN_RATE = 0.04
SMALL_RATE = 0.2
DECAY_RATE = 0.05
ADAM_EPS = 1e-08
MASKED = -1e+30

@jax.custom_vjp
def low(v):
    return lax.optimization_barrier(v.astype(jnp.bfloat16)).astype(jnp.float32)

@jax.custom_vjp
def low_back(v):
    return v

def low_keep(v):
    return (low(v), None)

def low_pass(kept, grad):
    return (grad,)

def back_keep(v):
    return (v, None)

def back_low(kept, grad):
    return (low(grad),)
low.defvjp(low_keep, low_pass)
low_back.defvjp(back_keep, back_low)

def layer_norm(field, gain, offset):
    average = lax.optimization_barrier(jnp.mean(field, -1, keepdims=True))
    centered = field - average
    spread = lax.optimization_barrier(jnp.mean(centered * centered, -1, keepdims=True))
    return centered * lax.rsqrt(spread + NORM_EPS) * gain + offset

def window_split(field, images, grid, side, shifted):
    chans = field.shape[-1]
    count = grid // side
    field = field.reshape(images, grid, grid, chans)
    if shifted:
        field = jnp.roll(field, (-(side // 2), -(side // 2)), (1, 2))
    field = field.reshape(images, count, side, count, side, chans).transpose(0, 1, 3, 2, 4, 5)
    return field.reshape(images * count * count, side * side, chans)

def window_join(field, images, grid, side, shifted):
    chans = field.shape[-1]
    count = grid // side
    field = field.reshape(images, count, count, side, side, chans).transpose(0, 1, 3, 2, 4, 5)
    field = field.reshape(images, grid, grid, chans)
    if shifted:
        field = jnp.roll(field, (side // 2, side // 2), (1, 2))
    return field.reshape(images * grid * grid, chans)

def inside_map(valid_rows, valid_cols, grid):
    coord = jnp.arange(grid, dtype=jnp.int32)
    inside = (coord[None, :, None] < valid_rows[:, None, None]) & (coord[None, None, :] < valid_cols[:, None, None])
    return inside.astype(jnp.float32).reshape(valid_rows.shape[0], grid * grid)

def allowed_mask(inside, grid, side, shifted):
    images = inside.shape[0]
    area = side * side
    key_inside = window_split(inside[:, :, None], images, grid, side, shifted)[:, :, 0]
    own = jnp.eye(area, dtype=bool)
    allowed = (key_inside[:, None, :] > 0.5) | own[None]
    if shifted:
        coord = jnp.arange(grid, dtype=jnp.int32)
        band = (coord >= grid - side).astype(jnp.int32) + (coord >= grid - side // 2).astype(jnp.int32)
        region = (3 * band[:, None] + band[None, :]).astype(jnp.float32).reshape(1, grid * grid, 1)
        region = window_split(region, 1, grid, side, False)[:, :, 0]
        region = jnp.tile(region, (images, 1))
        allowed = allowed & (region[:, :, None] == region[:, None, :])
    return allowed

def relative_onehot(side):
    span = 2 * side - 1
    place = jnp.arange(side * side, dtype=jnp.int32)
    place_row = place // side
    place_col = place % side
    index = (place_row[:, None] - place_row[None, :] + side - 1) * span + place_col[:, None] - place_col[None, :] + side - 1
    return (index.reshape(-1, 1) == jnp.arange(span * span, dtype=jnp.int32)[None, :]).astype(jnp.float32)

def adam_step(weight, grad, first, second, rate):
    new_first = 0.5 * first + 0.5 * grad
    new_second = 0.5 * second + 0.5 * grad * grad
    fix = 1.0 - 0.5 ** STEP
    update = new_first / fix / (jnp.sqrt(new_second / fix) + ADAM_EPS)
    return (new_first, new_second, weight - rate * (update + DECAY_RATE * weight))

def objective(params, field, rows, cols, own, other, mixing, total_images):
    qkv_w, proj_w, up_w, down_w, head_w = [low(item) for item in params[:5]]
    vec = params[5]
    table = params[6]
    images = rows.shape[0]
    cells = GRID * GRID
    area = WSIDE * WSIDE
    depth = C // HEADS
    scale = depth ** (-0.5)
    per_layer = 8 + HID // C
    onehot = relative_onehot(WSIDE)
    inside = inside_map(rows, cols, GRID)
    for layer in range(L):
        shifted = layer % 2 == 1
        allowed = allowed_mask(inside, GRID, WSIDE, shifted)
        small = vec[layer * per_layer:layer * per_layer + 8]
        fc_bias = vec[layer * per_layer + 8:(layer + 1) * per_layer].reshape(HID)
        normed = low(layer_norm(field, small[0], small[1]))
        qkv_bias = jnp.concatenate([small[2], jnp.zeros_like(small[2]), small[3]])
        qkv = low(low_back(jnp.dot(normed, qkv_w[layer], precision=HIGH) + qkv_bias))
        parts = window_split(qkv, images, GRID, WSIDE, shifted)
        windows = parts.shape[0]
        queries = parts[:, :, :C].reshape(windows, area, HEADS, depth)
        keys = parts[:, :, C:2 * C].reshape(windows, area, HEADS, depth)
        values = parts[:, :, 2 * C:].reshape(windows, area, HEADS, depth)
        raw = low_back(jnp.einsum('wihd,wjhd->whij', queries, keys, precision=HIGH) * scale)
        table_bias = jnp.dot(onehot, table[layer], precision=HIGH).reshape(area, area, HEADS).transpose(2, 0, 1)
        scores = jnp.where(allowed[:, None], raw + table_bias[None], MASKED)
        top = lax.optimization_barrier(jnp.max(scores, -1, keepdims=True))
        expo = jnp.exp(scores - top)
        probs = expo / lax.optimization_barrier(jnp.sum(expo, -1, keepdims=True))
        mixed = jnp.einsum('whij,wjhd->wihd', low(probs), values, precision=HIGH)
        attended = low(low_back(window_join(mixed.reshape(windows, area, C), images, GRID, WSIDE, shifted)))
        middle = field + low_back(jnp.dot(attended, proj_w[layer], precision=HIGH) + small[4])
        normed_two = low(layer_norm(middle, small[5], small[6]))
        pre = low_back(jnp.dot(normed_two, up_w[layer], precision=HIGH) + fc_bias)
        active = low(jax.nn.gelu(pre, approximate=False))
        field = middle + low_back(jnp.dot(active, down_w[layer], precision=HIGH) + small[7])
    base = L * per_layer
    final = layer_norm(field, vec[base], vec[base + 1]).reshape(images, cells, C)
    counts = (rows * cols).astype(jnp.float32)
    pooled = lax.optimization_barrier(jnp.sum(final * inside[:, :, None], 1)) / counts[:, None]
    head_bias = vec[base + 2:].reshape(-1)[:CLASSES]
    logits = low_back(jnp.dot(low(pooled), head_w, precision=HIGH) + head_bias)
    top = lax.optimization_barrier(jnp.max(logits, -1, keepdims=True))
    log_probs = logits - top - jnp.log(lax.optimization_barrier(jnp.sum(jnp.exp(logits - top), -1, keepdims=True)))
    class_ids = jnp.arange(CLASSES, dtype=jnp.int32)
    target = mixing[:, None] * (own[:, None] == class_ids[None]).astype(jnp.float32)
    target = target + (1.0 - mixing)[:, None] * (other[:, None] == class_ids[None]).astype(jnp.float32)
    total = -jnp.sum(target * log_probs)
    return (total / total_images, total)

def reference(tokens, valid_rows, valid_cols, partner, mix_level, labels, w_qkv, m_qkv, v_qkv, w_proj, m_proj, v_proj, w_fc1, m_fc1, v_fc1, w_fc2, m_fc2, v_fc2, w_head, m_head, v_head, vectors, m_vec, v_vec, rel_table, m_rel, v_rel):
    all_images = labels.shape[1]
    total_images = MICRO * all_images
    group = 16
    steps_count = total_images // group
    cells = GRID * GRID
    other_all = jnp.take_along_axis(labels, partner, 1)
    mixing_all = mix_level.astype(jnp.float32) / 16.0
    params = (w_qkv, w_proj, w_fc1, w_fc2, w_head, vectors, rel_table)
    items = (tokens.reshape(steps_count, group * cells, C), valid_rows.reshape(steps_count, group), valid_cols.reshape(steps_count, group), labels.reshape(steps_count, group), other_all.reshape(steps_count, group), mixing_all.reshape(steps_count, group))

    def group_step(carry, item):
        grads, loss_sum = carry
        field, rows, cols, own, other, mixing = item

        def run(values):
            return objective(values, field.astype(jnp.float32), rows, cols, own, other, mixing, total_images)
        value, pull, total = jax.vjp(run, params, has_aux=True)
        grads_now = pull(jnp.ones_like(value))[0]
        return ((jax.tree.map(jnp.add, grads, grads_now), loss_sum + total), None)
    zeros = jax.tree.map(jnp.zeros_like, params)
    (grads, loss_total), _ = lax.scan(group_step, (zeros, jnp.zeros((), jnp.float32)), items)
    square_sum = jnp.zeros((), jnp.float32)
    for grad in grads:
        square_sum = square_sum + jnp.sum(grad * grad)
    grad_norm = jnp.sqrt(square_sum)
    factor = CLIP_NORM / jnp.maximum(grad_norm, CLIP_NORM)
    qkv_first, qkv_second, qkv_weight = adam_step(w_qkv, factor * grads[0], m_qkv, v_qkv, LEARN_RATE)
    proj_first, proj_second, proj_weight = adam_step(w_proj, factor * grads[1], m_proj, v_proj, LEARN_RATE)
    expand_first, expand_second, expand_weight = adam_step(w_fc1, factor * grads[2], m_fc1, v_fc1, LEARN_RATE)
    reduce_first, reduce_second, reduce_weight = adam_step(w_fc2, factor * grads[3], m_fc2, v_fc2, LEARN_RATE)
    head_first, head_second, head_weight = adam_step(w_head, factor * grads[4], m_head, v_head, LEARN_RATE)
    vector_first, vector_second, vector_weight = adam_step(vectors, factor * grads[5], m_vec, v_vec, SMALL_RATE)
    table_first, table_second, table_weight = adam_step(rel_table, factor * grads[6], m_rel, v_rel, SMALL_RATE)
    return (loss_total, grad_norm, qkv_first, qkv_second, qkv_weight, proj_first, proj_second, proj_weight, expand_first, expand_second, expand_weight, reduce_first, reduce_second, reduce_weight, head_first, head_second, head_weight, vector_first, vector_second, vector_weight, table_first, table_second, table_weight)
```

```python
import functools

import jax
import jax.numpy as jnp
import numpy as np
from jax import lax
from jax.experimental import pallas as pl
from jax.experimental.pallas import tpu as pltpu
from jax.sharding import PartitionSpec as P

C = 384
HID = 1536
CLASSES = 1000
CLASS_PAD = 1024
WSIDE = 7
GRID = 14
STEP = 10
HEADS = 12
DEPTH = 32
CELLS = GRID * GRID
ROWS = 208
AREA = WSIDE * WSIDE
SLOT = 64
NWIN = 4
NGRP = 3
PACK = 4
WROWS = NWIN * SLOT
LANES = PACK * SLOT

NORM_EPS = 1e-05
CLIP_NORM = 0.05
LEARN_RATE = 0.04
SMALL_RATE = 0.2
DECAY_RATE = 0.05
ADAM_EPS = 1e-08
MASKED = -1e30
SCALE = DEPTH ** (-0.5)
F32 = jnp.float32
BF16 = jnp.bfloat16
NN = (((1,), (0,)), ((), ()))
NT = (((1,), (1,)), ((), ()))
TN = (((0,), (0,)), ((), ()))
VMEM_LIMIT = 58 * 1024 * 1024


def dot(a, b, dims=NN):
    return lax.dot_general(a, b, dims, preferred_element_type=F32)


@functools.lru_cache(None)
def window_tables(shifted):
    perm = np.zeros((WROWS, ROWS), np.float32)
    row_limit = np.full((NWIN, SLOT, 2 * SLOT), 99, np.int32)
    col_limit = np.full((NWIN, SLOT, 2 * SLOT), 99, np.int32)
    shift = WSIDE // 2 if shifted else 0

    def band(v):
        return 0 if v < GRID - WSIDE else (1 if v < GRID - WSIDE // 2 else 2)

    for window in range(NWIN):
        wr, wc = divmod(window, GRID // WSIDE)
        place = []
        for j in range(AREA):
            r, c = wr * WSIDE + j // WSIDE, wc * WSIDE + j % WSIDE
            region = 3 * band(r) + band(c) if shifted else 0
            source = ((r + shift) % GRID, (c + shift) % GRID)
            place.append((region, source))
            perm[window * SLOT + j, source[0] * GRID + source[1]] = 1
        for j in range(SLOT):
            for i in range(SLOT):
                if i == j:
                    pair = (-1, -1)
                elif i < AREA and j < AREA and place[i][0] == place[j][0]:
                    pair = place[j][1]
                else:
                    pair = (99, 99)
                row_limit[window, j, i::SLOT] = pair[0]
                col_limit[window, j, i::SLOT] = pair[1]
    return perm, row_limit, col_limit


@functools.lru_cache(None)
def relative_onehot():
    span = 2 * WSIDE - 1
    place = np.arange(AREA)
    row, col = place // WSIDE, place % WSIDE
    index = (row[:, None] - row[None] + WSIDE - 1) * span + col[:, None] - col[None] + WSIDE - 1
    onehot = np.zeros((SLOT, SLOT, span * span), np.float32)
    for i in range(AREA):
        for j in range(AREA):
            onehot[j, i, index[i, j]] = 1
    return onehot.reshape(SLOT * SLOT, span * span)


def norm_parts(field):
    average = jnp.mean(field, -1, keepdims=True)
    centered = field - average
    spread = jnp.mean(centered * centered, -1, keepdims=True)
    rate = lax.rsqrt(spread + NORM_EPS)
    return centered * rate, rate


def norm_back(grad, hat, rate, gain):
    scaled = grad * gain
    return rate * (
        scaled
        - jnp.mean(scaled, -1, keepdims=True)
        - hat * jnp.mean(scaled * hat, -1, keepdims=True)
    )


def col_sum(field):
    return jnp.sum(field, 0, keepdims=True)


def head_masks(dtype):
    lane = lax.broadcasted_iota(jnp.int32, (SLOT, 128), 1)
    return [((lane // DEPTH) == h).astype(F32).astype(dtype) for h in range(PACK)]


def spread_heads(block, masks):
    return jnp.concatenate([block * m for m in masks], 0)


def fold_heads(full, masks):
    total = full[:SLOT] * masks[0]
    for h in range(1, PACK):
        total = total + full[h * SLOT : (h + 1) * SLOT] * masks[h]
    return total


def forward_layer(
    field, rows, cols, weights, consts, small, qkv_bias, up_bias, qkv_ref, prob_ref, mixed_ref
):
    w_qkv, w_proj, w_up, w_down = weights
    perm, perm_t, row_limit, col_limit, bias = consts
    hat, _ = norm_parts(field)
    normed = (hat * small[0:1] + small[1:2]).astype(BF16)
    windowed = dot(perm[...], normed).astype(BF16)
    qkv_ref[...] = (dot(windowed, w_qkv[...]) + qkv_bias[...]).astype(BF16)
    low_masks = head_masks(BF16)
    masks = head_masks(F32)

    def window_step(w, carry):
        at = pl.ds(pl.multiple_of(w * SLOT, SLOT), SLOT)
        allowed = (row_limit[w] < rows) & (col_limit[w] < cols)
        block = jnp.where(allowed, 0.0, MASKED).astype(F32)
        block = jnp.concatenate([block, block], 1)
        for g in range(NGRP):
            query = qkv_ref[at, g * 128 : (g + 1) * 128]
            key = qkv_ref[at, C + g * 128 : C + (g + 1) * 128]
            value = qkv_ref[at, 2 * C + g * 128 : 2 * C + (g + 1) * 128]
            score = dot(key, spread_heads(query, low_masks), NT) * SCALE + bias[g] + block
            top = jnp.max(score, 0, keepdims=True)
            expo = jnp.exp(score - top)
            prob = (expo / jnp.sum(expo, 0, keepdims=True)).astype(BF16)
            prob_ref[w, g] = prob
            mixed_ref[at, g * 128 : (g + 1) * 128] = fold_heads(dot(prob, value, TN), masks).astype(
                BF16
            )
        return carry

    lax.fori_loop(0, NWIN, window_step, 0)
    attended = dot(perm_t[...], mixed_ref[...]).astype(BF16)
    middle = field + dot(attended, w_proj[...]) + small[4:5]
    hat, _ = norm_parts(middle)
    mlp_in = (hat * small[5:6] + small[6:7]).astype(BF16)
    return normed, attended, middle, mlp_in


def forward_mlp(middle, mlp_in, weights, small, up_bias, active_ref, slope_ref):
    _, _, w_up, w_down = weights
    branch = jnp.zeros((ROWS, C), F32)
    width = 512
    for part in range(HID // width):
        at = slice(part * width, (part + 1) * width)
        pre = dot(mlp_in, w_up[:, at]) + up_bias[:, at]
        half = 0.5 * (1.0 + lax.erf(pre * (0.5**0.5)))
        active = (pre * half).astype(BF16)
        slope = half + pre * (jnp.exp(-0.5 * pre * pre) * ((2.0 * np.pi) ** -0.5))
        active_ref[:, at] = active
        slope_ref[:, at] = slope.astype(BF16)
        branch = branch + dot(active, w_down[:, at], NT)
    return middle + branch + small[7:8]


def backward_layer(
    grad,
    field,
    middle,
    qkv_ref,
    prob_ref,
    slope_ref,
    weights,
    consts,
    small,
    spread_ref,
    dqkv_ref,
    low_ref,
    attn_ref,
    pre_ref,
    joined_ref,
    rows_ref,
    up_rows_ref,
    qkv_rows_ref,
    bias_grad_ref,
    place,
):
    w_qkv, w_proj, w_up, w_down = weights
    perm, perm_t, _, _, _ = consts
    low = grad.astype(BF16)
    low_ref[place, :] = low
    rows_ref[7:8, :] += col_sum(low.astype(F32))
    normed_grad = jnp.zeros((ROWS, C), F32)
    width = 512
    for part in range(HID // width):
        at = slice(part * width, (part + 1) * width)
        pre = (dot(low, w_down[:, at]) * slope_ref[:, at].astype(F32)).astype(BF16)
        pre_ref[place, at] = pre
        up_rows_ref[:, at] += col_sum(pre.astype(F32))
        normed_grad = normed_grad + dot(pre, w_up[:, at], NT)
    hat, rate = norm_parts(middle)
    rows_ref[5:6, :] += col_sum(normed_grad * hat)
    rows_ref[6:7, :] += col_sum(normed_grad)
    grad_mid = norm_back(normed_grad, hat, rate, small[5:6]) + grad
    attn = grad_mid.astype(BF16)
    attn_ref[place, :] = attn
    rows_ref[4:5, :] += col_sum(attn.astype(F32))
    joined = dot(attn, w_proj[...], NT).astype(BF16)
    joined_ref[...] = dot(perm[...], joined).astype(BF16)
    low_masks = head_masks(BF16)
    masks = head_masks(F32)

    def window_step(w, carry):
        at = pl.ds(pl.multiple_of(w * SLOT, SLOT), SLOT)
        for g in range(NGRP):
            cut = [slice(n * C + g * 128, n * C + (g + 1) * 128) for n in range(3)]
            query = spread_heads(qkv_ref[at, cut[0]], low_masks)
            key = qkv_ref[at, cut[1]]
            value = qkv_ref[at, cut[2]]
            out = spread_heads(joined_ref[at, cut[0]], low_masks)
            prob = prob_ref[w, g]
            wide = prob.astype(F32)
            prob_grad = dot(value, out, NT)
            score = wide * (prob_grad - jnp.sum(wide * prob_grad, 0, keepdims=True))
            bias_grad_ref[g] += score
            score = score.astype(BF16)
            dqkv_ref[at, cut[2]] = dot(prob, out).astype(BF16)
            dqkv_ref[at, cut[1]] = (dot(score, query) * SCALE).astype(BF16)
            dqkv_ref[at, cut[0]] = (fold_heads(dot(score, key, TN), masks) * SCALE).astype(BF16)
        return carry

    lax.fori_loop(0, NWIN, window_step, 0)
    back = dot(perm_t[...], dqkv_ref[...]).astype(BF16)
    spread_ref[place, :] = back
    qkv_rows_ref[...] += col_sum(back.astype(F32))
    normed_grad = dot(back, w_qkv[...], NT)
    hat, rate = norm_parts(field)
    rows_ref[0:1, :] += col_sum(normed_grad * hat)
    rows_ref[1:2, :] += col_sum(normed_grad)
    return norm_back(normed_grad, hat, rate, small[0:1]) + grad_mid


def write_grads(out_ref, normed_ref, spread_ref, attended_ref, attn_ref, mlp_ref, pre_ref, low_ref, active_ref):
    owners = out_ref.shape[0]
    start = 0
    for left, right in (
        (normed_ref, spread_ref),
        (attended_ref, attn_ref),
        (mlp_ref, pre_ref),
        (low_ref, active_ref),
    ):
        total = dot(left[...], right[...], TN).astype(BF16)
        width = total.shape[1] // owners
        for owner in range(owners):
            out_ref[owner, :, start : start + width] = total[:, owner * width : (owner + 1) * width]
        start += width


def first_forward_kernel(
    rows_ref,
    cols_ref,
    tokens_ref,
    w_qkv,
    w_proj,
    w_up,
    w_down,
    perm,
    perm_t,
    row_limit,
    col_limit,
    bias,
    small_ref,
    qkv_bias,
    up_bias,
    result_ref,
    middle_ref,
    normed_ref,
    qkv_ref,
    prob_ref,
    attended_ref,
    mlp_ref,
    slope_ref,
    active_ref,
    mixed_ref,
):
    image = pl.program_id(0)
    weights = (w_qkv, w_proj, w_up, w_down)
    consts = (perm, perm_t, row_limit, col_limit, bias)
    small = small_ref[...]
    field = tokens_ref[...].astype(F32)
    normed, attended, middle, mlp_in = forward_layer(
        field, rows_ref[image], cols_ref[image], weights, consts, small, qkv_bias, up_bias,
        qkv_ref, prob_ref, mixed_ref,
    )
    normed_ref[...] = normed
    attended_ref[...] = attended
    middle_ref[...] = middle
    mlp_ref[...] = mlp_in
    result_ref[...] = forward_mlp(middle, mlp_in, weights, small, up_bias, active_ref, slope_ref)


def last_layer_kernel(
    rows_ref,
    cols_ref,
    own_ref,
    other_ref,
    mix_ref,
    field_ref,
    w_qkv,
    w_proj,
    w_up,
    w_down,
    w_head,
    perm,
    perm_t,
    row_limit,
    col_limit,
    bias,
    small_ref,
    qkv_bias,
    up_bias,
    final_ref,
    head_bias,
    cell_row,
    cell_col,
    grad_ref,
    weight_grad_ref,
    head_grad_ref,
    rows_out_ref,
    up_rows_ref,
    qkv_rows_ref,
    bias_grad_ref,
    final_rows_ref,
    head_rows_ref,
    loss_ref,
    mixed_ref,
    qkv_ref,
    prob_ref,
    slope_ref,
    dqkv_ref,
    joined_ref,
    middle_ref,
    normed_all,
    attended_all,
    mlp_all,
    active_all,
    spread_all,
    attn_all,
    pre_all,
    low_all,
    pooled_all,
    logit_all,
    *,
    total_images,
):
    image = pl.program_id(0)
    rows, cols = rows_ref[image], cols_ref[image]

    @pl.when(image == 0)
    def _():
        for ref in (rows_out_ref, up_rows_ref, qkv_rows_ref, bias_grad_ref, final_rows_ref,
                    head_rows_ref, loss_ref, pooled_all, logit_all):
            ref[...] = jnp.zeros(ref.shape, ref.dtype)

    place = pl.ds(pl.multiple_of(image * ROWS, 16), ROWS)
    weights = (w_qkv, w_proj, w_up, w_down)
    consts = (perm, perm_t, row_limit, col_limit, bias)
    small = small_ref[...]
    field = field_ref[...]
    normed, attended, middle, mlp_in = forward_layer(
        field, rows, cols, weights, consts, small, qkv_bias, up_bias, qkv_ref, prob_ref, mixed_ref
    )
    normed_all[place, :] = normed
    attended_all[place, :] = attended
    mlp_all[place, :] = mlp_in
    middle_ref[...] = middle
    result = forward_mlp(
        middle, mlp_in, weights, small, up_bias, active_all.at[place], slope_ref
    )
    hat, rate = norm_parts(result)
    inside = ((cell_row[...] < rows) & (cell_col[...] < cols)).astype(F32)
    share = inside / (rows * cols).astype(F32)
    final = hat * final_ref[0:1] + final_ref[1:2]
    pooled = col_sum(final * inside) / (rows * cols).astype(F32)
    pooled = jnp.broadcast_to(pooled, (16, C)).astype(BF16)
    logits = dot(pooled, w_head[...])[0:1] + head_bias[...]
    top = jnp.max(logits, -1, keepdims=True)
    expo = jnp.exp(logits - top)
    log_probs = logits - top - jnp.log(jnp.sum(expo, -1, keepdims=True))
    lane = lax.broadcasted_iota(jnp.int32, (1, CLASS_PAD), 1)
    mixing = mix_ref[image].astype(F32) / 16.0
    target = jnp.where(lane == own_ref[image], mixing, 0.0)
    target = target + jnp.where(lane == other_ref[image], 1.0 - mixing, 0.0)
    loss = jnp.sum(jnp.where(target > 0.0, target * log_probs, 0.0), -1, keepdims=True)
    loss_ref[...] -= jnp.broadcast_to(loss, loss_ref.shape)
    logit_grad = (jnp.exp(log_probs) - target) / total_images
    logit_low = jnp.broadcast_to(logit_grad, (16, CLASS_PAD)).astype(BF16)
    head_rows_ref[...] += logit_low[0:1].astype(F32)
    pooled_all[pl.ds(image, 1), :] = pooled[0:1].astype(F32)
    logit_all[pl.ds(image, 1), :] = logit_low[0:1].astype(F32)
    pooled_grad = dot(logit_low, w_head[...], NT)[0:1]
    final_grad = pooled_grad * share
    final_rows_ref[0:1, :] += col_sum(final_grad * hat)
    final_rows_ref[1:2, :] += col_sum(final_grad)
    grad = norm_back(final_grad, hat, rate, final_ref[0:1])
    grad_ref[...] = backward_layer(
        grad, field, middle_ref[...], qkv_ref, prob_ref, slope_ref, weights, consts, small,
        spread_all, dqkv_ref, low_all, attn_all, pre_all, joined_ref,
        rows_out_ref, up_rows_ref, qkv_rows_ref, bias_grad_ref, place,
    )

    @pl.when(image == pl.num_programs(0) - 1)
    def _():
        write_grads(weight_grad_ref, normed_all, spread_all, attended_all, attn_all, mlp_all,
                    pre_all, low_all, active_all)
        total = dot(pooled_all[...].astype(BF16), logit_all[...].astype(BF16), TN).astype(BF16)
        owners = head_grad_ref.shape[0]
        width = CLASSES // owners
        for owner in range(owners):
            head_grad_ref[owner, :, :width] = total[:, owner * width : (owner + 1) * width]
            head_grad_ref[owner, :, width:] = jnp.zeros(
                (C, head_grad_ref.shape[2] - width), BF16
            )


def first_backward_kernel(
    grad_ref,
    tokens_ref,
    middle_ref,
    normed_ref,
    qkv_ref,
    prob_ref,
    attended_ref,
    mlp_ref,
    slope_ref,
    active_ref,
    w_qkv,
    w_proj,
    w_up,
    w_down,
    perm,
    perm_t,
    small_ref,
    weight_grad_ref,
    rows_out_ref,
    up_rows_ref,
    qkv_rows_ref,
    bias_grad_ref,
    dqkv_ref,
    joined_ref,
    normed_all,
    attended_all,
    mlp_all,
    active_all,
    spread_all,
    attn_all,
    pre_all,
    low_all,
):
    image = pl.program_id(0)

    @pl.when(image == 0)
    def _():
        for ref in (rows_out_ref, up_rows_ref, qkv_rows_ref, bias_grad_ref):
            ref[...] = jnp.zeros(ref.shape, ref.dtype)

    place = pl.ds(pl.multiple_of(image * ROWS, 16), ROWS)
    normed_all[place, :] = normed_ref[...]
    attended_all[place, :] = attended_ref[...]
    mlp_all[place, :] = mlp_ref[...]
    active_all[place, :] = active_ref[...]
    backward_layer(
        grad_ref[...], tokens_ref[...].astype(F32), middle_ref[...], qkv_ref, prob_ref, slope_ref,
        (w_qkv, w_proj, w_up, w_down), (perm, perm_t, None, None, None), small_ref[...],
        spread_all, dqkv_ref, low_all, attn_all, pre_all, joined_ref,
        rows_out_ref, up_rows_ref, qkv_rows_ref, bias_grad_ref, place,
    )

    @pl.when(image == pl.num_programs(0) - 1)
    def _():
        write_grads(weight_grad_ref, normed_all, spread_all, attended_all, attn_all, mlp_all,
                    pre_all, low_all, active_all)


def whole(shape):
    return pl.BlockSpec(shape, lambda i: (0,) * len(shape))


def per_image(*shape):
    return pl.BlockSpec((None,) + shape, lambda i: (i,) + (0,) * len(shape))


SCALARS = pl.BlockSpec(memory_space=pltpu.SMEM)
WEIGHT_SPECS = [whole((C, 3 * C)), whole((C, C)), whole((C, HID)), whole((C, HID))]


def params():
    return pltpu.CompilerParams(
        dimension_semantics=("arbitrary",), vmem_limit_bytes=VMEM_LIMIT
    )


def axis_perm(size, bit):
    return [(i, i ^ (1 << bit)) for i in range(size)]


def axis_bits(axis):
    return int(lax.axis_size(axis)).bit_length() - 1


def link_order():
    order = [("win", b) for b in reversed(range(axis_bits("win")))]
    return order + [("ch", b) for b in reversed(range(axis_bits("ch")))]


def my_bit(axis, bit):
    return (lax.axis_index(axis) >> bit) & 1


def gather_blocks(block):
    order = link_order()
    gathered = block
    for axis, bit in order:
        other = lax.ppermute(gathered, axis, axis_perm(lax.axis_size(axis), bit))
        mine = my_bit(axis, bit)
        gathered = jnp.where(
            mine == 0, jnp.stack([gathered, other]), jnp.stack([other, gathered])
        )
    count = len(order)
    places = {step: count - 1 - n for n, step in enumerate(order)}
    axes = [places[("win", b)] for b in reversed(range(axis_bits("win")))]
    axes += [places[("ch", b)] for b in reversed(range(axis_bits("ch")))]
    gathered = gathered.transpose(*axes, *range(count, gathered.ndim))
    return gathered.reshape(
        (lax.axis_size("win"), lax.axis_size("ch")) + block.shape
    )


def scatter_sum(blocks):
    order = link_order()[::-1]
    names = [("ch", b) for b in reversed(range(axis_bits("ch")))]
    names += [("win", b) for b in reversed(range(axis_bits("win")))]
    held = blocks.reshape((2,) * len(names) + blocks.shape[2:])
    for axis, bit in order:
        at = names.index((axis, bit))
        mine = my_bit(axis, bit)
        keep = lax.dynamic_index_in_dim(held, mine, at, False)
        send = lax.dynamic_index_in_dim(held, 1 - mine, at, False)
        other = lax.ppermute(send, axis, axis_perm(lax.axis_size(axis), bit))
        held = (keep.astype(F32) + other.astype(F32)).astype(BF16)
        names.pop(at)
    return held


def adam_step(weight, grad, first, second, rate):
    new_first = 0.5 * first + 0.5 * grad
    new_second = 0.5 * second + 0.5 * grad * grad
    fix = 1.0 - 0.5**STEP
    update = new_first / fix / (jnp.sqrt(new_second / fix) + ADAM_EPS)
    return (new_first, new_second, weight - rate * (update + DECAY_RATE * weight))


def per_device(
    tokens, valid_rows, valid_cols, partner, mix_level, labels,
    w_qkv, m_qkv, v_qkv, w_proj, m_proj, v_proj, w_fc1, m_fc1, v_fc1, w_fc2, m_fc2, v_fc2,
    w_head, m_head, v_head, vectors, m_vec, v_vec, rel_table, m_rel, v_rel,
):
    micro, images, cells, chans = tokens.shape
    layers = rel_table.shape[0]
    per_layer = 8 + HID // C
    base = layers * per_layer
    head_rows = vectors.shape[0] - base - 2
    all_images = labels.shape[1]
    total_images = micro * all_images
    local = micro * images
    ch_count = lax.axis_size("ch")
    ch_index = lax.axis_index("ch")

    def low(v):
        return v.astype(BF16)

    blocks = [
        jnp.concatenate(
            [low(w_qkv[l]), low(w_proj[l]), low(w_fc1[l]), low(w_fc2[l]).T], 1
        )
        for l in range(layers)
    ]
    gathered = [gather_blocks(block) for block in blocks]
    head_all = gather_blocks(low(w_head))
    cuts = np.cumsum([0, w_qkv.shape[2], w_proj.shape[2], w_fc1.shape[2], w_fc2.shape[1]])

    def assemble(block):
        return block.transpose(0, 2, 1, 3).reshape(C, -1)

    weights = [
        [assemble(full[..., cuts[n] : cuts[n + 1]]) for n in range(4)] for full in gathered
    ]
    head_full = jnp.pad(assemble(head_all), ((0, 0), (0, CLASS_PAD - CLASSES)))

    small = [vectors[l * per_layer : l * per_layer + 8] for l in range(layers)]
    up_bias = [
        vectors[l * per_layer + 8 : (l + 1) * per_layer].reshape(1, HID) for l in range(layers)
    ]
    qkv_bias = [
        jnp.concatenate([s[2], jnp.zeros_like(s[2]), s[3]]).reshape(1, 3 * C) for s in small
    ]
    final = vectors[base : base + 2]
    head_bias = jnp.concatenate(
        [
            vectors[base + 2 :].reshape(-1)[:CLASSES],
            jnp.full((CLASS_PAD - CLASSES,), MASKED, F32),
        ]
    ).reshape(1, CLASS_PAD)
    onehot = jnp.asarray(relative_onehot())
    bias = [
        jnp.dot(onehot, rel_table[l], precision=lax.Precision.HIGHEST)
        .reshape(SLOT, SLOT, NGRP, PACK)
        .transpose(2, 0, 3, 1)
        .reshape(NGRP, SLOT, LANES)
        for l in range(layers)
    ]
    tables = [window_tables(l % 2 == 1) for l in range(layers)]
    perms = [jnp.asarray(t[0], BF16) for t in tables]
    perms_t = [jnp.asarray(t[0].T, BF16) for t in tables]
    row_limits = [jnp.asarray(t[1]) for t in tables]
    col_limits = [jnp.asarray(t[2]) for t in tables]

    rows = valid_rows.reshape(local)
    cols = valid_cols.reshape(local)
    image_ids = (lax.axis_index("win") * ch_count + ch_index) * images + jnp.arange(
        images, dtype=jnp.int32
    )
    all_ids = jnp.arange(all_images, dtype=jnp.int32)
    own = jnp.sum(
        jnp.where(image_ids[None, :, None] == all_ids, labels[:, None, :], 0), -1
    ).reshape(local)
    other = jnp.sum(
        jnp.where(partner[:, :, None] == all_ids, labels[:, None, :], 0), -1
    ).reshape(local)
    mix = mix_level.reshape(local)
    padded = jnp.pad(tokens.reshape(local, cells, chans), ((0, 0), (0, ROWS - cells), (0, 0)))

    def shape(dims, dtype=F32):
        return jax.ShapeDtypeStruct(dims, dtype)

    const_specs = [
        whole((WROWS, ROWS)), whole((ROWS, WROWS)), whole((NWIN, SLOT, 128)),
        whole((NWIN, SLOT, 128)), whole((NGRP, SLOT, LANES)),
    ]
    vector_specs = [whole((8, C)), whole((1, 3 * C)), whole((1, HID))]
    saved_specs = [
        per_image(ROWS, C), per_image(ROWS, C), per_image(WROWS, 3 * C),
        per_image(NWIN, NGRP, SLOT, LANES), per_image(ROWS, C), per_image(ROWS, C),
        per_image(ROWS, HID), per_image(ROWS, HID),
    ]
    result, *saved = pl.pallas_call(
        first_forward_kernel,
        grid=(local,),
        in_specs=[SCALARS, SCALARS, per_image(ROWS, C)] + WEIGHT_SPECS + const_specs + vector_specs,
        out_specs=[per_image(ROWS, C)] + saved_specs,
        out_shape=[
            shape((local, ROWS, C)), shape((local, ROWS, C)), shape((local, ROWS, C), BF16),
            shape((local, WROWS, 3 * C), BF16), shape((local, NWIN, NGRP, SLOT, LANES), BF16),
            shape((local, ROWS, C), BF16), shape((local, ROWS, C), BF16),
            shape((local, ROWS, HID), BF16), shape((local, ROWS, HID), BF16),
        ],
        scratch_shapes=[pltpu.VMEM((WROWS, C), BF16)],
        compiler_params=params(),
        name="first_forward",
    )(rows, cols, padded, *weights[0], perms[0], perms_t[0], row_limits[0], col_limits[0], bias[0],
      small[0], qkv_bias[0], up_bias[0])

    grad_cols = int(cuts[-1])
    head_cols = -(-(CLASSES // ch_count) // 128) * 128
    cell = np.arange(ROWS)
    cell_row = jnp.asarray(np.where(cell < CELLS, cell // GRID, 99)[:, None].astype(np.int32))
    cell_col = jnp.asarray(np.where(cell < CELLS, cell % GRID, 99)[:, None].astype(np.int32))
    all_rows = local * ROWS
    row_scratch = [
        pltpu.VMEM((all_rows, n), BF16) for n in (C, C, C, HID, 3 * C, C, HID, C)
    ]
    row_shapes = [shape((8, C)), shape((1, HID)), shape((1, 3 * C)), shape((NGRP, SLOT, LANES))]
    row_specs = [whole((8, C)), whole((1, HID)), whole((1, 3 * C)), whole((NGRP, SLOT, LANES))]
    grad, last_grad, head_grad, *last_rows, final_rows, head_bias_rows, loss = pl.pallas_call(
        functools.partial(last_layer_kernel, total_images=float(total_images)),
        grid=(local,),
        in_specs=[SCALARS] * 5 + [per_image(ROWS, C)] + WEIGHT_SPECS + [whole((C, CLASS_PAD))]
        + const_specs + vector_specs
        + [whole((2, C)), whole((1, CLASS_PAD)), whole((ROWS, 1)), whole((ROWS, 1))],
        out_specs=[per_image(ROWS, C), whole((ch_count, C, grad_cols)),
                   whole((ch_count, C, head_cols))]
        + row_specs + [whole((2, C)), whole((1, CLASS_PAD)), whole((1, 128))],
        out_shape=[shape((local, ROWS, C)), shape((ch_count, C, grad_cols), BF16),
                   shape((ch_count, C, head_cols), BF16)]
        + row_shapes + [shape((2, C)), shape((1, CLASS_PAD)), shape((1, 128))],
        scratch_shapes=[
            pltpu.VMEM((WROWS, C), BF16), pltpu.VMEM((WROWS, 3 * C), BF16),
            pltpu.VMEM((NWIN, NGRP, SLOT, LANES), BF16), pltpu.VMEM((ROWS, HID), BF16),
            pltpu.VMEM((WROWS, 3 * C), BF16), pltpu.VMEM((WROWS, C), BF16),
            pltpu.VMEM((ROWS, C), F32),
        ] + row_scratch + [pltpu.VMEM((16, C), F32), pltpu.VMEM((16, CLASS_PAD), F32)],
        compiler_params=params(),
        name="last_layer",
    )(rows, cols, own, other, mix, result, *weights[1], head_full, perms[1], perms_t[1],
      row_limits[1], col_limits[1], bias[1], small[1], qkv_bias[1], up_bias[1], final, head_bias,
      cell_row, cell_col)

    first_grad, *first_rows = pl.pallas_call(
        first_backward_kernel,
        grid=(local,),
        in_specs=[per_image(ROWS, C), per_image(ROWS, C)] + saved_specs + WEIGHT_SPECS
        + const_specs[:2] + [whole((8, C))],
        out_specs=[whole((ch_count, C, grad_cols))] + row_specs,
        out_shape=[shape((ch_count, C, grad_cols), BF16)] + row_shapes,
        scratch_shapes=[pltpu.VMEM((WROWS, 3 * C), BF16), pltpu.VMEM((WROWS, C), BF16)]
        + row_scratch,
        compiler_params=params(),
        name="first_backward",
    )(grad, padded, *saved, *weights[0], perms[0], perms_t[0], small[0])

    win_count = lax.axis_size("win")

    def own_part(packed):
        return scatter_sum(
            packed.reshape(ch_count, win_count, C // win_count, packed.shape[2])
        ).astype(F32)

    head_own = own_part(head_grad)[:, : CLASSES // ch_count]
    owned = [own_part(first_grad), own_part(last_grad)]

    def pick(n):
        return jnp.stack([part[:, cuts[n] : cuts[n + 1]] for part in owned])

    qkv_own, proj_own, up_own = pick(0), pick(1), pick(2)
    down_own = pick(3).transpose(0, 2, 1)

    vector_parts, table_parts = [], []
    for rows_small, rows_up, rows_qkv, bias_rows in (first_rows, last_rows):
        vector_parts += [
            rows_small[0:2], rows_qkv[:, :C], rows_qkv[:, 2 * C :], rows_small[4:8],
            rows_up.reshape(-1, C),
        ]
        folded = (
            bias_rows.reshape(NGRP, SLOT, PACK, SLOT).transpose(1, 3, 0, 2)
            .reshape(SLOT * SLOT, HEADS)
        )
        table_parts.append(
            lax.dot_general(onehot, folded, TN, precision=lax.Precision.HIGHEST)
        )
    head_row = jnp.pad(head_bias_rows[0, :CLASSES], (0, head_rows * C - CLASSES))
    vector_grad = jnp.concatenate(
        vector_parts + [final_rows, head_row.reshape(head_rows, C)], 0
    )
    table_grad = jnp.stack(table_parts)
    vector_grad, table_grad, loss_total = lax.psum(
        (vector_grad, table_grad, loss[0, 0]), ("win", "ch")
    )

    square = jnp.zeros((), F32)
    for grad in (qkv_own, proj_own, up_own, down_own, head_own):
        square = square + jnp.sum(grad * grad)
    square = lax.psum(square, ("win", "ch"))
    grad_norm = jnp.sqrt(
        square + jnp.sum(vector_grad * vector_grad) + jnp.sum(table_grad * table_grad)
    )
    factor = CLIP_NORM / jnp.maximum(grad_norm, CLIP_NORM)
    outs = [loss_total, grad_norm]
    for weight, grad, first, second, rate in (
        (w_qkv, qkv_own, m_qkv, v_qkv, LEARN_RATE),
        (w_proj, proj_own, m_proj, v_proj, LEARN_RATE),
        (w_fc1, up_own, m_fc1, v_fc1, LEARN_RATE),
        (w_fc2, down_own, m_fc2, v_fc2, LEARN_RATE),
        (w_head, head_own, m_head, v_head, LEARN_RATE),
        (vectors, vector_grad, m_vec, v_vec, SMALL_RATE),
        (rel_table, table_grad, m_rel, v_rel, SMALL_RATE),
    ):
        outs += adam_step(weight, factor * grad, first, second, rate)
    return tuple(outs)


def solution(mesh):
    cut = P(None, "win", "ch")
    down = P(None, "ch", "win")
    head = P("win", "ch")
    rows = P(None, ("win", "ch"))
    in_specs = (
        (P(None, ("win", "ch"), None, None),) + (rows,) * 4 + (P(),)
        + (cut,) * 9 + (down,) * 3 + (head,) * 3 + (P(),) * 6
    )
    out_specs = (P(),) * 2 + (cut,) * 9 + (down,) * 3 + (head,) * 3 + (P(),) * 6
    return jax.shard_map(
        per_device, mesh=mesh, in_specs=in_specs, out_specs=out_specs, check_vma=False
    )
```

```python
import functools

import jax
import jax.numpy as jnp
import numpy as np
from jax import lax
from jax.experimental import pallas as pl
from jax.experimental.pallas import tpu as pltpu
from jax.sharding import PartitionSpec as P

C = 384
HID = 1536
CLASSES = 1000
CLASS_PAD = 1024
WSIDE = 7
GRID = 14
STEP = 10
HEADS = 12
DEPTH = 32
CELLS = GRID * GRID
ROWS = 208
AREA = WSIDE * WSIDE
SLOT = 64
NWIN = 4
NGRP = 3
PACK = 4
WROWS = NWIN * SLOT
LANES = PACK * SLOT

NORM_EPS = 1e-05
CLIP_NORM = 0.05
LEARN_RATE = 0.04
SMALL_RATE = 0.2
DECAY_RATE = 0.05
ADAM_EPS = 1e-08
MASKED = -1e30
SCALE = DEPTH ** (-0.5)
F32 = jnp.float32
BF16 = jnp.bfloat16
NN = (((1,), (0,)), ((), ()))
NT = (((1,), (1,)), ((), ()))
TN = (((0,), (0,)), ((), ()))
VMEM_LIMIT = 58 * 1024 * 1024


def dot(a, b, dims=NN):
    return lax.dot_general(a, b, dims, preferred_element_type=F32)


@functools.lru_cache(None)
def window_tables(shifted):
    perm = np.zeros((WROWS, ROWS), np.float32)
    row_limit = np.full((NWIN, SLOT, 2 * SLOT), 99, np.int32)
    col_limit = np.full((NWIN, SLOT, 2 * SLOT), 99, np.int32)
    shift = WSIDE // 2 if shifted else 0

    def band(v):
        return 0 if v < GRID - WSIDE else (1 if v < GRID - WSIDE // 2 else 2)

    for window in range(NWIN):
        wr, wc = divmod(window, GRID // WSIDE)
        place = []
        for j in range(AREA):
            r, c = wr * WSIDE + j // WSIDE, wc * WSIDE + j % WSIDE
            region = 3 * band(r) + band(c) if shifted else 0
            source = ((r + shift) % GRID, (c + shift) % GRID)
            place.append((region, source))
            perm[window * SLOT + j, source[0] * GRID + source[1]] = 1
        for j in range(SLOT):
            for i in range(SLOT):
                if i == j:
                    pair = (-1, -1)
                elif i < AREA and j < AREA and place[i][0] == place[j][0]:
                    pair = place[j][1]
                else:
                    pair = (99, 99)
                row_limit[window, j, i::SLOT] = pair[0]
                col_limit[window, j, i::SLOT] = pair[1]
    return perm, row_limit, col_limit


@functools.lru_cache(None)
def relative_onehot():
    span = 2 * WSIDE - 1
    place = np.arange(AREA)
    row, col = place // WSIDE, place % WSIDE
    index = (row[:, None] - row[None] + WSIDE - 1) * span + col[:, None] - col[None] + WSIDE - 1
    onehot = np.zeros((SLOT, SLOT, span * span), np.float32)
    for i in range(AREA):
        for j in range(AREA):
            onehot[j, i, index[i, j]] = 1
    return onehot.reshape(SLOT * SLOT, span * span)


def norm_parts(field):
    average = jnp.mean(field, -1, keepdims=True)
    centered = field - average
    spread = jnp.mean(centered * centered, -1, keepdims=True)
    rate = lax.rsqrt(spread + NORM_EPS)
    return centered * rate, rate


def norm_back(grad, hat, rate, gain):
    scaled = grad * gain
    return rate * (
        scaled
        - jnp.mean(scaled, -1, keepdims=True)
        - hat * jnp.mean(scaled * hat, -1, keepdims=True)
    )


def col_sum(field):
    return jnp.sum(field, 0, keepdims=True)


def head_masks(dtype):
    lane = lax.broadcasted_iota(jnp.int32, (SLOT, 128), 1)
    return [((lane // DEPTH) == h).astype(F32).astype(dtype) for h in range(PACK)]


def spread_heads(block, masks):
    return jnp.concatenate([block * m for m in masks], 0)


def fold_heads(full, masks):
    total = full[:SLOT] * masks[0]
    for h in range(1, PACK):
        total = total + full[h * SLOT : (h + 1) * SLOT] * masks[h]
    return total


def all_bits(sizes):
    return [(axis, bit) for axis in ("win", "ch") for bit in range(sizes[axis].bit_length() - 1)]


def relative_places(bits):
    places = []
    for index in range(1 << len(bits)):
        offset = {"win": 0, "ch": 0}
        for n, (axis, bit) in enumerate(bits):
            offset[axis] |= ((index >> (len(bits) - 1 - n)) & 1) << bit
        places.append((offset["win"], offset["ch"]))
    return places


def load_blocks(pieces, target, where, sem, me_ref, block_rows):
    if block_rows is None:
        (ref, _, _), = pieces
        pltpu.make_async_copy(ref, target, sem).start()
        return
    for (ref, places, _), (source, width, start) in zip(pieces, where):
        for n, (win, ch) in enumerate(places):
            row = pl.multiple_of((me_ref[0] ^ win) * block_rows, block_rows)
            pltpu.make_async_copy(
                ref.at[n, :, source : source + width],
                target.at[me_ref[1] ^ ch, pl.ds(row, block_rows), start : start + width],
                sem,
            ).start()


def wait_all(ref, sem):
    pltpu.make_async_copy(ref, ref, sem).wait()


def store_blocks(source, outs, sems, me_ref, block_rows):
    if block_rows is None:
        pltpu.make_async_copy(source, outs[0][0], sems.at[0]).start()
        return
    for number, (ref, places) in enumerate(outs):
        for n, (win, ch) in enumerate(places):
            row = pl.multiple_of((me_ref[0] ^ win) * block_rows, block_rows)
            pltpu.make_async_copy(
                source.at[me_ref[1] ^ ch, pl.ds(row, block_rows), :], ref.at[n], sems.at[number]
            ).start()


def wait_blocks(outs, sems):
    for number, (ref, _) in enumerate(outs):
        wait_all(ref, sems.at[number])


def join_attention(stage, w_qkv, w_proj):
    owners = stage.shape[0]
    wide, narrow = 3 * C // owners, C // owners
    w_qkv[...] = jnp.concatenate([stage[n, :, :wide] for n in range(owners)], 1)
    w_proj[...] = jnp.concatenate([stage[n, :, wide : wide + narrow] for n in range(owners)], 1)


def forward_attention(
    field, rows, cols, w_qkv, w_proj, perm, perm_t, row_limit, col_limit, bias, small, qkv_bias,
    qkv_ref, prob_ref, mixed_ref,
):
    hat, _ = norm_parts(field)
    normed = (hat * small[0:1] + small[1:2]).astype(BF16)
    windowed = dot(perm[...], normed).astype(BF16)
    qkv_ref[...] = (dot(windowed, w_qkv[...]) + qkv_bias[...]).astype(BF16)
    low_masks = head_masks(BF16)
    masks = head_masks(F32)

    def window_step(w, carry):
        at = pl.ds(pl.multiple_of(w * SLOT, SLOT), SLOT)
        allowed = (row_limit[w] < rows) & (col_limit[w] < cols)
        block = jnp.where(allowed, 0.0, MASKED).astype(F32)
        block = jnp.concatenate([block, block], 1)
        for g in range(NGRP):
            query = qkv_ref[at, g * 128 : (g + 1) * 128]
            key = qkv_ref[at, C + g * 128 : C + (g + 1) * 128]
            value = qkv_ref[at, 2 * C + g * 128 : 2 * C + (g + 1) * 128]
            score = dot(key, spread_heads(query, low_masks), NT) * SCALE + bias[g] + block
            top = jnp.max(score, 0, keepdims=True)
            expo = jnp.exp(score - top)
            prob = (expo / jnp.sum(expo, 0, keepdims=True)).astype(BF16)
            prob_ref[w, g] = prob
            mixed_ref[at, g * 128 : (g + 1) * 128] = fold_heads(
                dot(prob, value, TN), masks
            ).astype(BF16)
        return carry

    lax.fori_loop(0, NWIN, window_step, 0)
    attended = dot(perm_t[...], mixed_ref[...]).astype(BF16)
    middle = field + dot(attended, w_proj[...]) + small[4:5]
    return normed, attended, middle


def forward_mlp(middle, w_up, w_down, small, up_bias, active_ref, slope_ref):
    hat, _ = norm_parts(middle)
    mlp_in = (hat * small[5:6] + small[6:7]).astype(BF16)
    branch = jnp.zeros((ROWS, C), F32)
    width = w_up.shape[2]
    for part in range(w_up.shape[0]):
        at = slice(part * width, (part + 1) * width)
        pre = dot(mlp_in, w_up[part]) + up_bias[:, at]
        half = 0.5 * (1.0 + lax.erf(pre * (0.5**0.5)))
        active = (pre * half).astype(BF16)
        slope = half + pre * (jnp.exp(-0.5 * pre * pre) * ((2.0 * np.pi) ** -0.5))
        active_ref[:, at] = active
        slope_ref[:, at] = slope.astype(BF16)
        branch = branch + dot(active, w_down[part], NT)
    return mlp_in, middle + branch + small[7:8]


def backward_mlp(
    grad, middle, slope_ref, w_up, w_down, small, low_ref, pre_ref, rows_ref, up_rows_ref, place
):
    low = grad.astype(BF16)
    low_ref[place, :] = low
    rows_ref[7:8, :] += col_sum(low.astype(F32))
    normed_grad = jnp.zeros((ROWS, C), F32)
    width = w_up.shape[2]
    for part in range(w_up.shape[0]):
        at = slice(part * width, (part + 1) * width)
        pre = (dot(low, w_down[part]) * slope_ref[:, at].astype(F32)).astype(BF16)
        pre_ref[place, at] = pre
        up_rows_ref[:, at] += col_sum(pre.astype(F32))
        normed_grad = normed_grad + dot(pre, w_up[part], NT)
    hat, rate = norm_parts(middle)
    rows_ref[5:6, :] += col_sum(normed_grad * hat)
    rows_ref[6:7, :] += col_sum(normed_grad)
    return norm_back(normed_grad, hat, rate, small[5:6]) + grad


def backward_attention(
    grad_mid, field, qkv_ref, prob_ref, w_qkv, w_proj, perm, perm_t, small,
    spread_ref, dqkv_ref, attn_ref, joined_ref, rows_ref, qkv_rows_ref, bias_grad_ref, place,
):
    attn = grad_mid.astype(BF16)
    attn_ref[place, :] = attn
    rows_ref[4:5, :] += col_sum(attn.astype(F32))
    joined = dot(attn, w_proj[...], NT).astype(BF16)
    joined_ref[...] = dot(perm[...], joined).astype(BF16)
    low_masks = head_masks(BF16)
    masks = head_masks(F32)

    def window_step(w, carry):
        at = pl.ds(pl.multiple_of(w * SLOT, SLOT), SLOT)
        for g in range(NGRP):
            cut = [slice(n * C + g * 128, n * C + (g + 1) * 128) for n in range(3)]
            query = spread_heads(qkv_ref[at, cut[0]], low_masks)
            key = qkv_ref[at, cut[1]]
            value = qkv_ref[at, cut[2]]
            out = spread_heads(joined_ref[at, cut[0]], low_masks)
            prob = prob_ref[w, g]
            wide = prob.astype(F32)
            prob_grad = dot(value, out, NT)
            score = wide * (prob_grad - jnp.sum(wide * prob_grad, 0, keepdims=True))
            bias_grad_ref[g] += score
            score = score.astype(BF16)
            dqkv_ref[at, cut[2]] = dot(prob, out).astype(BF16)
            dqkv_ref[at, cut[1]] = (dot(score, query) * SCALE).astype(BF16)
            dqkv_ref[at, cut[0]] = (fold_heads(dot(score, key, TN), masks) * SCALE).astype(BF16)
        return carry

    lax.fori_loop(0, NWIN, window_step, 0)
    back = dot(perm_t[...], dqkv_ref[...]).astype(BF16)
    spread_ref[place, :] = back
    qkv_rows_ref[...] += col_sum(back.astype(F32))
    normed_grad = dot(back, w_qkv[...], NT)
    hat, rate = norm_parts(field)
    rows_ref[0:1, :] += col_sum(normed_grad * hat)
    rows_ref[1:2, :] += col_sum(normed_grad)
    return norm_back(normed_grad, hat, rate, small[0:1]) + grad_mid


def image_place():
    return pl.ds(pl.multiple_of(pl.program_id(0) * ROWS, 16), ROWS)


def is_first():
    return pl.program_id(0) == 0


def is_last():
    return pl.program_id(0) == pl.num_programs(0) - 1


def clear(*refs):
    @pl.when(is_first())
    def _():
        for ref in refs:
            ref[...] = jnp.zeros(ref.shape, ref.dtype)


def by_owner(left, right, target):
    owners, _, width = target.shape
    for n in range(owners):
        target[n] = dot(left[...], right[:, n * width : (n + 1) * width], TN).astype(BF16)


class Names:
    def __init__(self, **refs):
        self.__dict__.update(refs)


def fetch_attention(k, plan):
    @pl.when(is_first())
    def _():
        load_blocks(plan.pieces(k, "attn"), k.stage, plan.where["attn"], k.load_sem.at[0], k.me, plan.block_rows)
        wait_all(k.stage, k.load_sem.at[0])
        join_attention(k.stage, k.w_qkv, k.w_proj)


def fetch_mlp(k, plan):
    @pl.when(is_first())
    def _():
        load_blocks(plan.pieces(k, "down"), k.w_down, plan.where["down"], k.load_sem.at[1], k.me, plan.block_rows)
        load_blocks(plan.pieces(k, "up"), k.w_up, plan.where["up"], k.load_sem.at[2], k.me, plan.block_rows)
        wait_all(k.w_down, k.load_sem.at[1])
        wait_all(k.w_up, k.load_sem.at[2])


def run_forward_attention(k):
    image = pl.program_id(0)
    normed, attended, middle = forward_attention(
        k.field[...].astype(F32), k.rows[image], k.cols[image], k.w_qkv, k.w_proj, k.perm, k.perm_t,
        k.row_limit, k.col_limit, k.bias, k.small[...], k.qkv_bias, k.qkv, k.prob, k.mixed,
    )
    k.normed[...] = normed
    k.attended[...] = attended
    return middle


def first_attention_kernel(k, plan):
    fetch_attention(k, plan)
    k.middle[...] = run_forward_attention(k)


def first_mlp_kernel(k, plan):
    fetch_mlp(k, plan)
    mlp_in, result = forward_mlp(
        k.middle[...], k.w_up, k.w_down, k.small[...], k.up_bias, k.active, k.slope
    )
    k.mlp_in[...] = mlp_in
    k.result[...] = result


def store_mlp_grads(k, plan):
    by_owner(k.mlp_all, k.pre_all, k.up_grad)
    store_blocks(k.up_grad, plan.outs(k, "up"), k.up_sem, k.me, plan.block_rows)
    by_owner(k.low_all, k.active_all, k.down_grad)
    store_blocks(k.down_grad, plan.outs(k, "down"), k.down_sem, k.me, plan.block_rows)


def wait_mlp_grads(k, plan):
    wait_blocks(plan.outs(k, "up"), k.up_sem)
    wait_blocks(plan.outs(k, "down"), k.down_sem)


def head_pass(k, result, rows, cols, total_images):
    image = pl.program_id(0)
    hat, rate = norm_parts(result)
    inside = ((k.cell_row[...] < rows) & (k.cell_col[...] < cols)).astype(F32)
    count = (rows * cols).astype(F32)
    final = hat * k.final[0:1] + k.final[1:2]
    pooled = col_sum(final * inside) / count
    pooled = jnp.broadcast_to(pooled, (16, C)).astype(BF16)
    owners, _, width = k.w_head.shape
    classes = owners * width
    logits = jnp.concatenate([dot(pooled, k.w_head[n])[0:1] for n in range(owners)], 1)
    logits = logits + k.head_bias[...]
    top = jnp.max(logits, -1, keepdims=True)
    expo = jnp.exp(logits - top)
    log_probs = logits - top - jnp.log(jnp.sum(expo, -1, keepdims=True))
    lane = lax.broadcasted_iota(jnp.int32, (1, classes), 1)
    mixing = k.mix[image].astype(F32) / 16.0
    target = jnp.where(lane == k.own[image], mixing, 0.0)
    target = target + jnp.where(lane == k.other[image], 1.0 - mixing, 0.0)
    loss = jnp.sum(jnp.where(target > 0.0, target * log_probs, 0.0), -1, keepdims=True)
    k.loss[...] -= jnp.broadcast_to(loss, k.loss.shape)
    logit_grad = (jnp.exp(log_probs) - target) / total_images
    logit_low = jnp.broadcast_to(logit_grad, (16, classes)).astype(BF16)
    k.head_rows[...] += logit_low[0:1].astype(F32)
    k.pooled_all[pl.ds(image, 1), :] = pooled[0:1].astype(F32)
    k.logit_all[pl.ds(image, 1), :] = logit_low[0:1].astype(F32)
    pooled_grad = jnp.zeros((16, C), F32)
    for n in range(owners):
        pooled_grad += dot(logit_low[:, n * width : (n + 1) * width], k.w_head[n], NT)
    final_grad = pooled_grad[0:1] * (inside / count)
    k.final_rows[0:1, :] += col_sum(final_grad * hat)
    k.final_rows[1:2, :] += col_sum(final_grad)
    return norm_back(final_grad, hat, rate, k.final[0:1])


def last_kernel(k, plan, total_images):
    image = pl.program_id(0)
    place = image_place()

    @pl.when(is_first())
    def _():
        load_blocks(plan.pieces(k, "head"), k.w_head, plan.where["head"], k.load_sem.at[3], k.me, plan.block_rows)

    fetch_attention(k, plan)
    fetch_mlp(k, plan)

    @pl.when(is_first())
    def _():
        wait_all(k.w_head, k.load_sem.at[3])

    clear(k.row_sums, k.up_rows, k.final_rows, k.head_rows, k.loss, k.pooled_all, k.logit_all)
    middle = run_forward_attention(k)
    k.middle[...] = middle
    mlp_in, result = forward_mlp(
        middle, k.w_up, k.w_down, k.small[...], k.up_bias, k.active_all.at[place], k.slope
    )
    k.mlp_all[place, :] = mlp_in
    grad = head_pass(k, result, k.rows[image], k.cols[image], total_images)
    k.grad_mid[...] = backward_mlp(
        grad, k.middle[...], k.slope, k.w_up, k.w_down, k.small[...], k.low_all, k.pre_all,
        k.row_sums, k.up_rows, place,
    )

    @pl.when(is_last())
    def _():
        store_mlp_grads(k, plan)
        total = dot(k.pooled_all[...].astype(BF16), k.logit_all[...].astype(BF16), TN).astype(BF16)
        owners, _, width = k.head_grad.shape
        for n in range(owners):
            k.head_grad[n] = total[:, n * width : (n + 1) * width]
        store_blocks(k.head_grad, plan.outs(k, "head"), k.head_sem, k.me, plan.block_rows)
        wait_mlp_grads(k, plan)
        wait_blocks(plan.outs(k, "head"), k.head_sem)


def backward_mlp_kernel(k, plan):
    fetch_mlp(k, plan)
    clear(k.row_sums, k.up_rows)
    place = image_place()
    k.mlp_all[place, :] = k.mlp_in[...]
    k.active_all[place, :] = k.active[...]
    k.grad_mid[...] = backward_mlp(
        k.grad[...], k.middle[...], k.slope, k.w_up, k.w_down, k.small[...], k.low_all, k.pre_all,
        k.row_sums, k.up_rows, place,
    )

    @pl.when(is_last())
    def _():
        store_mlp_grads(k, plan)
        wait_mlp_grads(k, plan)


def backward_attention_kernel(k, plan):
    fetch_attention(k, plan)
    clear(k.row_sums, k.qkv_rows, k.bias_grad)
    place = image_place()
    k.normed_all[place, :] = k.normed[...]
    k.attended_all[place, :] = k.attended[...]
    k.grad[...] = backward_attention(
        k.grad_mid[...], k.field[...].astype(F32), k.qkv, k.prob, k.w_qkv, k.w_proj, k.perm,
        k.perm_t, k.small[...], k.spread_all, k.dqkv, k.attn_all, k.joined, k.row_sums, k.qkv_rows,
        k.bias_grad, place,
    )

    @pl.when(is_last())
    def _():
        owners, _, _ = k.attn_grad.shape
        wide, narrow = 3 * C // owners, C // owners
        total = dot(k.normed_all[...], k.spread_all[...], TN).astype(BF16)
        for n in range(owners):
            k.attn_grad[n, :, :wide] = total[:, n * wide : (n + 1) * wide]
        total = dot(k.attended_all[...], k.attn_all[...], TN).astype(BF16)
        for n in range(owners):
            k.attn_grad[n, :, wide:] = total[:, n * narrow : (n + 1) * narrow]
        store_blocks(k.attn_grad, plan.outs(k, "attn"), k.attn_sem, k.me, plan.block_rows)
        wait_blocks(plan.outs(k, "attn"), k.attn_sem)


class Plan:
    def __init__(self, block_rows):
        self.block_rows = block_rows
        self.sources = {}
        self.where = {}
        self.targets = {}

    def pieces(self, k, name):
        return [(getattr(k, ref), places, None) for ref, places in self.sources[name]]

    def outs(self, k, name):
        return [(getattr(k, ref), places) for ref, places in self.targets[name]]


def whole(shape):
    return pl.BlockSpec(shape, lambda i: (0,) * len(shape))


def per_image(*shape):
    return pl.BlockSpec((None,) + shape, lambda i: (i,) + (0,) * len(shape))


SCALARS = pl.BlockSpec(memory_space=pltpu.SMEM)
FAR = pl.BlockSpec(memory_space=pl.ANY)


def call(body, name, local, ins, outs, scratch, flops):
    def kernel(*refs):
        body(Names(**dict(zip(list(ins) + list(outs) + list(scratch), refs))))

    moved = sum(a.size * a.dtype.itemsize for _, a in ins.values())
    results = pl.pallas_call(
        kernel,
        grid=(local,),
        in_specs=[spec for spec, _ in ins.values()],
        out_specs=[spec for spec, _, _ in outs.values()],
        out_shape=[jax.ShapeDtypeStruct(dims, dtype) for _, dims, dtype in outs.values()],
        scratch_shapes=list(scratch.values()),
        compiler_params=pltpu.CompilerParams(
            dimension_semantics=("arbitrary",), vmem_limit_bytes=VMEM_LIMIT
        ),
        cost_estimate=pl.CostEstimate(flops=int(flops), bytes_accessed=int(moved), transcendentals=0),
        name=name,
    )(*[array for _, array in ins.values()])
    return dict(zip(outs, results))


def exchange(array, step):
    axis, bit = step
    size = lax.axis_size(axis)
    return lax.ppermute(array, axis, [(i, i ^ (1 << bit)) for i in range(size)])


def double(held, step):
    return jnp.stack([held, exchange(held, step)])


def add_low(a, b):
    return (a.astype(F32) + b.astype(F32)).astype(BF16)


def halve(keep, received):
    return add_low(keep[0], received[0]), add_low(keep[1], received[1])


def tie(*values):
    return lax.optimization_barrier(values)


def adam_step(weight, grad, first, second, rate):
    new_first = 0.5 * first + 0.5 * grad
    new_second = 0.5 * second + 0.5 * grad * grad
    fix = 1.0 - 0.5**STEP
    update = new_first / fix / (jnp.sqrt(new_second / fix) + ADAM_EPS)
    return (new_first, new_second, weight - rate * (update + DECAY_RATE * weight))


class Chain:
    def __init__(self, keep, send, steps):
        self.keep, self.send, self.steps = keep, send, list(steps)

    def step(self):
        received = exchange(self.send, self.steps.pop(0))
        if self.steps:
            self.keep, self.send = halve(self.keep, received)
        else:
            self.keep, self.send = add_low(self.keep, received), None
        return self

    @staticmethod
    def merge(chains):
        return Chain(
            jnp.concatenate([chain.keep for chain in chains], -1),
            jnp.concatenate([chain.send for chain in chains], -1),
            chains[0].steps,
        )

    @staticmethod
    def tie(chains, *values):
        held = [chain.keep for chain in chains] + [chain.send for chain in chains]
        tied = tie(*values, *held)
        rest = tied[len(values) :]
        for n, chain in enumerate(chains):
            chain.keep, chain.send = rest[n], rest[n + len(chains)]
        return tied[: len(values)]


def per_device(
    tokens, valid_rows, valid_cols, partner, mix_level, labels,
    w_qkv, m_qkv, v_qkv, w_proj, m_proj, v_proj, w_fc1, m_fc1, v_fc1, w_fc2, m_fc2, v_fc2,
    w_head, m_head, v_head, vectors, m_vec, v_vec, rel_table, m_rel, v_rel,
):
    micro, images, cells, chans = tokens.shape
    layers = rel_table.shape[0]
    per_layer = 8 + HID // C
    base = layers * per_layer
    head_rows = vectors.shape[0] - base - 2
    all_images = labels.shape[1]
    total_images = micro * all_images
    local = micro * images
    sizes = {axis: lax.axis_size(axis) for axis in ("win", "ch")}
    win_count, ch_count = sizes["win"], sizes["ch"]
    device_count = win_count * ch_count
    win_index, ch_index = lax.axis_index("win"), lax.axis_index("ch")
    me = jnp.stack([win_index, ch_index]).astype(jnp.int32)
    block_rows = C // win_count
    widths = {"attn": 4 * C // ch_count, "down": HID // ch_count, "up": HID // ch_count}
    head_real = CLASSES // ch_count
    widths["head"] = -(-head_real // 128) * 128
    head_classes = widths["head"] * ch_count
    direct = block_rows % 16 == 0 and all(w % 128 == 0 for w in widths.values())

    core = ("ch", 0)
    ch_high = [("ch", b) for b in range(1, ch_count.bit_length() - 1)]
    win_low = [("win", 0)]
    win_high = [("win", b) for b in range(1, win_count.bit_length() - 1)]

    def low(v):
        return v.astype(BF16)

    def flipped(places):
        return [(win, ch ^ 1) for win, ch in places]

    packed = [
        jnp.concatenate([low(w_qkv[l]), low(w_proj[l]), low(w_fc2[l]).T, low(w_fc1[l])], 1)
        for l in range(layers)
    ]
    packed[-1] = jnp.concatenate(
        [packed[-1], jnp.pad(low(w_head), ((0, 0), (0, widths["head"] - head_real)))], 1
    )
    names = [["attn", "down", "up"], ["attn", "down", "up", "head"]]
    cuts = [widths["attn"] + 2 * widths["down"] // 3 // 128 * 128, widths["attn"] + widths["down"]]
    rest = [ch_high[::-1] + win_low, win_low + ch_high[::-1]]
    common = win_high[::-1]

    def far_gather(block):
        for step in common:
            block = double(block, step)
        return block

    def near_gather(block, cut, group, step_at):
        held = block[..., :cut] if group == 0 else block[..., cut:]
        return double(held, rest[group][step_at])

    far = [far_gather(packed[0])]
    second, far[0] = tie(packed[1], far[0])
    far.append(far_gather(second))
    held = [[far[0][..., : cuts[0]], far[0][..., cuts[0] :]]]
    for at in range(len(rest[0])):
        held[0] = [double(held[0][g], rest[g][at]) for g in range(2)]
    other = [[exchange(part, core) for part in held[0]]]
    held.append([far[1][..., : cuts[1]], far[1][..., cuts[1] :]])

    def weight_inputs(layer, wanted):
        plan = Plan(block_rows if direct else None)
        ins = {}
        starts, at = {}, 0
        for name in names[layer]:
            starts[name] = at
            at += widths[name]
        bounds = [(0, cuts[layer]), (cuts[layer], at)]
        blocks = []
        for group in range(2):
            places = relative_places((common + rest[group])[::-1])
            for number, array in enumerate((held[layer][group], other[layer][group])):
                flat = array.reshape((-1,) + array.shape[-2:])
                blocks.append((group, places if number == 0 else flipped(places), flat))
        for name in wanted:
            plan.sources[name], plan.where[name] = [], []
            columns = []
            for number, (group, places, flat) in enumerate(blocks):
                begin = max(starts[name], bounds[group][0])
                end = min(starts[name] + widths[name], bounds[group][1])
                if begin >= end:
                    continue
                cut = (begin - bounds[group][0], end - begin, begin - starts[name])
                if direct:
                    ref = f"blocks{number}"
                    ins[ref] = (FAR, flat)
                    plan.sources[name].append((ref, places))
                    plan.where[name].append(cut)
                elif number % 2 == 0:
                    table = np.zeros((ch_count, win_count), np.int32)
                    for n, (win, ch) in enumerate(places + blocks[number + 1][1]):
                        table[ch, win] = n
                    both = jnp.concatenate([flat, blocks[number + 1][2]])
                    index = jnp.asarray(table)[jnp.arange(ch_count) ^ ch_index][
                        :, jnp.arange(win_count) ^ win_index
                    ]
                    full = jnp.take(both, index.reshape(-1), axis=0).reshape(
                        ch_count, C, flat.shape[-1]
                    )
                    columns.append(full[..., cut[0] : cut[0] + cut[1]])
            if not direct:
                ref = f"staged_{name}"
                ins[ref] = (FAR, jnp.concatenate(columns, -1))
                plan.sources[name] = [(ref, None)]
        ins["me"] = (SCALARS, me)
        return ins, plan

    orders = {
        "up": ch_high + win_low, "attn": ch_high + win_low,
        "down": win_low + ch_high, "head": win_low + ch_high,
    }

    def grad_outputs(plan, wanted):
        outs = {}
        for name in wanted:
            width = widths[name]
            if direct:
                places = relative_places(orders[name] + win_high)
                plan.targets[name] = [
                    (f"keep_{name}", places), (f"send_{name}", flipped(places))
                ]
                for ref, _ in plan.targets[name]:
                    outs[ref] = (FAR, (len(places), block_rows, width), BF16)
            else:
                plan.targets[name] = [(f"full_{name}", None)]
                outs[f"full_{name}"] = (FAR, (ch_count, C, width), BF16)
        return outs

    def chain_of(results, name):
        bits = orders[name] + win_high
        if direct:
            keep, send = results[f"keep_{name}"], results[f"send_{name}"]
        else:
            full = results[f"full_{name}"].reshape(device_count, block_rows, widths[name])
            places = np.asarray(relative_places(bits))

            def ordered(flip):
                index = ((places[:, 1] ^ flip) ^ ch_index) * win_count + (places[:, 0] ^ win_index)
                return jnp.take(full, index, axis=0)

            keep, send = ordered(0), ordered(1)
        dims = (2,) * len(bits) + (block_rows, widths[name])
        return Chain(keep.reshape(dims), send.reshape(dims), [core] + bits)

    small = [vectors[l * per_layer : l * per_layer + 8] for l in range(layers)]
    up_bias = [
        vectors[l * per_layer + 8 : (l + 1) * per_layer].reshape(1, HID) for l in range(layers)
    ]
    qkv_bias = [
        jnp.concatenate([s[2], jnp.zeros_like(s[2]), s[3]]).reshape(1, 3 * C) for s in small
    ]
    final = vectors[base : base + 2]
    head_bias = jnp.pad(
        vectors[base + 2 :].reshape(-1)[:CLASSES].reshape(ch_count, head_real),
        ((0, 0), (0, widths["head"] - head_real)),
        constant_values=MASKED,
    ).reshape(1, head_classes)
    onehot = jnp.asarray(relative_onehot())
    bias = [
        jnp.dot(onehot, rel_table[l], precision=lax.Precision.HIGHEST)
        .reshape(SLOT, SLOT, NGRP, PACK)
        .transpose(2, 0, 3, 1)
        .reshape(NGRP, SLOT, LANES)
        for l in range(layers)
    ]
    tables = [window_tables(l % 2 == 1) for l in range(layers)]
    perms = [jnp.asarray(t[0], BF16) for t in tables]
    perms_t = [jnp.asarray(t[0].T, BF16) for t in tables]
    row_limits = [jnp.asarray(t[1]) for t in tables]
    col_limits = [jnp.asarray(t[2]) for t in tables]

    rows = valid_rows.reshape(local)
    cols = valid_cols.reshape(local)
    image_ids = (win_index * ch_count + ch_index) * images + jnp.arange(images, dtype=jnp.int32)
    all_ids = jnp.arange(all_images, dtype=jnp.int32)
    own = jnp.sum(
        jnp.where(image_ids[None, :, None] == all_ids, labels[:, None, :], 0), -1
    ).reshape(local)
    partner_label = jnp.sum(
        jnp.where(partner[:, :, None] == all_ids, labels[:, None, :], 0), -1
    ).reshape(local)

    def class_lane(label):
        return label // head_real * widths["head"] + label % head_real

    padded = jnp.pad(tokens.reshape(local, cells, chans), ((0, 0), (0, ROWS - cells), (0, 0)))

    def attention_consts(l, forward):
        ins = {
            "perm": (whole((WROWS, ROWS)), perms[l]),
            "perm_t": (whole((ROWS, WROWS)), perms_t[l]),
            "small": (whole((8, C)), small[l]),
        }
        if forward:
            ins["rows"] = (SCALARS, rows)
            ins["cols"] = (SCALARS, cols)
            ins["row_limit"] = (whole((NWIN, SLOT, 128)), row_limits[l])
            ins["col_limit"] = (whole((NWIN, SLOT, 128)), col_limits[l])
            ins["bias"] = (whole((NGRP, SLOT, LANES)), bias[l])
            ins["qkv_bias"] = (whole((1, 3 * C)), qkv_bias[l])
        return ins

    def vmem(*dims, dtype=BF16):
        return pltpu.VMEM(dims, dtype)

    attn_weights = {
        "stage": vmem(ch_count, C, widths["attn"]),
        "w_qkv": vmem(C, 3 * C),
        "w_proj": vmem(C, C),
        "load_sem": pltpu.SemaphoreType.DMA((4,)),
    }
    mlp_weights = {
        "w_down": vmem(ch_count, C, widths["down"]),
        "w_up": vmem(ch_count, C, widths["up"]),
        "load_sem": pltpu.SemaphoreType.DMA((4,)),
    }
    all_rows = local * ROWS
    mlp_rows = {
        "mlp_all": vmem(all_rows, C), "active_all": vmem(all_rows, HID),
        "pre_all": vmem(all_rows, HID), "low_all": vmem(all_rows, C),
        "up_grad": vmem(ch_count, C, widths["up"]), "down_grad": vmem(ch_count, C, widths["down"]),
        "up_sem": pltpu.SemaphoreType.DMA((2,)), "down_sem": pltpu.SemaphoreType.DMA((2,)),
    }
    wide = (per_image(ROWS, C), (local, ROWS, C), F32)
    thin = (per_image(ROWS, C), (local, ROWS, C), BF16)
    hidden = (per_image(ROWS, HID), (local, ROWS, HID), BF16)
    attn_saved = {
        "normed": thin,
        "qkv": (per_image(WROWS, 3 * C), (local, WROWS, 3 * C), BF16),
        "prob": (per_image(NWIN, NGRP, SLOT, LANES), (local, NWIN, NGRP, SLOT, LANES), BF16),
        "attended": thin,
    }
    sums = {"row_sums": (whole((8, C)), (8, C), F32)}
    up_sums = {**sums, "up_rows": (whole((1, HID)), (1, HID), F32)}
    attn_sums = {
        **sums,
        "qkv_rows": (whole((1, 3 * C)), (1, 3 * C), F32),
        "bias_grad": (whole((NGRP, SLOT, LANES)), (NGRP, SLOT, LANES), F32),
    }

    def given(spec, array):
        return (spec[0], array)

    mlp_flops = 2 * all_rows * C * HID * 2
    attn_flops = 2 * all_rows * C * C * 8

    ins, plan = weight_inputs(0, ["attn"])
    tied, far[1] = tie(padded, far[1])
    ins["field"] = given(thin, tied)
    ins.update(attention_consts(0, True))
    saved0 = call(
        functools.partial(first_attention_kernel, plan=plan), "first_attention", local, ins,
        {"middle": wide, **attn_saved}, {"mixed": vmem(WROWS, C), **attn_weights}, attn_flops,
    )
    held[1] = [far[1][..., : cuts[1]], far[1][..., cuts[1] :]]
    at = 0
    held[1] = [double(held[1][g], rest[g][at]) for g in range(2)]
    middle0, *held[1] = tie(saved0["middle"], *held[1])
    ins, plan = weight_inputs(0, ["down", "up"])
    ins["middle"] = given(wide, middle0)
    ins["small"] = (whole((8, C)), small[0])
    ins["up_bias"] = (whole((1, HID)), up_bias[0])
    mlp0 = call(
        functools.partial(first_mlp_kernel, plan=plan), "first_mlp", local, ins,
        {"result": wide, "mlp_in": thin, "active": hidden, "slope": hidden}, dict(mlp_weights),
        mlp_flops,
    )
    for at in range(1, len(rest[0])):
        held[1] = [double(held[1][g], rest[g][at]) for g in range(2)]
    other.append([exchange(part, core) for part in held[1]])

    ins, plan = weight_inputs(1, ["attn", "down", "up", "head"])
    ins["field"] = given(wide, mlp0["result"])
    ins.update(attention_consts(1, True))
    ins["up_bias"] = (whole((1, HID)), up_bias[1])
    ins["own"] = (SCALARS, class_lane(own))
    ins["other"] = (SCALARS, class_lane(partner_label))
    ins["mix"] = (SCALARS, mix_level.reshape(local))
    ins["final"] = (whole((2, C)), final)
    ins["head_bias"] = (whole((1, head_classes)), head_bias)
    cell = np.arange(ROWS)
    for name, place in (("cell_row", cell // GRID), ("cell_col", cell % GRID)):
        place = np.where(cell < CELLS, place, 99)[:, None].astype(np.int32)
        ins[name] = (whole((ROWS, 1)), jnp.asarray(place))
    outs = {
        "grad_mid": wide, **attn_saved, **up_sums,
        "final_rows": (whole((2, C)), (2, C), F32),
        "head_rows": (whole((1, head_classes)), (1, head_classes), F32),
        "loss": (whole((1, 128)), (1, 128), F32),
        **grad_outputs(plan, ["up", "down", "head"]),
    }
    last = call(
        functools.partial(last_kernel, plan=plan, total_images=float(total_images)), "last_block",
        local, ins, outs,
        {
            "mixed": vmem(WROWS, C), "middle": vmem(ROWS, C, dtype=F32), "slope": vmem(ROWS, HID),
            "w_head": vmem(ch_count, C, widths["head"]), **attn_weights, **mlp_weights, **mlp_rows,
            "pooled_all": vmem(16, C, dtype=F32), "logit_all": vmem(16, head_classes, dtype=F32),
            "head_grad": vmem(ch_count, C, widths["head"]),
            "head_sem": pltpu.SemaphoreType.DMA((2,)),
        },
        attn_flops + 3 * mlp_flops,
    )

    def attention_backward(l, grad_mid, field_spec, field, saved):
        ins, plan = weight_inputs(l, ["attn"])
        ins["grad_mid"] = given(wide, grad_mid)
        ins["field"] = given(field_spec, field)
        for name, spec in attn_saved.items():
            ins[name] = given(spec, saved[name])
        ins.update(attention_consts(l, False))
        return call(
            functools.partial(backward_attention_kernel, plan=plan), f"attention_backward{l}",
            local, ins, {"grad": wide, **attn_sums, **grad_outputs(plan, ["attn"])},
            {
                **attn_weights, "dqkv": vmem(WROWS, 3 * C), "joined": vmem(WROWS, C),
                "normed_all": vmem(all_rows, C), "attended_all": vmem(all_rows, C),
                "spread_all": vmem(all_rows, 3 * C), "attn_all": vmem(all_rows, C),
                "attn_grad": vmem(ch_count, C, widths["attn"]),
                "attn_sem": pltpu.SemaphoreType.DMA((2,)),
            },
            2 * attn_flops,
        )

    chains1 = [chain_of(last, name) for name in ("up", "down", "head")]
    back1 = attention_backward(1, last["grad_mid"], wide, mlp0["result"], last)
    for chain in chains1:
        chain.step()
    (grad,) = Chain.tie(chains1, back1["grad"])

    ins, plan = weight_inputs(0, ["down", "up"])
    ins["grad"] = given(wide, grad)
    ins["middle"] = given(wide, saved0["middle"])
    ins["mlp_in"] = given(thin, mlp0["mlp_in"])
    ins["active"] = given(hidden, mlp0["active"])
    ins["slope"] = given(hidden, mlp0["slope"])
    ins["small"] = (whole((8, C)), small[0])
    first = call(
        functools.partial(backward_mlp_kernel, plan=plan), "mlp_backward0", local, ins,
        {"grad_mid": wide, **up_sums, **grad_outputs(plan, ["up", "down"])},
        {**mlp_weights, **mlp_rows}, 2 * mlp_flops,
    )
    chains1.append(chain_of(back1, "attn"))
    for chain in chains1:
        chain.step()
    (grad_mid,) = Chain.tie(chains1, first["grad_mid"])
    chains0 = [chain_of(first, name) for name in ("up", "down")]
    back0 = attention_backward(0, grad_mid, thin, padded, saved0)
    for chain in chains1 + chains0:
        chain.step()
    chains0.append(chain_of(back0, "attn"))

    def near_steps(chains):
        while any(len(chain.steps) > len(win_high) for chain in chains):
            for chain in chains:
                if len(chain.steps) > len(win_high):
                    chain.step()
        return Chain.merge(chains)

    merged = [near_steps(chains0), near_steps(chains1)]
    total = Chain.merge(merged)
    while total.steps:
        total.step()
    owned, at = [{}, {}], 0
    for l, order in ((0, ("up", "down", "attn")), (1, ("up", "down", "head", "attn"))):
        for name in order:
            owned[l][name] = total.keep[:, at : at + widths[name]].astype(F32)
            at += widths[name]

    qkv_width = 3 * C // ch_count
    qkv_own = jnp.stack([o["attn"][:, :qkv_width] for o in owned])
    proj_own = jnp.stack([o["attn"][:, qkv_width:] for o in owned])
    up_own = jnp.stack([o["up"] for o in owned])
    down_own = jnp.stack([o["down"].T for o in owned])
    head_own = owned[1]["head"][:, :head_real]

    parts = []
    for mlp_part, attn_part in ((first, back0), (last, back1)):
        parts += [
            attn_part["row_sums"][0:2], attn_part["qkv_rows"][:, :C],
            attn_part["qkv_rows"][:, 2 * C :], attn_part["row_sums"][4:5],
            mlp_part["row_sums"][5:8], mlp_part["up_rows"].reshape(-1, C),
        ]
    head_row = last["head_rows"].reshape(ch_count, widths["head"])[:, :head_real].reshape(-1)
    head_row = jnp.pad(head_row, (0, head_rows * C - CLASSES))
    vector_grad = jnp.concatenate(parts + [last["final_rows"], head_row.reshape(head_rows, C)], 0)
    table_grad = jnp.stack(
        [
            lax.dot_general(
                onehot,
                part["bias_grad"].reshape(NGRP, SLOT, PACK, SLOT).transpose(1, 3, 0, 2)
                .reshape(SLOT * SLOT, HEADS),
                TN,
                precision=lax.Precision.HIGHEST,
            )
            for part in (back0, back1)
        ]
    )
    flat = jnp.concatenate([vector_grad.reshape(-1), table_grad.reshape(-1), last["loss"][0, :1]])
    count = flat.shape[0]
    share = -(-count // (device_count * 128)) * 128
    flat = jnp.pad(flat, (0, share * device_count - count)).reshape(device_count, share)
    flat = lax.all_to_all(flat, ("win", "ch"), 0, 0, tiled=True)
    mine = jnp.sum(flat, 0)

    square = jnp.zeros((), F32)
    for grad in (qkv_own, proj_own, up_own, down_own, head_own):
        square = square + jnp.sum(grad * grad)
    message = jnp.concatenate([mine, jnp.broadcast_to(square, (128,))])
    message = lax.all_to_all(
        jnp.broadcast_to(message, (device_count, share + 128)), ("win", "ch"), 0, 0, tiled=True
    )
    flat = message[:, :share].reshape(-1)
    vector_grad = flat[: vectors.size].reshape(vectors.shape)
    table_grad = flat[vectors.size : vectors.size + rel_table.size].reshape(rel_table.shape)
    loss_total = flat[count - 1]
    grad_norm = jnp.sqrt(
        jnp.sum(message[:, share])
        + jnp.sum(vector_grad * vector_grad)
        + jnp.sum(table_grad * table_grad)
    )
    factor = CLIP_NORM / jnp.maximum(grad_norm, CLIP_NORM)
    outs = [loss_total, grad_norm]
    for weight, grad, moment, second, rate in (
        (w_qkv, qkv_own, m_qkv, v_qkv, LEARN_RATE),
        (w_proj, proj_own, m_proj, v_proj, LEARN_RATE),
        (w_fc1, up_own, m_fc1, v_fc1, LEARN_RATE),
        (w_fc2, down_own, m_fc2, v_fc2, LEARN_RATE),
        (w_head, head_own, m_head, v_head, LEARN_RATE),
        (vectors, vector_grad, m_vec, v_vec, SMALL_RATE),
        (rel_table, table_grad, m_rel, v_rel, SMALL_RATE),
    ):
        outs += adam_step(weight, factor * grad, moment, second, rate)
    return tuple(outs)


def solution(mesh):
    cut = P(None, "win", "ch")
    down = P(None, "ch", "win")
    head = P("win", "ch")
    rows = P(None, ("win", "ch"))
    in_specs = (
        (P(None, ("win", "ch"), None, None),) + (rows,) * 4 + (P(),)
        + (cut,) * 9 + (down,) * 3 + (head,) * 3 + (P(),) * 6
    )
    out_specs = (P(),) * 2 + (cut,) * 9 + (down,) * 3 + (head,) * 3 + (P(),) * 6
    return jax.shard_map(
        per_device, mesh=mesh, in_specs=in_specs, out_specs=out_specs, check_vma=False
    )
```

```python
import functools

import jax
import jax.numpy as jnp
import numpy as np
from jax import lax
from jax.experimental import pallas as pl
from jax.experimental.pallas import tpu as pltpu
from jax.sharding import PartitionSpec as P

C = 384
HID = 1536
CLASSES = 1000
CLASS_PAD = 1024
WSIDE = 7
GRID = 14
STEP = 10
HEADS = 12
DEPTH = 32
CELLS = GRID * GRID
ROWS = 208
AREA = WSIDE * WSIDE
SLOT = 64
NWIN = 4
NGRP = 3
PACK = 4
WROWS = NWIN * SLOT
LANES = PACK * SLOT

NORM_EPS = 1e-05
CLIP_NORM = 0.05
LEARN_RATE = 0.04
SMALL_RATE = 0.2
DECAY_RATE = 0.05
ADAM_EPS = 1e-08
MASKED = -1e30
SCALE = DEPTH ** (-0.5)
F32 = jnp.float32
BF16 = jnp.bfloat16
NN = (((1,), (0,)), ((), ()))
NT = (((1,), (1,)), ((), ()))
TN = (((0,), (0,)), ((), ()))
VMEM_LIMIT = 58 * 1024 * 1024


def dot(a, b, dims=NN):
    return lax.dot_general(a, b, dims, preferred_element_type=F32)


@functools.lru_cache(None)
def window_tables(shifted):
    perm = np.zeros((WROWS, ROWS), np.float32)
    row_limit = np.full((NWIN, SLOT, 2 * SLOT), 99, np.int32)
    col_limit = np.full((NWIN, SLOT, 2 * SLOT), 99, np.int32)
    shift = WSIDE // 2 if shifted else 0

    def band(v):
        return 0 if v < GRID - WSIDE else (1 if v < GRID - WSIDE // 2 else 2)

    for window in range(NWIN):
        wr, wc = divmod(window, GRID // WSIDE)
        place = []
        for j in range(AREA):
            r, c = wr * WSIDE + j // WSIDE, wc * WSIDE + j % WSIDE
            region = 3 * band(r) + band(c) if shifted else 0
            source = ((r + shift) % GRID, (c + shift) % GRID)
            place.append((region, source))
            perm[window * SLOT + j, source[0] * GRID + source[1]] = 1
        for j in range(SLOT):
            for i in range(SLOT):
                if i == j:
                    pair = (-1, -1)
                elif i < AREA and j < AREA and place[i][0] == place[j][0]:
                    pair = place[j][1]
                else:
                    pair = (99, 99)
                row_limit[window, j, i::SLOT] = pair[0]
                col_limit[window, j, i::SLOT] = pair[1]
    return perm, row_limit, col_limit


@functools.lru_cache(None)
def relative_onehot():
    span = 2 * WSIDE - 1
    onehot = np.zeros((span * span, SLOT, SLOT), np.float32)
    for i in range(AREA):
        for j in range(AREA):
            row, col = i // WSIDE - j // WSIDE, i % WSIDE - j % WSIDE
            onehot[(row + WSIDE - 1) * span + col + WSIDE - 1, j, i] = 1
    return onehot.reshape(span * span, SLOT * SLOT)


def norm_parts(field):
    average = jnp.mean(field, -1, keepdims=True)
    centered = field - average
    spread = jnp.mean(centered * centered, -1, keepdims=True)
    rate = lax.rsqrt(spread + NORM_EPS)
    return centered * rate, rate


def norm_back(grad, hat, rate, gain):
    scaled = grad * gain
    return rate * (
        scaled
        - jnp.mean(scaled, -1, keepdims=True)
        - hat * jnp.mean(scaled * hat, -1, keepdims=True)
    )


def col_sum(field):
    return jnp.sum(field, 0, keepdims=True)


def head_masks(dtype):
    lane = lax.broadcasted_iota(jnp.int32, (SLOT, 128), 1)
    return [((lane // DEPTH) == h).astype(F32).astype(dtype) for h in range(PACK)]


def spread_heads(block, masks):
    return jnp.concatenate([block * m for m in masks], 0)


def all_bits(sizes):
    return [(axis, bit) for axis in ("win", "ch") for bit in range(sizes[axis].bit_length() - 1)]


def relative_places(bits):
    places = []
    for index in range(1 << len(bits)):
        offset = {"win": 0, "ch": 0}
        for n, (axis, bit) in enumerate(bits):
            offset[axis] |= ((index >> (len(bits) - 1 - n)) & 1) << bit
        places.append((offset["win"], offset["ch"]))
    return places


def load_blocks(pieces, target, where, sem, me_ref, block_rows):
    if block_rows is None:
        (ref, _, _), = pieces
        pltpu.make_async_copy(ref, target, sem).start()
        return
    for (ref, places, _), (source, width, start) in zip(pieces, where):
        for n, (win, ch) in enumerate(places):
            row = pl.multiple_of((me_ref[0] ^ win) * block_rows, block_rows)
            pltpu.make_async_copy(
                ref.at[n, :, source : source + width],
                target.at[me_ref[1] ^ ch, pl.ds(row, block_rows), start : start + width],
                sem,
            ).start()


def wait_all(ref, sem):
    pltpu.make_async_copy(ref, ref, sem).wait()


def store_blocks(source, outs, sems, me_ref, block_rows):
    width = source.shape[2]
    for number, (ref, places, start) in enumerate(outs):
        if block_rows is None:
            copy = pltpu.make_async_copy(source, ref, sems.at[number])
            copy.start()
            copy.wait()
            continue
        for n, (win, ch) in enumerate(places):
            row = pl.multiple_of((me_ref[0] ^ win) * block_rows, block_rows)
            pltpu.make_async_copy(
                source.at[me_ref[1] ^ ch, pl.ds(row, block_rows), :],
                ref.at[n, :, start : start + width],
                sems.at[number],
            ).start()


def wait_blocks(outs, sems, block_rows):
    if block_rows is None:
        return
    for number, (ref, _, _) in enumerate(outs):
        wait_all(ref, sems.at[number])


def join_attention(stage, w_qkv, w_proj):
    owners = stage.shape[0]
    wide, narrow = 3 * C // owners, C // owners
    w_qkv[...] = jnp.concatenate([stage[n, :, :wide] for n in range(owners)], 1)
    w_proj[...] = jnp.concatenate([stage[n, :, wide : wide + narrow] for n in range(owners)], 1)


def pick_heads(first, second):
    lane = lax.broadcasted_iota(jnp.int32, (DEPTH, 128), 1)
    parts = []
    for h in range(PACK):
        at = (slice(h * DEPTH, (h + 1) * DEPTH), slice(h // 2 * 128, (h // 2 + 1) * 128))
        one, two = first[at], second[at]
        if h % 2:
            one = pltpu.roll(one, SLOT, 1)
        else:
            two = pltpu.roll(two, SLOT, 1)
        parts.append(jnp.where(lane < SLOT, one, two))
    return jnp.concatenate(parts, 0)


def apply_pair(rows_ref, cut, eye, first, second):
    turned = dot(eye, rows_ref[cut], NT).astype(BF16)
    empty = jnp.zeros_like(first)
    full = dot(
        turned,
        jnp.concatenate(
            [jnp.concatenate([first, empty], 1), jnp.concatenate([empty, second], 1)], 0
        ),
    )
    return pick_heads(full[:, :LANES], full[:, LANES:])


def identity():
    shape = (128, 128)
    same = lax.broadcasted_iota(jnp.int32, shape, 0) == lax.broadcasted_iota(jnp.int32, shape, 1)
    return same.astype(F32).astype(BF16)


def forward_attention(
    field, rows, cols, w_qkv, w_proj, perm, perm_t, row_limit, col_limit, bias, small, qkv_bias,
    qkv_ref, prob_ref, mixed_ref,
):
    hat, _ = norm_parts(field)
    normed = (hat * small[0:1] + small[1:2]).astype(BF16)
    windowed = dot(perm[...], normed).astype(BF16)
    qkv_ref[...] = (dot(windowed, w_qkv[...]) + qkv_bias[...]).astype(BF16)
    low_masks = head_masks(BF16)
    eye = identity()
    for pair in range(NWIN // 2):
        blocks = []
        for w in (2 * pair, 2 * pair + 1):
            allowed = (row_limit[w] < rows) & (col_limit[w] < cols)
            block = jnp.where(allowed, 0.0, MASKED).astype(F32)
            blocks.append(jnp.concatenate([block, block], 1))
        both = slice(pair * 2 * SLOT, (pair + 1) * 2 * SLOT)
        for g in range(NGRP):
            probs = []
            for n in range(2):
                w = 2 * pair + n
                at = slice(w * SLOT, (w + 1) * SLOT)
                query = qkv_ref[at, g * 128 : (g + 1) * 128]
                key = qkv_ref[at, C + g * 128 : C + (g + 1) * 128]
                score = dot(key, spread_heads(query, low_masks), NT) * SCALE + bias[g] + blocks[n]
                top = jnp.max(score, 0, keepdims=True)
                expo = jnp.exp(score - top)
                prob = (expo * (1.0 / jnp.sum(expo, 0, keepdims=True))).astype(BF16)
                prob_ref[w, g] = prob
                probs.append(prob)
            value = (both, slice(2 * C + g * 128, 2 * C + (g + 1) * 128))
            mixed_ref[g * 128 : (g + 1) * 128, both] = apply_pair(
                qkv_ref, value, eye, probs[0], probs[1]
            ).astype(BF16)
    attended = dot(perm_t[...], mixed_ref[...], NT).astype(BF16)
    middle = field + dot(attended, w_proj[...]) + small[4:5]
    return normed, attended, middle


def forward_mlp(middle, w_up, w_down, small, up_bias, active_ref, slope_ref):
    hat, _ = norm_parts(middle)
    mlp_in = (hat * small[5:6] + small[6:7]).astype(BF16)
    branch = jnp.zeros((ROWS, C), F32)
    width = w_up.shape[2]
    for part in range(w_up.shape[0]):
        at = slice(part * width, (part + 1) * width)
        pre = dot(mlp_in, w_up[part]) + up_bias[:, at]
        half = 0.5 * (1.0 + lax.erf(pre * (0.5**0.5)))
        active = (pre * half).astype(BF16)
        slope = half + pre * (jnp.exp(-0.5 * pre * pre) * ((2.0 * np.pi) ** -0.5))
        active_ref[:, at] = active
        slope_ref[:, at] = slope.astype(BF16)
        branch = branch + dot(active, w_down[part], NT)
    return mlp_in, middle + branch + small[7:8]


def backward_mlp(
    grad, middle, slope_ref, w_up, w_down, small, low_ref, pre_ref, rows_ref, up_rows_ref, place
):
    low = grad.astype(BF16)
    low_ref[place, :] = low
    rows_ref[7:8, :] += col_sum(low.astype(F32))
    normed_grad = jnp.zeros((ROWS, C), F32)
    width = w_up.shape[2]
    for part in range(w_up.shape[0]):
        at = slice(part * width, (part + 1) * width)
        pre = (dot(low, w_down[part]) * slope_ref[:, at].astype(F32)).astype(BF16)
        pre_ref[place, at] = pre
        up_rows_ref[:, at] += col_sum(pre.astype(F32))
        normed_grad = normed_grad + dot(pre, w_up[part], NT)
    hat, rate = norm_parts(middle)
    rows_ref[5:6, :] += col_sum(normed_grad * hat)
    rows_ref[6:7, :] += col_sum(normed_grad)
    return norm_back(normed_grad, hat, rate, small[5:6]) + grad


def backward_attention(
    grad_mid, field, qkv_ref, prob_ref, w_qkv, w_proj, perm, perm_t, small,
    spread_ref, dq_ref, dkv_ref, attn_ref, joined_ref, rows_ref, qkv_rows_ref, bias_grad_ref, place,
):
    attn = grad_mid.astype(BF16)
    attn_ref[place, :] = attn
    rows_ref[4:5, :] += col_sum(attn.astype(F32))
    joined = dot(attn, w_proj[...], NT).astype(BF16)
    joined_ref[...] = dot(perm[...], joined).astype(BF16)
    low_masks = head_masks(BF16)
    eye = identity()
    for pair in range(NWIN // 2):
        both = slice(pair * 2 * SLOT, (pair + 1) * 2 * SLOT)
        for g in range(NGRP):
            cut = [slice(n * C + g * 128, n * C + (g + 1) * 128) for n in range(3)]
            scores = []
            for w in (2 * pair, 2 * pair + 1):
                at = slice(w * SLOT, (w + 1) * SLOT)
                query = spread_heads(qkv_ref[at, cut[0]], low_masks)
                value = qkv_ref[at, cut[2]]
                out = spread_heads(joined_ref[at, cut[0]], low_masks)
                prob = prob_ref[w, g]
                wide = prob.astype(F32)
                prob_grad = dot(value, out, NT)
                score = wide * (prob_grad - jnp.sum(wide * prob_grad, 0, keepdims=True))
                bias_grad_ref[g] += score
                score = score.astype(BF16)
                dkv_ref[at, cut[1]] = dot(prob, out).astype(BF16)
                dkv_ref[at, cut[0]] = (dot(score, query) * SCALE).astype(BF16)
                scores.append(score)
            dq_ref[cut[0], both] = (
                apply_pair(qkv_ref, (both, cut[1]), eye, scores[0], scores[1]) * SCALE
            ).astype(BF16)
    back_q = dot(perm_t[...], dq_ref[...], NT).astype(BF16)
    back_kv = dot(perm_t[...], dkv_ref[...]).astype(BF16)
    spread_ref[place, :C] = back_q
    spread_ref[place, C:] = back_kv
    qkv_rows_ref[:, :C] += col_sum(back_q.astype(F32))
    qkv_rows_ref[:, 2 * C :] += col_sum(back_kv[:, C:].astype(F32))
    back = spread_ref[place, :]
    normed_grad = dot(back, w_qkv[...], NT)
    hat, rate = norm_parts(field)
    rows_ref[0:1, :] += col_sum(normed_grad * hat)
    rows_ref[1:2, :] += col_sum(normed_grad)
    return norm_back(normed_grad, hat, rate, small[0:1]) + grad_mid


def image_place():
    return pl.ds(pl.multiple_of(pl.program_id(0) * ROWS, 16), ROWS)


def is_first():
    return pl.program_id(0) == 0


def is_last():
    return pl.program_id(0) == pl.num_programs(0) - 1


def clear(*refs):
    @pl.when(is_first())
    def _():
        for ref in refs:
            ref[...] = jnp.zeros(ref.shape, ref.dtype)


def by_owner(left, right, target):
    owners, _, width = target.shape
    for n in range(owners):
        target[n] = dot(left[...], right[:, n * width : (n + 1) * width], TN).astype(BF16)


class Names:
    def __init__(self, **refs):
        self.__dict__.update(refs)


def fetch_attention(k, plan):
    @pl.when(is_first())
    def _():
        load_blocks(plan.pieces(k, "attn"), k.stage, plan.where["attn"], k.load_sem.at[0], k.me, plan.block_rows)
        wait_all(k.stage, k.load_sem.at[0])
        join_attention(k.stage, k.w_qkv, k.w_proj)


def fetch_mlp(k, plan):
    @pl.when(is_first())
    def _():
        load_blocks(plan.pieces(k, "down"), k.w_down, plan.where["down"], k.load_sem.at[1], k.me, plan.block_rows)
        load_blocks(plan.pieces(k, "up"), k.w_up, plan.where["up"], k.load_sem.at[2], k.me, plan.block_rows)
        wait_all(k.w_down, k.load_sem.at[1])
        wait_all(k.w_up, k.load_sem.at[2])


def run_forward_attention(k):
    image = pl.program_id(0)
    normed, attended, middle = forward_attention(
        k.field[...].astype(F32), k.rows[image], k.cols[image], k.w_qkv, k.w_proj, k.perm, k.perm_t,
        k.row_limit, k.col_limit, k.bias, k.small[...], k.qkv_bias, k.qkv, k.prob, k.mixed,
    )
    k.normed[...] = normed
    k.attended[...] = attended
    return middle


def first_attention_kernel(k, plan):
    fetch_attention(k, plan)
    k.middle[...] = run_forward_attention(k)


def first_mlp_kernel(k, plan):
    fetch_mlp(k, plan)
    mlp_in, result = forward_mlp(
        k.middle[...], k.w_up, k.w_down, k.small[...], k.up_bias, k.active, k.slope
    )
    k.mlp_in[...] = mlp_in
    k.result[...] = result


def store_mlp_grads(k, plan):
    by_owner(k.mlp_all, k.pre_all, k.up_grad)
    store_blocks(k.up_grad, plan.outs(k, "up"), k.sem_x, k.me, plan.block_rows)
    by_owner(k.low_all, k.active_all, k.down_grad)
    store_blocks(k.down_grad, plan.outs(k, "down"), k.sem_y, k.me, plan.block_rows)


def wait_mlp_grads(k, plan):
    wait_blocks(plan.outs(k, "up"), k.sem_x, plan.block_rows)
    wait_blocks(plan.outs(k, "down"), k.sem_y, plan.block_rows)


def head_pass(k, result, rows, cols, total_images):
    image = pl.program_id(0)
    hat, rate = norm_parts(result)
    inside = ((k.cell_row[...] < rows) & (k.cell_col[...] < cols)).astype(F32)
    count = (rows * cols).astype(F32)
    final = hat * k.final[0:1] + k.final[1:2]
    pooled = col_sum(final * inside) / count
    pooled = jnp.broadcast_to(pooled, (16, C)).astype(BF16)
    owners, _, width = k.w_head.shape
    classes = owners * width
    logits = jnp.concatenate([dot(pooled, k.w_head[n])[0:1] for n in range(owners)], 1)
    logits = logits + k.head_bias[...]
    top = jnp.max(logits, -1, keepdims=True)
    expo = jnp.exp(logits - top)
    log_probs = logits - top - jnp.log(jnp.sum(expo, -1, keepdims=True))
    lane = lax.broadcasted_iota(jnp.int32, (1, classes), 1)
    mixing = k.mix[image].astype(F32) / 16.0
    target = jnp.where(lane == k.own[image], mixing, 0.0)
    target = target + jnp.where(lane == k.other[image], 1.0 - mixing, 0.0)
    loss = jnp.sum(jnp.where(target > 0.0, target * log_probs, 0.0), -1, keepdims=True)
    k.loss[...] -= jnp.broadcast_to(loss, k.loss.shape)
    logit_grad = (jnp.exp(log_probs) - target) / total_images
    logit_low = jnp.broadcast_to(logit_grad, (16, classes)).astype(BF16)
    k.head_rows[...] += logit_low[0:1].astype(F32)
    k.pooled_all[pl.ds(image, 1), :] = pooled[0:1].astype(F32)
    k.logit_all[pl.ds(image, 1), :] = logit_low[0:1].astype(F32)
    pooled_grad = jnp.zeros((16, C), F32)
    for n in range(owners):
        pooled_grad += dot(logit_low[:, n * width : (n + 1) * width], k.w_head[n], NT)
    final_grad = pooled_grad[0:1] * (inside / count)
    k.final_rows[0:1, :] += col_sum(final_grad * hat)
    k.final_rows[1:2, :] += col_sum(final_grad)
    return norm_back(final_grad, hat, rate, k.final[0:1])


def last_mlp_kernel(k, plan, total_images):
    image = pl.program_id(0)
    place = image_place()

    @pl.when(is_first())
    def _():
        load_blocks(plan.pieces(k, "head"), k.w_head, plan.where["head"], k.load_sem.at[3], k.me, plan.block_rows)

    fetch_mlp(k, plan)

    @pl.when(is_first())
    def _():
        wait_all(k.w_head, k.load_sem.at[3])

    clear(k.row_sums, k.up_rows, k.final_rows, k.head_rows, k.loss, k.pooled_all, k.logit_all)
    mlp_in, result = forward_mlp(
        k.middle[...], k.w_up, k.w_down, k.small[...], k.up_bias, k.active_all.at[place], k.slope
    )
    k.mlp_all[place, :] = mlp_in
    grad = head_pass(k, result, k.rows[image], k.cols[image], total_images)
    k.grad_mid[...] = backward_mlp(
        grad, k.middle[...], k.slope, k.w_up, k.w_down, k.small[...], k.low_all, k.pre_all,
        k.row_sums, k.up_rows, place,
    )

    @pl.when(is_last())
    def _():
        store_mlp_grads(k, plan)
        total = dot(k.pooled_all[...].astype(BF16), k.logit_all[...].astype(BF16), TN).astype(BF16)
        owners, _, width = k.head_grad.shape
        for n in range(owners):
            k.head_grad[n] = total[:, n * width : (n + 1) * width]
        store_blocks(k.head_grad, plan.outs(k, "head"), k.sem_x, k.me, plan.block_rows)
        wait_mlp_grads(k, plan)


def backward_mlp_kernel(k, plan):
    fetch_mlp(k, plan)
    clear(k.row_sums, k.up_rows)
    place = image_place()
    k.mlp_all[place, :] = k.mlp_in[...]
    k.active_all[place, :] = k.active[...]
    k.grad_mid[...] = backward_mlp(
        k.grad[...], k.middle[...], k.slope, k.w_up, k.w_down, k.small[...], k.low_all, k.pre_all,
        k.row_sums, k.up_rows, place,
    )

    @pl.when(is_last())
    def _():
        store_mlp_grads(k, plan)
        wait_mlp_grads(k, plan)


def backward_attention_kernel(k, plan):
    fetch_attention(k, plan)
    clear(k.row_sums, k.qkv_rows, k.bias_grad)
    place = image_place()
    k.normed_all[place, :] = k.normed[...]
    k.attended_all[place, :] = k.attended[...]
    k.grad[...] = backward_attention(
        k.grad_mid[...], k.field[...].astype(F32), k.qkv, k.prob, k.w_qkv, k.w_proj, k.perm,
        k.perm_t, k.small[...], k.spread_all, k.dq, k.dkv, k.attn_all, k.joined, k.row_sums, k.qkv_rows,
        k.bias_grad, place,
    )

    @pl.when(is_last())
    def _():
        owners, _, _ = k.attn_grad.shape
        wide, narrow = 3 * C // owners, C // owners
        total = dot(k.normed_all[...], k.spread_all[...], TN).astype(BF16)
        for n in range(owners):
            k.attn_grad[n, :, :wide] = total[:, n * wide : (n + 1) * wide]
        total = dot(k.attended_all[...], k.attn_all[...], TN).astype(BF16)
        for n in range(owners):
            k.attn_grad[n, :, wide:] = total[:, n * narrow : (n + 1) * narrow]
        store_blocks(k.attn_grad, plan.outs(k, "attn"), k.sem_a, k.me, plan.block_rows)
        wait_blocks(plan.outs(k, "attn"), k.sem_a, plan.block_rows)


class Plan:
    def __init__(self, block_rows):
        self.block_rows = block_rows
        self.sources = {}
        self.where = {}
        self.targets = {}

    def pieces(self, k, name):
        return [(getattr(k, ref), places, None) for ref, places in self.sources[name]]

    def outs(self, k, name):
        return [(getattr(k, ref), places, start) for ref, places, start in self.targets[name]]


def whole(shape):
    return pl.BlockSpec(shape, lambda i: (0,) * len(shape))


def per_image(*shape):
    return pl.BlockSpec((None,) + shape, lambda i: (i,) + (0,) * len(shape))


SCALARS = pl.BlockSpec(memory_space=pltpu.SMEM)
FAR = pl.BlockSpec(memory_space=pl.ANY)


def call(body, name, local, ins, outs, scratch, flops):
    def kernel(*refs):
        body(Names(**dict(zip(list(ins) + list(outs) + list(scratch), refs))))

    moved = sum(a.size * a.dtype.itemsize for _, a in ins.values())
    results = pl.pallas_call(
        kernel,
        grid=(local,),
        in_specs=[spec for spec, _ in ins.values()],
        out_specs=[spec for spec, _, _ in outs.values()],
        out_shape=[jax.ShapeDtypeStruct(dims, dtype) for _, dims, dtype in outs.values()],
        scratch_shapes=list(scratch.values()),
        compiler_params=pltpu.CompilerParams(
            dimension_semantics=("arbitrary",), vmem_limit_bytes=VMEM_LIMIT
        ),
        cost_estimate=pl.CostEstimate(flops=int(flops), bytes_accessed=int(moved), transcendentals=0),
        name=name,
    )(*[array for _, array in ins.values()])
    return dict(zip(outs, results))


def exchange(array, step):
    axis, bit = step
    size = lax.axis_size(axis)
    return lax.ppermute(array, axis, [(i, i ^ (1 << bit)) for i in range(size)])


def double(held, step):
    return jnp.stack([held, exchange(held, step)])


def tie(*values):
    return lax.optimization_barrier(values)


def small_call(kernel, name, args, outs, flops=0, stream=False, scratch=()):
    moved = sum(a.size * a.dtype.itemsize for a in args)

    def spec(dims):
        return whole(dims) if stream else pl.BlockSpec(memory_space=pltpu.VMEM)

    return pl.pallas_call(
        kernel,
        grid=(1,) if stream else (),
        out_shape=[jax.ShapeDtypeStruct(dims, dtype) for dims, dtype in outs],
        in_specs=[spec(a.shape) for a in args],
        out_specs=[spec(dims) for dims, _ in outs],
        scratch_shapes=list(scratch),
        compiler_params=pltpu.CompilerParams(vmem_limit_bytes=24 * 1024 * 1024),
        cost_estimate=pl.CostEstimate(flops=flops, bytes_accessed=2 * moved, transcendentals=0),
        name=name,
    )(*args)


class Chain:
    def __init__(self, keep, send, steps):
        self.keep, self.send, self.steps = keep, send, list(steps)

    def start(self):
        self.received = exchange(self.send, self.steps.pop(0))


def combine(groups, name):
    args, outs = [], []
    for group in groups:
        for chain in group:
            args += [chain.keep, chain.received]
        count, rows, _ = group[0].keep.shape
        width = sum(chain.keep.shape[2] for chain in group)
        outs += [((count // 2, rows, width), BF16)] * 2

    def kernel(*refs):
        ins, results = list(refs[: len(args)]), list(refs[len(args) :])
        for group in groups:
            keep_out, send_out = results.pop(0), results.pop(0)
            half, at = keep_out.shape[0], 0
            for _ in group:
                keep, received = ins.pop(0), ins.pop(0)
                width = keep.shape[2]
                for n in range(2 * half):
                    out = keep_out if n < half else send_out
                    out[n % half, :, at : at + width] = (
                        keep[n].astype(F32) + received[n].astype(F32)
                    ).astype(BF16)
                at += width

    results = small_call(kernel, name, args, outs)
    return [
        Chain(results[2 * n], results[2 * n + 1], group[0].steps) for n, group in enumerate(groups)
    ]


def finish(chain, name):
    _, rows, width = chain.keep.shape

    def kernel(keep, received, own, square):
        total = keep[0].astype(F32) + received[0].astype(F32)
        own[...] = total
        square[...] = jnp.broadcast_to(jnp.sum(total * total), (1, 128))

    return small_call(
        kernel, name, [chain.keep, chain.received], [((rows, width), F32), ((1, 128), F32)]
    )


def adam_step(weight, grad, first, second, rate):
    new_first = 0.5 * first + 0.5 * grad
    new_second = 0.5 * second + 0.5 * grad * grad
    fix = 1.0 - 0.5**STEP
    update = new_first / fix / (jnp.sqrt(new_second / fix) + ADAM_EPS)
    return (new_first, new_second, weight - rate * (update + DECAY_RATE * weight))


def update_kernel(starts, widths, layout, *refs):
    own, message, rest = refs[:2], refs[2], list(refs[3:])
    groups = [rest[3 * n : 3 * n + 3] for n in range(7)]
    loss_ref, norm_ref = rest[21], rest[22]
    outs = [rest[23 + 3 * n : 26 + 3 * n] for n in range(7)]
    vector_rows, table_rows, offsets, square_at, loss_at = layout
    vector_grad = message[:vector_rows, :C]
    table_grad = message[:table_rows, C : C + offsets]
    total = (
        jnp.sum(message[:, square_at : square_at + 1])
        + jnp.sum(vector_grad * vector_grad)
        + jnp.sum(table_grad * table_grad)
    )
    norm = jnp.sqrt(jnp.broadcast_to(total, (1, 1)))
    factor = CLIP_NORM / jnp.maximum(norm, CLIP_NORM)
    norm_ref[...] = norm
    loss_ref[...] = message[0:1, loss_at : loss_at + 1]

    def put(number, layer, grad, rate):
        weight, first, second = groups[number]
        index = (Ellipsis,) if layer is None else (layer, Ellipsis)
        if number == 6:
            index = (slice(None), layer, slice(None))
        results = adam_step(weight[index], factor * grad, first[index], second[index], rate)
        for ref, value in zip(outs[number], results):
            ref[index] = value

    layers = len(starts)
    for l in range(layers):
        qkv_width = outs[0][0].shape[2]
        at = starts[l]["attn"]
        put(0, l, own[l][:, at : at + qkv_width], LEARN_RATE)
        put(1, l, own[l][:, at + qkv_width : at + widths["attn"]], LEARN_RATE)
        at = starts[l]["up"]
        put(2, l, own[l][:, at : at + widths["up"]], LEARN_RATE)
        at = starts[l]["down"]
        put(3, l, own[l][:, at : at + widths["down"]], LEARN_RATE)
        heads = table_rows // layers
        put(6, l, table_grad[l * heads : (l + 1) * heads], SMALL_RATE)
    at = starts[-1]["head"]
    put(4, None, own[-1][:, at : at + outs[4][0].shape[1]], LEARN_RATE)
    put(5, None, vector_grad, SMALL_RATE)


def collect_kernel(layers, head_real, loss_at, *refs):
    *ins, out, spread = refs
    out[...] = jnp.zeros(out.shape, F32)
    row_of_slot = lax.broadcasted_iota(jnp.int32, (SLOT, 128), 0)
    lane = lax.broadcasted_iota(jnp.int32, (SLOT, 128), 1)
    target = row_of_slot // WSIDE * (2 * WSIDE - 1) + row_of_slot % WSIDE
    spreader = ((lane == target) & (row_of_slot < AREA)).astype(F32).astype(BF16)
    row = 0
    for l in range(layers):
        attn_rows, qkv_rows, mlp_rows, up_rows, bias_grad = ins[5 * l : 5 * l + 5]
        parts = [
            attn_rows[0:2], qkv_rows[:, :C], qkv_rows[:, 2 * C :], attn_rows[4:5], mlp_rows[5:8],
        ] + [up_rows[:, n * C : (n + 1) * C] for n in range(HID // C)]
        for part in parts:
            out[row : row + part.shape[0], :C] = part
            row += part.shape[0]
        for head in range(HEADS):
            g, h = divmod(head, PACK)
            left = bias_grad[g, :, h * SLOT : (h + 1) * SLOT]
            total = jnp.zeros((SLOT, 128), F32)
            for _ in range(3):
                low = left.astype(BF16)
                total = total + dot(low, spreader)
                left = left - low.astype(F32)
            spread[head * SLOT : (head + 1) * SLOT, :] = total
        table = jnp.zeros((HEADS, 256), F32)
        span = 2 * WSIDE - 1
        for j in range(AREA):
            wide = jnp.concatenate(
                [spread[pl.ds(j, HEADS, stride=SLOT), :], jnp.zeros((HEADS, 128), F32)], 1
            )
            shift = (WSIDE - 1 - j // WSIDE) * span + WSIDE - 1 - j % WSIDE
            table = table + (pltpu.roll(wide, shift, 1) if shift else wide)
        width = out.shape[1] - C
        out[l * HEADS : (l + 1) * HEADS, C:] = table[:, :width]
    final_rows, head_rows, loss = ins[5 * layers :]
    out[row : row + 2, :C] = final_rows[...]
    row += 2
    owners = CLASSES // head_real
    width = head_rows.shape[1] // owners
    classes = jnp.concatenate(
        [head_rows[:, n * width : n * width + head_real] for n in range(owners)]
        + [jnp.zeros((1, -CLASSES % C), F32)], 1
    )
    for n in range(classes.shape[1] // C):
        out[row + n : row + n + 1, :C] = classes[:, n * C : (n + 1) * C]
    out[0:1, loss_at : loss_at + 1] = loss[:, 0:1]


def pack_kernel(head_width, qkv, proj, down, up, head, *outs):
    for l, out in enumerate(outs):
        parts = [qkv[l], proj[l], down[l], up[l]]
        if l == len(outs) - 1:
            parts.append(head[...])
            pad = head_width - head.shape[1]
            if pad:
                parts.append(jnp.zeros((head.shape[0], pad), F32))
        out[...] = jnp.concatenate(parts, 1).astype(BF16)


def per_device(
    tokens, valid_rows, valid_cols, partner, mix_level, labels,
    w_qkv, m_qkv, v_qkv, w_proj, m_proj, v_proj, w_fc1, m_fc1, v_fc1, w_fc2, m_fc2, v_fc2,
    w_head, m_head, v_head, vectors, m_vec, v_vec, rel_table, m_rel, v_rel,
):
    micro, images, cells, chans = tokens.shape
    layers = rel_table.shape[0]
    per_layer = 8 + HID // C
    base = layers * per_layer
    head_rows = vectors.shape[0] - base - 2
    all_images = labels.shape[1]
    total_images = micro * all_images
    local = micro * images
    sizes = {axis: lax.axis_size(axis) for axis in ("win", "ch")}
    win_count, ch_count = sizes["win"], sizes["ch"]
    device_count = win_count * ch_count
    win_index, ch_index = lax.axis_index("win"), lax.axis_index("ch")
    me = jnp.stack([win_index, ch_index]).astype(jnp.int32)
    block_rows = C // win_count
    widths = {"attn": 4 * C // ch_count, "down": HID // ch_count, "up": HID // ch_count}
    head_real = CLASSES // ch_count
    widths["head"] = -(-head_real // 128) * 128
    head_classes = widths["head"] * ch_count
    direct = block_rows % 16 == 0 and all(w % 128 == 0 for w in widths.values())

    core = ("ch", 0)
    ch_high = [("ch", b) for b in range(1, ch_count.bit_length() - 1)]
    win_low = [("win", 0)]
    win_high = [("win", b) for b in range(1, win_count.bit_length() - 1)]

    def low(v):
        return v.astype(BF16)

    def flipped(places):
        return [(win, ch ^ 1) for win, ch in places]

    packed = small_call(
        functools.partial(pack_kernel, widths["head"]), "pack",
        [w_qkv, w_proj, w_fc2.transpose(0, 2, 1), w_fc1, w_head],
        [((block_rows, sum(widths[n] for n in names)), BF16) for names in (
            ("attn", "down", "up"), ("attn", "down", "up", "head"))],
        stream=True,
    )
    names = [["attn", "down", "up"], ["attn", "down", "up", "head"]]
    cuts = [widths["attn"] + 2 * widths["down"] // 3 // 128 * 128] * 2
    rest = [ch_high[::-1] + win_low, win_low + ch_high[::-1]]
    common = win_high[::-1]

    def far_gather(block):
        for step in common:
            block = double(block, step)
        return block

    def near_gather(block, cut, group, step_at):
        held = block[..., :cut] if group == 0 else block[..., cut:]
        return double(held, rest[group][step_at])

    far = [far_gather(packed[0])]
    second, far[0] = tie(packed[1], far[0])
    far.append(far_gather(second))

    def split(layer):
        return [far[layer][..., : cuts[layer]], far[layer][..., cuts[layer] :]]

    held, other = [split(0)], []
    for at in range(len(rest[0])):
        held[0] = [double(held[0][g], rest[g][at]) for g in range(2)]
    other.append([exchange(part, core) for part in held[0]])
    held.append(split(1))

    def weight_inputs(layer, wanted):
        plan = Plan(block_rows if direct else None)
        ins = {}
        starts, at = {}, 0
        for name in names[layer]:
            starts[name] = at
            at += widths[name]
        bounds = [(0, cuts[layer]), (cuts[layer], at)]
        blocks = []
        for group in range(2):
            places = relative_places((common + rest[group])[::-1])
            for number, array in enumerate((held[layer][group], other[layer][group])):
                flat = array.reshape((-1,) + array.shape[-2:])
                blocks.append((group, places if number == 0 else flipped(places), flat))
        for name in wanted:
            plan.sources[name], plan.where[name] = [], []
            columns = []
            for number, (group, places, flat) in enumerate(blocks):
                begin = max(starts[name], bounds[group][0])
                end = min(starts[name] + widths[name], bounds[group][1])
                if begin >= end:
                    continue
                cut = (begin - bounds[group][0], end - begin, begin - starts[name])
                if direct:
                    ref = f"blocks{number}"
                    ins[ref] = (FAR, flat)
                    plan.sources[name].append((ref, places))
                    plan.where[name].append(cut)
                elif number % 2 == 0:
                    table = np.zeros((ch_count, win_count), np.int32)
                    for n, (win, ch) in enumerate(places + blocks[number + 1][1]):
                        table[ch, win] = n
                    both = jnp.concatenate([flat, blocks[number + 1][2]])
                    index = jnp.asarray(table)[jnp.arange(ch_count) ^ ch_index][
                        :, jnp.arange(win_count) ^ win_index
                    ]
                    full = jnp.take(both, index.reshape(-1), axis=0).reshape(
                        ch_count, C, flat.shape[-1]
                    )
                    columns.append(full[..., cut[0] : cut[0] + cut[1]])
            if not direct:
                ref = f"staged_{name}"
                ins[ref] = (FAR, jnp.concatenate(columns, -1))
                plan.sources[name] = [(ref, None)]
        ins["me"] = (SCALARS, me)
        return ins, plan

    orders = {
        "x": ch_high + win_low + win_high, "a": ch_high + win_low + win_high,
        "y": win_low + ch_high + win_high,
    }
    regular = direct and len(ch_high) == 1

    def grad_outputs(plan, **members):
        outs = {}
        for group, wanted in members.items():
            places = relative_places(orders[group])
            starts = np.cumsum([0] + [widths[name] for name in wanted])
            if direct:
                refs = [(f"keep_{group}", places), (f"send_{group}", flipped(places))]
                dims = (len(places), block_rows, int(starts[-1]))
            else:
                for name in wanted:
                    plan.targets[name] = [(f"full_{name}", None, 0)]
                    outs[f"full_{name}"] = (FAR, (ch_count, C, widths[name]), BF16)
                continue
            for ref, _ in refs:
                outs[ref] = (FAR, dims, BF16)
            for name, start in zip(wanted, starts):
                plan.targets[name] = [(ref, at, int(start)) for ref, at in refs]
        return outs

    def chain_of(results, group, *members):
        bits = orders[group]
        if direct:
            return Chain(results[f"keep_{group}"], results[f"send_{group}"], [core] + bits)
        full = jnp.concatenate([results[f"full_{name}"] for name in members], -1)
        full = full.reshape(device_count, block_rows, full.shape[-1])
        places = np.asarray(relative_places(bits))

        def ordered(flip):
            index = ((places[:, 1] ^ flip) ^ ch_index) * win_count + (places[:, 0] ^ win_index)
            return jnp.take(full, index, axis=0)

        return Chain(ordered(0), ordered(1), [core] + bits)

    def start(*chains):
        for chain in chains:
            chain.start()

    def after(value, *chains):
        held_back = [array for chain in chains for array in (chain.keep, chain.send)]
        value, *held_back = tie(value, *held_back)
        for n, chain in enumerate(chains):
            chain.keep, chain.send = held_back[2 * n], held_back[2 * n + 1]
        return value

    small = [vectors[l * per_layer : l * per_layer + 8] for l in range(layers)]
    up_bias = [
        vectors[l * per_layer + 8 : (l + 1) * per_layer].reshape(1, HID) for l in range(layers)
    ]
    qkv_bias = [
        jnp.concatenate([s[2], jnp.zeros_like(s[2]), s[3]]).reshape(1, 3 * C) for s in small
    ]
    final = vectors[base : base + 2]
    head_bias = jnp.pad(
        vectors[base + 2 :].reshape(-1)[:CLASSES].reshape(ch_count, head_real),
        ((0, 0), (0, widths["head"] - head_real)),
        constant_values=MASKED,
    ).reshape(1, head_classes)
    onehot = jnp.asarray(relative_onehot(), BF16)
    offsets = rel_table.shape[1]
    table = rel_table.transpose(0, 2, 1).reshape(layers * HEADS, offsets)
    table_parts = []
    for _ in range(3):
        table_parts.append(low(table))
        table = table - table_parts[-1].astype(F32)
    bias = dot(jnp.concatenate(table_parts, 0), onehot).reshape(3, layers, HEADS, SLOT * SLOT)
    bias = (bias[0] + bias[1]) + bias[2]
    bias = (
        bias.reshape(layers, NGRP, PACK, SLOT, SLOT)
        .transpose(0, 1, 3, 2, 4)
        .reshape(layers, NGRP, SLOT, LANES)
    )
    tables = [window_tables(l % 2 == 1) for l in range(layers)]
    perms = [jnp.asarray(t[0], BF16) for t in tables]
    perms_t = [jnp.asarray(t[0].T, BF16) for t in tables]
    row_limits = [jnp.asarray(t[1]) for t in tables]
    col_limits = [jnp.asarray(t[2]) for t in tables]

    rows = valid_rows.reshape(local)
    cols = valid_cols.reshape(local)
    image_ids = (win_index * ch_count + ch_index) * images + jnp.arange(images, dtype=jnp.int32)
    all_ids = jnp.arange(all_images, dtype=jnp.int32)
    own = jnp.sum(
        jnp.where(image_ids[None, :, None] == all_ids, labels[:, None, :], 0), -1
    ).reshape(local)
    partner_label = jnp.sum(
        jnp.where(partner[:, :, None] == all_ids, labels[:, None, :], 0), -1
    ).reshape(local)

    def class_lane(label):
        return label // head_real * widths["head"] + label % head_real

    padded = jnp.pad(tokens.reshape(local, cells, chans), ((0, 0), (0, ROWS - cells), (0, 0)))

    def attention_consts(l, forward):
        ins = {
            "perm": (whole((WROWS, ROWS)), perms[l]),
            "perm_t": (whole((ROWS, WROWS)), perms_t[l]),
            "small": (whole((8, C)), small[l]),
        }
        if forward:
            ins["rows"] = (SCALARS, rows)
            ins["cols"] = (SCALARS, cols)
            ins["row_limit"] = (whole((NWIN, SLOT, 128)), row_limits[l])
            ins["col_limit"] = (whole((NWIN, SLOT, 128)), col_limits[l])
            ins["bias"] = (whole((NGRP, SLOT, LANES)), bias[l])
            ins["qkv_bias"] = (whole((1, 3 * C)), qkv_bias[l])
        return ins

    def vmem(*dims, dtype=BF16):
        return pltpu.VMEM(dims, dtype)

    attn_weights = {
        "stage": vmem(ch_count, C, widths["attn"]),
        "w_qkv": vmem(C, 3 * C),
        "w_proj": vmem(C, C),
        "load_sem": pltpu.SemaphoreType.DMA((4,)),
    }
    mlp_weights = {
        "w_down": vmem(ch_count, C, widths["down"]),
        "w_up": vmem(ch_count, C, widths["up"]),
        "load_sem": pltpu.SemaphoreType.DMA((4,)),
    }
    all_rows = local * ROWS
    mlp_rows = {
        "mlp_all": vmem(all_rows, C), "active_all": vmem(all_rows, HID),
        "pre_all": vmem(all_rows, HID), "low_all": vmem(all_rows, C),
        "up_grad": vmem(ch_count, C, widths["up"]), "down_grad": vmem(ch_count, C, widths["down"]),
        "sem_x": pltpu.SemaphoreType.DMA((2,)), "sem_y": pltpu.SemaphoreType.DMA((2,)),
    }
    wide = (per_image(ROWS, C), (local, ROWS, C), F32)
    thin = (per_image(ROWS, C), (local, ROWS, C), BF16)
    hidden = (per_image(ROWS, HID), (local, ROWS, HID), BF16)
    attn_saved = {
        "normed": thin,
        "qkv": (per_image(WROWS, 3 * C), (local, WROWS, 3 * C), BF16),
        "prob": (per_image(NWIN, NGRP, SLOT, LANES), (local, NWIN, NGRP, SLOT, LANES), BF16),
        "attended": thin,
    }
    sums = {"row_sums": (whole((8, C)), (8, C), F32)}
    up_sums = {**sums, "up_rows": (whole((1, HID)), (1, HID), F32)}
    attn_sums = {
        **sums,
        "qkv_rows": (whole((1, 3 * C)), (1, 3 * C), F32),
        "bias_grad": (whole((NGRP, SLOT, LANES)), (NGRP, SLOT, LANES), F32),
    }

    def given(spec, array):
        return (spec[0], array)

    mlp_flops = 2 * all_rows * C * HID * 2
    attn_flops = 2 * all_rows * C * C * 8

    def attention_forward(l, field_spec, field):
        ins, plan = weight_inputs(l, ["attn"])
        ins["field"] = given(field_spec, field)
        ins.update(attention_consts(l, True))
        return call(
            functools.partial(first_attention_kernel, plan=plan), f"attention_forward{l}", local,
            ins, {"middle": wide, **attn_saved}, {"mixed": vmem(C, WROWS), **attn_weights},
            attn_flops,
        )

    tied, *held[1] = tie(padded, *held[1])
    late = len(rest[0]) - 1
    for at in range(late):
        held[1] = [double(held[1][g], rest[g][at]) for g in range(2)]
    saved0 = attention_forward(0, thin, tied)
    middle0, *held[1] = tie(saved0["middle"], *held[1])
    held[1] = [double(held[1][g], rest[g][late]) for g in range(2)]
    ins, plan = weight_inputs(0, ["down", "up"])
    ins["middle"] = given(wide, middle0)
    ins["small"] = (whole((8, C)), small[0])
    ins["up_bias"] = (whole((1, HID)), up_bias[0])
    mlp0 = call(
        functools.partial(first_mlp_kernel, plan=plan), "first_mlp", local, ins,
        {"result": wide, "mlp_in": thin, "active": hidden, "slope": hidden}, dict(mlp_weights),
        mlp_flops,
    )
    result0, *held[1] = tie(mlp0["result"], *held[1])
    other.append([exchange(part, core) for part in held[1]])

    saved1 = attention_forward(1, wide, result0)
    ins, plan = weight_inputs(1, ["down", "up", "head"])
    ins["middle"] = given(wide, saved1["middle"])
    ins["small"] = (whole((8, C)), small[1])
    ins["up_bias"] = (whole((1, HID)), up_bias[1])
    ins["rows"] = (SCALARS, rows)
    ins["cols"] = (SCALARS, cols)
    ins["own"] = (SCALARS, class_lane(own))
    ins["other"] = (SCALARS, class_lane(partner_label))
    ins["mix"] = (SCALARS, mix_level.reshape(local))
    ins["final"] = (whole((2, C)), final)
    ins["head_bias"] = (whole((1, head_classes)), head_bias)
    cell = np.arange(ROWS)
    for name, place in (("cell_row", cell // GRID), ("cell_col", cell % GRID)):
        place = np.where(cell < CELLS, place, 99)[:, None].astype(np.int32)
        ins[name] = (whole((ROWS, 1)), jnp.asarray(place))
    outs = {
        "grad_mid": wide, **up_sums,
        "final_rows": (whole((2, C)), (2, C), F32),
        "head_rows": (whole((1, head_classes)), (1, head_classes), F32),
        "loss": (whole((1, 128)), (1, 128), F32),
        **grad_outputs(plan, x=["up", "head"], y=["down"]),
    }
    last = call(
        functools.partial(last_mlp_kernel, plan=plan, total_images=float(total_images)),
        "last_mlp", local, ins, outs,
        {
            "slope": vmem(ROWS, HID), "w_head": vmem(ch_count, C, widths["head"]),
            **mlp_weights, **mlp_rows,
            "pooled_all": vmem(16, C, dtype=F32), "logit_all": vmem(16, head_classes, dtype=F32),
            "head_grad": vmem(ch_count, C, widths["head"]),
        },
        3 * mlp_flops,
    )

    def attention_backward(l, grad_mid, field_spec, field, saved):
        ins, plan = weight_inputs(l, ["attn"])
        ins["grad_mid"] = given(wide, grad_mid)
        ins["field"] = given(field_spec, field)
        for name, spec in attn_saved.items():
            ins[name] = given(spec, saved[name])
        ins.update(attention_consts(l, False))
        return call(
            functools.partial(backward_attention_kernel, plan=plan), f"attention_backward{l}",
            local, ins, {"grad": wide, **attn_sums, **grad_outputs(plan, a=["attn"])},
            {
                **attn_weights, "dq": vmem(C, WROWS), "dkv": vmem(WROWS, 2 * C), "joined": vmem(WROWS, C),
                "normed_all": vmem(all_rows, C), "attended_all": vmem(all_rows, C),
                "spread_all": vmem(all_rows, 3 * C), "attn_all": vmem(all_rows, C),
                "attn_grad": vmem(ch_count, C, widths["attn"]),
                "sem_a": pltpu.SemaphoreType.DMA((2,)),
            },
            2 * attn_flops,
        )

    x1, y1 = chain_of(last, "x", "up", "head"), chain_of(last, "y", "down")
    if regular:
        start(x1, y1)
    back1 = attention_backward(1, last["grad_mid"], wide, mlp0["result"], saved1)
    a1 = chain_of(back1, "a", "attn")
    grad = back1["grad"]
    if regular:
        x1, y1 = combine([[x1], [y1]], "sum1")
        grad = after(grad, x1, y1)
        start(x1, y1, a1)

    ins, plan = weight_inputs(0, ["down", "up"])
    ins["grad"] = given(wide, grad)
    ins["middle"] = given(wide, saved0["middle"])
    ins["mlp_in"] = given(thin, mlp0["mlp_in"])
    ins["active"] = given(hidden, mlp0["active"])
    ins["slope"] = given(hidden, mlp0["slope"])
    ins["small"] = (whole((8, C)), small[0])
    first = call(
        functools.partial(backward_mlp_kernel, plan=plan), "mlp_backward0", local, ins,
        {"grad_mid": wide, **up_sums, **grad_outputs(plan, x=["up"], y=["down"])},
        {**mlp_weights, **mlp_rows}, 2 * mlp_flops,
    )
    x0, y0 = chain_of(first, "x", "up"), chain_of(first, "y", "down")
    grad_mid = first["grad_mid"]
    if regular:
        x1, y1, a1 = combine([[x1], [y1], [a1]], "sum2")
        grad_mid = after(grad_mid, x1, y1, a1)
        start(x1, y1, a1, x0, y0)
    back0 = attention_backward(0, grad_mid, thin, padded, saved0)
    a0 = chain_of(back0, "a", "attn")

    if regular:
        a1, x0, y0 = combine([[a1], [x0], [y0]], "sum3")
        start(a0, x0, y0, a1)
        a0, x0, y0, z1 = combine([[a0], [x0], [y0], [a1, x1, y1]], "sum4")
        start(a0, x0, y0, z1)
        a0, z1 = combine([[a0], [z1]], "sum5")
        start(a0, z1)
        (z0,) = combine([[a0, x0, y0]], "sum6")
        start(z0)
        (z0,) = combine([[z0]], "sum7")
        start(z0)
        own1, square1 = finish(z1, "own1")
        own0, square0 = finish(z0, "own0")
        square = square0 + square1
    else:
        square, own = jnp.zeros((1, 128), F32), []
        for chain in (a0, x0, y0, a1, x1, y1):
            start(chain)
            while chain.steps:
                (chain,) = combine([[chain]], "sum")
                start(chain)
            part, part_square = finish(chain, "own")
            square = square + part_square
            own.append(part)
        own0, own1 = jnp.concatenate(own[:3], 1), jnp.concatenate(own[3:], 1)
    starts = []
    for order in (("attn", "up", "down"), ("attn", "up", "head", "down")):
        starts.append(dict(zip(order, np.cumsum([0] + [widths[n] for n in order]).tolist())))

    offsets = rel_table.shape[1]
    table_width = -(-(offsets + 1) // 128) * 128
    share = C + table_width
    (flat,) = small_call(
        functools.partial(collect_kernel, layers, head_real, share - 1), "collect",
        [part[name] for part in ((first, back0), (last, back1))
         for part, name in (
             (part[1], "row_sums"), (part[1], "qkv_rows"), (part[0], "row_sums"),
             (part[0], "up_rows"), (part[1], "bias_grad"))]
        + [last["final_rows"], last["head_rows"], last["loss"]],
        [((device_count, share), F32)],
        stream=True,
        scratch=[pltpu.VMEM((HEADS * SLOT, 128), F32)],
    )
    flat = lax.all_to_all(flat, ("win", "ch"), 0, 0, tiled=True)
    message = jnp.concatenate([jnp.sum(flat, 0, keepdims=True), square], 1)
    message = lax.all_to_all(
        jnp.broadcast_to(message, (device_count, share + 128)), ("win", "ch"), 0, 0, tiled=True
    )
    arrays = [
        [w_qkv, m_qkv, v_qkv], [w_proj, m_proj, v_proj], [w_fc1, m_fc1, v_fc1],
        [w_fc2, m_fc2, v_fc2], [w_head, m_head, v_head], [vectors, m_vec, v_vec],
        [rel_table, m_rel, v_rel],
    ]
    turns = {3: (0, 2, 1), 6: (2, 0, 1)}
    turned = [
        a.transpose(turns[n]) if n in turns else a for n, group in enumerate(arrays) for a in group
    ]
    results = small_call(
        functools.partial(
            update_kernel, starts, widths,
            (vectors.shape[0], layers * HEADS, offsets, share, share - 1),
        ),
        "update",
        [own0, own1, message] + turned,
        [((1, 1), F32)] * 2 + [(a.shape, F32) for a in turned],
        stream=True,
    )
    loss_total, grad_norm, *results = results
    outs = [loss_total[0, 0], grad_norm[0, 0]]
    for n in range(0, len(results), 3):
        back = {3: (0, 2, 1), 6: (1, 2, 0)}.get(n // 3)
        outs += [r if back is None else r.transpose(back) for r in results[n : n + 3]]
    return tuple(outs)


def solution(mesh):
    cut = P(None, "win", "ch")
    down = P(None, "ch", "win")
    head = P("win", "ch")
    rows = P(None, ("win", "ch"))
    in_specs = (
        (P(None, ("win", "ch"), None, None),) + (rows,) * 4 + (P(),)
        + (cut,) * 9 + (down,) * 3 + (head,) * 3 + (P(),) * 6
    )
    out_specs = (P(),) * 2 + (cut,) * 9 + (down,) * 3 + (head,) * 3 + (P(),) * 6
    return jax.shard_map(
        per_device, mesh=mesh, in_specs=in_specs, out_specs=out_specs, check_vma=False
    )
```

```python
import functools

import jax
import jax.numpy as jnp
import numpy as np
from jax import lax
from jax.experimental import pallas as pl
from jax.experimental.pallas import tpu as pltpu
from jax.sharding import PartitionSpec as P

C = 384
HID = 1536
CLASSES = 1000
CLASS_PAD = 1024
WSIDE = 7
GRID = 14
STEP = 10
HEADS = 12
PER_LAYER = 8 + HID // C
DEPTH = 32
CELLS = GRID * GRID
ROWS = 208
AREA = WSIDE * WSIDE
SLOT = 64
NWIN = 4
NGRP = 3
PACK = 4
WROWS = NWIN * SLOT
LANES = PACK * SLOT

NORM_EPS = 1e-05
CLIP_NORM = 0.05
LEARN_RATE = 0.04
SMALL_RATE = 0.2
DECAY_RATE = 0.05
ADAM_EPS = 1e-08
MASKED = -1e30
SCALE = DEPTH ** (-0.5)
F32 = jnp.float32
BF16 = jnp.bfloat16
NN = (((1,), (0,)), ((), ()))
NT = (((1,), (1,)), ((), ()))
TN = (((0,), (0,)), ((), ()))
VMEM_LIMIT = 58 * 1024 * 1024
GROUP = 2
CHUNK = 512


def dot(a, b, dims=NN):
    return lax.dot_general(a, b, dims, preferred_element_type=F32)


@functools.lru_cache(None)
def window_tables(shifted):
    perm = np.zeros((WROWS, ROWS), np.float32)
    row_limit = np.full((NWIN, SLOT, 2 * SLOT), 99, np.int32)
    col_limit = np.full((NWIN, SLOT, 2 * SLOT), 99, np.int32)
    shift = WSIDE // 2 if shifted else 0

    def band(v):
        return 0 if v < GRID - WSIDE else (1 if v < GRID - WSIDE // 2 else 2)

    for window in range(NWIN):
        wr, wc = divmod(window, GRID // WSIDE)
        place = []
        for j in range(AREA):
            r, c = wr * WSIDE + j // WSIDE, wc * WSIDE + j % WSIDE
            region = 3 * band(r) + band(c) if shifted else 0
            source = ((r + shift) % GRID, (c + shift) % GRID)
            place.append((region, source))
            perm[window * SLOT + j, source[0] * GRID + source[1]] = 1
        for j in range(SLOT):
            for i in range(SLOT):
                if i == j:
                    pair = (-1, -1)
                elif i < AREA and j < AREA and place[i][0] == place[j][0]:
                    pair = place[j][1]
                else:
                    pair = (99, 99)
                row_limit[window, j, i::SLOT] = pair[0]
                col_limit[window, j, i::SLOT] = pair[1]
    return perm, row_limit, col_limit


@functools.lru_cache(None)
def relative_onehot():
    span = 2 * WSIDE - 1
    onehot = np.zeros((span * span, SLOT, SLOT), np.float32)
    for i in range(AREA):
        for j in range(AREA):
            row, col = i // WSIDE - j // WSIDE, i % WSIDE - j % WSIDE
            onehot[(row + WSIDE - 1) * span + col + WSIDE - 1, j, i] = 1
    return onehot.reshape(span * span, SLOT * SLOT)


def norm_parts(field):
    average = jnp.mean(field, -1, keepdims=True)
    centered = field - average
    spread = jnp.mean(centered * centered, -1, keepdims=True)
    rate = lax.rsqrt(spread + NORM_EPS)
    return centered * rate, rate


def norm_back(grad, hat, rate, gain):
    scaled = grad * gain
    return rate * (
        scaled
        - jnp.mean(scaled, -1, keepdims=True)
        - hat * jnp.mean(scaled * hat, -1, keepdims=True)
    )


def col_sum(field):
    return jnp.sum(field, 0, keepdims=True)


def head_masks(dtype):
    lane = lax.broadcasted_iota(jnp.int32, (SLOT, 128), 1)
    return [((lane // DEPTH) == h).astype(F32).astype(dtype) for h in range(PACK)]


def spread_heads(block, masks):
    return jnp.concatenate([block * m for m in masks], 0)


def relative_owners(bits):
    owners = []
    for index in range(1 << len(bits)):
        offset = 0
        for n, (_, bit) in enumerate(bits):
            offset |= ((index >> (len(bits) - 1 - n)) & 1) << bit
        owners.append(offset)
    return owners


def owner_part(ref, owner, width, start, size):
    if len(ref.shape) == 3:
        return ref.at[owner, :, start : start + size]
    return ref.at[:, pl.ds(pl.multiple_of(owner * width + start, 128), size)]


def load_blocks(pieces, target, width, sem, me_ref):
    for ref, owners, cut in pieces:
        if owners is None:
            pltpu.make_async_copy(ref, target, sem).start()
            continue
        source, size, start = cut
        for n, owner in enumerate(owners):
            pltpu.make_async_copy(
                ref.at[n, :, source : source + size],
                owner_part(target, me_ref[1] ^ owner, width, start, size),
                sem,
            ).start()


def wait_all(ref, sem):
    pltpu.make_async_copy(ref, ref, sem).wait()


def store_blocks(source, outs, width, sems, me_ref):
    for number, (ref, owners, start) in enumerate(outs):
        if owners is None:
            copy = pltpu.make_async_copy(source, ref, sems.at[number])
            copy.start()
            copy.wait()
            continue
        for n, owner in enumerate(owners):
            pltpu.make_async_copy(
                owner_part(source, me_ref[1] ^ owner, width, 0, width),
                ref.at[n, :, start : start + width],
                sems.at[number],
            ).start()


def wait_blocks(outs, sems):
    for number, (ref, owners, _) in enumerate(outs):
        if owners is not None:
            wait_all(ref, sems.at[number])


def join_attention(stage, w_qkv, w_proj):
    owners = stage.shape[0]
    wide, narrow = 3 * C // owners, C // owners
    w_qkv[...] = jnp.concatenate([stage[n, :, :wide] for n in range(owners)], 1)
    w_proj[...] = jnp.concatenate([stage[n, :, wide : wide + narrow] for n in range(owners)], 1)


def pick_heads(first, second):
    lane = lax.broadcasted_iota(jnp.int32, (DEPTH, 128), 1)
    parts = []
    for h in range(PACK):
        at = (slice(h * DEPTH, (h + 1) * DEPTH), slice(h // 2 * 128, (h // 2 + 1) * 128))
        one, two = first[at], second[at]
        if h % 2:
            one = pltpu.roll(one, SLOT, 1)
        else:
            two = pltpu.roll(two, SLOT, 1)
        parts.append(jnp.where(lane < SLOT, one, two))
    return jnp.concatenate(parts, 0)


def apply_pair(rows_ref, cut, eye, first, second):
    turned = dot(eye, rows_ref[cut], NT).astype(BF16)
    empty = jnp.zeros_like(first)
    full = dot(
        turned,
        jnp.concatenate(
            [jnp.concatenate([first, empty], 1), jnp.concatenate([empty, second], 1)], 0
        ),
    )
    return pick_heads(full[:, :LANES], full[:, LANES:])


def identity():
    shape = (128, 128)
    same = lax.broadcasted_iota(jnp.int32, shape, 0) == lax.broadcasted_iota(jnp.int32, shape, 1)
    return same.astype(F32).astype(BF16)


def pipelined(units, first, second, third):
    ones, twos = {}, {}
    count = len(units)
    for n in range(count + 2):
        if n < count:
            ones[n] = first(*units[n])
        if 1 <= n <= count:
            twos[n - 1] = second(*units[n - 1], ones.pop(n - 1))
        if n >= 2:
            third(*units[n - 2], twos.pop(n - 2))


def forward_attention(
    field, sizes, w_qkv, w_proj, perm, perm_t, row_limit, col_limit, bias, small, qkv_bias,
    qkv_ref, prob_ref, windowed_ref, mixed_ref, attended_ref,
):
    hat, _ = norm_parts(field)
    normed = (hat * small[0:1] + small[1:2]).astype(BF16)
    images = len(sizes)
    for b in range(images):
        windowed_ref[b] = dot(perm[...], normed[b * ROWS : (b + 1) * ROWS]).astype(BF16)
    flat = windowed_ref[...].reshape(images * WROWS, C)
    qkv = (dot(flat, w_qkv[...]) + qkv_bias).astype(BF16)
    qkv_ref[...] = qkv.reshape(images, WROWS, 3 * C)
    low_masks = head_masks(BF16)
    eye = identity()
    blocks = {}
    for b, (rows, cols) in enumerate(sizes):
        for w in range(NWIN):
            allowed = (row_limit[w] < rows) & (col_limit[w] < cols)
            blocks[b, w] = jnp.where(allowed, 0.0, MASKED).astype(F32)

    def raw_scores(b, pair, g):
        results = []
        for w in (2 * pair, 2 * pair + 1):
            at = slice(w * SLOT, (w + 1) * SLOT)
            query = qkv_ref[b, at, g * 128 : (g + 1) * 128]
            key = qkv_ref[b, at, C + g * 128 : C + (g + 1) * 128]
            results.append(dot(key, spread_heads(query, low_masks), NT))
        return results

    def softmax(b, pair, g, raw):
        probs = []
        for n, score in enumerate(raw):
            w = 2 * pair + n
            block = jnp.concatenate([blocks[b, w]] * 2, 1)
            score = score * SCALE + (bias[g] + block)
            top = jnp.max(score, 0, keepdims=True)
            expo = jnp.exp(score - top)
            prob = (expo * (1.0 / jnp.sum(expo, 0, keepdims=True))).astype(BF16)
            prob_ref[b, w, g] = prob
            probs.append(prob)
        return probs

    def apply(b, pair, g, probs):
        both = slice(pair * 2 * SLOT, (pair + 1) * 2 * SLOT)
        value = (b, both, slice(2 * C + g * 128, 2 * C + (g + 1) * 128))
        mixed_ref[b, g * 128 : (g + 1) * 128, both] = apply_pair(qkv_ref, value, eye, *probs).astype(BF16)

    units = [(b, pair, g) for b in range(images) for pair in range(NWIN // 2) for g in range(NGRP)]
    pipelined(units, raw_scores, softmax, apply)
    for b in range(images):
        attended_ref[b] = dot(perm_t[...], mixed_ref[b], NT).astype(BF16)
    attended = attended_ref[...].reshape(images * ROWS, C)
    middle = field + dot(attended, w_proj[...]) + small[4:5]
    return normed, middle


def forward_mlp(middle, w_up, w_down, small, up_bias, active_ref, slope_ref):
    hat, _ = norm_parts(middle)
    mlp_in = (hat * small[5:6] + small[6:7]).astype(BF16)
    branch = jnp.zeros(middle.shape, F32)
    width = CHUNK
    for part in range(HID // width):
        at = slice(part * width, (part + 1) * width)
        pre = dot(mlp_in, w_up[:, at]) + up_bias[:, at]
        half = 0.5 * (1.0 + lax.erf(pre * (0.5**0.5)))
        active = (pre * half).astype(BF16)
        slope = half + pre * (jnp.exp(-0.5 * pre * pre) * ((2.0 * np.pi) ** -0.5))
        active_ref[..., at] = active.reshape(active_ref.shape[:-1] + (width,))
        slope_ref[..., at] = slope.astype(BF16).reshape(slope_ref.shape[:-1] + (width,))
        branch = branch + dot(active, w_down[:, at], NT)
    return mlp_in, middle + branch + small[7:8]


def backward_mlp(
    grad, middle, slope_ref, w_up, w_down, small, low_ref, pre_ref, rows_ref, up_rows_ref, place
):
    low = grad.astype(BF16)
    low_ref[place, :] = low
    rows_ref[7:8, :] += col_sum(low.astype(F32))
    normed_grad = jnp.zeros(grad.shape, F32)
    width = CHUNK
    for part in range(HID // width):
        at = slice(part * width, (part + 1) * width)
        slope = slope_ref[..., at].reshape(-1, width).astype(F32)
        pre = (dot(low, w_down[:, at]) * slope).astype(BF16)
        pre_ref[place, at] = pre
        up_rows_ref[:, at] += col_sum(pre.astype(F32))
        normed_grad = normed_grad + dot(pre, w_up[:, at], NT)
    hat, rate = norm_parts(middle)
    rows_ref[5:6, :] += col_sum(normed_grad * hat)
    rows_ref[6:7, :] += col_sum(normed_grad)
    return norm_back(normed_grad, hat, rate, small[5:6]) + grad


def backward_attention(
    grad_mid, field, qkv_ref, prob_ref, w_qkv, w_proj, perm, perm_t, small,
    spread_ref, dq_ref, dkv_ref, attn_ref, joined_ref, rows_ref, qkv_rows_ref, bias_grad_ref, start,
    need_grad,
):
    images = qkv_ref.shape[0]
    place = pl.ds(start, images * ROWS)
    attn = grad_mid.astype(BF16)
    attn_ref[place, :] = attn
    rows_ref[4:5, :] += col_sum(attn.astype(F32))
    joined = dot(attn, w_proj[...], NT).astype(BF16)
    for b in range(images):
        joined_ref[b] = dot(perm[...], joined[b * ROWS : (b + 1) * ROWS]).astype(BF16)
    low_masks = head_masks(BF16)
    eye = identity()

    def cut(n, g):
        return slice(n * C + g * 128, n * C + (g + 1) * 128)

    def prob_grads(b, pair, g):
        results = []
        for w in (2 * pair, 2 * pair + 1):
            at = slice(w * SLOT, (w + 1) * SLOT)
            out = spread_heads(joined_ref[b, at, cut(0, g)], low_masks)
            results.append(dot(qkv_ref[b, at, cut(2, g)], out, NT))
            dkv_ref[b, at, cut(1, g)] = dot(prob_ref[b, 2 * pair + len(results) - 1, g], out).astype(BF16)
        return results

    def score_grads(b, pair, g, grads):
        results = []
        for n, prob_grad in enumerate(grads):
            wide = prob_ref[b, 2 * pair + n, g].astype(F32)
            weighted = wide * prob_grad
            score = weighted - wide * jnp.sum(weighted, 0, keepdims=True)
            bias_grad_ref[g] += score
            results.append(score.astype(BF16))
        return results

    def products(b, pair, g, scores):
        both = slice(pair * 2 * SLOT, (pair + 1) * 2 * SLOT)
        for n, score in enumerate(scores):
            w = 2 * pair + n
            at = slice(w * SLOT, (w + 1) * SLOT)
            query = spread_heads(qkv_ref[b, at, cut(0, g)], low_masks)
            dkv_ref[b, at, cut(0, g)] = (dot(score, query) * SCALE).astype(BF16)
        dq_ref[b, cut(0, g), both] = (
            apply_pair(qkv_ref, (b, both, cut(1, g)), eye, *scores) * SCALE
        ).astype(BF16)

    units = [(b, pair, g) for b in range(images) for pair in range(NWIN // 2) for g in range(NGRP)]
    pipelined(units, prob_grads, score_grads, products)
    for b in range(images):
        rows = pl.ds(pl.multiple_of(start + b * ROWS, 16), ROWS)
        spread_ref[rows, :C] = dot(perm_t[...], dq_ref[b], NT).astype(BF16)
        spread_ref[rows, C:] = dot(perm_t[...], dkv_ref[b]).astype(BF16)
    back = spread_ref[place, :]
    qkv_rows_ref[:, :C] += col_sum(back[:, :C].astype(F32))
    qkv_rows_ref[:, 2 * C :] += col_sum(back[:, 2 * C :].astype(F32))
    normed_grad = dot(back, w_qkv[...], NT)
    hat, rate = norm_parts(field)
    rows_ref[0:1, :] += col_sum(normed_grad * hat)
    rows_ref[1:2, :] += col_sum(normed_grad)
    if not need_grad:
        return None
    return norm_back(normed_grad, hat, rate, small[0:1]) + grad_mid


def image_place():
    return pl.ds(pl.multiple_of(pl.program_id(0) * GROUP * ROWS, 16), GROUP * ROWS)


def flat(ref):
    return ref[...].reshape(-1, ref.shape[-1])


def put_rows(ref, value):
    ref[...] = value.reshape(ref.shape)


def is_first():
    return pl.program_id(0) == 0


def is_last():
    return pl.program_id(0) == pl.num_programs(0) - 1


def clear(*refs):
    @pl.when(is_first())
    def _():
        for ref in refs:
            ref[...] = jnp.zeros(ref.shape, ref.dtype)


class Names:
    def __init__(self, **refs):
        self.__dict__.update(refs)


def fetch_attention(k, plan):
    @pl.when(is_first())
    def _():
        load_blocks(plan.pieces(k, "attn"), k.stage, plan.widths["attn"], k.load_sem.at[0], k.me)
        wait_all(k.stage, k.load_sem.at[0])
        join_attention(k.stage, k.w_qkv, k.w_proj)
        for n, (source, target) in enumerate(((k.w_qkv, k.qkv_out), (k.w_proj, k.proj_out))):
            pltpu.make_async_copy(source, target, k.out_sem.at[n]).start()


def fetch_mlp(k, plan):
    @pl.when(is_first())
    def _():
        load_blocks(plan.pieces(k, "down"), k.w_down, plan.widths["down"], k.load_sem.at[1], k.me)
        load_blocks(plan.pieces(k, "up"), k.w_up, plan.widths["up"], k.load_sem.at[2], k.me)
        wait_all(k.w_down, k.load_sem.at[1])
        wait_all(k.w_up, k.load_sem.at[2])


def group_images(k):
    images = k.rows.shape[1]
    first = pl.program_id(0) * GROUP
    return [((first + b) // images, (first + b) % images) for b in range(GROUP)]


def group_sizes(k):
    return [(k.rows[m, n], k.cols[m, n]) for m, n in group_images(k)]


def small_rows(k, plan):
    return k.vec[plan.layer * PER_LAYER : plan.layer * PER_LAYER + 8]


def joined_rows(k, start, end):
    return jnp.concatenate([k.vec[n : n + 1] for n in range(start, end)], 1)


def up_bias_row(k, plan):
    return joined_rows(k, plan.layer * PER_LAYER + 8, (plan.layer + 1) * PER_LAYER)


def attention_forward_kernel(k, plan):
    fetch_attention(k, plan)
    small = small_rows(k, plan)
    qkv_bias = jnp.concatenate([small[2:3], jnp.zeros((1, C), F32), small[3:4]], 1)
    normed, middle = forward_attention(
        flat(k.field).astype(F32), group_sizes(k), k.w_qkv, k.w_proj, k.perm, k.perm_t,
        k.row_limit, k.col_limit, k.bias, small, qkv_bias, k.qkv, k.prob, k.windowed,
        k.mixed, k.attended,
    )
    put_rows(k.normed, normed)
    put_rows(k.middle, middle)

    @pl.when(is_last())
    def _():
        wait_all(k.w_qkv, k.out_sem.at[0])
        wait_all(k.w_proj, k.out_sem.at[1])


def first_mlp_kernel(k, plan):
    fetch_mlp(k, plan)

    @pl.when(is_first())
    def _():
        for n, (source, target) in enumerate(((k.w_down, k.down_out), (k.w_up, k.up_out))):
            pltpu.make_async_copy(source, target, k.out_sem.at[n]).start()

    mlp_in, result = forward_mlp(
        flat(k.middle), k.w_up, k.w_down, small_rows(k, plan), up_bias_row(k, plan), k.active, k.slope
    )
    put_rows(k.mlp_in, mlp_in)
    put_rows(k.result, result)

    @pl.when(is_last())
    def _():
        wait_all(k.w_down, k.out_sem.at[0])
        wait_all(k.w_up, k.out_sem.at[1])


def store_mlp_grads(k, plan):
    for at in range(0, HID, CHUNK):
        k.up_grad[:, at : at + CHUNK] = dot(k.mlp_all[...], k.pre_all[:, at : at + CHUNK], TN).astype(BF16)
    store_blocks(k.up_grad, plan.outs(k, "up"), plan.widths["up"], k.sem_x, k.me)
    for at in range(0, HID, CHUNK):
        k.down_grad[:, at : at + CHUNK] = dot(k.low_all[...], k.active_all[:, at : at + CHUNK], TN).astype(BF16)
    store_blocks(k.down_grad, plan.outs(k, "down"), plan.widths["down"], k.sem_y, k.me)


def wait_mlp_grads(k, plan):
    wait_blocks(plan.outs(k, "up"), k.sem_x)
    wait_blocks(plan.outs(k, "down"), k.sem_y)


def head_pass(k, plan, result, sizes, total_images):
    first = pl.program_id(0) * GROUP
    base = plan.layers * PER_LAYER
    gain = k.vec[base : base + 1]
    hat, rate = norm_parts(result)
    final = hat * gain + k.vec[base + 1 : base + 2]
    places = group_images(k)
    owners, _, width = k.w_head.shape
    row = lax.broadcasted_iota(jnp.int32, (16, 1), 0)
    pooled = jnp.zeros((16, C), F32)
    own = other = jnp.full((16, 1), -1, jnp.int32)
    mixing = jnp.zeros((16, 1), F32)
    shares = []
    for b, (rows, cols) in enumerate(sizes):
        inside = ((k.cell_row[...] < rows) & (k.cell_col[...] < cols)).astype(F32)
        count = (rows * cols).astype(F32)
        mean = col_sum(final[b * ROWS : (b + 1) * ROWS] * inside) / count
        shares.append(inside / count)
        pooled = jnp.where(row == b, mean, pooled)
        m, n = places[b]
        mine = (k.me[0] * owners + k.me[1]) * k.rows.shape[1] + n
        own = jnp.where(row == b, k.labels[m, mine], own)
        other = jnp.where(row == b, k.labels[m, k.partner[m, n]], other)
        mixing = jnp.where(row == b, k.mix[m, n].astype(F32) / 16.0, mixing)
    pooled = pooled.astype(BF16)
    classes = owners * width
    real = CLASSES // owners
    bias = joined_rows(k, base + 2, base + 2 - (-CLASSES // C))
    empty = jnp.full((1, width - real), MASKED, F32)
    bias = jnp.concatenate(
        [part for n in range(owners) for part in (bias[:, n * real : (n + 1) * real], empty)], 1
    )
    logits = jnp.concatenate([dot(pooled, k.w_head[n]) for n in range(owners)], 1)
    logits = logits + bias
    top = jnp.max(logits, -1, keepdims=True)
    expo = jnp.exp(logits - top)
    log_probs = logits - top - jnp.log(jnp.sum(expo, -1, keepdims=True))
    lane = lax.broadcasted_iota(jnp.int32, (16, classes), 1)
    label = lane // width * real + lane % width
    label = jnp.where(lane % width < real, label, -2)
    target = jnp.where(label == own, mixing, 0.0)
    target = target + jnp.where(label == other, 1.0 - mixing, 0.0)
    loss = jnp.where(target > 0.0, target * log_probs, 0.0)
    loss = jnp.sum(jnp.sum(loss, -1, keepdims=True), 0, keepdims=True)
    k.loss[...] -= jnp.broadcast_to(loss, k.loss.shape)
    logit_grad = jnp.where(row < GROUP, (jnp.exp(log_probs) - target) / total_images, 0.0)
    logit_low = logit_grad.astype(BF16)
    wide = logit_low.astype(F32)
    k.head_rows[...] += col_sum(wide)
    for b in range(GROUP):
        k.pooled_all[pl.ds(first + b, 1), :] = pooled[b : b + 1].astype(F32)
        k.logit_all[pl.ds(first + b, 1), :] = wide[b : b + 1]
    pooled_grad = jnp.zeros((16, C), F32)
    for n in range(owners):
        pooled_grad += dot(logit_low[:, n * width : (n + 1) * width], k.w_head[n], NT)
    final_grad = jnp.concatenate(
        [pooled_grad[b : b + 1] * share for b, share in enumerate(shares)], 0
    )
    k.final_rows[0:1, :] += col_sum(final_grad * hat)
    k.final_rows[1:2, :] += col_sum(final_grad)
    return norm_back(final_grad, hat, rate, gain)


def last_mlp_kernel(k, plan, total_images):
    place = image_place()

    @pl.when(is_first())
    def _():
        load_blocks(plan.pieces(k, "head"), k.w_head, plan.widths["head"], k.load_sem.at[3], k.me)

    fetch_mlp(k, plan)

    @pl.when(is_first())
    def _():
        wait_all(k.w_head, k.load_sem.at[3])

    clear(k.row_sums, k.up_rows, k.final_rows, k.head_rows, k.loss, k.pooled_all, k.logit_all)
    middle = flat(k.middle)
    mlp_in, result = forward_mlp(
        middle, k.w_up, k.w_down, small_rows(k, plan), up_bias_row(k, plan), k.active_all.at[place], k.slope
    )
    k.mlp_all[place, :] = mlp_in
    grad = head_pass(k, plan, result, group_sizes(k), total_images)
    put_rows(k.grad_mid, backward_mlp(
        grad, flat(k.middle), k.slope, k.w_up, k.w_down, small_rows(k, plan), k.low_all, k.pre_all,
        k.row_sums, k.up_rows, place,
    ))

    @pl.when(is_last())
    def _():
        store_mlp_grads(k, plan)
        total = dot(k.pooled_all[...].astype(BF16), k.logit_all[...].astype(BF16), TN).astype(BF16)
        owners, _, width = k.head_grad.shape
        for n in range(owners):
            k.head_grad[n] = total[:, n * width : (n + 1) * width]
        store_blocks(k.head_grad, plan.outs(k, "head"), plan.widths["head"], k.sem_x, k.me)
        wait_mlp_grads(k, plan)


def backward_mlp_kernel(k, plan):
    clear(k.row_sums, k.up_rows)
    place = image_place()
    k.mlp_all[place, :] = flat(k.mlp_in)
    k.active_all[place, :] = flat(k.active)
    put_rows(k.grad_mid, backward_mlp(
        flat(k.grad), flat(k.middle), k.slope, k.w_up, k.w_down, small_rows(k, plan), k.low_all, k.pre_all,
        k.row_sums, k.up_rows, place,
    ))

    @pl.when(is_last())
    def _():
        store_mlp_grads(k, plan)
        wait_mlp_grads(k, plan)


def backward_attention_kernel(k, plan, earlier, need_grad):
    sums = ("row_sums", "qkv_rows", "bias_grad")
    if earlier:
        @pl.when(is_first())
        def _():
            for name in sums:
                getattr(k, name)[...] = getattr(k, name + "_in")[...]
    else:
        clear(*[getattr(k, name) for name in sums])
    start = pl.multiple_of(earlier * ROWS + pl.program_id(0) * GROUP * ROWS, 16)
    grad = backward_attention(
        flat(k.grad_mid), flat(k.field).astype(F32), k.qkv, k.prob, k.w_qkv, k.w_proj, k.perm,
        k.perm_t, small_rows(k, plan), k.spread_all, k.dq, k.dkv, k.attn_all, k.joined, k.row_sums,
        k.qkv_rows, k.bias_grad, start, need_grad,
    )
    if need_grad:
        put_rows(k.grad, grad)
    if "attn" not in plan.targets:
        return
    place = pl.ds(start, GROUP * ROWS)
    k.normed_all[place, :] = flat(k.normed)
    k.attended_all[place, :] = flat(k.attended)

    @pl.when(is_last())
    def _():
        if earlier:
            before = slice(0, earlier * ROWS)
            k.normed_all[before, :] = flat(k.normed_in)
            k.attended_all[before, :] = flat(k.attended_in)
            k.spread_all[before, :] = k.spread_in[...]
            k.attn_all[before, :] = k.attn_in[...]
        owners, _, _ = k.attn_grad.shape
        wide, narrow = 3 * C // owners, C // owners
        if plan.collect is not None:
            layers, head_real, loss_at, near = plan.collect
            own = [k.row_sums, k.qkv_rows, k.mlp_rows0, k.up_rows0, k.bias_grad]
            collect_rows(
                layers, head_real, loss_at,
                own + [k.row_sums1, k.qkv_rows1, k.mlp_rows1, k.up_rows1, k.bias_grad1]
                + [k.final_rows, k.head_rows, k.loss],
                k.small_rows, k.spread_table,
            )
            pair_rows(k.small_rows, owners, near, k.me, k.pairs)
            for flip, (ref, _, _) in enumerate(plan.outs(k, "attn")):
                width = ref.shape[2]
                pltpu.make_async_copy(
                    k.pairs.at[flip], ref.at[:, :, width - 128 : width], k.sem_a.at[flip]
                ).start()
        total = dot(k.normed_all[...], k.spread_all[...], TN).astype(BF16)
        for n in range(owners):
            k.attn_grad[n, :, :wide] = total[:, n * wide : (n + 1) * wide]
        total = dot(k.attended_all[...], k.attn_all[...], TN).astype(BF16)
        for n in range(owners):
            k.attn_grad[n, :, wide:] = total[:, n * narrow : (n + 1) * narrow]
        store_blocks(k.attn_grad, plan.outs(k, "attn"), plan.widths["attn"], k.sem_a, k.me)
        wait_blocks(plan.outs(k, "attn"), k.sem_a)


class Plan:
    def __init__(self, widths, layer, layers):
        self.widths, self.layer, self.layers = widths, layer, layers
        self.sources = {}
        self.targets = {}
        self.collect = None

    def pieces(self, k, name):
        return [(getattr(k, ref), owners, cut) for ref, owners, cut in self.sources[name]]

    def outs(self, k, name):
        return [(getattr(k, ref), owners, start) for ref, owners, start in self.targets[name]]


def whole(shape):
    return pl.BlockSpec(shape, lambda i: (0,) * len(shape))


def per_image(*shape, first=0):
    return pl.BlockSpec((GROUP,) + shape, lambda i: (i + first,) + (0,) * len(shape))


SCALARS = pl.BlockSpec(memory_space=pltpu.SMEM)
FAR = pl.BlockSpec(memory_space=pl.ANY)


def call(body, name, groups, ins, outs, scratch, flops):
    def kernel(*refs):
        body(Names(**dict(zip(list(ins) + list(outs) + list(scratch), refs))))

    moved = sum(a.size * a.dtype.itemsize for _, a in ins.values())
    results = pl.pallas_call(
        kernel,
        grid=(groups,),
        in_specs=[spec for spec, _ in ins.values()],
        out_specs=[spec for spec, _, _ in outs.values()],
        out_shape=[jax.ShapeDtypeStruct(dims, dtype) for _, dims, dtype in outs.values()],
        scratch_shapes=list(scratch.values()),
        compiler_params=pltpu.CompilerParams(
            dimension_semantics=("arbitrary",), vmem_limit_bytes=VMEM_LIMIT
        ),
        cost_estimate=pl.CostEstimate(flops=int(flops), bytes_accessed=int(moved), transcendentals=0),
        name=name,
    )(*[array for _, array in ins.values()])
    return dict(zip(outs, results))


def exchange(array, step):
    axis, bit = step
    size = lax.axis_size(axis)
    return lax.ppermute(array, axis, [(i, i ^ (1 << bit)) for i in range(size)])


class Held:
    def __init__(self, array, dims=()):
        self.array, self.dims = array, list(dims)


def stack_blocks(parts, me, name, cuts=None):
    cuts = cuts or [None] * len(parts)
    args, outs, results = [], [], []
    for (held, received, step), cut in zip(parts, cuts):
        count, rows, columns = held.array.shape
        args += [held.array, received]
        axis, bit = step
        place = sum(d[0] == "win" and d[1] < bit for d in held.dims) if axis == "win" else len(held.dims)
        at = len(held.dims) - place
        dims = held.dims[:at] + [step] + held.dims[at:]
        bounds = [0, columns] if cut is None else [0, cut, columns]
        pieces = list(zip(bounds, bounds[1:]))
        outs += [((2 * count, rows, end - start), BF16) for start, end in pieces]
        results.append((place, axis, bit, pieces, dims))

    def kernel(me_ref, *refs):
        ins, targets = list(refs[: len(args)]), list(refs[len(args) :])
        for place, axis, bit, pieces, _ in results:
            held, received = ins.pop(0), ins.pop(0)
            mine = (me_ref[0] >> bit) & 1 if axis == "win" else 0
            for start, end in pieces:
                out = targets.pop(0)
                for n in range(held.shape[0]):
                    base = (n >> place << (place + 1)) + (n & ((1 << place) - 1))
                    out[base + (mine << place)] = held[n, :, start:end]
                    out[base + ((1 - mine) << place)] = received[n, :, start:end]

    arrays = list(small_call(kernel, name, [me] + args, outs, scalars=1))
    return [
        [Held(arrays.pop(0), dims) for _ in pieces] for _, _, _, pieces, dims in results
    ]


def tie(*values):
    return lax.optimization_barrier(values)


def small_call(kernel, name, args, outs, stream=False, scratch=(), scalars=0, limit=24):
    def spec(dims):
        return whole(dims) if stream else pl.BlockSpec(memory_space=pltpu.VMEM)

    return pl.pallas_call(
        kernel,
        grid=(1,) if stream else (),
        out_shape=[jax.ShapeDtypeStruct(dims, dtype) for dims, dtype in outs],
        in_specs=[SCALARS] * scalars + [spec(a.shape) for a in args[scalars:]],
        out_specs=[spec(dims) for dims, _ in outs],
        scratch_shapes=list(scratch),
        compiler_params=pltpu.CompilerParams(
            vmem_limit_bytes=limit * 1024 * 1024
        ),
        cost_estimate=pl.CostEstimate(flops=1, bytes_accessed=1, transcendentals=0),
        name=name,
    )(*args)


class Chain:
    def __init__(self, keep, send, dims, steps, pair_at=None):
        self.keep, self.send, self.dims, self.steps = keep, send, list(dims), list(steps)
        self.pair_at = pair_at

    def start(self):
        self.received = exchange(self.send, self.steps.pop(0))


def add_blocks(keep, received, pair_at):
    total = keep.astype(F32) + received.astype(F32)
    if pair_at is None:
        return total.astype(BF16)
    pair = total[:16, pair_at:] + total[16:32, pair_at:]
    high = pair.astype(BF16)
    tail = jnp.zeros((total.shape[0] - 32, pair.shape[1]), BF16)
    parts = [jnp.concatenate([high, (pair - high.astype(F32)).astype(BF16), tail], 0)]
    if pair_at:
        parts = [total[:, :pair_at].astype(BF16)] + parts
    return jnp.concatenate(parts, 1)


def combine(groups, me, name):
    args, outs = [], []
    for group in groups:
        for chain in group:
            args += [chain.keep, chain.received]
        count, rows, _ = group[0].keep.shape
        width = sum(chain.keep.shape[2] for chain in group)
        outs += [((count // 2, rows, width), BF16)] * 2

    def kernel(me_ref, *refs):
        ins, results = list(refs[: len(args)]), list(refs[len(args) :])
        for group in groups:
            keep_out, send_out = results.pop(0), results.pop(0)
            start = 0
            for chain in group:
                keep, received = ins.pop(0), ins.pop(0)
                width = keep.shape[2]
                axis, bit = chain.steps[0]
                place = len(chain.dims) - 1 - chain.dims.index((axis, bit))
                mine = (me_ref[0] >> bit) & 1 if axis == "win" else 0
                for n in range(keep_out.shape[0]):
                    base = (n >> place << (place + 1)) + (n & ((1 << place) - 1))
                    for out, at in (
                        (keep_out, base + (mine << place)), (send_out, base + ((1 - mine) << place))
                    ):
                        out[n, :, start : start + width] = add_blocks(
                            keep[at], received[at], chain.pair_at
                        )
                start += width

    results = small_call(kernel, name, [me] + args, outs, scalars=1)
    chains = []
    for n, group in enumerate(groups):
        step = group[0].steps[0]
        at, pair_at = 0, None
        for chain in group:
            if chain.pair_at is not None:
                pair_at = at + chain.pair_at
            at += chain.keep.shape[2]
        dims = [d for d in group[0].dims if d != step]
        chains.append(Chain(results[2 * n], results[2 * n + 1], dims, group[0].steps, pair_at))
    return chains


def finish(chain, name):
    _, rows, width = chain.keep.shape

    def kernel(keep, received, own, square):
        total = keep[0].astype(F32) + received[0].astype(F32)
        own[...] = total
        square[...] = jnp.broadcast_to(jnp.sum(total * total), (1, 128))

    return small_call(
        kernel, name, [chain.keep, chain.received], [((rows, width), F32), ((1, 128), F32)]
    )


def finish_pair(chain, squares, devices, share, name):
    _, rows, width = chain.keep.shape
    at = chain.pair_at

    def kernel(keep, received, *refs):
        total = keep[0].astype(F32) + received[0].astype(F32)
        own, message = refs[-2:]
        own[...] = total[:, :at]
        pair = total[:16, at:] + total[16:32, at:]
        square = jnp.sum(total[:, :at] * total[:, :at])
        square = jnp.broadcast_to(square, (1, 128))
        for ref in refs[:-2]:
            square = square + ref[...]
        row = [pair[n : n + 1] for n in range(share // 128)] + [square]
        message[...] = jnp.broadcast_to(jnp.concatenate(row, 1), message.shape)

    return small_call(
        kernel, name, [chain.keep, chain.received] + squares,
        [((rows, at), F32), ((devices, share + 128), F32)],
    )


def adam_step(weight, grad, first, second, rate):
    new_first = 0.5 * first + 0.5 * grad
    new_second = 0.5 * second + 0.5 * grad * grad
    fix = 1.0 - 0.5**STEP
    update = new_first / fix / (jnp.sqrt(new_second / fix) + ADAM_EPS)
    return (new_first, new_second, weight - rate * (update + DECAY_RATE * weight))


def update_kernel(starts, widths, layout, *refs):
    own, message, rest = refs[:3], refs[3], list(refs[4:])
    groups = [rest[3 * n : 3 * n + 3] for n in range(7)]
    loss_ref, norm_ref = rest[21], rest[22]
    outs = [rest[23 + 3 * n : 26 + 3 * n] for n in range(7)]
    vector_rows, table_rows, offsets, square_at, loss_at = layout
    vector_grad = message[:vector_rows, :C]
    table_grad = message[:table_rows, C : C + offsets]
    total = (
        jnp.sum(message[:, square_at : square_at + 1])
        + jnp.sum(vector_grad * vector_grad)
        + jnp.sum(table_grad * table_grad)
    )
    norm = jnp.sqrt(jnp.broadcast_to(total, (1, 1)))
    factor = CLIP_NORM / jnp.maximum(norm, CLIP_NORM)
    norm_ref[...] = norm
    loss_ref[...] = message[0:1, loss_at : loss_at + 1]

    def put(number, layer, grad, rate):
        weight, first, second = groups[number]
        index = (Ellipsis,) if layer is None else (layer, Ellipsis)
        if number == 6:
            index = (slice(None), layer, slice(None))
        results = adam_step(weight[index], factor * grad, first[index], second[index], rate)
        for ref, value in zip(outs[number], results):
            ref[index] = value

    layers = len(starts)
    for l in range(layers):
        qkv_width = outs[0][0].shape[2]
        part, at = starts[l]["attn"]
        put(0, l, own[part][:, at : at + qkv_width], LEARN_RATE)
        put(1, l, own[part][:, at + qkv_width : at + widths["attn"]], LEARN_RATE)
        part, at = starts[l]["up"]
        put(2, l, own[part][:, at : at + widths["up"]], LEARN_RATE)
        part, at = starts[l]["down"]
        put(3, l, own[part][:, at : at + widths["down"]], LEARN_RATE)
        heads = table_rows // layers
        put(6, l, table_grad[l * heads : (l + 1) * heads], SMALL_RATE)
    part, at = starts[-1]["head"]
    put(4, None, own[part][:, at : at + outs[4][0].shape[1]], LEARN_RATE)
    put(5, None, vector_grad, SMALL_RATE)


def collect_rows(layers, head_real, loss_at, ins, out, spread):
    out[...] = jnp.zeros(out.shape, F32)
    row_of_slot = lax.broadcasted_iota(jnp.int32, (SLOT, 128), 0)
    lane = lax.broadcasted_iota(jnp.int32, (SLOT, 128), 1)
    target = row_of_slot // WSIDE * (2 * WSIDE - 1) + row_of_slot % WSIDE
    spreader = ((lane == target) & (row_of_slot < AREA)).astype(F32).astype(BF16)
    row = 0
    for l in range(layers):
        attn_rows, qkv_rows, mlp_rows, up_rows, bias_grad = ins[5 * l : 5 * l + 5]
        parts = [
            attn_rows[0:2], qkv_rows[:, :C], qkv_rows[:, 2 * C :], attn_rows[4:5], mlp_rows[5:8],
        ] + [up_rows[:, n * C : (n + 1) * C] for n in range(HID // C)]
        for part in parts:
            out[row : row + part.shape[0], :C] = part
            row += part.shape[0]
        for head in range(HEADS):
            g, h = divmod(head, PACK)
            left = bias_grad[g, :, h * SLOT : (h + 1) * SLOT]
            total = jnp.zeros((SLOT, 128), F32)
            for _ in range(3):
                low = left.astype(BF16)
                total = total + dot(low, spreader)
                left = left - low.astype(F32)
            spread[head * SLOT : (head + 1) * SLOT, :] = total
        table = jnp.zeros((HEADS, 256), F32)
        span = 2 * WSIDE - 1
        for j in range(AREA):
            wide = jnp.concatenate(
                [spread[pl.ds(j, HEADS, stride=SLOT), :], jnp.zeros((HEADS, 128), F32)], 1
            )
            shift = (WSIDE - 1 - j // WSIDE) * span + WSIDE - 1 - j % WSIDE
            table = table + (pltpu.roll(wide, shift, 1) if shift else wide)
        width = out.shape[1] - C
        out[l * HEADS : (l + 1) * HEADS, C:] = table[:, :width]
    final_rows, head_rows, loss = ins[5 * layers :]
    out[row : row + 2, :C] = final_rows[...]
    row += 2
    cuts = CLASSES // head_real
    width = head_rows.shape[1] // cuts
    classes = jnp.concatenate(
        [head_rows[:, n * width : n * width + head_real] for n in range(cuts)]
        + [jnp.zeros((1, -CLASSES % C), F32)], 1
    )
    for n in range(classes.shape[1] // C):
        out[row + n : row + n + 1, :C] = classes[:, n * C : (n + 1) * C]
    out[0:1, loss_at : loss_at + 1] = loss[:, 0:1]


def pair_rows(rows, ch_count, owners, me_ref, pairs):
    count = rows.shape[1] // 128
    wins = rows.shape[0] // ch_count
    high_rows = pairs.shape[2] // wins
    for flip in range(2):
        for n, owner in enumerate(owners):
            for win in range(wins):
                values = rows[pl.ds(win * ch_count + (me_ref[1] ^ (owner ^ flip)), 1), :]
                values = jnp.concatenate(
                    [values[:, m * 128 : (m + 1) * 128] for m in range(count)]
                    + [jnp.zeros((16 - count, 128), F32)], 0
                )
                high = values.astype(BF16)
                at = win * high_rows
                pairs[flip, n, at : at + 16] = high
                pairs[flip, n, at + 16 : at + 32] = (values - high.astype(F32)).astype(BF16)
                pairs[flip, n, at + 32 : at + high_rows] = jnp.zeros((high_rows - 32, 128), BF16)


def pack_kernel(head_width, qkv, proj, down, up, head, *outs):
    for l, out in enumerate(outs):
        parts = [qkv[l], proj[l], down[l], up[l]]
        if l == len(outs) - 1:
            parts.append(head[...])
            pad = head_width - head.shape[1]
            if pad:
                parts.append(jnp.zeros((head.shape[0], pad), F32))
        out[...] = jnp.concatenate(parts, 1).astype(BF16)


def per_device(
    tokens, valid_rows, valid_cols, partner, mix_level, labels,
    w_qkv, m_qkv, v_qkv, w_proj, m_proj, v_proj, w_fc1, m_fc1, v_fc1, w_fc2, m_fc2, v_fc2,
    w_head, m_head, v_head, vectors, m_vec, v_vec, rel_table, m_rel, v_rel,
):
    micro, images, cells, chans = tokens.shape
    layers = rel_table.shape[0]
    per_layer = 8 + HID // C
    base = layers * per_layer
    head_rows = vectors.shape[0] - base - 2
    all_images = labels.shape[1]
    total_images = micro * all_images
    local = micro * images
    groups = local // GROUP
    sizes = {axis: lax.axis_size(axis) for axis in ("win", "ch")}
    win_count, ch_count = sizes["win"], sizes["ch"]
    device_count = win_count * ch_count
    win_index, ch_index = lax.axis_index("win"), lax.axis_index("ch")
    me = jnp.stack([win_index, ch_index]).astype(jnp.int32)
    block_rows = C // win_count
    widths = {"attn": 4 * C // ch_count, "down": HID // ch_count, "up": HID // ch_count}
    head_real = CLASSES // ch_count
    widths["head"] = -(-head_real // 128) * 128
    head_classes = widths["head"] * ch_count
    direct = block_rows % 16 == 0 and block_rows >= 32 and all(w % 128 == 0 for w in widths.values())

    core = ("ch", 0)
    ch_high = [("ch", b) for b in range(1, ch_count.bit_length() - 1)]
    win_low = [("win", 0)]
    win_high = [("win", b) for b in range(1, win_count.bit_length() - 1)]

    def low(v):
        return v.astype(BF16)

    packed = small_call(
        functools.partial(pack_kernel, widths["head"]), "pack",
        [w_qkv, w_proj, w_fc2.transpose(0, 2, 1), w_fc1, w_head],
        [((block_rows, sum(widths[n] for n in names)), BF16) for names in (
            ("attn", "down", "up"), ("attn", "down", "up", "head"))],
        stream=True,
        limit=56,
    )
    names = [["attn", "down", "up"], ["attn", "down", "up", "head"]]
    cuts = [widths["attn"] + 2 * widths["down"] // 3 // 128 * 128] * 2
    onehot = jnp.asarray(relative_onehot(), BF16)
    offsets = rel_table.shape[1]
    table_width = -(-(offsets + 1) // 128) * 128
    share = C + table_width
    tables = [window_tables(l % 2 == 1) for l in range(layers)]
    perms = [jnp.asarray(t[0], BF16) for t in tables]
    perms_t = [jnp.asarray(t[0].T, BF16) for t in tables]
    row_limits = [jnp.asarray(t[1]) for t in tables]
    col_limits = [jnp.asarray(t[2]) for t in tables]

    def bias_of(table):
        table = table.transpose(0, 2, 1).reshape(layers * HEADS, offsets)
        table_parts = []
        for _ in range(3):
            table_parts.append(low(table))
            table = table - table_parts[-1].astype(F32)
        bias = dot(jnp.concatenate(table_parts, 0), onehot).reshape(3, layers, HEADS, SLOT * SLOT)
        bias = (bias[0] + bias[1]) + bias[2]
        return (
            bias.reshape(layers, NGRP, PACK, SLOT, SLOT)
            .transpose(0, 1, 3, 2, 4)
            .reshape(layers, NGRP, SLOT, LANES)
        )

    padded = jnp.pad(tokens.reshape(local, cells, chans), ((0, 0), (0, ROWS - cells), (0, 0)))

    def stage(number, *moves, cuts=None, more=()):
        received = [exchange(part.array, step) for part, step in moves]
        tied = tie(*received, *more)
        received, more = tied[: len(moves)], tied[len(moves) :]
        stacked = stack_blocks(
            [(part, got, step) for (part, step), got in zip(moves, received)],
            me, f"stack{number}", cuts,
        )
        return (stacked, *more)

    def wait_for(value, *parts):
        value, *arrays = tie(value, *[part.array for part in parts])
        for part, array in zip(parts, arrays):
            part.array = array
        return value

    far = [Held(block[None]) for block in packed]
    if win_count == 8 and ch_count == 4:
        zh, zl, y, x = ("win", 2), ("win", 1), ("win", 0), ("ch", 1)
        ((far[0],),), padded = stage(0, (far[0], zh), more=(padded,))
        (near0,), packed1, bias = stage(
            1, (far[0], zl), cuts=[cuts[0]], more=(far[1].array, bias_of(rel_table))
        )
        far[1] = Held(packed1)
        ((one,), (two,), (far[1],)), = stage(2, (near0[0], y), (near0[1], x), (far[1], zh))
        ((one,), (two,), near1), = stage(
            3, (one, x), (two, y), (far[1], zl), cuts=[None, None, cuts[1]]
        )
        held = [[one, two]]
        other = [tie(*[exchange(part.array, core) for part in held[0]])]
        padded = wait_for(padded, *near1)
        steps1 = [(y, x), (x, y)]
    else:
        bias = bias_of(rel_table)
        bits = win_high[::-1] + win_low + ch_high[::-1]
        held = []
        for layer in range(2):
            part = far[layer]
            for n, step in enumerate(bits):
                ((part,),), = stage(10 * layer + n, (part, step))
            held.append([
                Held(part.array[..., : cuts[layer]], part.dims),
                Held(part.array[..., cuts[layer] :], part.dims),
            ])
        other = [[exchange(part.array, core) for part in held[0]]]
        near1, steps1 = held.pop(), []

    def weight_inputs(layer, wanted):
        plan = Plan(widths, layer, layers)
        ins = {}
        starts, at = {}, 0
        for name in names[layer]:
            starts[name] = at
            at += widths[name]
        bounds = [(0, cuts[layer]), (cuts[layer], at)]
        blocks = []
        for group in range(2):
            part = held[layer][group]
            owners = relative_owners([d for d in part.dims if d[0] == "ch"])
            for number, array in enumerate((part.array, other[layer][group])):
                flat_array = array.reshape(-1, C, array.shape[-1])
                blocks.append((group, [owner ^ number for owner in owners], flat_array))
        for name in wanted:
            plan.sources[name] = []
            columns = []
            for number, (group, owners, array) in enumerate(blocks):
                begin = max(starts[name], bounds[group][0])
                end = min(starts[name] + widths[name], bounds[group][1])
                if begin >= end:
                    continue
                cut = (begin - bounds[group][0], end - begin, begin - starts[name])
                if direct:
                    ref = f"blocks{number}"
                    ins[ref] = (FAR, array)
                    plan.sources[name].append((ref, owners, cut))
                elif number % 2 == 0:
                    table = np.argsort(np.asarray(owners + blocks[number + 1][1]))
                    both = jnp.concatenate([array, blocks[number + 1][2]])
                    index = jnp.asarray(table)[jnp.arange(ch_count) ^ ch_index]
                    columns.append(jnp.take(both, index, axis=0)[..., cut[0] : cut[0] + cut[1]])
            if not direct:
                full = jnp.concatenate(columns, -1)
                if name in ("up", "down"):
                    full = full.transpose(1, 0, 2).reshape(C, -1)
                ins[f"staged_{name}"] = (FAR, full)
                plan.sources[name] = [(f"staged_{name}", None, None)]
        ins["me"] = (SCALARS, me)
        return ins, plan

    orders = {
        "x": ch_high + win_low + win_high, "a": ch_high + win_low + win_high,
        "y": win_low + ch_high + win_high,
    }
    block_dims = ch_high + [("win", b) for b in reversed(range(win_count.bit_length() - 1))]
    owners = relative_owners(ch_high)
    regular = direct and len(ch_high) == 1

    def grad_outputs(plan, extra=0, **members):
        outs = {}
        for group, wanted in members.items():
            if not direct:
                for name in wanted:
                    plan.targets[name] = [(f"full_{name}", None, 0)]
                    dims = (C, HID) if name in ("up", "down") else (ch_count, C, widths[name])
                    outs[f"full_{name}"] = (FAR, dims, BF16)
                continue
            starts = np.cumsum([0] + [widths[name] for name in wanted])
            refs = [
                (f"keep_{group}", owners), (f"send_{group}", [owner ^ 1 for owner in owners])
            ]
            for ref, _ in refs:
                outs[ref] = (FAR, (len(owners), C, int(starts[-1]) + extra), BF16)
            for name, start in zip(wanted, starts):
                plan.targets[name] = [(ref, at, int(start)) for ref, at in refs]
        return outs

    def chain_of(results, group, *members, pair_at=None):
        if direct:
            keep, send = results[f"keep_{group}"], results[f"send_{group}"]
        else:
            full = []
            for name in members:
                part = results[f"full_{name}"]
                if name in ("up", "down"):
                    part = part.reshape(C, ch_count, -1).transpose(1, 0, 2)
                full.append(part)
            full = jnp.concatenate(full, -1)
            keep, send = [
                jnp.take(full, np.asarray(owners) ^ flip ^ ch_index, axis=0) for flip in (0, 1)
            ]
        dims = (-1, block_rows, keep.shape[-1])
        return Chain(
            keep.reshape(dims), send.reshape(dims), block_dims, [core] + orders[group], pair_at
        )

    def start(*chains):
        for chain in chains:
            chain.start()

    def meet(value, *chains):
        value, *got = tie(value, *[chain.received for chain in chains])
        for chain, array in zip(chains, got):
            chain.received = array
        return value

    def after(value, *chains):
        held_back = [array for chain in chains for array in (chain.keep, chain.send)]
        value, *held_back = tie(value, *held_back)
        for n, chain in enumerate(chains):
            chain.keep, chain.send = held_back[2 * n], held_back[2 * n + 1]
        return value

    def attention_consts(l, forward):
        ins = {
            "perm": (whole((WROWS, ROWS)), perms[l]),
            "perm_t": (whole((ROWS, WROWS)), perms_t[l]),
            "vec": (whole(vectors.shape), vectors),
        }
        if forward:
            ins["rows"] = (SCALARS, valid_rows)
            ins["cols"] = (SCALARS, valid_cols)
            ins["row_limit"] = (whole((NWIN, SLOT, 128)), row_limits[l])
            ins["col_limit"] = (whole((NWIN, SLOT, 128)), col_limits[l])
            ins["bias"] = (
                pl.BlockSpec((None, NGRP, SLOT, LANES), lambda i, l=l: (l, 0, 0, 0)), bias
            )
        return ins

    def vmem(*dims, dtype=BF16):
        return pltpu.VMEM(dims, dtype)

    attn_weights = {
        "stage": vmem(ch_count, C, widths["attn"]),
        "w_qkv": vmem(C, 3 * C),
        "w_proj": vmem(C, C),
        "load_sem": pltpu.SemaphoreType.DMA((4,)),
    }
    mlp_weights = {
        "w_down": vmem(C, HID),
        "w_up": vmem(C, HID),
        "load_sem": pltpu.SemaphoreType.DMA((4,)),
    }
    all_rows = local * ROWS
    mlp_rows = {
        "mlp_all": vmem(all_rows, C), "active_all": vmem(all_rows, HID),
        "pre_all": vmem(all_rows, HID), "low_all": vmem(all_rows, C),
        "up_grad": vmem(C, HID), "down_grad": vmem(C, HID),
        "sem_x": pltpu.SemaphoreType.DMA((2,)), "sem_y": pltpu.SemaphoreType.DMA((2,)),
    }
    wide = (per_image(ROWS, C), (local, ROWS, C), F32)
    thin = (per_image(ROWS, C), (local, ROWS, C), BF16)
    hidden = (per_image(ROWS, HID), (local, ROWS, HID), BF16)
    attn_saved = {
        "normed": thin,
        "qkv": (per_image(WROWS, 3 * C), (local, WROWS, 3 * C), BF16),
        "prob": (per_image(NWIN, NGRP, SLOT, LANES), (local, NWIN, NGRP, SLOT, LANES), BF16),
        "attended": thin,
    }
    sums = {"row_sums": (whole((8, C)), (8, C), F32)}
    up_sums = {**sums, "up_rows": (whole((1, HID)), (1, HID), F32)}
    attn_sums = {
        **sums,
        "qkv_rows": (whole((1, 3 * C)), (1, 3 * C), F32),
        "bias_grad": (whole((NGRP, SLOT, LANES)), (NGRP, SLOT, LANES), F32),
    }

    def given(spec, array):
        return (spec[0], array)

    mlp_flops = 2 * all_rows * C * HID * 2
    attn_flops = 2 * all_rows * C * C * 8

    def attention_forward(l, field_spec, field):
        ins, plan = weight_inputs(l, ["attn"])
        ins["field"] = given(field_spec, field)
        ins.update(attention_consts(l, True))
        return call(
            functools.partial(attention_forward_kernel, plan=plan), f"attention_forward{l}", groups,
            ins,
            {
                "middle": wide, **attn_saved,
                "qkv_out": (FAR, (C, 3 * C), BF16), "proj_out": (FAR, (C, C), BF16),
            },
            {
                "mixed": vmem(GROUP, C, WROWS), "windowed": vmem(GROUP, WROWS, C), **attn_weights,
                "out_sem": pltpu.SemaphoreType.DMA((2,)),
            },
            attn_flops,
        )

    saved0 = attention_forward(0, thin, padded)
    middle0 = saved0["middle"]
    if steps1:
        ((one,), (two,)), middle0 = stage(4, *zip(near1, steps1[0]), more=(middle0,))
        near1 = [one, two]
        middle0 = wait_for(middle0, *near1)
    ins, plan = weight_inputs(0, ["down", "up"])
    ins["middle"] = given(wide, middle0)
    ins["vec"] = (whole(vectors.shape), vectors)
    mlp0 = call(
        functools.partial(first_mlp_kernel, plan=plan), "first_mlp", groups, ins,
        {
            "result": wide, "mlp_in": thin, "active": hidden, "slope": hidden,
            "down_out": (FAR, (C, HID), BF16),
            "up_out": (FAR, (C, HID), BF16),
        },
        {**mlp_weights, "out_sem": pltpu.SemaphoreType.DMA((2,))},
        mlp_flops,
    )
    result0 = mlp0["result"]
    if steps1:
        ((one,), (two,)), result0 = stage(5, *zip(near1, steps1[1]), more=(result0,))
        near1 = [one, two]
        result0 = wait_for(result0, *near1)
    held.append(near1)
    other.append([exchange(part.array, core) for part in held[1]])

    saved1 = attention_forward(1, wide, result0)
    ins, plan = weight_inputs(1, ["down", "up", "head"])
    ins["middle"] = given(wide, saved1["middle"])
    ins["vec"] = (whole(vectors.shape), vectors)
    ins["rows"] = (SCALARS, valid_rows)
    ins["cols"] = (SCALARS, valid_cols)
    ins["labels"] = (SCALARS, labels)
    ins["partner"] = (SCALARS, partner)
    ins["mix"] = (SCALARS, mix_level)
    cell = np.arange(ROWS)
    for name, place in (("cell_row", cell // GRID), ("cell_col", cell % GRID)):
        place = np.where(cell < CELLS, place, 99)[:, None].astype(np.int32)
        ins[name] = (whole((ROWS, 1)), jnp.asarray(place))
    outs = {
        "grad_mid": wide, **up_sums,
        "final_rows": (whole((2, C)), (2, C), F32),
        "head_rows": (whole((1, head_classes)), (1, head_classes), F32),
        "loss": (whole((1, 128)), (1, 128), F32),
        **grad_outputs(plan, x=["up", "head"], y=["down"]),
    }
    last = call(
        functools.partial(last_mlp_kernel, plan=plan, total_images=float(total_images)),
        "last_mlp", groups, ins, outs,
        {
            "slope": vmem(GROUP * ROWS, HID), "w_head": vmem(ch_count, C, widths["head"]),
            **mlp_weights, **mlp_rows,
            "pooled_all": vmem(16, C, dtype=F32), "logit_all": vmem(16, head_classes, dtype=F32),
            "head_grad": vmem(ch_count, C, widths["head"]),
        },
        3 * mlp_flops,
    )

    def attention_backward(l, grad_mid, field, saved, first, count, before=None, store=True, collect=None):
        plan = Plan(widths, l, layers)
        ins = {
            "me": (SCALARS, me), "w_qkv": (whole((C, 3 * C)), saved["qkv_out"]),
            "w_proj": (whole((C, C)), saved["proj_out"]),
        }
        ins.update(attention_consts(l, False))
        wanted = ["qkv", "prob"] + (["normed", "attended"] if store else [])
        for name, array in [("grad_mid", grad_mid), ("field", field)] + [
            (name, saved[name]) for name in wanted
        ]:
            ins[name] = (per_image(*array.shape[1:], first=first), array)
        if before is not None:
            for name, (spec, _, _) in attn_sums.items():
                ins[name + "_in"] = (spec, before[name])
            for name in ("normed", "attended"):
                ins[name + "_in"] = (whole((first * GROUP, ROWS, C)), saved[name])
            for name in ("spread", "attn"):
                array = before[name + "_all"]
                ins[name + "_in"] = (whole(array.shape), array)
        rows_here = count * GROUP * ROWS
        outs = dict(attn_sums)
        scratch = {
            "dq": vmem(GROUP, C, WROWS), "dkv": vmem(GROUP, WROWS, 2 * C),
            "joined": vmem(GROUP, WROWS, C),
        }
        need_grad = l > 0
        if need_grad:
            outs["grad"] = wide
        if store:
            outs.update(grad_outputs(plan, extra=0 if collect is None else 128, a=["attn"]))
            if collect is not None:
                plan.collect = (layers, head_real, share - 1, owners)
                ins.update({name: (whole(array.shape), array) for name, array in collect.items()})
                scratch["small_rows"] = vmem(device_count, share, dtype=F32)
                scratch["spread_table"] = vmem(HEADS * SLOT, 128, dtype=F32)
                scratch["pairs"] = vmem(2, len(owners), C, 128)
            scratch.update({
                "normed_all": vmem(all_rows, C), "attended_all": vmem(all_rows, C),
                "spread_all": vmem(all_rows, 3 * C), "attn_all": vmem(all_rows, C),
                "attn_grad": vmem(ch_count, C, widths["attn"]),
                "sem_a": pltpu.SemaphoreType.DMA((2,)),
            })
        else:
            outs["spread_all"] = (whole((rows_here, 3 * C)), (rows_here, 3 * C), BF16)
            outs["attn_all"] = (whole((rows_here, C)), (rows_here, C), BF16)
        return call(
            functools.partial(
                backward_attention_kernel, plan=plan,
                earlier=0 if before is None else first * GROUP, need_grad=need_grad,
            ),
            f"attention_backward{l}_{first}", count, ins, outs, scratch,
            2 * attn_flops * count // groups,
        )

    x1, y1 = chain_of(last, "x", "up", "head"), chain_of(last, "y", "down")
    if regular:
        start(x1, y1)
    back1 = attention_backward(1, last["grad_mid"], mlp0["result"], saved1, 0, groups)
    a1 = chain_of(back1, "a", "attn")
    grad = back1["grad"]
    if regular:
        grad = meet(grad, x1, y1)
        x1, y1 = combine([[x1], [y1]], me, "sum1")
        grad = after(grad, x1, y1)
        start(x1, y1, a1)

    plan = Plan(widths, 0, layers)
    ins = {
        "me": (SCALARS, me),
        "w_down": (whole((C, HID)), mlp0["down_out"]),
        "w_up": (whole((C, HID)), mlp0["up_out"]),
    }
    ins["grad"] = given(wide, grad)
    ins["middle"] = given(wide, saved0["middle"])
    ins["mlp_in"] = given(thin, mlp0["mlp_in"])
    ins["active"] = given(hidden, mlp0["active"])
    ins["slope"] = given(hidden, mlp0["slope"])
    ins["vec"] = (whole(vectors.shape), vectors)
    first = call(
        functools.partial(backward_mlp_kernel, plan=plan), "mlp_backward0", groups, ins,
        {"grad_mid": wide, **up_sums, **grad_outputs(plan, x=["up"], y=["down"])},
        dict(mlp_rows), 2 * mlp_flops,
    )
    x0, y0 = chain_of(first, "x", "up"), chain_of(first, "y", "down")
    grad_mid = first["grad_mid"]
    if regular:
        grad_mid = meet(grad_mid, x1, y1, a1)
        x1, y1, a1 = combine([[x1], [y1], [a1]], me, "sum2")
        grad_mid = after(grad_mid, x1, y1, a1)
        start(x1, y1, a1, x0, y0)
    before0 = attention_backward(0, grad_mid, padded, saved0, 0, groups - 1, store=False)
    if regular:
        before0["row_sums"] = meet(before0["row_sums"], a1, x0, y0)
        a1, x0, y0 = combine([[a1], [x0], [y0]], me, "sum3")
        grad_mid = after(grad_mid, a1, x0, y0)
        start(a1, x0, y0)
    small_parts = None
    if regular:
        small_parts = {
            "mlp_rows0": first["row_sums"], "up_rows0": first["up_rows"],
            "row_sums1": back1["row_sums"], "qkv_rows1": back1["qkv_rows"],
            "mlp_rows1": last["row_sums"], "up_rows1": last["up_rows"],
            "bias_grad1": back1["bias_grad"], "final_rows": last["final_rows"],
            "head_rows": last["head_rows"], "loss": last["loss"],
        }
    back0 = attention_backward(
        0, grad_mid, padded, saved0, groups - 1, 1, before0, collect=small_parts
    )
    a0 = chain_of(back0, "a", "attn", pair_at=widths["attn"] if regular else None)
    if regular:
        waiting = (a1, x1, y1, x0, y0)
        a0.send, *got = tie(a0.send, *[chain.received for chain in waiting])
        for chain, array in zip(waiting, got):
            chain.received = array

    if regular:
        (z1,) = combine([[a1, x1, y1]], me, "sum4")
        x0, y0 = combine([[x0], [y0]], me, "sum5")
        start(a0, z1, x0, y0)
        (a0,) = combine([[a0]], me, "sum6")
        start(a0)
        z0, z1 = combine([[x0, y0], [z1]], me, "sum7")
        start(z0, z1)
        (a0,) = combine([[a0]], me, "sum8")
        start(a0)
        (z0,) = combine([[z0]], me, "sum9")
        start(z0)
        own1, square1 = finish(z1, "own1")
        (a0,) = combine([[a0]], me, "sum10")
        start(a0)
        own0, square0 = finish(z0, "own0")
        (a0,) = combine([[a0]], me, "sum11")
        start(a0)
        own_attn, message = finish_pair(a0, [square0, square1], device_count, share, "own_attn")
    else:
        square, own_parts = jnp.zeros((1, 128), F32), []
        for chain in (a0, x0, y0, a1, x1, y1):
            start(chain)
            while chain.steps:
                (chain,) = combine([[chain]], me, "sum")
                start(chain)
            part, part_square = finish(chain, "own")
            square = square + part_square
            own_parts.append(part)
        own_attn = own_parts[0]
        own0, own1 = jnp.concatenate(own_parts[1:3], 1), jnp.concatenate(own_parts[3:], 1)
        (rows_all,) = small_call(
            lambda *refs: collect_rows(
                layers, head_real, share - 1, refs[:-2], refs[-2], refs[-1]
            ),
            "collect",
            [part[name] for part in ((first, back0), (last, back1))
             for part, name in (
                 (part[1], "row_sums"), (part[1], "qkv_rows"), (part[0], "row_sums"),
                 (part[0], "up_rows"), (part[1], "bias_grad"))]
            + [last["final_rows"], last["head_rows"], last["loss"]],
            [((device_count, share), F32)],
            stream=True,
            scratch=[pltpu.VMEM((HEADS * SLOT, 128), F32)],
        )
        rows_all = lax.all_to_all(rows_all, ("win", "ch"), 0, 0, tiled=True)
        message = jnp.concatenate([jnp.sum(rows_all, 0, keepdims=True), square], 1)
        message = jnp.broadcast_to(message, (device_count, share + 128))
    message = lax.all_to_all(message, ("win", "ch"), 0, 0, tiled=True)
    starts = []
    for order in ((("attn",), ("up", "down")), (("attn", "up", "head", "down"),)):
        starts.append({})
        for part in order:
            number = 0 if len(order) == 1 else 1 + (part != order[0])
            ends = np.cumsum([0] + [widths[n] for n in part]).tolist()
            starts[-1].update({name: (number, at) for name, at in zip(part, ends)})
    arrays = [
        [w_qkv, m_qkv, v_qkv], [w_proj, m_proj, v_proj], [w_fc1, m_fc1, v_fc1],
        [w_fc2, m_fc2, v_fc2], [w_head, m_head, v_head], [vectors, m_vec, v_vec],
        [rel_table, m_rel, v_rel],
    ]
    turns = {3: (0, 2, 1), 6: (2, 0, 1)}
    turned = [
        a.transpose(turns[n]) if n in turns else a for n, group in enumerate(arrays) for a in group
    ]
    results = small_call(
        functools.partial(
            update_kernel, starts, widths,
            (vectors.shape[0], layers * HEADS, offsets, share, share - 1),
        ),
        "update",
        [own1, own_attn, own0, message] + turned,
        [((1, 1), F32)] * 2 + [(a.shape, F32) for a in turned],
        stream=True,
    )
    loss_total, grad_norm, *results = results
    outs = [loss_total[0, 0], grad_norm[0, 0]]
    for n in range(0, len(results), 3):
        back = {3: (0, 2, 1), 6: (1, 2, 0)}.get(n // 3)
        outs += [r if back is None else r.transpose(back) for r in results[n : n + 3]]
    return tuple(outs)


def solution(mesh):
    cut = P(None, "win", "ch")
    down = P(None, "ch", "win")
    head = P("win", "ch")
    rows = P(None, ("win", "ch"))
    in_specs = (
        (P(None, ("win", "ch"), None, None),) + (rows,) * 4 + (P(),)
        + (cut,) * 9 + (down,) * 3 + (head,) * 3 + (P(),) * 6
    )
    out_specs = (P(),) * 2 + (cut,) * 9 + (down,) * 3 + (head,) * 3 + (P(),) * 6
    return jax.shard_map(
        per_device, mesh=mesh, in_specs=in_specs, out_specs=out_specs, check_vma=False
    )
```

```python
import functools

import jax
import jax.numpy as jnp
import numpy as np
from jax import lax
from jax.experimental import pallas as pl
from jax.experimental.pallas import tpu as pltpu
from jax.sharding import PartitionSpec as P

C = 384
HID = 1536
CLASSES = 1000
CLASS_PAD = 1024
WSIDE = 7
GRID = 14
STEP = 10
HEADS = 12
PER_LAYER = 8 + HID // C
DEPTH = 32
CELLS = GRID * GRID
ROWS = 208
AREA = WSIDE * WSIDE
SLOT = 64
NWIN = 4
NGRP = 3
PACK = 4
WROWS = NWIN * SLOT
LANES = PACK * SLOT

NORM_EPS = 1e-05
CLIP_NORM = 0.05
LEARN_RATE = 0.04
SMALL_RATE = 0.2
DECAY_RATE = 0.05
ADAM_EPS = 1e-08
MASKED = -1e30
SCALE = DEPTH ** (-0.5)
F32 = jnp.float32
BF16 = jnp.bfloat16
NN = (((1,), (0,)), ((), ()))
NT = (((1,), (1,)), ((), ()))
TN = (((0,), (0,)), ((), ()))
VMEM_LIMIT = 58 * 1024 * 1024
GROUP = 2
CHUNK = 512


def dot(a, b, dims=NN):
    return lax.dot_general(a, b, dims, preferred_element_type=F32)


@functools.lru_cache(None)
def window_tables(shifted):
    perm = np.zeros((WROWS, ROWS), np.float32)
    row_limit = np.full((NWIN, SLOT, 2 * SLOT), 99, np.int32)
    col_limit = np.full((NWIN, SLOT, 2 * SLOT), 99, np.int32)
    shift = WSIDE // 2 if shifted else 0

    def band(v):
        return 0 if v < GRID - WSIDE else (1 if v < GRID - WSIDE // 2 else 2)

    for window in range(NWIN):
        wr, wc = divmod(window, GRID // WSIDE)
        place = []
        for j in range(AREA):
            r, c = wr * WSIDE + j // WSIDE, wc * WSIDE + j % WSIDE
            region = 3 * band(r) + band(c) if shifted else 0
            source = ((r + shift) % GRID, (c + shift) % GRID)
            place.append((region, source))
            perm[window * SLOT + j, source[0] * GRID + source[1]] = 1
        for j in range(SLOT):
            for i in range(SLOT):
                if i == j:
                    pair = (-1, -1)
                elif i < AREA and j < AREA and place[i][0] == place[j][0]:
                    pair = place[j][1]
                else:
                    pair = (99, 99)
                row_limit[window, j, i::SLOT] = pair[0]
                col_limit[window, j, i::SLOT] = pair[1]
    return perm, row_limit, col_limit


@functools.lru_cache(None)
def relative_onehot():
    span = 2 * WSIDE - 1
    onehot = np.zeros((span * span, SLOT, SLOT), np.float32)
    for i in range(AREA):
        for j in range(AREA):
            row, col = i // WSIDE - j // WSIDE, i % WSIDE - j % WSIDE
            onehot[(row + WSIDE - 1) * span + col + WSIDE - 1, j, i] = 1
    return onehot.reshape(span * span, SLOT * SLOT)


def norm_parts(field):
    average = jnp.mean(field, -1, keepdims=True)
    centered = field - average
    spread = jnp.mean(centered * centered, -1, keepdims=True)
    rate = lax.rsqrt(spread + NORM_EPS)
    return centered * rate, rate


def norm_back(grad, hat, rate, gain):
    scaled = grad * gain
    return rate * (
        scaled
        - jnp.mean(scaled, -1, keepdims=True)
        - hat * jnp.mean(scaled * hat, -1, keepdims=True)
    )


def col_sum(field):
    return jnp.sum(field, 0, keepdims=True)


def head_masks(dtype):
    lane = lax.broadcasted_iota(jnp.int32, (SLOT, 128), 1)
    return [((lane // DEPTH) == h).astype(F32).astype(dtype) for h in range(PACK)]


def spread_heads(block, masks):
    return jnp.concatenate([block * m for m in masks], 0)


def relative_owners(bits):
    owners = []
    for index in range(1 << len(bits)):
        offset = 0
        for n, (_, bit) in enumerate(bits):
            offset |= ((index >> (len(bits) - 1 - n)) & 1) << bit
        owners.append(offset)
    return owners


def owner_part(ref, owner, width, start, size):
    if len(ref.shape) == 3:
        return ref.at[owner, :, start : start + size]
    return ref.at[:, pl.ds(pl.multiple_of(owner * width + start, 128), size)]


def load_blocks(pieces, target, width, sem, me_ref):
    for ref, owners, cut in pieces:
        if owners is None:
            pltpu.make_async_copy(ref, target, sem).start()
            continue
        source, size, start = cut
        for n, owner in enumerate(owners):
            pltpu.make_async_copy(
                ref.at[n, :, source : source + size],
                owner_part(target, me_ref[1] ^ owner, width, start, size),
                sem,
            ).start()


def wait_all(ref, sem):
    pltpu.make_async_copy(ref, ref, sem).wait()


def store_blocks(source, outs, width, sems, me_ref):
    for number, (ref, owners, start, source_start, size) in enumerate(outs):
        if owners is None:
            copy = pltpu.make_async_copy(source, ref, sems.at[number])
            copy.start()
            copy.wait()
            continue
        for n, owner in enumerate(owners):
            pltpu.make_async_copy(
                owner_part(source, me_ref[1] ^ owner, width, source_start, size),
                ref.at[n, :, start : start + size],
                sems.at[number],
            ).start()


def wait_blocks(outs, sems):
    for number, (ref, owners, *_) in enumerate(outs):
        if owners is not None:
            wait_all(ref, sems.at[number])


def join_attention(stage, w_qkv, w_proj):
    owners = stage.shape[0]
    wide, narrow = 3 * C // owners, C // owners
    w_qkv[...] = jnp.concatenate([stage[n, :, :wide] for n in range(owners)], 1)
    w_proj[...] = jnp.concatenate([stage[n, :, wide : wide + narrow] for n in range(owners)], 1)


def pick_heads(first, second):
    lane = lax.broadcasted_iota(jnp.int32, (DEPTH, 128), 1)
    parts = []
    for h in range(PACK):
        at = (slice(h * DEPTH, (h + 1) * DEPTH), slice(h // 2 * 128, (h // 2 + 1) * 128))
        one, two = first[at], second[at]
        if h % 2:
            one = pltpu.roll(one, SLOT, 1)
        else:
            two = pltpu.roll(two, SLOT, 1)
        parts.append(jnp.where(lane < SLOT, one, two))
    return jnp.concatenate(parts, 0)


def apply_pair(rows_ref, cut, eye, first, second):
    turned = dot(eye, rows_ref[cut], NT).astype(BF16)
    empty = jnp.zeros_like(first)
    full = dot(
        turned,
        jnp.concatenate(
            [jnp.concatenate([first, empty], 1), jnp.concatenate([empty, second], 1)], 0
        ),
    )
    return pick_heads(full[:, :LANES], full[:, LANES:])


def identity():
    shape = (128, 128)
    same = lax.broadcasted_iota(jnp.int32, shape, 0) == lax.broadcasted_iota(jnp.int32, shape, 1)
    return same.astype(F32).astype(BF16)


def pipelined(units, first, second, third):
    ones, twos = {}, {}
    count = len(units)
    for n in range(count + 2):
        if n < count:
            ones[n] = first(*units[n])
        if 1 <= n <= count:
            twos[n - 1] = second(*units[n - 1], ones.pop(n - 1))
        if n >= 2:
            third(*units[n - 2], twos.pop(n - 2))


def each_image(images, body, unrolled):
    lax.fori_loop(0, images, body, 0, unroll=images if unrolled else 1)


def forward_attention(
    field, sizes, w_qkv, w_proj, perm, perm_t, row_limit, col_limit, bias, small, qkv_bias,
    qkv_ref, prob_ref, windowed_ref, mixed_ref, attended_ref, unrolled,
):
    hat, _ = norm_parts(field)
    normed = (hat * small[0:1] + small[1:2]).astype(BF16)
    images = len(sizes)
    for b in range(images):
        windowed_ref[b] = dot(perm[...], normed[b * ROWS : (b + 1) * ROWS]).astype(BF16)
    flat = windowed_ref[...].reshape(images * WROWS, C)
    qkv = (dot(flat, w_qkv[...]) + qkv_bias).astype(BF16)
    qkv_ref[...] = qkv.reshape(images, WROWS, 3 * C)
    low_masks = head_masks(BF16)
    eye = identity()
    def one_image(b, carry):
        rows, cols = sizes[0]
        for n in range(1, images):
            rows = jnp.where(b == n, sizes[n][0], rows)
            cols = jnp.where(b == n, sizes[n][1], cols)
        blocks = {}
        for w in range(NWIN):
            allowed = (row_limit[w] < rows) & (col_limit[w] < cols)
            blocks[w] = jnp.where(allowed, 0.0, MASKED).astype(F32)
        attend(b, blocks)
        return carry

    def attend(b, blocks):
        units = [(b, pair, g, blocks) for pair in range(NWIN // 2) for g in range(NGRP)]
        pipelined(units, raw_scores, softmax, apply)

    def raw_scores(b, pair, g, blocks):
        results = []
        for w in (2 * pair, 2 * pair + 1):
            at = slice(w * SLOT, (w + 1) * SLOT)
            query = qkv_ref[b, at, g * 128 : (g + 1) * 128]
            key = qkv_ref[b, at, C + g * 128 : C + (g + 1) * 128]
            results.append(dot(key, spread_heads(query, low_masks), NT))
        return results

    def softmax(b, pair, g, blocks, raw):
        probs = []
        for n, score in enumerate(raw):
            w = 2 * pair + n
            block = jnp.concatenate([blocks[w]] * 2, 1)
            score = score * SCALE + (bias[g] + block)
            top = jnp.max(score, 0, keepdims=True)
            expo = jnp.exp(score - top)
            prob = (expo * (1.0 / jnp.sum(expo, 0, keepdims=True))).astype(BF16)
            prob_ref[b, w, g] = prob
            probs.append(prob)
        return probs

    def apply(b, pair, g, blocks, probs):
        both = slice(pair * 2 * SLOT, (pair + 1) * 2 * SLOT)
        value = (b, both, slice(2 * C + g * 128, 2 * C + (g + 1) * 128))
        mixed_ref[b, g * 128 : (g + 1) * 128, both] = apply_pair(qkv_ref, value, eye, *probs).astype(BF16)

    each_image(images, one_image, unrolled)
    for b in range(images):
        attended_ref[b] = dot(perm_t[...], mixed_ref[b], NT).astype(BF16)
    attended = attended_ref[...].reshape(images * ROWS, C)
    middle = field + dot(attended, w_proj[...]) + small[4:5]
    return normed, middle


def forward_mlp(middle, w_up, w_down, small, up_bias, active_ref, slope_ref):
    hat, _ = norm_parts(middle)
    mlp_in = (hat * small[5:6] + small[6:7]).astype(BF16)
    branch = jnp.zeros(middle.shape, F32)
    width = CHUNK
    for part in range(HID // width):
        at = slice(part * width, (part + 1) * width)
        pre = dot(mlp_in, w_up[:, at]) + up_bias[:, at]
        half = 0.5 * (1.0 + lax.erf(pre * (0.5**0.5)))
        active = (pre * half).astype(BF16)
        slope = half + pre * (jnp.exp(-0.5 * pre * pre) * ((2.0 * np.pi) ** -0.5))
        active_ref[..., at] = active.reshape(active_ref.shape[:-1] + (width,))
        slope_ref[..., at] = slope.astype(BF16).reshape(slope_ref.shape[:-1] + (width,))
        branch = branch + dot(active, w_down[:, at], NT)
    return mlp_in, middle + branch + small[7:8]


def backward_mlp(
    grad, middle, slope_ref, w_up, w_down, small, low_ref, pre_ref, rows_ref, up_rows_ref, place
):
    low = grad.astype(BF16)
    low_ref[place, :] = low
    rows_ref[7:8, :] += col_sum(low.astype(F32))
    normed_grad = jnp.zeros(grad.shape, F32)
    width = CHUNK
    for part in range(HID // width):
        at = slice(part * width, (part + 1) * width)
        slope = slope_ref[..., at].reshape(-1, width).astype(F32)
        pre = (dot(low, w_down[:, at]) * slope).astype(BF16)
        pre_ref[place, at] = pre
        up_rows_ref[:, at] += col_sum(pre.astype(F32))
        normed_grad = normed_grad + dot(pre, w_up[:, at], NT)
    hat, rate = norm_parts(middle)
    rows_ref[5:6, :] += col_sum(normed_grad * hat)
    rows_ref[6:7, :] += col_sum(normed_grad)
    return norm_back(normed_grad, hat, rate, small[5:6]) + grad


def backward_attention(
    grad_mid, field, qkv_ref, prob_ref, w_qkv, w_proj, perm, perm_t, small,
    spread_ref, dq_ref, dkv_ref, attn_ref, joined_ref, rows_ref, qkv_rows_ref, bias_grad_ref, start,
    need_grad, unrolled,
):
    images = qkv_ref.shape[0]
    place = pl.ds(start, images * ROWS)
    attn = grad_mid.astype(BF16)
    attn_ref[place, :] = attn
    rows_ref[4:5, :] += col_sum(attn.astype(F32))
    joined = dot(attn, w_proj[...], NT).astype(BF16)
    for b in range(images):
        joined_ref[b] = dot(perm[...], joined[b * ROWS : (b + 1) * ROWS]).astype(BF16)
    low_masks = head_masks(BF16)
    eye = identity()

    def cut(n, g):
        return slice(n * C + g * 128, n * C + (g + 1) * 128)

    def prob_grads(b, pair, g):
        results = []
        for w in (2 * pair, 2 * pair + 1):
            at = slice(w * SLOT, (w + 1) * SLOT)
            out = spread_heads(joined_ref[b, at, cut(0, g)], low_masks)
            results.append(dot(qkv_ref[b, at, cut(2, g)], out, NT))
            dkv_ref[b, at, cut(1, g)] = dot(prob_ref[b, 2 * pair + len(results) - 1, g], out).astype(BF16)
        return results

    def score_grads(b, pair, g, grads):
        results = []
        for n, prob_grad in enumerate(grads):
            wide = prob_ref[b, 2 * pair + n, g].astype(F32)
            weighted = wide * prob_grad
            score = weighted - wide * jnp.sum(weighted, 0, keepdims=True)
            bias_grad_ref[g] += score
            results.append(score.astype(BF16))
        return results

    def products(b, pair, g, scores):
        both = slice(pair * 2 * SLOT, (pair + 1) * 2 * SLOT)
        for n, score in enumerate(scores):
            w = 2 * pair + n
            at = slice(w * SLOT, (w + 1) * SLOT)
            query = spread_heads(qkv_ref[b, at, cut(0, g)], low_masks)
            dkv_ref[b, at, cut(0, g)] = (dot(score, query) * SCALE).astype(BF16)
        dq_ref[b, cut(0, g), both] = (
            apply_pair(qkv_ref, (b, both, cut(1, g)), eye, *scores) * SCALE
        ).astype(BF16)

    def one_image(b, carry):
        units = [(b, pair, g) for pair in range(NWIN // 2) for g in range(NGRP)]
        pipelined(units, prob_grads, score_grads, products)
        return carry

    each_image(images, one_image, unrolled)
    for b in range(images):
        rows = pl.ds(pl.multiple_of(start + b * ROWS, 16), ROWS)
        spread_ref[rows, :C] = dot(perm_t[...], dq_ref[b], NT).astype(BF16)
        spread_ref[rows, C:] = dot(perm_t[...], dkv_ref[b]).astype(BF16)
    back = spread_ref[place, :]
    qkv_rows_ref[:, :C] += col_sum(back[:, :C].astype(F32))
    qkv_rows_ref[:, 2 * C :] += col_sum(back[:, 2 * C :].astype(F32))
    normed_grad = dot(back, w_qkv[...], NT)
    hat, rate = norm_parts(field)
    rows_ref[0:1, :] += col_sum(normed_grad * hat)
    rows_ref[1:2, :] += col_sum(normed_grad)
    if not need_grad:
        return None
    return norm_back(normed_grad, hat, rate, small[0:1]) + grad_mid


def image_place():
    return pl.ds(pl.multiple_of(pl.program_id(0) * GROUP * ROWS, 16), GROUP * ROWS)


def flat(ref):
    return ref[...].reshape(-1, ref.shape[-1])


def rows_in(k, name):
    if hasattr(k, name):
        return flat(getattr(k, name))
    rows = flat(getattr(k, name + "0"))
    number = 1
    while hasattr(k, f"{name}{number}"):
        rows = jnp.where(pl.program_id(0) == number, flat(getattr(k, f"{name}{number}")), rows)
        number += 1
    return rows


def put_rows(ref, value):
    ref[...] = value.reshape(ref.shape)


def is_first():
    return pl.program_id(0) == 0


def is_last():
    return pl.program_id(0) == pl.num_programs(0) - 1


def clear(*refs):
    @pl.when(is_first())
    def _():
        for ref in refs:
            ref[...] = jnp.zeros(ref.shape, ref.dtype)


class Names:
    def __init__(self, **refs):
        self.__dict__.update(refs)


def fetch_attention(k, plan):
    if not plan.sources:
        return

    @pl.when(is_first())
    def _():
        load_blocks(plan.pieces(k, "attn"), k.stage, plan.widths["attn"], k.load_sem.at[0], k.me)
        wait_all(k.stage, k.load_sem.at[0])
        join_attention(k.stage, k.w_qkv, k.w_proj)
        for n, (source, target) in enumerate(((k.w_qkv, k.qkv_out), (k.w_proj, k.proj_out))):
            pltpu.make_async_copy(source, target, k.out_sem.at[n]).start()


def fetch_mlp(k, plan):
    @pl.when(is_first())
    def _():
        load_blocks(plan.pieces(k, "down"), k.w_down, plan.widths["down"], k.load_sem.at[1], k.me)
        load_blocks(plan.pieces(k, "up"), k.w_up, plan.widths["up"], k.load_sem.at[2], k.me)
        wait_all(k.w_down, k.load_sem.at[1])
        wait_all(k.w_up, k.load_sem.at[2])


def group_images(k, group=0):
    images = k.rows.shape[1]
    first = (pl.program_id(0) + group) * GROUP
    return [((first + b) // images, (first + b) % images) for b in range(GROUP)]


def group_sizes(k, group=0):
    return [(k.rows[m, n], k.cols[m, n]) for m, n in group_images(k, group)]


def small_rows(k, plan):
    return k.vec[plan.layer * PER_LAYER : plan.layer * PER_LAYER + 8]


def joined_rows(k, start, end):
    return jnp.concatenate([k.vec[n : n + 1] for n in range(start, end)], 1)


def up_bias_row(k, plan):
    return joined_rows(k, plan.layer * PER_LAYER + 8, (plan.layer + 1) * PER_LAYER)


def attention_forward_kernel(k, plan):
    fetch_attention(k, plan)
    small = small_rows(k, plan)
    qkv_bias = jnp.concatenate([small[2:3], jnp.zeros((1, C), F32), small[3:4]], 1)
    normed, middle = forward_attention(
        flat(k.field).astype(F32), group_sizes(k, plan.group), k.w_qkv, k.w_proj, k.perm, k.perm_t,
        k.row_limit, k.col_limit, k.bias, small, qkv_bias, k.qkv, k.prob, k.windowed,
        k.mixed, k.attended, plan.layer > 0,
    )
    put_rows(k.normed, normed)
    put_rows(k.middle, middle)
    if not plan.sources:
        return

    @pl.when(is_last())
    def _():
        wait_all(k.w_qkv, k.out_sem.at[0])
        wait_all(k.w_proj, k.out_sem.at[1])


def first_mlp_kernel(k, plan):
    fetch_mlp(k, plan)

    @pl.when(is_first())
    def _():
        for n, (source, target) in enumerate(((k.w_down, k.down_out), (k.w_up, k.up_out))):
            pltpu.make_async_copy(source, target, k.out_sem.at[n]).start()

    mlp_in, result = forward_mlp(
        rows_in(k, "middle"), k.w_up, k.w_down, small_rows(k, plan), up_bias_row(k, plan), k.active,
        k.slope,
    )
    put_rows(k.mlp_in, mlp_in)
    put_rows(k.result, result)

    @pl.when(is_last())
    def _():
        wait_all(k.w_down, k.out_sem.at[0])
        wait_all(k.w_up, k.out_sem.at[1])


def store_mlp_grads(k, plan):
    for at in range(0, HID, CHUNK):
        k.up_grad[:, at : at + CHUNK] = dot(k.mlp_all[...], k.pre_all[:, at : at + CHUNK], TN).astype(BF16)
    store_blocks(k.up_grad, plan.outs(k, "up"), plan.widths["up"], k.sem_x, k.me)
    for at in range(0, HID, CHUNK):
        k.down_grad[:, at : at + CHUNK] = dot(k.low_all[...], k.active_all[:, at : at + CHUNK], TN).astype(BF16)
    store_blocks(k.down_grad, plan.outs(k, "down"), plan.widths["down"], k.sem_y, k.me)


def wait_mlp_grads(k, plan):
    wait_blocks(plan.outs(k, "up"), k.sem_x)
    wait_blocks(plan.outs(k, "down"), k.sem_y)


def head_pass(k, plan, result, sizes, total_images):
    first = pl.program_id(0) * GROUP
    base = plan.layers * PER_LAYER
    gain = k.vec[base : base + 1]
    hat, rate = norm_parts(result)
    final = hat * gain + k.vec[base + 1 : base + 2]
    places = group_images(k)
    owners, _, width = k.w_head.shape
    row = lax.broadcasted_iota(jnp.int32, (16, 1), 0)
    pooled = jnp.zeros((16, C), F32)
    own = other = jnp.full((16, 1), -1, jnp.int32)
    mixing = jnp.zeros((16, 1), F32)
    shares = []
    for b, (rows, cols) in enumerate(sizes):
        inside = ((k.cell_row[...] < rows) & (k.cell_col[...] < cols)).astype(F32)
        count = (rows * cols).astype(F32)
        mean = col_sum(final[b * ROWS : (b + 1) * ROWS] * inside) / count
        shares.append(inside / count)
        pooled = jnp.where(row == b, mean, pooled)
        m, n = places[b]
        mine = (k.me[0] * owners + k.me[1]) * k.rows.shape[1] + n
        own = jnp.where(row == b, k.labels[m, mine], own)
        other = jnp.where(row == b, k.labels[m, k.partner[m, n]], other)
        mixing = jnp.where(row == b, k.mix[m, n].astype(F32) / 16.0, mixing)
    pooled = pooled.astype(BF16)
    classes = owners * width
    real = CLASSES // owners
    bias = joined_rows(k, base + 2, base + 2 - (-CLASSES // C))
    empty = jnp.full((1, width - real), MASKED, F32)
    bias = jnp.concatenate(
        [part for n in range(owners) for part in (bias[:, n * real : (n + 1) * real], empty)], 1
    )
    logits = jnp.concatenate([dot(pooled, k.w_head[n]) for n in range(owners)], 1)
    logits = logits + bias
    top = jnp.max(logits, -1, keepdims=True)
    expo = jnp.exp(logits - top)
    log_probs = logits - top - jnp.log(jnp.sum(expo, -1, keepdims=True))
    lane = lax.broadcasted_iota(jnp.int32, (16, classes), 1)
    label = lane // width * real + lane % width
    label = jnp.where(lane % width < real, label, -2)
    target = jnp.where(label == own, mixing, 0.0)
    target = target + jnp.where(label == other, 1.0 - mixing, 0.0)
    loss = jnp.where(target > 0.0, target * log_probs, 0.0)
    loss = jnp.sum(jnp.sum(loss, -1, keepdims=True), 0, keepdims=True)
    k.loss[...] -= jnp.broadcast_to(loss, k.loss.shape)
    logit_grad = jnp.where(row < GROUP, (jnp.exp(log_probs) - target) / total_images, 0.0)
    logit_low = logit_grad.astype(BF16)
    wide = logit_low.astype(F32)
    k.head_rows[...] += col_sum(wide)
    for b in range(GROUP):
        k.pooled_all[pl.ds(first + b, 1), :] = pooled[b : b + 1].astype(F32)
        k.logit_all[pl.ds(first + b, 1), :] = wide[b : b + 1]
    pooled_grad = jnp.zeros((16, C), F32)
    for n in range(owners):
        pooled_grad += dot(logit_low[:, n * width : (n + 1) * width], k.w_head[n], NT)
    final_grad = jnp.concatenate(
        [pooled_grad[b : b + 1] * share for b, share in enumerate(shares)], 0
    )
    k.final_rows[0:1, :] += col_sum(final_grad * hat)
    k.final_rows[1:2, :] += col_sum(final_grad)
    return norm_back(final_grad, hat, rate, gain)


def last_mlp_kernel(k, plan, total_images):
    place = image_place()

    @pl.when(is_first())
    def _():
        load_blocks(plan.pieces(k, "head"), k.w_head, plan.widths["head"], k.load_sem.at[3], k.me)

    fetch_mlp(k, plan)

    @pl.when(is_first())
    def _():
        wait_all(k.w_head, k.load_sem.at[3])

    clear(k.row_sums, k.up_rows, k.final_rows, k.head_rows, k.loss, k.pooled_all, k.logit_all)
    middle = flat(k.middle)
    mlp_in, result = forward_mlp(
        middle, k.w_up, k.w_down, small_rows(k, plan), up_bias_row(k, plan), k.active_all.at[place], k.slope
    )
    k.mlp_all[place, :] = mlp_in
    grad = head_pass(k, plan, result, group_sizes(k), total_images)
    put_rows(k.grad_mid, backward_mlp(
        grad, flat(k.middle), k.slope, k.w_up, k.w_down, small_rows(k, plan), k.low_all, k.pre_all,
        k.row_sums, k.up_rows, place,
    ))

    @pl.when(is_last())
    def _():
        store_mlp_grads(k, plan)
        total = dot(k.pooled_all[...].astype(BF16), k.logit_all[...].astype(BF16), TN).astype(BF16)
        owners, _, width = k.head_grad.shape
        for n in range(owners):
            k.head_grad[n] = total[:, n * width : (n + 1) * width]
        store_blocks(k.head_grad, plan.outs(k, "head"), plan.widths["head"], k.sem_x, k.me)
        wait_mlp_grads(k, plan)


def backward_mlp_kernel(k, plan):
    clear(k.row_sums, k.up_rows)
    place = image_place()
    k.mlp_all[place, :] = flat(k.mlp_in)
    k.active_all[place, :] = flat(k.active)
    put_rows(k.grad_mid, backward_mlp(
        flat(k.grad), rows_in(k, "middle"), k.slope, k.w_up, k.w_down, small_rows(k, plan), k.low_all, k.pre_all,
        k.row_sums, k.up_rows, place,
    ))

    @pl.when(is_last())
    def _():
        store_mlp_grads(k, plan)
        wait_mlp_grads(k, plan)


def backward_attention_kernel(k, plan, earlier, need_grad):
    sums = ("row_sums", "qkv_rows", "bias_grad")
    if earlier:
        @pl.when(is_first())
        def _():
            for name in sums:
                getattr(k, name)[...] = getattr(k, name + "_in")[...]
    else:
        clear(*[getattr(k, name) for name in sums])
    start = pl.multiple_of(earlier * ROWS + pl.program_id(0) * GROUP * ROWS, 16)
    grad = backward_attention(
        flat(k.grad_mid), flat(k.field).astype(F32), k.qkv, k.prob, k.w_qkv, k.w_proj, k.perm,
        k.perm_t, small_rows(k, plan), k.spread_all, k.dq, k.dkv, k.attn_all, k.joined, k.row_sums,
        k.qkv_rows, k.bias_grad, start, need_grad, plan.layer > 0,
    )
    if need_grad:
        put_rows(k.grad, grad)
    if "attn" not in plan.targets:
        return
    place = pl.ds(start, GROUP * ROWS)
    k.normed_all[place, :] = flat(k.normed)
    k.attended_all[place, :] = flat(k.attended)

    @pl.when(is_last())
    def _():
        if earlier:
            before = slice(0, earlier * ROWS)
            k.normed_all[before, :] = flat(k.normed_in)
            k.attended_all[before, :] = flat(k.attended_in)
            k.spread_all[before, :] = k.spread_in[...]
            k.attn_all[before, :] = k.attn_in[...]
        owners, _, _ = k.attn_grad.shape
        wide, narrow = 3 * C // owners, C // owners
        if plan.collect is not None:
            layers, head_real, loss_at, near = plan.collect
            own = [k.row_sums, k.qkv_rows, k.mlp_rows0, k.up_rows0, k.bias_grad]
            collect_rows(
                layers, head_real, loss_at,
                own + [k.row_sums1, k.qkv_rows1, k.mlp_rows1, k.up_rows1, k.bias_grad1]
                + [k.final_rows, k.head_rows, k.loss],
                k.small_rows, k.spread_table,
            )
            pair_rows(k.small_rows, owners, near, k.me, k.pairs)
            for flip, (ref, *_) in enumerate(plan.outs(k, "attn")[2:]):
                width = ref.shape[2]
                pltpu.make_async_copy(
                    k.pairs.at[flip], ref.at[:, :, width - 128 : width], k.sem_a.at[2 + flip]
                ).start()
        total = dot(k.normed_all[...], k.spread_all[...], TN).astype(BF16)
        for n in range(owners):
            k.attn_grad[n, :, :wide] = total[:, n * wide : (n + 1) * wide]
        total = dot(k.attended_all[...], k.attn_all[...], TN).astype(BF16)
        for n in range(owners):
            k.attn_grad[n, :, wide:] = total[:, n * narrow : (n + 1) * narrow]
        store_blocks(k.attn_grad, plan.outs(k, "attn"), plan.widths["attn"], k.sem_a, k.me)
        wait_blocks(plan.outs(k, "attn"), k.sem_a)


class Plan:
    def __init__(self, widths, layer, layers):
        self.widths, self.layer, self.layers = widths, layer, layers
        self.sources = {}
        self.targets = {}
        self.collect = None
        self.group = 0

    def pieces(self, k, name):
        return [(getattr(k, ref), owners, cut) for ref, owners, cut in self.sources[name]]

    def outs(self, k, name):
        return [(getattr(k, ref), *rest) for ref, *rest in self.targets[name]]


def whole(shape):
    return pl.BlockSpec(shape, lambda i: (0,) * len(shape))


def per_image(*shape, first=0):
    return pl.BlockSpec((GROUP,) + shape, lambda i: (i + first,) + (0,) * len(shape))


SCALARS = pl.BlockSpec(memory_space=pltpu.SMEM)
FAR = pl.BlockSpec(memory_space=pl.ANY)


def call(body, name, groups, ins, outs, scratch, flops):
    def kernel(*refs):
        body(Names(**dict(zip(list(ins) + list(outs) + list(scratch), refs))))

    moved = sum(a.size * a.dtype.itemsize for _, a in ins.values())
    results = pl.pallas_call(
        kernel,
        grid=(groups,),
        in_specs=[spec for spec, _ in ins.values()],
        out_specs=[spec for spec, _, _ in outs.values()],
        out_shape=[jax.ShapeDtypeStruct(dims, dtype) for _, dims, dtype in outs.values()],
        scratch_shapes=list(scratch.values()),
        compiler_params=pltpu.CompilerParams(
            dimension_semantics=("arbitrary",), vmem_limit_bytes=VMEM_LIMIT
        ),
        cost_estimate=pl.CostEstimate(flops=int(flops), bytes_accessed=int(moved), transcendentals=0),
        name=name,
    )(*[array for _, array in ins.values()])
    return dict(zip(outs, results))


def exchange(array, step):
    axis, bit = step
    size = lax.axis_size(axis)
    return lax.ppermute(array, axis, [(i, i ^ (1 << bit)) for i in range(size)])


class Held:
    def __init__(self, array, dims=()):
        self.array, self.dims = array, list(dims)


def stack_blocks(parts, me, name, cuts=None):
    cuts = cuts or [None] * len(parts)
    args, outs, results = [], [], []
    for (held, received, step), cut in zip(parts, cuts):
        count, rows, columns = held.array.shape
        args += [held.array, received]
        axis, bit = step
        place = sum(d[0] == "win" and d[1] < bit for d in held.dims) if axis == "win" else len(held.dims)
        at = len(held.dims) - place
        dims = held.dims[:at] + [step] + held.dims[at:]
        bounds = [0, *(cut or ()), columns]
        pieces = list(zip(bounds, bounds[1:]))
        outs += [((2 * count, rows, end - start), BF16) for start, end in pieces]
        results.append((place, axis, bit, pieces, dims))

    def kernel(me_ref, *refs):
        ins, targets = list(refs[: len(args)]), list(refs[len(args) :])
        for place, axis, bit, pieces, _ in results:
            held, received = ins.pop(0), ins.pop(0)
            mine = (me_ref[0] >> bit) & 1 if axis == "win" else 0
            for start, end in pieces:
                out = targets.pop(0)
                for n in range(held.shape[0]):
                    base = (n >> place << (place + 1)) + (n & ((1 << place) - 1))
                    out[base + (mine << place)] = held[n, :, start:end]
                    out[base + ((1 - mine) << place)] = received[n, :, start:end]

    arrays = list(small_call(kernel, name, [me] + args, outs, scalars=1))
    return [
        [Held(arrays.pop(0), dims) for _ in pieces] for _, _, _, pieces, dims in results
    ]


def tie(*values):
    return lax.optimization_barrier(values)


def small_call(kernel, name, args, outs, stream=False, scratch=(), scalars=0, limit=24):
    def spec(dims):
        return whole(dims) if stream else pl.BlockSpec(memory_space=pltpu.VMEM)

    return pl.pallas_call(
        kernel,
        grid=(1,) if stream else (),
        out_shape=[jax.ShapeDtypeStruct(dims, dtype) for dims, dtype in outs],
        in_specs=[SCALARS] * scalars + [spec(a.shape) for a in args[scalars:]],
        out_specs=[spec(dims) for dims, _ in outs],
        scratch_shapes=list(scratch),
        compiler_params=pltpu.CompilerParams(
            vmem_limit_bytes=limit * 1024 * 1024
        ),
        cost_estimate=pl.CostEstimate(flops=1, bytes_accessed=1, transcendentals=0),
        name=name,
    )(*args)


class Chain:
    def __init__(self, keep, send, dims, steps, pair_at=None):
        self.keep, self.send, self.dims, self.steps = keep, send, list(dims), list(steps)
        self.pair_at = pair_at

    def start(self):
        self.received = exchange(self.send, self.steps.pop(0))


def add_blocks(keep, received, pair_at):
    total = keep.astype(F32) + received.astype(F32)
    if pair_at is None:
        return total.astype(BF16)
    pair = total[:16, pair_at:] + total[16:32, pair_at:]
    high = pair.astype(BF16)
    tail = jnp.zeros((total.shape[0] - 32, pair.shape[1]), BF16)
    parts = [jnp.concatenate([high, (pair - high.astype(F32)).astype(BF16), tail], 0)]
    if pair_at:
        parts = [total[:, :pair_at].astype(BF16)] + parts
    return jnp.concatenate(parts, 1)


def combine(groups, me, name):
    args, outs = [], []
    for group in groups:
        for chain in group:
            args += [chain.keep, chain.received]
        count, rows, _ = group[0].keep.shape
        width = sum(chain.keep.shape[2] for chain in group)
        outs += [((count // 2, rows, width), BF16)] * 2

    def kernel(me_ref, *refs):
        ins, results = list(refs[: len(args)]), list(refs[len(args) :])
        for group in groups:
            keep_out, send_out = results.pop(0), results.pop(0)
            start = 0
            for chain in group:
                keep, received = ins.pop(0), ins.pop(0)
                width = keep.shape[2]
                axis, bit = chain.steps[0]
                place = len(chain.dims) - 1 - chain.dims.index((axis, bit))
                mine = (me_ref[0] >> bit) & 1 if axis == "win" else 0
                for n in range(keep_out.shape[0]):
                    base = (n >> place << (place + 1)) + (n & ((1 << place) - 1))
                    for out, at in (
                        (keep_out, base + (mine << place)), (send_out, base + ((1 - mine) << place))
                    ):
                        out[n, :, start : start + width] = add_blocks(
                            keep[at], received[at], chain.pair_at
                        )
                start += width

    results = small_call(kernel, name, [me] + args, outs, scalars=1)
    chains = []
    for n, group in enumerate(groups):
        step = group[0].steps[0]
        at, pair_at = 0, None
        for chain in group:
            if chain.pair_at is not None:
                pair_at = at + chain.pair_at
            at += chain.keep.shape[2]
        dims = [d for d in group[0].dims if d != step]
        chains.append(Chain(results[2 * n], results[2 * n + 1], dims, group[0].steps, pair_at))
    return chains


def finish(chain, name):
    _, rows, width = chain.keep.shape

    def kernel(keep, received, own, square):
        total = keep[0].astype(F32) + received[0].astype(F32)
        own[...] = total
        square[...] = jnp.broadcast_to(jnp.sum(total * total), (1, 128))

    return small_call(
        kernel, name, [chain.keep, chain.received], [((rows, width), F32), ((1, 128), F32)]
    )


def finish_pair(chain, squares, devices, share, name):
    _, rows, width = chain.keep.shape
    at = chain.pair_at

    def kernel(keep, received, *refs):
        total = keep[0].astype(F32) + received[0].astype(F32)
        own, message = refs[-2:]
        own[...] = total[:, :at]
        pair = total[:16, at:] + total[16:32, at:]
        square = jnp.sum(total[:, :at] * total[:, :at])
        square = jnp.broadcast_to(square, (1, 128))
        for ref in refs[:-2]:
            square = square + ref[...]
        row = [pair[n : n + 1] for n in range(share // 128)] + [square]
        message[...] = jnp.broadcast_to(jnp.concatenate(row, 1), message.shape)

    return small_call(
        kernel, name, [chain.keep, chain.received] + squares,
        [((rows, at), F32), ((devices, share + 128), F32)],
    )


def adam_step(weight, grad, first, second, rate):
    new_first = 0.5 * first + 0.5 * grad
    new_second = 0.5 * second + 0.5 * grad * grad
    fix = 1.0 - 0.5**STEP
    update = new_first / fix / (jnp.sqrt(new_second / fix) + ADAM_EPS)
    return (new_first, new_second, weight - rate * (update + DECAY_RATE * weight))


def update_kernel(starts, widths, layout, *refs):
    own, message, rest = refs[:3], refs[3], list(refs[4:])
    groups = [rest[3 * n : 3 * n + 3] for n in range(7)]
    loss_ref, norm_ref = rest[21], rest[22]
    outs = [rest[23 + 3 * n : 26 + 3 * n] for n in range(7)]
    vector_rows, table_rows, offsets, square_at, loss_at = layout
    vector_grad = message[:vector_rows, :C]
    table_grad = message[:table_rows, C : C + offsets]
    total = (
        jnp.sum(message[:, square_at : square_at + 1])
        + jnp.sum(vector_grad * vector_grad)
        + jnp.sum(table_grad * table_grad)
    )
    norm = jnp.sqrt(jnp.broadcast_to(total, (1, 1)))
    factor = CLIP_NORM / jnp.maximum(norm, CLIP_NORM)
    norm_ref[...] = norm
    loss_ref[...] = message[0:1, loss_at : loss_at + 1]

    def put(number, layer, grad, rate):
        weight, first, second = groups[number]
        index = (Ellipsis,) if layer is None else (layer, Ellipsis)
        if number == 6:
            index = (slice(None), layer, slice(None))
        results = adam_step(weight[index], factor * grad, first[index], second[index], rate)
        for ref, value in zip(outs[number], results):
            ref[index] = value

    layers = len(starts)
    for l in range(layers):
        qkv_width = outs[0][0].shape[2]
        part, at = starts[l]["attn"]
        put(0, l, own[part][:, at : at + qkv_width], LEARN_RATE)
        put(1, l, own[part][:, at + qkv_width : at + widths["attn"]], LEARN_RATE)
        part, at = starts[l]["up"]
        put(2, l, own[part][:, at : at + widths["up"]], LEARN_RATE)
        part, at = starts[l]["down"]
        put(3, l, own[part][:, at : at + widths["down"]], LEARN_RATE)
        heads = table_rows // layers
        put(6, l, table_grad[l * heads : (l + 1) * heads], SMALL_RATE)
    part, at = starts[-1]["head"]
    put(4, None, own[part][:, at : at + outs[4][0].shape[1]], LEARN_RATE)
    put(5, None, vector_grad, SMALL_RATE)


def collect_rows(layers, head_real, loss_at, ins, out, spread):
    out[...] = jnp.zeros(out.shape, F32)
    row_of_slot = lax.broadcasted_iota(jnp.int32, (SLOT, 128), 0)
    lane = lax.broadcasted_iota(jnp.int32, (SLOT, 128), 1)
    target = row_of_slot // WSIDE * (2 * WSIDE - 1) + row_of_slot % WSIDE
    spreader = ((lane == target) & (row_of_slot < AREA)).astype(F32).astype(BF16)
    row = 0
    for l in range(layers):
        attn_rows, qkv_rows, mlp_rows, up_rows, bias_grad = ins[5 * l : 5 * l + 5]
        parts = [
            attn_rows[0:2], qkv_rows[:, :C], qkv_rows[:, 2 * C :], attn_rows[4:5], mlp_rows[5:8],
        ] + [up_rows[:, n * C : (n + 1) * C] for n in range(HID // C)]
        for part in parts:
            out[row : row + part.shape[0], :C] = part
            row += part.shape[0]
        for head in range(HEADS):
            g, h = divmod(head, PACK)
            left = bias_grad[g, :, h * SLOT : (h + 1) * SLOT]
            total = jnp.zeros((SLOT, 128), F32)
            for _ in range(3):
                low = left.astype(BF16)
                total = total + dot(low, spreader)
                left = left - low.astype(F32)
            spread[head * SLOT : (head + 1) * SLOT, :] = total
        table = jnp.zeros((HEADS, 256), F32)
        span = 2 * WSIDE - 1
        for j in range(AREA):
            wide = jnp.concatenate(
                [spread[pl.ds(j, HEADS, stride=SLOT), :], jnp.zeros((HEADS, 128), F32)], 1
            )
            shift = (WSIDE - 1 - j // WSIDE) * span + WSIDE - 1 - j % WSIDE
            table = table + (pltpu.roll(wide, shift, 1) if shift else wide)
        width = out.shape[1] - C
        out[l * HEADS : (l + 1) * HEADS, C:] = table[:, :width]
    final_rows, head_rows, loss = ins[5 * layers :]
    out[row : row + 2, :C] = final_rows[...]
    row += 2
    cuts = CLASSES // head_real
    width = head_rows.shape[1] // cuts
    classes = jnp.concatenate(
        [head_rows[:, n * width : n * width + head_real] for n in range(cuts)]
        + [jnp.zeros((1, -CLASSES % C), F32)], 1
    )
    for n in range(classes.shape[1] // C):
        out[row + n : row + n + 1, :C] = classes[:, n * C : (n + 1) * C]
    out[0:1, loss_at : loss_at + 1] = loss[:, 0:1]


def pair_rows(rows, ch_count, owners, me_ref, pairs):
    count = rows.shape[1] // 128
    wins = rows.shape[0] // ch_count
    high_rows = pairs.shape[2] // wins
    for flip in range(2):
        for n, owner in enumerate(owners):
            for win in range(wins):
                values = rows[pl.ds(win * ch_count + (me_ref[1] ^ (owner ^ flip)), 1), :]
                values = jnp.concatenate(
                    [values[:, m * 128 : (m + 1) * 128] for m in range(count)]
                    + [jnp.zeros((16 - count, 128), F32)], 0
                )
                high = values.astype(BF16)
                at = win * high_rows
                pairs[flip, n, at : at + 16] = high
                pairs[flip, n, at + 16 : at + 32] = (values - high.astype(F32)).astype(BF16)
                pairs[flip, n, at + 32 : at + high_rows] = jnp.zeros((high_rows - 32, 128), BF16)


def pack_kernel(head_width, qkv, proj, down, up, head, attn0, mlp0, all1):
    attn0[...] = jnp.concatenate([qkv[0], proj[0]], 1).astype(BF16)
    mlp0[...] = jnp.concatenate([down[0], up[0]], 1).astype(BF16)
    parts = [qkv[1], proj[1], down[1], up[1], head[...]]
    pad = head_width - head.shape[1]
    if pad:
        parts.append(jnp.zeros((head.shape[0], pad), F32))
    all1[...] = jnp.concatenate(parts, 1).astype(BF16)


def per_device(
    tokens, valid_rows, valid_cols, partner, mix_level, labels,
    w_qkv, m_qkv, v_qkv, w_proj, m_proj, v_proj, w_fc1, m_fc1, v_fc1, w_fc2, m_fc2, v_fc2,
    w_head, m_head, v_head, vectors, m_vec, v_vec, rel_table, m_rel, v_rel,
):
    micro, images, cells, chans = tokens.shape
    layers = rel_table.shape[0]
    per_layer = 8 + HID // C
    base = layers * per_layer
    head_rows = vectors.shape[0] - base - 2
    all_images = labels.shape[1]
    total_images = micro * all_images
    local = micro * images
    groups = local // GROUP
    sizes = {axis: lax.axis_size(axis) for axis in ("win", "ch")}
    win_count, ch_count = sizes["win"], sizes["ch"]
    device_count = win_count * ch_count
    win_index, ch_index = lax.axis_index("win"), lax.axis_index("ch")
    me = jnp.stack([win_index, ch_index]).astype(jnp.int32)
    block_rows = C // win_count
    widths = {"attn": 4 * C // ch_count, "down": HID // ch_count, "up": HID // ch_count}
    head_real = CLASSES // ch_count
    widths["head"] = -(-head_real // 128) * 128
    head_classes = widths["head"] * ch_count
    direct = block_rows % 16 == 0 and block_rows >= 32 and all(w % 128 == 0 for w in widths.values())

    core = ("ch", 0)
    ch_high = [("ch", b) for b in range(1, ch_count.bit_length() - 1)]
    win_low = [("win", 0)]
    win_high = [("win", b) for b in range(1, win_count.bit_length() - 1)]

    def low(v):
        return v.astype(BF16)

    packed = small_call(
        functools.partial(pack_kernel, widths["head"]), "pack",
        [w_qkv, w_proj, w_fc2.transpose(0, 2, 1), w_fc1, w_head],
        [((block_rows, sum(widths[n] for n in names)), BF16) for names in (
            ("attn",), ("down", "up"), ("attn", "down", "up", "head"))],
        stream=True,
        limit=56,
    )
    names = [["attn", "down", "up"], ["attn", "down", "up", "head"]]
    onehot = jnp.asarray(relative_onehot(), BF16)
    offsets = rel_table.shape[1]
    table_width = -(-(offsets + 1) // 128) * 128
    share = C + table_width
    tables = [window_tables(l % 2 == 1) for l in range(layers)]
    perms = [jnp.asarray(t[0], BF16) for t in tables]
    perms_t = [jnp.asarray(t[0].T, BF16) for t in tables]
    row_limits = [jnp.asarray(t[1]) for t in tables]
    col_limits = [jnp.asarray(t[2]) for t in tables]

    def bias_of(table):
        table = table.transpose(0, 2, 1).reshape(layers * HEADS, offsets)
        table_parts = []
        for _ in range(3):
            table_parts.append(low(table))
            table = table - table_parts[-1].astype(F32)
        bias = dot(jnp.concatenate(table_parts, 0), onehot).reshape(3, layers, HEADS, SLOT * SLOT)
        bias = (bias[0] + bias[1]) + bias[2]
        return (
            bias.reshape(layers, NGRP, PACK, SLOT, SLOT)
            .transpose(0, 1, 3, 2, 4)
            .reshape(layers, NGRP, SLOT, LANES)
        )

    padded = jnp.pad(tokens.reshape(local, cells, chans), ((0, 0), (0, ROWS - cells), (0, 0)))

    def stage(number, *moves, cuts=None, more=()):
        received = [exchange(part.array, step) for part, step in moves]
        tied = tie(*received, *more)
        received, more = tied[: len(moves)], tied[len(moves) :]
        stacked = stack_blocks(
            [(part, got, step) for (part, step), got in zip(moves, received)],
            me, f"stack{number}", cuts,
        )
        return (stacked, *more)

    def wait_for(value, *parts):
        value, *arrays = tie(value, *[part.array for part in parts])
        for part, array in zip(parts, arrays):
            part.array = array
        return value

    far = [Held(block[None]) for block in packed]
    edges = [
        [0, widths["attn"] * 2 // 3, widths["attn"], widths["attn"] + widths["down"],
         widths["attn"] + widths["down"] + widths["up"]],
        [0, widths["attn"], widths["attn"] + widths["down"] + widths["up"] * 2 // 3,
         sum(widths[name] for name in ("attn", "down", "up", "head"))],
    ]
    staged = win_count == 8 and ch_count == 4
    if staged:
        zh, zl, y, x = ("win", 2), ("win", 1), ("win", 0), ("ch", 1)
        ((attn,),), mlp, padded = stage(0, (far[0], zh), more=(far[1].array, padded))
        (attn, (mlp,)), all1, bias = stage(
            1, (attn, zl), (Held(mlp), zh), cuts=[edges[0][1:2], None],
            more=(packed[2], bias_of(rel_table)),
        )
        floating = exchange(all1[None], zh)
        ((one,), (two,), mlp), = stage(
            2, (attn[0], y), (attn[1], x), (mlp, zl), cuts=[None, None, [widths["down"]]]
        )
        (((all1,),),) = [stack_blocks([(Held(all1[None]), floating, zh)], me, "stack10")]
        mlp[0].array, mlp[1].array, all1.array = tie(mlp[0].array, mlp[1].array, all1.array)
        near = [(one, x), (two, y), (mlp[0], x), (mlp[1], y)]
        received = [exchange(part.array, step) for part, step in near]
        floating = exchange(all1.array, zl)
        *received, floating = tie(*received, floating)
        ((one,), (two,), (down,), (up,)) = stack_blocks(
            [(part, got, step) for (part, step), got in zip(near, received)], me, "stack3"
        )
        held = [[one, two]]
        *got, floating = tie(*[exchange(part.array, core) for part in held[0]], floating)
        other = [got]
        (parts1,) = stack_blocks([(all1, floating, zl)], me, "stack11", [edges[1][1:-1]])
        padded = wait_for(padded, *parts1)
    else:
        bias = bias_of(rel_table)
        bits = win_high[::-1] + win_low + ch_high[::-1]
        held, other = [[], []], []
        for number, part in enumerate(far):
            for n, step in enumerate(bits):
                ((part,),), = stage(10 * number + n, (part, step))
            layer = number // 2
            base = 0 if number != 1 else widths["attn"]
            for start, end in zip(edges[layer], edges[layer][1:]):
                if start >= base and end - base <= part.array.shape[-1]:
                    held[layer].append(Held(part.array[..., start - base : end - base], part.dims))
        other.append([exchange(part.array, core) for part in held[0]])

    def weight_inputs(layer, wanted):
        plan = Plan(widths, layer, layers)
        ins = {}
        starts, at = {}, 0
        for name in names[layer]:
            starts[name] = at
            at += widths[name]
        bounds = list(zip(edges[layer], edges[layer][1:]))
        blocks = []
        for group, part in enumerate(held[layer]):
            if group >= len(other[layer]):
                break
            owners = relative_owners([d for d in part.dims if d[0] == "ch"])
            for number, array in enumerate((part.array, other[layer][group])):
                flat_array = array.reshape(-1, C, array.shape[-1])
                blocks.append((group, [owner ^ number for owner in owners], flat_array))
        for name in wanted:
            plan.sources[name] = []
            columns = []
            for number, (group, owners, array) in enumerate(blocks):
                begin = max(starts[name], bounds[group][0])
                end = min(starts[name] + widths[name], bounds[group][1])
                if begin >= end:
                    continue
                cut = (begin - bounds[group][0], end - begin, begin - starts[name])
                if direct:
                    ref = f"blocks{number}"
                    ins[ref] = (FAR, array)
                    plan.sources[name].append((ref, owners, cut))
                elif number % 2 == 0:
                    table = np.argsort(np.asarray(owners + blocks[number + 1][1]))
                    both = jnp.concatenate([array, blocks[number + 1][2]])
                    index = jnp.asarray(table)[jnp.arange(ch_count) ^ ch_index]
                    columns.append(jnp.take(both, index, axis=0)[..., cut[0] : cut[0] + cut[1]])
            if not direct:
                full = jnp.concatenate(columns, -1)
                if name in ("up", "down"):
                    full = full.transpose(1, 0, 2).reshape(C, -1)
                ins[f"staged_{name}"] = (FAR, full)
                plan.sources[name] = [(f"staged_{name}", None, None)]
        ins["me"] = (SCALARS, me)
        return ins, plan

    orders = {
        "x": ch_high + win_low + win_high, "a": ch_high + win_low + win_high,
        "y": win_low + ch_high + win_high, "b": win_low + ch_high + win_high,
    }
    block_dims = ch_high + [("win", b) for b in reversed(range(win_count.bit_length() - 1))]
    owners = relative_owners(ch_high)
    regular = direct and len(ch_high) == 1

    def grad_outputs(plan, **members):
        outs = {}
        for group, wanted in members.items():
            if not direct:
                for name in wanted:
                    plan.targets[name] = [(f"full_{name}", None, 0, 0, widths[name])]
                    dims = (C, HID) if name in ("up", "down") else (ch_count, C, widths[name])
                    outs[f"full_{name}"] = (FAR, dims, BF16)
                continue
            starts = np.cumsum([0] + [widths[name] for name in wanted])
            refs = [
                (f"keep_{group}", owners), (f"send_{group}", [owner ^ 1 for owner in owners])
            ]
            for ref, _ in refs:
                outs[ref] = (FAR, (len(owners), C, int(starts[-1])), BF16)
            for name, start in zip(wanted, starts):
                plan.targets[name] = [(ref, at, int(start), 0, widths[name]) for ref, at in refs]
        return outs

    def cut_attention_outputs(plan):
        cut = widths["attn"] * 2 // 3
        outs, plan.targets["attn"] = {}, []
        for group, start, size, extra in (("a", 0, cut, 0), ("b", cut, widths["attn"] - cut, 128)):
            for kind, flip in (("keep", 0), ("send", 1)):
                ref = f"{kind}_{group}"
                outs[ref] = (FAR, (len(owners), C, size + extra), BF16)
                plan.targets["attn"].append(
                    (ref, [owner ^ flip for owner in owners], 0, start, size)
                )
        return outs

    def chain_of(results, group, *members, pair_at=None):
        if direct:
            keep, send = results[f"keep_{group}"], results[f"send_{group}"]
        else:
            full = []
            for name in members:
                part = results[f"full_{name}"]
                if name in ("up", "down"):
                    part = part.reshape(C, ch_count, -1).transpose(1, 0, 2)
                full.append(part)
            full = jnp.concatenate(full, -1)
            keep, send = [
                jnp.take(full, np.asarray(owners) ^ flip ^ ch_index, axis=0) for flip in (0, 1)
            ]
        dims = (-1, block_rows, keep.shape[-1])
        return Chain(
            keep.reshape(dims), send.reshape(dims), block_dims, [core] + orders[group], pair_at
        )

    def start(*chains):
        for chain in chains:
            chain.start()

    def meet(value, *chains):
        value, *got = tie(value, *[chain.received for chain in chains])
        for chain, array in zip(chains, got):
            chain.received = array
        return value

    def after(value, *chains):
        held_back = [array for chain in chains for array in (chain.keep, chain.send)]
        value, *held_back = tie(value, *held_back)
        for n, chain in enumerate(chains):
            chain.keep, chain.send = held_back[2 * n], held_back[2 * n + 1]
        return value

    def attention_consts(l, forward):
        ins = {
            "perm": (whole((WROWS, ROWS)), perms[l]),
            "perm_t": (whole((ROWS, WROWS)), perms_t[l]),
            "vec": (whole(vectors.shape), vectors),
        }
        if forward:
            ins["rows"] = (SCALARS, valid_rows)
            ins["cols"] = (SCALARS, valid_cols)
            ins["row_limit"] = (whole((NWIN, SLOT, 128)), row_limits[l])
            ins["col_limit"] = (whole((NWIN, SLOT, 128)), col_limits[l])
            ins["bias"] = (
                pl.BlockSpec((None, NGRP, SLOT, LANES), lambda i, l=l: (l, 0, 0, 0)), bias
            )
        return ins

    def vmem(*dims, dtype=BF16):
        return pltpu.VMEM(dims, dtype)

    attn_weights = {
        "stage": vmem(ch_count, C, widths["attn"]),
        "w_qkv": vmem(C, 3 * C),
        "w_proj": vmem(C, C),
        "load_sem": pltpu.SemaphoreType.DMA((4,)),
    }
    mlp_weights = {
        "w_down": vmem(C, HID),
        "w_up": vmem(C, HID),
        "load_sem": pltpu.SemaphoreType.DMA((4,)),
    }
    all_rows = local * ROWS
    mlp_rows = {
        "mlp_all": vmem(all_rows, C), "active_all": vmem(all_rows, HID),
        "pre_all": vmem(all_rows, HID), "low_all": vmem(all_rows, C),
        "up_grad": vmem(C, HID), "down_grad": vmem(C, HID),
        "sem_x": pltpu.SemaphoreType.DMA((2,)), "sem_y": pltpu.SemaphoreType.DMA((2,)),
    }
    wide = (per_image(ROWS, C), (local, ROWS, C), F32)
    thin = (per_image(ROWS, C), (local, ROWS, C), BF16)
    hidden = (per_image(ROWS, HID), (local, ROWS, HID), BF16)
    attn_saved = {
        "normed": thin,
        "qkv": (per_image(WROWS, 3 * C), (local, WROWS, 3 * C), BF16),
        "prob": (per_image(NWIN, NGRP, SLOT, LANES), (local, NWIN, NGRP, SLOT, LANES), BF16),
        "attended": thin,
    }
    sums = {"row_sums": (whole((8, C)), (8, C), F32)}
    up_sums = {**sums, "up_rows": (whole((1, HID)), (1, HID), F32)}
    attn_sums = {
        **sums,
        "qkv_rows": (whole((1, 3 * C)), (1, 3 * C), F32),
        "bias_grad": (whole((NGRP, SLOT, LANES)), (NGRP, SLOT, LANES), F32),
    }

    def given(spec, array):
        return (spec[0], array)

    mlp_flops = 2 * all_rows * C * HID * 2
    attn_flops = 2 * all_rows * C * C * 8

    def attention_forward(l, field, first=0, count=groups, before=None):
        ins, plan = weight_inputs(l, ["attn"]) if before is None else ({}, Plan(widths, l, layers))
        plan.group = first
        ins["field"] = (per_image(*field.shape[1:], first=first), field)
        ins.update(attention_consts(l, True))
        outs = {
            name: (spec, (count * GROUP,) + dims[1:], dtype)
            for name, (spec, dims, dtype) in {"middle": wide, **attn_saved}.items()
        }
        scratch = {"mixed": vmem(GROUP, C, WROWS), "windowed": vmem(GROUP, WROWS, C)}
        if before is None:
            outs["qkv_out"] = (FAR, (C, 3 * C), BF16)
            outs["proj_out"] = (FAR, (C, C), BF16)
            scratch.update(attn_weights)
            scratch["out_sem"] = pltpu.SemaphoreType.DMA((2,))
        else:
            ins["w_qkv"] = (whole((C, 3 * C)), before["qkv_out"])
            ins["w_proj"] = (whole((C, C)), before["proj_out"])
        results = call(
            functools.partial(attention_forward_kernel, plan=plan), f"attention_forward{l}_{first}",
            count, ins, outs, scratch, attn_flops * count // groups,
        )
        return results if before is None else {**before, **results}

    def rows_of(name, arrays):
        if len(arrays) == 1:
            return {name: given(wide, arrays[0])}
        return {f"{name}{n}": (whole(array.shape), array) for n, array in enumerate(arrays)}

    def begin(*moves):
        return [(part, step, exchange(part.array, step)) for part, step in moves]

    def arrive(number, value, moves):
        value, *received = tie(value, *[got for _, _, got in moves])
        stacked = stack_blocks(
            [(part, got, step) for (part, step, _), got in zip(moves, received)], me, f"stack{number}"
        )
        return value, [parts[0] for parts in stacked]

    if staged:
        moves = begin((down, y), (up, x), (parts1[0], y), (parts1[1], x), (parts1[2], y))
        early0 = attention_forward(0, padded, 0, groups - 1)
        early0["proj_out"], (down, up, *parts1) = arrive(4, early0["proj_out"], moves)
        early0["proj_out"] = wait_for(early0["proj_out"], down, up, *parts1)
        held[0] += [down, up]
        got = [exchange(part.array, core) for part in (down, up)]
        moves = begin((parts1[0], x), (parts1[1], y), (parts1[2], x))
        saved0 = attention_forward(0, padded, groups - 1, 1, early0)
        saved0["middle"], *got = tie(saved0["middle"], *got)
        other[0] = list(other[0]) + got
        saved0["middle"], parts1 = arrive(5, saved0["middle"], moves[:1])
        middle0 = [early0["middle"], wait_for(saved0["middle"], *parts1)]
        held.append(parts1)
    else:
        saved0 = early0 = attention_forward(0, padded)
        middle0 = [saved0["middle"]]
    ins, plan = weight_inputs(0, ["down", "up"])
    ins.update(rows_of("middle", middle0))
    ins["vec"] = (whole(vectors.shape), vectors)
    mlp0 = call(
        functools.partial(first_mlp_kernel, plan=plan), "first_mlp", groups, ins,
        {
            "result": wide, "mlp_in": thin, "active": hidden, "slope": hidden,
            "down_out": (FAR, (C, HID), BF16),
            "up_out": (FAR, (C, HID), BF16),
        },
        {**mlp_weights, "out_sem": pltpu.SemaphoreType.DMA((2,))},
        mlp_flops,
    )
    result0 = mlp0["result"]
    got = [exchange(part.array, core) for part in held[1]]
    result0, *got = tie(result0, *got)
    other.append(got)
    if staged:
        result0, late1 = arrive(6, result0, moves[1:])
        result0 = wait_for(result0, *late1)
        late_got = [exchange(part.array, core) for part in late1]

    saved1 = attention_forward(1, result0)
    if staged:
        saved1["middle"], *late_got = tie(saved1["middle"], *late_got)
        held[1] = held[1] + late1
        other[1] = other[1] + late_got
    ins, plan = weight_inputs(1, ["down", "up", "head"])
    ins["middle"] = given(wide, saved1["middle"])
    ins["vec"] = (whole(vectors.shape), vectors)
    ins["rows"] = (SCALARS, valid_rows)
    ins["cols"] = (SCALARS, valid_cols)
    ins["labels"] = (SCALARS, labels)
    ins["partner"] = (SCALARS, partner)
    ins["mix"] = (SCALARS, mix_level)
    cell = np.arange(ROWS)
    for name, place in (("cell_row", cell // GRID), ("cell_col", cell % GRID)):
        place = np.where(cell < CELLS, place, 99)[:, None].astype(np.int32)
        ins[name] = (whole((ROWS, 1)), jnp.asarray(place))
    outs = {
        "grad_mid": wide, **up_sums,
        "final_rows": (whole((2, C)), (2, C), F32),
        "head_rows": (whole((1, head_classes)), (1, head_classes), F32),
        "loss": (whole((1, 128)), (1, 128), F32),
        **grad_outputs(plan, x=["up", "head"], y=["down"]),
    }
    last = call(
        functools.partial(last_mlp_kernel, plan=plan, total_images=float(total_images)),
        "last_mlp", groups, ins, outs,
        {
            "slope": vmem(GROUP * ROWS, HID), "w_head": vmem(ch_count, C, widths["head"]),
            **mlp_weights, **mlp_rows,
            "pooled_all": vmem(16, C, dtype=F32), "logit_all": vmem(16, head_classes, dtype=F32),
            "head_grad": vmem(ch_count, C, widths["head"]),
        },
        3 * mlp_flops,
    )

    def attention_backward(l, grad_mid, field, saved, first, count, before=None, before_saved=None, store=True, collect=None):
        plan = Plan(widths, l, layers)
        ins = {
            "me": (SCALARS, me), "w_qkv": (whole((C, 3 * C)), saved["qkv_out"]),
            "w_proj": (whole((C, C)), saved["proj_out"]),
        }
        ins.update(attention_consts(l, False))
        wanted = ["qkv", "prob"] + (["normed", "attended"] if store else [])
        for name, array in [("grad_mid", grad_mid), ("field", field)] + [
            (name, saved[name]) for name in wanted
        ]:
            skip = first if array.shape[0] == local else 0
            ins[name] = (per_image(*array.shape[1:], first=skip), array)
        if before is not None:
            for name, (spec, _, _) in attn_sums.items():
                ins[name + "_in"] = (spec, before[name])
            for name in ("normed", "attended"):
                ins[name + "_in"] = (whole((first * GROUP, ROWS, C)), before_saved[name])
            for name in ("spread", "attn"):
                array = before[name + "_all"]
                ins[name + "_in"] = (whole(array.shape), array)
        rows_here = count * GROUP * ROWS
        outs = dict(attn_sums)
        scratch = {
            "dq": vmem(GROUP, C, WROWS), "dkv": vmem(GROUP, WROWS, 2 * C),
            "joined": vmem(GROUP, WROWS, C),
        }
        need_grad = l > 0
        if need_grad:
            outs["grad"] = wide
        if store:
            if collect is None:
                outs.update(grad_outputs(plan, a=["attn"]))
            else:
                outs.update(cut_attention_outputs(plan))
                plan.collect = (layers, head_real, share - 1, owners)
                ins.update({name: (whole(array.shape), array) for name, array in collect.items()})
                scratch["small_rows"] = vmem(device_count, share, dtype=F32)
                scratch["spread_table"] = vmem(HEADS * SLOT, 128, dtype=F32)
                scratch["pairs"] = vmem(2, len(owners), C, 128)
            scratch.update({
                "normed_all": vmem(all_rows, C), "attended_all": vmem(all_rows, C),
                "spread_all": vmem(all_rows, 3 * C), "attn_all": vmem(all_rows, C),
                "attn_grad": vmem(ch_count, C, widths["attn"]),
                "sem_a": pltpu.SemaphoreType.DMA((4,)),
            })
        else:
            outs["spread_all"] = (whole((rows_here, 3 * C)), (rows_here, 3 * C), BF16)
            outs["attn_all"] = (whole((rows_here, C)), (rows_here, C), BF16)
        return call(
            functools.partial(
                backward_attention_kernel, plan=plan,
                earlier=0 if before is None else first * GROUP, need_grad=need_grad,
            ),
            f"attention_backward{l}_{first}", count, ins, outs, scratch,
            2 * attn_flops * count // groups,
        )

    x1, y1 = chain_of(last, "x", "up", "head"), chain_of(last, "y", "down")
    if regular:
        start(x1, y1)
    back1 = attention_backward(1, last["grad_mid"], mlp0["result"], saved1, 0, groups)
    a1 = chain_of(back1, "a", "attn")
    grad = back1["grad"]
    if regular:
        grad = meet(grad, x1, y1)
        x1, y1 = combine([[x1], [y1]], me, "sum1")
        grad = after(grad, x1, y1)
        start(x1, y1, a1)

    plan = Plan(widths, 0, layers)
    ins = {
        "me": (SCALARS, me),
        "w_down": (whole((C, HID)), mlp0["down_out"]),
        "w_up": (whole((C, HID)), mlp0["up_out"]),
    }
    ins["grad"] = given(wide, grad)
    ins.update(rows_of("middle", middle0))
    ins["mlp_in"] = given(thin, mlp0["mlp_in"])
    ins["active"] = given(hidden, mlp0["active"])
    ins["slope"] = given(hidden, mlp0["slope"])
    ins["vec"] = (whole(vectors.shape), vectors)
    first = call(
        functools.partial(backward_mlp_kernel, plan=plan), "mlp_backward0", groups, ins,
        {"grad_mid": wide, **up_sums, **grad_outputs(plan, x=["up"], y=["down"])},
        dict(mlp_rows), 2 * mlp_flops,
    )
    x0, y0 = chain_of(first, "x", "up"), chain_of(first, "y", "down")
    grad_mid = first["grad_mid"]
    if regular:
        grad_mid = meet(grad_mid, x1, y1, a1)
        x1, y1, a1 = combine([[x1], [y1], [a1]], me, "sum2")
        grad_mid = after(grad_mid, x1, y1, a1)
        start(x1, y1, a1, x0, y0)
    before0 = attention_backward(0, grad_mid, padded, early0, 0, groups - 1, store=False)
    if regular:
        before0["row_sums"] = meet(before0["row_sums"], a1, x0, y0, x1, y1)
        a1, x0, y0, z1 = combine([[a1], [x0], [y0], [x1, y1]], me, "sum3")
        grad_mid = after(grad_mid, a1, x0, y0, z1)
        start(a1, x0, y0, z1)
    small_parts = None
    if regular:
        small_parts = {
            "mlp_rows0": first["row_sums"], "up_rows0": first["up_rows"],
            "row_sums1": back1["row_sums"], "qkv_rows1": back1["qkv_rows"],
            "mlp_rows1": last["row_sums"], "up_rows1": last["up_rows"],
            "bias_grad1": back1["bias_grad"], "final_rows": last["final_rows"],
            "head_rows": last["head_rows"], "loss": last["loss"],
        }
    back0 = attention_backward(
        0, grad_mid, padded, saved0, groups - 1, 1, before0, early0, collect=small_parts
    )
    a0 = chain_of(back0, "a", "attn")
    if regular:
        b0 = chain_of(back0, "b", pair_at=widths["attn"] - widths["attn"] * 2 // 3)
        waiting = (a1, x0, y0, z1)
        a0.send, b0.send, *got = tie(a0.send, b0.send, *[chain.received for chain in waiting])
        for chain, array in zip(waiting, got):
            chain.received = array

    if regular:
        start(a0, b0)
        z1, x0, y0 = combine([[z1], [x0], [y0]], me, "sum5")
        start(z1, x0, y0)
        a0.received, b0.received, x0.keep = tie(a0.received, b0.received, x0.keep)
        a0, b0 = combine([[a0], [b0]], me, "sum6")
        start(a0, b0)
        x0.received, y0.received, z1.received = tie(x0.received, y0.received, z1.received)
        (z0,) = combine([[x0, y0, a1]], me, "sum7")
        start(z0)
        a0, b0 = combine([[a0], [b0]], me, "sum8")
        start(a0, b0)
        (z0,) = combine([[z0]], me, "sum9")
        start(z0)
        own1, square1 = finish(z1, "own1")
        (a0,) = combine([[a0, b0]], me, "sum10")
        start(a0)
        own0, square0 = finish(z0, "own0")
        (a0,) = combine([[a0]], me, "sum11")
        start(a0)
        own_attn, message = finish_pair(a0, [square0, square1], device_count, share, "own_attn")
    else:
        square, own_parts = jnp.zeros((1, 128), F32), []
        for chain in (a0, x0, y0, a1, x1, y1):
            start(chain)
            while chain.steps:
                (chain,) = combine([[chain]], me, "sum")
                start(chain)
            part, part_square = finish(chain, "own")
            square = square + part_square
            own_parts.append(part)
        own_attn = own_parts[0]
        own0, own1 = jnp.concatenate(own_parts[1:4], 1), jnp.concatenate(own_parts[4:], 1)
        (rows_all,) = small_call(
            lambda *refs: collect_rows(
                layers, head_real, share - 1, refs[:-2], refs[-2], refs[-1]
            ),
            "collect",
            [part[name] for part in ((first, back0), (last, back1))
             for part, name in (
                 (part[1], "row_sums"), (part[1], "qkv_rows"), (part[0], "row_sums"),
                 (part[0], "up_rows"), (part[1], "bias_grad"))]
            + [last["final_rows"], last["head_rows"], last["loss"]],
            [((device_count, share), F32)],
            stream=True,
            scratch=[pltpu.VMEM((HEADS * SLOT, 128), F32)],
        )
        rows_all = lax.all_to_all(rows_all, ("win", "ch"), 0, 0, tiled=True)
        message = jnp.concatenate([jnp.sum(rows_all, 0, keepdims=True), square], 1)
        message = jnp.broadcast_to(message, (device_count, share + 128))
    message = lax.all_to_all(message, ("win", "ch"), 0, 0, tiled=True)
    starts = [
        {"attn": (1, 0), "up": (2, 0), "down": (2, widths["up"])},
        {
            "attn": (2, widths["up"] + widths["down"]), "up": (0, 0), "head": (0, widths["up"]),
            "down": (0, widths["up"] + widths["head"]),
        },
    ]
    arrays = [
        [w_qkv, m_qkv, v_qkv], [w_proj, m_proj, v_proj], [w_fc1, m_fc1, v_fc1],
        [w_fc2, m_fc2, v_fc2], [w_head, m_head, v_head], [vectors, m_vec, v_vec],
        [rel_table, m_rel, v_rel],
    ]
    turns = {3: (0, 2, 1), 6: (2, 0, 1)}
    turned = [
        a.transpose(turns[n]) if n in turns else a for n, group in enumerate(arrays) for a in group
    ]
    results = small_call(
        functools.partial(
            update_kernel, starts, widths,
            (vectors.shape[0], layers * HEADS, offsets, share, share - 1),
        ),
        "update",
        [own1, own_attn, own0, message] + turned,
        [((1, 1), F32)] * 2 + [(a.shape, F32) for a in turned],
        stream=True,
    )
    loss_total, grad_norm, *results = results
    outs = [loss_total[0, 0], grad_norm[0, 0]]
    for n in range(0, len(results), 3):
        back = {3: (0, 2, 1), 6: (1, 2, 0)}.get(n // 3)
        outs += [r if back is None else r.transpose(back) for r in results[n : n + 3]]
    return tuple(outs)


def solution(mesh):
    cut = P(None, "win", "ch")
    down = P(None, "ch", "win")
    head = P("win", "ch")
    rows = P(None, ("win", "ch"))
    in_specs = (
        (P(None, ("win", "ch"), None, None),) + (rows,) * 4 + (P(),)
        + (cut,) * 9 + (down,) * 3 + (head,) * 3 + (P(),) * 6
    )
    out_specs = (P(),) * 2 + (cut,) * 9 + (down,) * 3 + (head,) * 3 + (P(),) * 6
    return jax.shard_map(
        per_device, mesh=mesh, in_specs=in_specs, out_specs=out_specs, check_vma=False
    )
```

```python
import functools

import jax
import jax.numpy as jnp
import numpy as np
from jax import lax
from jax.experimental import pallas as pl
from jax.experimental.pallas import tpu as pltpu
from jax.sharding import PartitionSpec as P

C = 384
HID = 1536
CLASSES = 1000
CLASS_PAD = 1024
WSIDE = 7
GRID = 14
STEP = 10
HEADS = 12
PER_LAYER = 8 + HID // C
DEPTH = 32
CELLS = GRID * GRID
ROWS = 208
AREA = WSIDE * WSIDE
SLOT = 64
NWIN = 4
NGRP = 3
PACK = 4
WROWS = NWIN * SLOT
LANES = PACK * SLOT

NORM_EPS = 1e-05
CLIP_NORM = 0.05
LEARN_RATE = 0.04
SMALL_RATE = 0.2
DECAY_RATE = 0.05
ADAM_EPS = 1e-08
MASKED = -1e30
SCALE = DEPTH ** (-0.5)
F32 = jnp.float32
BF16 = jnp.bfloat16
NN = (((1,), (0,)), ((), ()))
NT = (((1,), (1,)), ((), ()))
TN = (((0,), (0,)), ((), ()))
VMEM_LIMIT = 24 * 1024 * 1024
GROUP = 2
CHUNK = 512


def dot(a, b, dims=NN):
    return lax.dot_general(a, b, dims, preferred_element_type=F32)


@functools.lru_cache(None)
def window_tables(shifted):
    perm = np.zeros((WROWS, ROWS), np.float32)
    row_limit = np.full((NWIN, SLOT, 2 * SLOT), 99, np.int32)
    col_limit = np.full((NWIN, SLOT, 2 * SLOT), 99, np.int32)
    shift = WSIDE // 2 if shifted else 0

    def band(v):
        return 0 if v < GRID - WSIDE else (1 if v < GRID - WSIDE // 2 else 2)

    for window in range(NWIN):
        wr, wc = divmod(window, GRID // WSIDE)
        place = []
        for j in range(AREA):
            r, c = wr * WSIDE + j // WSIDE, wc * WSIDE + j % WSIDE
            region = 3 * band(r) + band(c) if shifted else 0
            source = ((r + shift) % GRID, (c + shift) % GRID)
            place.append((region, source))
            perm[window * SLOT + j, source[0] * GRID + source[1]] = 1
        for j in range(SLOT):
            for i in range(SLOT):
                if i == j:
                    pair = (-1, -1)
                elif i < AREA and j < AREA and place[i][0] == place[j][0]:
                    pair = place[j][1]
                else:
                    pair = (99, 99)
                row_limit[window, j, i::SLOT] = pair[0]
                col_limit[window, j, i::SLOT] = pair[1]
    return perm, row_limit, col_limit


@functools.lru_cache(None)
def relative_onehot():
    span = 2 * WSIDE - 1
    onehot = np.zeros((span * span, SLOT, SLOT), np.float32)
    for i in range(AREA):
        for j in range(AREA):
            row, col = i // WSIDE - j // WSIDE, i % WSIDE - j % WSIDE
            onehot[(row + WSIDE - 1) * span + col + WSIDE - 1, j, i] = 1
    return onehot.reshape(span * span, SLOT * SLOT)


def norm_parts(field):
    average = jnp.mean(field, -1, keepdims=True)
    centered = field - average
    spread = jnp.mean(centered * centered, -1, keepdims=True)
    rate = lax.rsqrt(spread + NORM_EPS)
    return centered * rate, rate


def norm_back(grad, hat, rate, gain):
    scaled = grad * gain
    return rate * (
        scaled
        - jnp.mean(scaled, -1, keepdims=True)
        - hat * jnp.mean(scaled * hat, -1, keepdims=True)
    )


def col_sum(field):
    return jnp.sum(field, 0, keepdims=True)


def head_masks(dtype):
    lane = lax.broadcasted_iota(jnp.int32, (SLOT, 128), 1)
    return [((lane // DEPTH) == h).astype(F32).astype(dtype) for h in range(PACK)]


def spread_heads(block, masks):
    return jnp.concatenate([block * m for m in masks], 0)


def relative_owners(bits):
    owners = []
    for index in range(1 << len(bits)):
        offset = 0
        for n, (_, bit) in enumerate(bits):
            offset |= ((index >> (len(bits) - 1 - n)) & 1) << bit
        owners.append(offset)
    return owners


def owner_part(ref, owner, width, start, size):
    if len(ref.shape) == 3:
        return ref.at[owner, :, start : start + size]
    return ref.at[:, pl.ds(pl.multiple_of(owner * width + start, 128), size)]


def load_blocks(pieces, target, width, sem, me_ref):
    for ref, owners, cut in pieces:
        if owners is None:
            pltpu.make_async_copy(ref, target, sem).start()
            continue
        source, size, start = cut
        for n, owner in enumerate(owners):
            pltpu.make_async_copy(
                ref.at[n, :, source : source + size],
                owner_part(target, me_ref[1] ^ owner, width, start, size),
                sem,
            ).start()


def wait_all(ref, sem):
    pltpu.make_async_copy(ref, ref, sem).wait()


def store_blocks(source, outs, width, sems, me_ref):
    for number, (ref, owners, start, source_start, size) in enumerate(outs):
        if owners is None:
            copy = pltpu.make_async_copy(source, ref, sems.at[number])
            copy.start()
            copy.wait()
            continue
        for n, owner in enumerate(owners):
            pltpu.make_async_copy(
                owner_part(source, me_ref[1] ^ owner, width, source_start, size),
                ref.at[n, :, start : start + size],
                sems.at[number],
            ).start()


def wait_blocks(outs, sems):
    for number, (ref, owners, *_) in enumerate(outs):
        if owners is not None:
            wait_all(ref, sems.at[number])


def join_attention(stage, w_qkv, w_proj):
    owners = stage.shape[0]
    wide, narrow = 3 * C // owners, C // owners
    w_qkv[...] = jnp.concatenate([stage[n, :, :wide] for n in range(owners)], 1)
    w_proj[...] = jnp.concatenate([stage[n, :, wide : wide + narrow] for n in range(owners)], 1)


def pick_heads(first, second):
    lane = lax.broadcasted_iota(jnp.int32, (DEPTH, 128), 1)
    parts = []
    for h in range(PACK):
        at = (slice(h * DEPTH, (h + 1) * DEPTH), slice(h // 2 * 128, (h // 2 + 1) * 128))
        one, two = first[at], second[at]
        if h % 2:
            one = pltpu.roll(one, SLOT, 1)
        else:
            two = pltpu.roll(two, SLOT, 1)
        parts.append(jnp.where(lane < SLOT, one, two))
    return jnp.concatenate(parts, 0)


def apply_pair(rows_ref, cut, eye, first, second):
    turned = dot(eye, rows_ref[cut], NT).astype(BF16)
    empty = jnp.zeros_like(first)
    full = dot(
        turned,
        jnp.concatenate(
            [jnp.concatenate([first, empty], 1), jnp.concatenate([empty, second], 1)], 0
        ),
    )
    return pick_heads(full[:, :LANES], full[:, LANES:])


def identity():
    shape = (128, 128)
    same = lax.broadcasted_iota(jnp.int32, shape, 0) == lax.broadcasted_iota(jnp.int32, shape, 1)
    return same.astype(F32).astype(BF16)


def pipelined(units, first, second, third):
    ones, twos = {}, {}
    count = len(units)
    for n in range(count + 2):
        if n < count:
            ones[n] = first(*units[n])
        if 1 <= n <= count:
            twos[n - 1] = second(*units[n - 1], ones.pop(n - 1))
        if n >= 2:
            third(*units[n - 2], twos.pop(n - 2))


def each_image(images, body, unrolled):
    lax.fori_loop(0, images, body, 0, unroll=images if unrolled else 1)


def forward_attention(
    field, sizes, w_qkv, w_proj, perm, perm_t, row_limit, col_limit, bias, small, qkv_bias,
    qkv_ref, prob_ref, windowed_ref, mixed_ref, attended_ref, unrolled,
):
    hat, _ = norm_parts(field)
    normed = (hat * small[0:1] + small[1:2]).astype(BF16)
    images = len(sizes)
    for b in range(images):
        windowed_ref[b] = dot(perm[...], normed[b * ROWS : (b + 1) * ROWS]).astype(BF16)
    flat = windowed_ref[...].reshape(images * WROWS, C)
    qkv = (dot(flat, w_qkv[...]) + qkv_bias).astype(BF16)
    qkv_ref[...] = qkv.reshape(images, WROWS, 3 * C)
    low_masks = head_masks(BF16)
    eye = identity()
    def one_image(b, carry):
        rows, cols = sizes[0]
        for n in range(1, images):
            rows = jnp.where(b == n, sizes[n][0], rows)
            cols = jnp.where(b == n, sizes[n][1], cols)
        blocks = {}
        for w in range(NWIN):
            allowed = (row_limit[w] < rows) & (col_limit[w] < cols)
            blocks[w] = jnp.where(allowed, 0.0, MASKED).astype(F32)
        attend(b, blocks)
        return carry

    def attend(b, blocks):
        units = [(b, pair, g, blocks) for pair in range(NWIN // 2) for g in range(NGRP)]
        pipelined(units, raw_scores, softmax, apply)

    def raw_scores(b, pair, g, blocks):
        results = []
        for w in (2 * pair, 2 * pair + 1):
            at = slice(w * SLOT, (w + 1) * SLOT)
            query = qkv_ref[b, at, g * 128 : (g + 1) * 128]
            key = qkv_ref[b, at, C + g * 128 : C + (g + 1) * 128]
            results.append(dot(key, spread_heads(query, low_masks), NT))
        return results

    def softmax(b, pair, g, blocks, raw):
        probs = []
        for n, score in enumerate(raw):
            w = 2 * pair + n
            block = jnp.concatenate([blocks[w]] * 2, 1)
            score = score * SCALE + (bias[g] + block)
            top = jnp.max(score, 0, keepdims=True)
            expo = jnp.exp(score - top)
            prob = (expo * (1.0 / jnp.sum(expo, 0, keepdims=True))).astype(BF16)
            prob_ref[b, w, g] = prob
            probs.append(prob)
        return probs

    def apply(b, pair, g, blocks, probs):
        both = slice(pair * 2 * SLOT, (pair + 1) * 2 * SLOT)
        value = (b, both, slice(2 * C + g * 128, 2 * C + (g + 1) * 128))
        mixed_ref[b, g * 128 : (g + 1) * 128, both] = apply_pair(qkv_ref, value, eye, *probs).astype(BF16)

    each_image(images, one_image, unrolled)
    for b in range(images):
        attended_ref[b] = dot(perm_t[...], mixed_ref[b], NT).astype(BF16)
    attended = attended_ref[...].reshape(images * ROWS, C)
    middle = field + dot(attended, w_proj[...]) + small[4:5]
    return normed, middle


def forward_mlp(middle, w_up, w_down, small, up_bias, active_ref, slope_ref):
    hat, _ = norm_parts(middle)
    mlp_in = (hat * small[5:6] + small[6:7]).astype(BF16)
    branch = jnp.zeros(middle.shape, F32)
    width = CHUNK
    for part in range(HID // width):
        at = slice(part * width, (part + 1) * width)
        pre = dot(mlp_in, w_up[:, at]) + up_bias[:, at]
        half = 0.5 * (1.0 + lax.erf(pre * (0.5**0.5)))
        active = (pre * half).astype(BF16)
        slope = half + pre * (jnp.exp(-0.5 * pre * pre) * ((2.0 * np.pi) ** -0.5))
        active_ref[..., at] = active.reshape(active_ref.shape[:-1] + (width,))
        slope_ref[..., at] = slope.astype(BF16).reshape(slope_ref.shape[:-1] + (width,))
        branch = branch + dot(active, w_down[:, at], NT)
    return mlp_in, middle + branch + small[7:8]


def backward_mlp(
    grad, middle, slope_ref, w_up, w_down, small, low_ref, pre_ref, rows_ref, up_rows_ref, place
):
    low = grad.astype(BF16)
    low_ref[place, :] = low
    rows_ref[7:8, :] += col_sum(low.astype(F32))
    normed_grad = jnp.zeros(grad.shape, F32)
    width = CHUNK
    for part in range(HID // width):
        at = slice(part * width, (part + 1) * width)
        slope = slope_ref[..., at].reshape(-1, width).astype(F32)
        pre = (dot(low, w_down[:, at]) * slope).astype(BF16)
        pre_ref[place, at] = pre
        up_rows_ref[:, at] += col_sum(pre.astype(F32))
        normed_grad = normed_grad + dot(pre, w_up[:, at], NT)
    hat, rate = norm_parts(middle)
    rows_ref[5:6, :] += col_sum(normed_grad * hat)
    rows_ref[6:7, :] += col_sum(normed_grad)
    return norm_back(normed_grad, hat, rate, small[5:6]) + grad


def backward_attention(
    grad_mid, field, qkv_ref, prob_ref, w_qkv, w_proj, perm, perm_t, small,
    spread_ref, dq_ref, dkv_ref, attn_ref, joined_ref, rows_ref, qkv_rows_ref, bias_grad_ref, start,
    need_grad, unrolled,
):
    images = qkv_ref.shape[0]
    place = pl.ds(start, images * ROWS)
    attn = grad_mid.astype(BF16)
    attn_ref[place, :] = attn
    rows_ref[4:5, :] += col_sum(attn.astype(F32))
    joined = dot(attn, w_proj[...], NT).astype(BF16)
    for b in range(images):
        joined_ref[b] = dot(perm[...], joined[b * ROWS : (b + 1) * ROWS]).astype(BF16)
    low_masks = head_masks(BF16)
    eye = identity()

    def cut(n, g):
        return slice(n * C + g * 128, n * C + (g + 1) * 128)

    def prob_grads(b, pair, g):
        results = []
        for w in (2 * pair, 2 * pair + 1):
            at = slice(w * SLOT, (w + 1) * SLOT)
            out = spread_heads(joined_ref[b, at, cut(0, g)], low_masks)
            results.append(dot(qkv_ref[b, at, cut(2, g)], out, NT))
            dkv_ref[b, at, cut(1, g)] = dot(prob_ref[b, 2 * pair + len(results) - 1, g], out).astype(BF16)
        return results

    def score_grads(b, pair, g, grads):
        results = []
        for n, prob_grad in enumerate(grads):
            wide = prob_ref[b, 2 * pair + n, g].astype(F32)
            weighted = wide * prob_grad
            score = weighted - wide * jnp.sum(weighted, 0, keepdims=True)
            bias_grad_ref[g] += score
            results.append(score.astype(BF16))
        return results

    def products(b, pair, g, scores):
        both = slice(pair * 2 * SLOT, (pair + 1) * 2 * SLOT)
        for n, score in enumerate(scores):
            w = 2 * pair + n
            at = slice(w * SLOT, (w + 1) * SLOT)
            query = spread_heads(qkv_ref[b, at, cut(0, g)], low_masks)
            dkv_ref[b, at, cut(0, g)] = (dot(score, query) * SCALE).astype(BF16)
        dq_ref[b, cut(0, g), both] = (
            apply_pair(qkv_ref, (b, both, cut(1, g)), eye, *scores) * SCALE
        ).astype(BF16)

    def one_image(b, carry):
        units = [(b, pair, g) for pair in range(NWIN // 2) for g in range(NGRP)]
        pipelined(units, prob_grads, score_grads, products)
        return carry

    each_image(images, one_image, unrolled)
    for b in range(images):
        rows = pl.ds(pl.multiple_of(start + b * ROWS, 16), ROWS)
        spread_ref[rows, :C] = dot(perm_t[...], dq_ref[b], NT).astype(BF16)
        spread_ref[rows, C:] = dot(perm_t[...], dkv_ref[b]).astype(BF16)
    back = spread_ref[place, :]
    qkv_rows_ref[:, :C] += col_sum(back[:, :C].astype(F32))
    qkv_rows_ref[:, 2 * C :] += col_sum(back[:, 2 * C :].astype(F32))
    normed_grad = dot(back, w_qkv[...], NT)
    hat, rate = norm_parts(field)
    rows_ref[0:1, :] += col_sum(normed_grad * hat)
    rows_ref[1:2, :] += col_sum(normed_grad)
    if not need_grad:
        return None
    return norm_back(normed_grad, hat, rate, small[0:1]) + grad_mid


def image_place():
    return pl.ds(pl.multiple_of(pl.program_id(0) * GROUP * ROWS, 16), GROUP * ROWS)


def flat(ref):
    return ref[...].reshape(-1, ref.shape[-1])


def rows_in(k, name):
    if hasattr(k, name):
        return flat(getattr(k, name))
    rows = flat(getattr(k, name + "0"))
    number = 1
    while hasattr(k, f"{name}{number}"):
        rows = jnp.where(pl.program_id(0) == number, flat(getattr(k, f"{name}{number}")), rows)
        number += 1
    return rows


def put_rows(ref, value):
    ref[...] = value.reshape(ref.shape)


def is_first():
    return pl.program_id(0) == 0


def is_last():
    return pl.program_id(0) == pl.num_programs(0) - 1


def clear(*refs):
    @pl.when(is_first())
    def _():
        for ref in refs:
            ref[...] = jnp.zeros(ref.shape, ref.dtype)


class Names:
    def __init__(self, **refs):
        self.__dict__.update(refs)


def fetch_attention(k, plan):
    if not plan.sources:
        return

    @pl.when(is_first())
    def _():
        load_blocks(plan.pieces(k, "attn"), k.stage, plan.widths["attn"], k.load_sem.at[0], k.me)
        wait_all(k.stage, k.load_sem.at[0])
        join_attention(k.stage, k.w_qkv, k.w_proj)
        for n, (source, target) in enumerate(((k.w_qkv, k.qkv_out), (k.w_proj, k.proj_out))):
            pltpu.make_async_copy(source, target, k.out_sem.at[n]).start()


def fetch_mlp(k, plan):
    @pl.when(is_first())
    def _():
        load_blocks(plan.pieces(k, "down"), k.w_down, plan.widths["down"], k.load_sem.at[1], k.me)
        load_blocks(plan.pieces(k, "up"), k.w_up, plan.widths["up"], k.load_sem.at[2], k.me)
        wait_all(k.w_down, k.load_sem.at[1])
        wait_all(k.w_up, k.load_sem.at[2])


def group_images(k, group=0):
    images = k.rows.shape[1]
    first = (pl.program_id(0) + group) * GROUP
    return [((first + b) // images, (first + b) % images) for b in range(GROUP)]


def group_sizes(k, group=0):
    return [(k.rows[m, n], k.cols[m, n]) for m, n in group_images(k, group)]


def small_rows(k, plan):
    return k.vec[plan.layer * PER_LAYER : plan.layer * PER_LAYER + 8]


def joined_rows(k, start, end):
    return jnp.concatenate([k.vec[n : n + 1] for n in range(start, end)], 1)


def up_bias_row(k, plan):
    return joined_rows(k, plan.layer * PER_LAYER + 8, (plan.layer + 1) * PER_LAYER)


def attention_forward_kernel(k, plan):
    fetch_attention(k, plan)
    small = small_rows(k, plan)
    qkv_bias = jnp.concatenate([small[2:3], jnp.zeros((1, C), F32), small[3:4]], 1)
    normed, middle = forward_attention(
        flat(k.field).astype(F32), group_sizes(k, plan.group), k.w_qkv, k.w_proj, k.perm, k.perm_t,
        k.row_limit, k.col_limit, k.bias, small, qkv_bias, k.qkv, k.prob, k.windowed,
        k.mixed, k.attended, plan.layer > 0,
    )
    put_rows(k.normed, normed)
    put_rows(k.middle, middle)
    if not plan.sources:
        return

    @pl.when(is_last())
    def _():
        wait_all(k.w_qkv, k.out_sem.at[0])
        wait_all(k.w_proj, k.out_sem.at[1])


def first_mlp_kernel(k, plan):
    fetch_mlp(k, plan)

    @pl.when(is_first())
    def _():
        for n, (source, target) in enumerate(((k.w_down, k.down_out), (k.w_up, k.up_out))):
            pltpu.make_async_copy(source, target, k.out_sem.at[n]).start()

    mlp_in, result = forward_mlp(
        rows_in(k, "middle"), k.w_up, k.w_down, small_rows(k, plan), up_bias_row(k, plan), k.active,
        k.slope,
    )
    put_rows(k.mlp_in, mlp_in)
    put_rows(k.result, result)

    @pl.when(is_last())
    def _():
        wait_all(k.w_down, k.out_sem.at[0])
        wait_all(k.w_up, k.out_sem.at[1])


def store_mlp_grads(k, plan):
    for at in range(0, HID, CHUNK):
        k.up_grad[:, at : at + CHUNK] = dot(k.mlp_all[...], k.pre_all[:, at : at + CHUNK], TN).astype(BF16)
    store_blocks(k.up_grad, plan.outs(k, "up"), plan.widths["up"], k.sem_x, k.me)
    for at in range(0, HID, CHUNK):
        k.down_grad[:, at : at + CHUNK] = dot(k.low_all[...], k.active_all[:, at : at + CHUNK], TN).astype(BF16)
    store_blocks(k.down_grad, plan.outs(k, "down"), plan.widths["down"], k.sem_y, k.me)


def wait_mlp_grads(k, plan):
    wait_blocks(plan.outs(k, "up"), k.sem_x)
    wait_blocks(plan.outs(k, "down"), k.sem_y)


def head_pass(k, plan, result, sizes, total_images):
    first = pl.program_id(0) * GROUP
    base = plan.layers * PER_LAYER
    gain = k.vec[base : base + 1]
    hat, rate = norm_parts(result)
    final = hat * gain + k.vec[base + 1 : base + 2]
    places = group_images(k)
    owners, _, width = k.w_head.shape
    row = lax.broadcasted_iota(jnp.int32, (16, 1), 0)
    pooled = jnp.zeros((16, C), F32)
    own = other = jnp.full((16, 1), -1, jnp.int32)
    mixing = jnp.zeros((16, 1), F32)
    shares = []
    for b, (rows, cols) in enumerate(sizes):
        inside = ((k.cell_row[...] < rows) & (k.cell_col[...] < cols)).astype(F32)
        count = (rows * cols).astype(F32)
        mean = col_sum(final[b * ROWS : (b + 1) * ROWS] * inside) / count
        shares.append(inside / count)
        pooled = jnp.where(row == b, mean, pooled)
        m, n = places[b]
        mine = (k.me[0] * owners + k.me[1]) * k.rows.shape[1] + n
        own = jnp.where(row == b, k.labels[m, mine], own)
        other = jnp.where(row == b, k.labels[m, k.partner[m, n]], other)
        mixing = jnp.where(row == b, k.mix[m, n].astype(F32) / 16.0, mixing)
    pooled = pooled.astype(BF16)
    classes = owners * width
    real = CLASSES // owners
    bias = joined_rows(k, base + 2, base + 2 - (-CLASSES // C))
    empty = jnp.full((1, width - real), MASKED, F32)
    bias = jnp.concatenate(
        [part for n in range(owners) for part in (bias[:, n * real : (n + 1) * real], empty)], 1
    )
    logits = jnp.concatenate([dot(pooled, k.w_head[n]) for n in range(owners)], 1)
    logits = logits + bias
    top = jnp.max(logits, -1, keepdims=True)
    expo = jnp.exp(logits - top)
    log_probs = logits - top - jnp.log(jnp.sum(expo, -1, keepdims=True))
    lane = lax.broadcasted_iota(jnp.int32, (16, classes), 1)
    label = lane // width * real + lane % width
    label = jnp.where(lane % width < real, label, -2)
    target = jnp.where(label == own, mixing, 0.0)
    target = target + jnp.where(label == other, 1.0 - mixing, 0.0)
    loss = jnp.where(target > 0.0, target * log_probs, 0.0)
    loss = jnp.sum(jnp.sum(loss, -1, keepdims=True), 0, keepdims=True)
    k.loss[...] -= jnp.broadcast_to(loss, k.loss.shape)
    logit_grad = jnp.where(row < GROUP, (jnp.exp(log_probs) - target) / total_images, 0.0)
    logit_low = logit_grad.astype(BF16)
    wide = logit_low.astype(F32)
    k.head_rows[...] += col_sum(wide)
    for b in range(GROUP):
        k.pooled_all[pl.ds(first + b, 1), :] = pooled[b : b + 1].astype(F32)
        k.logit_all[pl.ds(first + b, 1), :] = wide[b : b + 1]
    pooled_grad = jnp.zeros((16, C), F32)
    for n in range(owners):
        pooled_grad += dot(logit_low[:, n * width : (n + 1) * width], k.w_head[n], NT)
    final_grad = jnp.concatenate(
        [pooled_grad[b : b + 1] * share for b, share in enumerate(shares)], 0
    )
    k.final_rows[0:1, :] += col_sum(final_grad * hat)
    k.final_rows[1:2, :] += col_sum(final_grad)
    return norm_back(final_grad, hat, rate, gain)


def last_mlp_kernel(k, plan, total_images):
    place = image_place()

    @pl.when(is_first())
    def _():
        load_blocks(plan.pieces(k, "head"), k.w_head, plan.widths["head"], k.load_sem.at[3], k.me)

    fetch_mlp(k, plan)

    @pl.when(is_first())
    def _():
        wait_all(k.w_head, k.load_sem.at[3])

    clear(k.row_sums, k.up_rows, k.final_rows, k.head_rows, k.loss, k.pooled_all, k.logit_all)
    middle = flat(k.middle)
    mlp_in, result = forward_mlp(
        middle, k.w_up, k.w_down, small_rows(k, plan), up_bias_row(k, plan), k.active_all.at[place], k.slope
    )
    k.mlp_all[place, :] = mlp_in
    grad = head_pass(k, plan, result, group_sizes(k), total_images)
    put_rows(k.grad_mid, backward_mlp(
        grad, flat(k.middle), k.slope, k.w_up, k.w_down, small_rows(k, plan), k.low_all, k.pre_all,
        k.row_sums, k.up_rows, place,
    ))

    @pl.when(is_last())
    def _():
        store_mlp_grads(k, plan)
        total = dot(k.pooled_all[...].astype(BF16), k.logit_all[...].astype(BF16), TN).astype(BF16)
        owners, _, width = k.head_grad.shape
        for n in range(owners):
            k.head_grad[n] = total[:, n * width : (n + 1) * width]
        store_blocks(k.head_grad, plan.outs(k, "head"), plan.widths["head"], k.sem_x, k.me)
        wait_mlp_grads(k, plan)


def backward_mlp_kernel(k, plan):
    clear(k.row_sums, k.up_rows)
    place = image_place()
    k.mlp_all[place, :] = flat(k.mlp_in)
    k.active_all[place, :] = flat(k.active)
    put_rows(k.grad_mid, backward_mlp(
        flat(k.grad), rows_in(k, "middle"), k.slope, k.w_up, k.w_down, small_rows(k, plan), k.low_all, k.pre_all,
        k.row_sums, k.up_rows, place,
    ))

    @pl.when(is_last())
    def _():
        store_mlp_grads(k, plan)
        wait_mlp_grads(k, plan)


def backward_attention_kernel(k, plan, earlier, need_grad):
    sums = ("row_sums", "qkv_rows", "bias_grad")
    if earlier:
        @pl.when(is_first())
        def _():
            for name in sums:
                getattr(k, name)[...] = getattr(k, name + "_in")[...]
    else:
        clear(*[getattr(k, name) for name in sums])
    start = pl.multiple_of(earlier * ROWS + pl.program_id(0) * GROUP * ROWS, 16)
    grad = backward_attention(
        flat(k.grad_mid), flat(k.field).astype(F32), k.qkv, k.prob, k.w_qkv, k.w_proj, k.perm,
        k.perm_t, small_rows(k, plan), k.spread_all, k.dq, k.dkv, k.attn_all, k.joined, k.row_sums,
        k.qkv_rows, k.bias_grad, start, need_grad, True,
    )
    if need_grad:
        put_rows(k.grad, grad)
    if "attn" not in plan.targets:
        return
    place = pl.ds(start, GROUP * ROWS)
    k.normed_all[place, :] = flat(k.normed)
    k.attended_all[place, :] = flat(k.attended)

    @pl.when(is_last())
    def _():
        if earlier:
            before = slice(0, earlier * ROWS)
            k.normed_all[before, :] = flat(k.normed_in)
            k.attended_all[before, :] = flat(k.attended_in)
            k.spread_all[before, :] = k.spread_in[...]
            k.attn_all[before, :] = k.attn_in[...]
        owners, _, _ = k.attn_grad.shape
        wide, narrow = 3 * C // owners, C // owners
        if plan.collect is not None:
            layers, head_real, loss_at, near = plan.collect
            own = [k.row_sums, k.qkv_rows, k.mlp_rows0, k.up_rows0, k.bias_grad]
            collect_rows(
                layers, head_real, loss_at,
                own + [k.row_sums1, k.qkv_rows1, k.mlp_rows1, k.up_rows1, k.bias_grad1]
                + [k.final_rows, k.head_rows, k.loss],
                k.small_rows, k.spread_table,
            )
            pair_rows(k.small_rows, owners, near, k.me, k.pairs)
            for flip, (ref, *_) in enumerate(plan.outs(k, "attn")[2:]):
                width = ref.shape[2]
                pltpu.make_async_copy(
                    k.pairs.at[flip], ref.at[:, :, width - 128 : width], k.sem_a.at[2 + flip]
                ).start()
        total = dot(k.normed_all[...], k.spread_all[...], TN).astype(BF16)
        for n in range(owners):
            k.attn_grad[n, :, :wide] = total[:, n * wide : (n + 1) * wide]
        total = dot(k.attended_all[...], k.attn_all[...], TN).astype(BF16)
        for n in range(owners):
            k.attn_grad[n, :, wide:] = total[:, n * narrow : (n + 1) * narrow]
        store_blocks(k.attn_grad, plan.outs(k, "attn"), plan.widths["attn"], k.sem_a, k.me)
        wait_blocks(plan.outs(k, "attn"), k.sem_a)


class Plan:
    def __init__(self, widths, layer, layers):
        self.widths, self.layer, self.layers = widths, layer, layers
        self.sources = {}
        self.targets = {}
        self.collect = None
        self.group = 0

    def pieces(self, k, name):
        return [(getattr(k, ref), owners, cut) for ref, owners, cut in self.sources[name]]

    def outs(self, k, name):
        return [(getattr(k, ref), *rest) for ref, *rest in self.targets[name]]


def whole(shape):
    return pl.BlockSpec(shape, lambda i: (0,) * len(shape))


def per_image(*shape, first=0):
    return pl.BlockSpec((GROUP,) + shape, lambda i: (i + first,) + (0,) * len(shape))


SCALARS = pl.BlockSpec(memory_space=pltpu.SMEM)
FAR = pl.BlockSpec(memory_space=pl.ANY)
NEAR = pl.BlockSpec(memory_space=pltpu.VMEM)


def call(body, name, groups, ins, outs, scratch, flops):
    def kernel(*refs):
        body(Names(**dict(zip(list(ins) + list(outs) + list(scratch), refs))))

    moved = sum(a.size * a.dtype.itemsize for _, a in ins.values())
    results = pl.pallas_call(
        kernel,
        grid=(groups,),
        in_specs=[spec for spec, _ in ins.values()],
        out_specs=[spec for spec, _, _ in outs.values()],
        out_shape=[jax.ShapeDtypeStruct(dims, dtype) for _, dims, dtype in outs.values()],
        scratch_shapes=list(scratch.values()),
        compiler_params=pltpu.CompilerParams(
            dimension_semantics=("arbitrary",), vmem_limit_bytes=VMEM_LIMIT
        ),
        cost_estimate=pl.CostEstimate(flops=int(flops), bytes_accessed=int(moved), transcendentals=0),
        name=name,
    )(*[array for _, array in ins.values()])
    return dict(zip(outs, results))


def exchange(array, step):
    axis, bit = step
    size = lax.axis_size(axis)
    return lax.ppermute(array, axis, [(i, i ^ (1 << bit)) for i in range(size)])


class Held:
    def __init__(self, array, dims=()):
        self.array, self.dims = array, list(dims)


def stack_blocks(parts, me, name, cuts=None):
    cuts = cuts or [None] * len(parts)
    args, outs, results = [], [], []
    for (held, received, step), cut in zip(parts, cuts):
        count, rows, columns = held.array.shape
        args += [held.array, received]
        axis, bit = step
        place = sum(d[0] == "win" and d[1] < bit for d in held.dims) if axis == "win" else len(held.dims)
        at = len(held.dims) - place
        dims = held.dims[:at] + [step] + held.dims[at:]
        bounds = [0, *(cut or ()), columns]
        pieces = list(zip(bounds, bounds[1:]))
        outs += [((2 * count, rows, end - start), BF16) for start, end in pieces]
        results.append((place, axis, bit, pieces, dims))

    def kernel(me_ref, *refs):
        ins, targets = list(refs[: len(args)]), list(refs[len(args) :])
        for place, axis, bit, pieces, _ in results:
            held, received = ins.pop(0), ins.pop(0)
            mine = (me_ref[0] >> bit) & 1 if axis == "win" else 0
            for start, end in pieces:
                out = targets.pop(0)
                for n in range(held.shape[0]):
                    base = (n >> place << (place + 1)) + (n & ((1 << place) - 1))
                    out[base + (mine << place)] = held[n, :, start:end]
                    out[base + ((1 - mine) << place)] = received[n, :, start:end]

    arrays = list(small_call(kernel, name, [me] + args, outs, scalars=1))
    return [
        [Held(arrays.pop(0), dims) for _ in pieces] for _, _, _, pieces, dims in results
    ]


def tie(*values):
    return lax.optimization_barrier(values)


def small_call(kernel, name, args, outs, stream=False, scratch=(), scalars=0, limit=24):
    def spec(dims):
        return whole(dims) if stream else pl.BlockSpec(memory_space=pltpu.VMEM)

    return pl.pallas_call(
        kernel,
        grid=(1,) if stream else (),
        out_shape=[jax.ShapeDtypeStruct(dims, dtype) for dims, dtype in outs],
        in_specs=[SCALARS] * scalars + [spec(a.shape) for a in args[scalars:]],
        out_specs=[spec(dims) for dims, _ in outs],
        scratch_shapes=list(scratch),
        compiler_params=pltpu.CompilerParams(
            vmem_limit_bytes=limit * 1024 * 1024
        ),
        cost_estimate=pl.CostEstimate(flops=1, bytes_accessed=1, transcendentals=0),
        name=name,
    )(*args)


class Chain:
    def __init__(self, keep, send, dims, steps, pair_at=None):
        self.keep, self.send, self.dims, self.steps = keep, send, list(dims), list(steps)
        self.pair_at = pair_at

    def start(self):
        self.received = exchange(self.send, self.steps.pop(0))


def add_blocks(keep, received, pair_at):
    total = keep.astype(F32) + received.astype(F32)
    if pair_at is None:
        return total.astype(BF16)
    pair = total[:16, pair_at:] + total[16:32, pair_at:]
    high = pair.astype(BF16)
    tail = jnp.zeros((total.shape[0] - 32, pair.shape[1]), BF16)
    parts = [jnp.concatenate([high, (pair - high.astype(F32)).astype(BF16), tail], 0)]
    if pair_at:
        parts = [total[:, :pair_at].astype(BF16)] + parts
    return jnp.concatenate(parts, 1)


def combine(groups, me, name):
    args, outs = [], []
    for group in groups:
        for chain in group:
            args += [chain.keep, chain.received]
        count, rows, _ = group[0].keep.shape
        width = sum(chain.keep.shape[2] for chain in group)
        outs += [((count // 2, rows, width), BF16)] * 2

    def kernel(me_ref, *refs):
        ins, results = list(refs[: len(args)]), list(refs[len(args) :])
        for group in groups:
            keep_out, send_out = results.pop(0), results.pop(0)
            start = 0
            for chain in group:
                keep, received = ins.pop(0), ins.pop(0)
                width = keep.shape[2]
                axis, bit = chain.steps[0]
                place = len(chain.dims) - 1 - chain.dims.index((axis, bit))
                mine = (me_ref[0] >> bit) & 1 if axis == "win" else 0
                for n in range(keep_out.shape[0]):
                    base = (n >> place << (place + 1)) + (n & ((1 << place) - 1))
                    for out, at in (
                        (keep_out, base + (mine << place)), (send_out, base + ((1 - mine) << place))
                    ):
                        out[n, :, start : start + width] = add_blocks(
                            keep[at], received[at], chain.pair_at
                        )
                start += width

    results = small_call(kernel, name, [me] + args, outs, scalars=1)
    chains = []
    for n, group in enumerate(groups):
        step = group[0].steps[0]
        at, pair_at = 0, None
        for chain in group:
            if chain.pair_at is not None:
                pair_at = at + chain.pair_at
            at += chain.keep.shape[2]
        dims = [d for d in group[0].dims if d != step]
        chains.append(Chain(results[2 * n], results[2 * n + 1], dims, group[0].steps, pair_at))
    return chains


def finish(chain, name):
    _, rows, width = chain.keep.shape

    def kernel(keep, received, own, square):
        total = keep[0].astype(F32) + received[0].astype(F32)
        own[...] = total
        square[...] = jnp.broadcast_to(jnp.sum(total * total), (1, 128))

    return small_call(
        kernel, name, [chain.keep, chain.received], [((rows, width), F32), ((1, 128), F32)]
    )


def finish_pair(chain, squares, devices, share, name):
    _, rows, width = chain.keep.shape
    at = chain.pair_at

    def kernel(keep, received, *refs):
        total = keep[0].astype(F32) + received[0].astype(F32)
        own, message = refs[-2:]
        own[...] = total[:, :at]
        pair = total[:16, at:] + total[16:32, at:]
        square = jnp.sum(total[:, :at] * total[:, :at])
        square = jnp.broadcast_to(square, (1, 128))
        for ref in refs[:-2]:
            square = square + ref[...]
        row = [pair[n : n + 1] for n in range(share // 128)] + [square]
        message[...] = jnp.broadcast_to(jnp.concatenate(row, 1), message.shape)

    return small_call(
        kernel, name, [chain.keep, chain.received] + squares,
        [((rows, at), F32), ((devices, share + 128), F32)],
    )


def adam_step(weight, grad, first, second, rate):
    new_first = 0.5 * first + 0.5 * grad
    new_second = 0.5 * second + 0.5 * grad * grad
    fix = 1.0 - 0.5**STEP
    update = new_first / fix / (jnp.sqrt(new_second / fix) + ADAM_EPS)
    return (new_first, new_second, weight - rate * (update + DECAY_RATE * weight))


def update_kernel(starts, widths, layout, *refs):
    own, message, rest = refs[:3], refs[3], list(refs[4:])
    groups = [rest[3 * n : 3 * n + 3] for n in range(7)]
    loss_ref, norm_ref = rest[21], rest[22]
    outs = [rest[23 + 3 * n : 26 + 3 * n] for n in range(7)]
    vector_rows, table_rows, offsets, square_at, loss_at = layout
    vector_grad = message[:vector_rows, :C]
    table_grad = message[:table_rows, C : C + offsets]
    total = (
        jnp.sum(message[:, square_at : square_at + 1])
        + jnp.sum(vector_grad * vector_grad)
        + jnp.sum(table_grad * table_grad)
    )
    norm = jnp.sqrt(jnp.broadcast_to(total, (1, 1)))
    factor = CLIP_NORM / jnp.maximum(norm, CLIP_NORM)
    norm_ref[...] = norm
    loss_ref[...] = message[0:1, loss_at : loss_at + 1]

    def put(number, layer, grad, rate):
        weight, first, second = groups[number]
        index = (Ellipsis,) if layer is None else (layer, Ellipsis)
        if number == 6:
            index = (slice(None), layer, slice(None))
        results = adam_step(weight[index], factor * grad, first[index], second[index], rate)
        for ref, value in zip(outs[number], results):
            ref[index] = value

    layers = len(starts)
    for l in range(layers):
        qkv_width = outs[0][0].shape[2]
        part, at = starts[l]["attn"]
        put(0, l, own[part][:, at : at + qkv_width], LEARN_RATE)
        put(1, l, own[part][:, at + qkv_width : at + widths["attn"]], LEARN_RATE)
        part, at = starts[l]["up"]
        put(2, l, own[part][:, at : at + widths["up"]], LEARN_RATE)
        part, at = starts[l]["down"]
        put(3, l, own[part][:, at : at + widths["down"]], LEARN_RATE)
        heads = table_rows // layers
        put(6, l, table_grad[l * heads : (l + 1) * heads], SMALL_RATE)
    part, at = starts[-1]["head"]
    put(4, None, own[part][:, at : at + outs[4][0].shape[1]], LEARN_RATE)
    put(5, None, vector_grad, SMALL_RATE)


def collect_rows(layers, head_real, loss_at, ins, out, spread):
    out[...] = jnp.zeros(out.shape, F32)
    row_of_slot = lax.broadcasted_iota(jnp.int32, (SLOT, 128), 0)
    lane = lax.broadcasted_iota(jnp.int32, (SLOT, 128), 1)
    target = row_of_slot // WSIDE * (2 * WSIDE - 1) + row_of_slot % WSIDE
    spreader = ((lane == target) & (row_of_slot < AREA)).astype(F32).astype(BF16)
    row = 0
    for l in range(layers):
        attn_rows, qkv_rows, mlp_rows, up_rows, bias_grad = ins[5 * l : 5 * l + 5]
        parts = [
            attn_rows[0:2], qkv_rows[:, :C], qkv_rows[:, 2 * C :], attn_rows[4:5], mlp_rows[5:8],
        ] + [up_rows[:, n * C : (n + 1) * C] for n in range(HID // C)]
        for part in parts:
            out[row : row + part.shape[0], :C] = part
            row += part.shape[0]
        for head in range(HEADS):
            g, h = divmod(head, PACK)
            left = bias_grad[g, :, h * SLOT : (h + 1) * SLOT]
            total = jnp.zeros((SLOT, 128), F32)
            for _ in range(3):
                low = left.astype(BF16)
                total = total + dot(low, spreader)
                left = left - low.astype(F32)
            spread[head * SLOT : (head + 1) * SLOT, :] = total
        table = jnp.zeros((HEADS, 256), F32)
        span = 2 * WSIDE - 1
        for j in range(AREA):
            wide = jnp.concatenate(
                [spread[pl.ds(j, HEADS, stride=SLOT), :], jnp.zeros((HEADS, 128), F32)], 1
            )
            shift = (WSIDE - 1 - j // WSIDE) * span + WSIDE - 1 - j % WSIDE
            table = table + (pltpu.roll(wide, shift, 1) if shift else wide)
        width = out.shape[1] - C
        out[l * HEADS : (l + 1) * HEADS, C:] = table[:, :width]
    final_rows, head_rows, loss = ins[5 * layers :]
    out[row : row + 2, :C] = final_rows[...]
    row += 2
    cuts = CLASSES // head_real
    width = head_rows.shape[1] // cuts
    classes = jnp.concatenate(
        [head_rows[:, n * width : n * width + head_real] for n in range(cuts)]
        + [jnp.zeros((1, -CLASSES % C), F32)], 1
    )
    for n in range(classes.shape[1] // C):
        out[row + n : row + n + 1, :C] = classes[:, n * C : (n + 1) * C]
    out[0:1, loss_at : loss_at + 1] = loss[:, 0:1]


def pair_rows(rows, ch_count, owners, me_ref, pairs):
    count = rows.shape[1] // 128
    wins = rows.shape[0] // ch_count
    high_rows = pairs.shape[2] // wins
    for flip in range(2):
        for n, owner in enumerate(owners):
            for win in range(wins):
                values = rows[pl.ds(win * ch_count + (me_ref[1] ^ (owner ^ flip)), 1), :]
                values = jnp.concatenate(
                    [values[:, m * 128 : (m + 1) * 128] for m in range(count)]
                    + [jnp.zeros((16 - count, 128), F32)], 0
                )
                high = values.astype(BF16)
                at = win * high_rows
                pairs[flip, n, at : at + 16] = high
                pairs[flip, n, at + 16 : at + 32] = (values - high.astype(F32)).astype(BF16)
                pairs[flip, n, at + 32 : at + high_rows] = jnp.zeros((high_rows - 32, 128), BF16)


def pack_kernel(head_width, qkv, proj, down, up, head, attn0, mlp0, all1):
    attn0[...] = jnp.concatenate([qkv[0], proj[0]], 1).astype(BF16)
    mlp0[...] = jnp.concatenate([down[0], up[0]], 1).astype(BF16)
    parts = [qkv[1], proj[1], down[1], up[1], head[...]]
    pad = head_width - head.shape[1]
    if pad:
        parts.append(jnp.zeros((head.shape[0], pad), F32))
    all1[...] = jnp.concatenate(parts, 1).astype(BF16)


def per_device(
    tokens, valid_rows, valid_cols, partner, mix_level, labels,
    w_qkv, m_qkv, v_qkv, w_proj, m_proj, v_proj, w_fc1, m_fc1, v_fc1, w_fc2, m_fc2, v_fc2,
    w_head, m_head, v_head, vectors, m_vec, v_vec, rel_table, m_rel, v_rel,
):
    micro, images, cells, chans = tokens.shape
    layers = rel_table.shape[0]
    per_layer = 8 + HID // C
    base = layers * per_layer
    head_rows = vectors.shape[0] - base - 2
    all_images = labels.shape[1]
    total_images = micro * all_images
    local = micro * images
    groups = local // GROUP
    sizes = {axis: lax.axis_size(axis) for axis in ("win", "ch")}
    win_count, ch_count = sizes["win"], sizes["ch"]
    device_count = win_count * ch_count
    win_index, ch_index = lax.axis_index("win"), lax.axis_index("ch")
    me = jnp.stack([win_index, ch_index]).astype(jnp.int32)
    block_rows = C // win_count
    widths = {"attn": 4 * C // ch_count, "down": HID // ch_count, "up": HID // ch_count}
    head_real = CLASSES // ch_count
    widths["head"] = -(-head_real // 128) * 128
    head_classes = widths["head"] * ch_count
    direct = block_rows % 16 == 0 and block_rows >= 32 and all(w % 128 == 0 for w in widths.values())

    core = ("ch", 0)
    ch_high = [("ch", b) for b in range(1, ch_count.bit_length() - 1)]
    win_low = [("win", 0)]
    win_high = [("win", b) for b in range(1, win_count.bit_length() - 1)]

    def low(v):
        return v.astype(BF16)

    packed = small_call(
        functools.partial(pack_kernel, widths["head"]), "pack",
        [w_qkv, w_proj, w_fc2.transpose(0, 2, 1), w_fc1, w_head],
        [((block_rows, sum(widths[n] for n in names)), BF16) for names in (
            ("attn",), ("down", "up"), ("attn", "down", "up", "head"))],
        stream=True,
        limit=56,
    )
    names = [["attn", "down", "up"], ["attn", "down", "up", "head"]]
    onehot = jnp.asarray(relative_onehot(), BF16)
    offsets = rel_table.shape[1]
    table_width = -(-(offsets + 1) // 128) * 128
    share = C + table_width
    tables = [window_tables(l % 2 == 1) for l in range(layers)]
    perms = [jnp.asarray(t[0], BF16) for t in tables]
    perms_t = [jnp.asarray(t[0].T, BF16) for t in tables]
    row_limits = [jnp.asarray(t[1]) for t in tables]
    col_limits = [jnp.asarray(t[2]) for t in tables]

    def bias_of(table):
        table = table.transpose(0, 2, 1).reshape(layers * HEADS, offsets)
        table_parts = []
        for _ in range(3):
            table_parts.append(low(table))
            table = table - table_parts[-1].astype(F32)
        bias = dot(jnp.concatenate(table_parts, 0), onehot).reshape(3, layers, HEADS, SLOT * SLOT)
        bias = (bias[0] + bias[1]) + bias[2]
        return (
            bias.reshape(layers, NGRP, PACK, SLOT, SLOT)
            .transpose(0, 1, 3, 2, 4)
            .reshape(layers, NGRP, SLOT, LANES)
        )

    padded = jnp.pad(tokens.reshape(local, cells, chans), ((0, 0), (0, ROWS - cells), (0, 0)))

    def stage(number, *moves, cuts=None, more=()):
        received = [exchange(part.array, step) for part, step in moves]
        tied = tie(*received, *more)
        received, more = tied[: len(moves)], tied[len(moves) :]
        stacked = stack_blocks(
            [(part, got, step) for (part, step), got in zip(moves, received)],
            me, f"stack{number}", cuts,
        )
        return (stacked, *more)

    def wait_for(value, *parts):
        value, *arrays = tie(value, *[part.array for part in parts])
        for part, array in zip(parts, arrays):
            part.array = array
        return value

    far = [Held(block[None]) for block in packed]
    edges = [
        [0, widths["attn"] * 2 // 3, widths["attn"], widths["attn"] + widths["down"],
         widths["attn"] + widths["down"] + widths["up"]],
        [0, widths["attn"], widths["attn"] + widths["down"] + widths["up"] * 2 // 3,
         sum(widths[name] for name in ("attn", "down", "up", "head"))],
    ]
    staged = win_count == 8 and ch_count == 4
    if staged:
        zh, zl, y, x = ("win", 2), ("win", 1), ("win", 0), ("ch", 1)
        ((attn,),), mlp, padded = stage(0, (far[0], zh), more=(far[1].array, padded))
        (attn, (mlp,)), all1, bias = stage(
            1, (attn, zl), (Held(mlp), zh), cuts=[edges[0][1:2], None],
            more=(packed[2], bias_of(rel_table)),
        )
        floating = exchange(all1[None], zh)
        ((one,), (two,), mlp), = stage(
            2, (attn[0], y), (attn[1], x), (mlp, zl), cuts=[None, None, [widths["down"]]]
        )
        (((all1,),),) = [stack_blocks([(Held(all1[None]), floating, zh)], me, "stack10")]
        mlp[0].array, mlp[1].array, all1.array = tie(mlp[0].array, mlp[1].array, all1.array)
        near = [(one, x), (two, y), (mlp[0], x), (mlp[1], y)]
        received = [exchange(part.array, step) for part, step in near]
        floating = exchange(all1.array, zl)
        *received, floating = tie(*received, floating)
        ((one,), (two,), (down,), (up,)) = stack_blocks(
            [(part, got, step) for (part, step), got in zip(near, received)], me, "stack3"
        )
        held = [[one, two]]
        *got, floating = tie(*[exchange(part.array, core) for part in held[0]], floating)
        other = [got]
        (parts1,) = stack_blocks([(all1, floating, zl)], me, "stack11", [edges[1][1:-1]])
        padded = wait_for(padded, *parts1)
    else:
        bias = bias_of(rel_table)
        bits = win_high[::-1] + win_low + ch_high[::-1]
        held, other = [[], []], []
        for number, part in enumerate(far):
            for n, step in enumerate(bits):
                ((part,),), = stage(10 * number + n, (part, step))
            layer = number // 2
            base = 0 if number != 1 else widths["attn"]
            for start, end in zip(edges[layer], edges[layer][1:]):
                if start >= base and end - base <= part.array.shape[-1]:
                    held[layer].append(Held(part.array[..., start - base : end - base], part.dims))
        other.append([exchange(part.array, core) for part in held[0]])

    def weight_inputs(layer, wanted):
        plan = Plan(widths, layer, layers)
        ins = {}
        starts, at = {}, 0
        for name in names[layer]:
            starts[name] = at
            at += widths[name]
        bounds = list(zip(edges[layer], edges[layer][1:]))
        blocks = []
        for group, part in enumerate(held[layer]):
            if group >= len(other[layer]):
                break
            owners = relative_owners([d for d in part.dims if d[0] == "ch"])
            for number, array in enumerate((part.array, other[layer][group])):
                flat_array = array.reshape(-1, C, array.shape[-1])
                blocks.append((group, [owner ^ number for owner in owners], flat_array))
        for name in wanted:
            plan.sources[name] = []
            columns = []
            for number, (group, owners, array) in enumerate(blocks):
                begin = max(starts[name], bounds[group][0])
                end = min(starts[name] + widths[name], bounds[group][1])
                if begin >= end:
                    continue
                cut = (begin - bounds[group][0], end - begin, begin - starts[name])
                if direct:
                    ref = f"blocks{number}"
                    ins[ref] = (FAR, array)
                    plan.sources[name].append((ref, owners, cut))
                elif number % 2 == 0:
                    table = np.argsort(np.asarray(owners + blocks[number + 1][1]))
                    both = jnp.concatenate([array, blocks[number + 1][2]])
                    index = jnp.asarray(table)[jnp.arange(ch_count) ^ ch_index]
                    columns.append(jnp.take(both, index, axis=0)[..., cut[0] : cut[0] + cut[1]])
            if not direct:
                full = jnp.concatenate(columns, -1)
                if name in ("up", "down"):
                    full = full.transpose(1, 0, 2).reshape(C, -1)
                ins[f"staged_{name}"] = (FAR, full)
                plan.sources[name] = [(f"staged_{name}", None, None)]
        ins["me"] = (SCALARS, me)
        return ins, plan

    orders = {
        "x": ch_high + win_low + win_high, "a": ch_high + win_low + win_high,
        "y": win_low + ch_high + win_high, "b": win_low + ch_high + win_high,
    }
    block_dims = ch_high + [("win", b) for b in reversed(range(win_count.bit_length() - 1))]
    owners = relative_owners(ch_high)
    regular = direct and len(ch_high) == 1

    def grad_outputs(plan, **members):
        outs = {}
        for group, wanted in members.items():
            if not direct:
                for name in wanted:
                    plan.targets[name] = [(f"full_{name}", None, 0, 0, widths[name])]
                    dims = (C, HID) if name in ("up", "down") else (ch_count, C, widths[name])
                    outs[f"full_{name}"] = (FAR, dims, BF16)
                continue
            starts = np.cumsum([0] + [widths[name] for name in wanted])
            refs = [
                (f"keep_{group}", owners), (f"send_{group}", [owner ^ 1 for owner in owners])
            ]
            for ref, _ in refs:
                outs[ref] = (FAR, (len(owners), C, int(starts[-1])), BF16)
            for name, start in zip(wanted, starts):
                plan.targets[name] = [(ref, at, int(start), 0, widths[name]) for ref, at in refs]
        return outs

    def cut_attention_outputs(plan):
        cut = widths["attn"] * 2 // 3
        outs, plan.targets["attn"] = {}, []
        for group, start, size, extra in (("a", 0, cut, 0), ("b", cut, widths["attn"] - cut, 128)):
            for kind, flip in (("keep", 0), ("send", 1)):
                ref = f"{kind}_{group}"
                outs[ref] = (NEAR, (len(owners), C, size + extra), BF16)
                plan.targets["attn"].append(
                    (ref, [owner ^ flip for owner in owners], 0, start, size)
                )
        return outs

    def chain_of(results, group, *members, pair_at=None):
        if direct:
            keep, send = results[f"keep_{group}"], results[f"send_{group}"]
        else:
            full = []
            for name in members:
                part = results[f"full_{name}"]
                if name in ("up", "down"):
                    part = part.reshape(C, ch_count, -1).transpose(1, 0, 2)
                full.append(part)
            full = jnp.concatenate(full, -1)
            keep, send = [
                jnp.take(full, np.asarray(owners) ^ flip ^ ch_index, axis=0) for flip in (0, 1)
            ]
        dims = (-1, block_rows, keep.shape[-1])
        return Chain(
            keep.reshape(dims), send.reshape(dims), block_dims, [core] + orders[group], pair_at
        )

    def start(*chains):
        for chain in chains:
            chain.start()

    def meet(value, *chains):
        value, *got = tie(value, *[chain.received for chain in chains])
        for chain, array in zip(chains, got):
            chain.received = array
        return value

    def after(value, *chains):
        held_back = [array for chain in chains for array in (chain.keep, chain.send)]
        value, *held_back = tie(value, *held_back)
        for n, chain in enumerate(chains):
            chain.keep, chain.send = held_back[2 * n], held_back[2 * n + 1]
        return value

    def attention_consts(l, forward):
        ins = {
            "perm": (whole((WROWS, ROWS)), perms[l]),
            "perm_t": (whole((ROWS, WROWS)), perms_t[l]),
            "vec": (whole(vectors.shape), vectors),
        }
        if forward:
            ins["rows"] = (SCALARS, valid_rows)
            ins["cols"] = (SCALARS, valid_cols)
            ins["row_limit"] = (whole((NWIN, SLOT, 128)), row_limits[l])
            ins["col_limit"] = (whole((NWIN, SLOT, 128)), col_limits[l])
            ins["bias"] = (
                pl.BlockSpec((None, NGRP, SLOT, LANES), lambda i, l=l: (l, 0, 0, 0)), bias
            )
        return ins

    def vmem(*dims, dtype=BF16):
        return pltpu.VMEM(dims, dtype)

    attn_weights = {
        "stage": vmem(ch_count, C, widths["attn"]),
        "w_qkv": vmem(C, 3 * C),
        "w_proj": vmem(C, C),
        "load_sem": pltpu.SemaphoreType.DMA((4,)),
    }
    mlp_weights = {
        "w_down": vmem(C, HID),
        "w_up": vmem(C, HID),
        "load_sem": pltpu.SemaphoreType.DMA((4,)),
    }
    all_rows = local * ROWS
    mlp_rows = {
        "mlp_all": vmem(all_rows, C), "active_all": vmem(all_rows, HID),
        "pre_all": vmem(all_rows, HID), "low_all": vmem(all_rows, C),
        "up_grad": vmem(C, HID), "down_grad": vmem(C, HID),
        "sem_x": pltpu.SemaphoreType.DMA((2,)), "sem_y": pltpu.SemaphoreType.DMA((2,)),
    }
    wide = (per_image(ROWS, C), (local, ROWS, C), F32)
    thin = (per_image(ROWS, C), (local, ROWS, C), BF16)
    hidden = (per_image(ROWS, HID), (local, ROWS, HID), BF16)
    attn_saved = {
        "normed": thin,
        "qkv": (per_image(WROWS, 3 * C), (local, WROWS, 3 * C), BF16),
        "prob": (per_image(NWIN, NGRP, SLOT, LANES), (local, NWIN, NGRP, SLOT, LANES), BF16),
        "attended": thin,
    }
    sums = {"row_sums": (whole((8, C)), (8, C), F32)}
    up_sums = {**sums, "up_rows": (whole((1, HID)), (1, HID), F32)}
    attn_sums = {
        **sums,
        "qkv_rows": (whole((1, 3 * C)), (1, 3 * C), F32),
        "bias_grad": (whole((NGRP, SLOT, LANES)), (NGRP, SLOT, LANES), F32),
    }

    def given(spec, array):
        return (spec[0], array)

    mlp_flops = 2 * all_rows * C * HID * 2
    attn_flops = 2 * all_rows * C * C * 8

    def attention_forward(l, field, first=0, count=groups, before=None):
        ins, plan = weight_inputs(l, ["attn"]) if before is None else ({}, Plan(widths, l, layers))
        plan.group = first
        ins["field"] = (per_image(*field.shape[1:], first=first), field)
        ins.update(attention_consts(l, True))
        outs = {
            name: (spec, (count * GROUP,) + dims[1:], dtype)
            for name, (spec, dims, dtype) in {"middle": wide, **attn_saved}.items()
        }
        scratch = {"mixed": vmem(GROUP, C, WROWS), "windowed": vmem(GROUP, WROWS, C)}
        if before is None:
            outs["qkv_out"] = (FAR, (C, 3 * C), BF16)
            outs["proj_out"] = (FAR, (C, C), BF16)
            scratch.update(attn_weights)
            scratch["out_sem"] = pltpu.SemaphoreType.DMA((2,))
        else:
            ins["w_qkv"] = (whole((C, 3 * C)), before["qkv_out"])
            ins["w_proj"] = (whole((C, C)), before["proj_out"])
        results = call(
            functools.partial(attention_forward_kernel, plan=plan), f"attention_forward{l}_{first}",
            count, ins, outs, scratch, attn_flops * count // groups,
        )
        return results if before is None else {**before, **results}

    def rows_of(name, arrays):
        if len(arrays) == 1:
            return {name: given(wide, arrays[0])}
        return {f"{name}{n}": (whole(array.shape), array) for n, array in enumerate(arrays)}

    def begin(*moves):
        return [(part, step, exchange(part.array, step)) for part, step in moves]

    def arrive(number, value, moves):
        value, *received = tie(value, *[got for _, _, got in moves])
        stacked = stack_blocks(
            [(part, got, step) for (part, step, _), got in zip(moves, received)], me, f"stack{number}"
        )
        return value, [parts[0] for parts in stacked]

    if staged:
        moves = begin((down, y), (up, x), (parts1[0], y), (parts1[1], x), (parts1[2], y))
        early0 = attention_forward(0, padded, 0, groups - 1)
        early0["proj_out"], (down, up, *parts1) = arrive(4, early0["proj_out"], moves)
        early0["proj_out"] = wait_for(early0["proj_out"], down, up, *parts1)
        held[0] += [down, up]
        got = [exchange(part.array, core) for part in (down, up)]
        moves = begin((parts1[0], x), (parts1[1], y), (parts1[2], x))
        saved0 = attention_forward(0, padded, groups - 1, 1, early0)
        saved0["middle"], *got = tie(saved0["middle"], *got)
        other[0] = list(other[0]) + got
        saved0["middle"], parts1 = arrive(5, saved0["middle"], moves[:1])
        middle0 = [early0["middle"], wait_for(saved0["middle"], *parts1)]
        held.append(parts1)
    else:
        saved0 = early0 = attention_forward(0, padded)
        middle0 = [saved0["middle"]]
    ins, plan = weight_inputs(0, ["down", "up"])
    ins.update(rows_of("middle", middle0))
    ins["vec"] = (whole(vectors.shape), vectors)
    mlp0 = call(
        functools.partial(first_mlp_kernel, plan=plan), "first_mlp", groups, ins,
        {
            "result": wide, "mlp_in": thin, "active": hidden, "slope": hidden,
            "down_out": (FAR, (C, HID), BF16),
            "up_out": (FAR, (C, HID), BF16),
        },
        {**mlp_weights, "out_sem": pltpu.SemaphoreType.DMA((2,))},
        mlp_flops,
    )
    result0 = mlp0["result"]
    got = [exchange(part.array, core) for part in held[1]]
    result0, *got = tie(result0, *got)
    other.append(got)
    if staged:
        result0, late1 = arrive(6, result0, moves[1:])
        result0 = wait_for(result0, *late1)
        late_got = [exchange(part.array, core) for part in late1]

    saved1 = attention_forward(1, result0)
    if staged:
        saved1["middle"], *late_got = tie(saved1["middle"], *late_got)
        held[1] = held[1] + late1
        other[1] = other[1] + late_got
    ins, plan = weight_inputs(1, ["down", "up", "head"])
    ins["middle"] = given(wide, saved1["middle"])
    ins["vec"] = (whole(vectors.shape), vectors)
    ins["rows"] = (SCALARS, valid_rows)
    ins["cols"] = (SCALARS, valid_cols)
    ins["labels"] = (SCALARS, labels)
    ins["partner"] = (SCALARS, partner)
    ins["mix"] = (SCALARS, mix_level)
    cell = np.arange(ROWS)
    for name, place in (("cell_row", cell // GRID), ("cell_col", cell % GRID)):
        place = np.where(cell < CELLS, place, 99)[:, None].astype(np.int32)
        ins[name] = (whole((ROWS, 1)), jnp.asarray(place))
    outs = {
        "grad_mid": wide, **up_sums,
        "final_rows": (whole((2, C)), (2, C), F32),
        "head_rows": (whole((1, head_classes)), (1, head_classes), F32),
        "loss": (whole((1, 128)), (1, 128), F32),
        **grad_outputs(plan, x=["up", "head"], y=["down"]),
    }
    last = call(
        functools.partial(last_mlp_kernel, plan=plan, total_images=float(total_images)),
        "last_mlp", groups, ins, outs,
        {
            "slope": vmem(GROUP * ROWS, HID), "w_head": vmem(ch_count, C, widths["head"]),
            **mlp_weights, **mlp_rows,
            "pooled_all": vmem(16, C, dtype=F32), "logit_all": vmem(16, head_classes, dtype=F32),
            "head_grad": vmem(ch_count, C, widths["head"]),
        },
        3 * mlp_flops,
    )

    def attention_backward(l, grad_mid, field, saved, first, count, before=None, before_saved=None, store=True, collect=None):
        plan = Plan(widths, l, layers)
        ins = {
            "me": (SCALARS, me), "w_qkv": (whole((C, 3 * C)), saved["qkv_out"]),
            "w_proj": (whole((C, C)), saved["proj_out"]),
        }
        ins.update(attention_consts(l, False))
        wanted = ["qkv", "prob"] + (["normed", "attended"] if store else [])
        for name, array in [("grad_mid", grad_mid), ("field", field)] + [
            (name, saved[name]) for name in wanted
        ]:
            skip = first if array.shape[0] == local else 0
            ins[name] = (per_image(*array.shape[1:], first=skip), array)
        if before is not None:
            for name, (spec, _, _) in attn_sums.items():
                ins[name + "_in"] = (spec, before[name])
            for name in ("normed", "attended"):
                ins[name + "_in"] = (whole((first * GROUP, ROWS, C)), before_saved[name])
            for name in ("spread", "attn"):
                array = before[name + "_all"]
                ins[name + "_in"] = (whole(array.shape), array)
        rows_here = count * GROUP * ROWS
        outs = dict(attn_sums)
        scratch = {
            "dq": vmem(GROUP, C, WROWS), "dkv": vmem(GROUP, WROWS, 2 * C),
            "joined": vmem(GROUP, WROWS, C),
        }
        need_grad = l > 0
        if need_grad:
            outs["grad"] = wide
        if store:
            if collect is None:
                outs.update(grad_outputs(plan, a=["attn"]))
            else:
                outs.update(cut_attention_outputs(plan))
                plan.collect = (layers, head_real, share - 1, owners)
                ins.update({name: (whole(array.shape), array) for name, array in collect.items()})
                scratch["small_rows"] = vmem(device_count, share, dtype=F32)
                scratch["spread_table"] = vmem(HEADS * SLOT, 128, dtype=F32)
                scratch["pairs"] = vmem(2, len(owners), C, 128)
            scratch.update({
                "normed_all": vmem(all_rows, C), "attended_all": vmem(all_rows, C),
                "spread_all": vmem(all_rows, 3 * C), "attn_all": vmem(all_rows, C),
                "attn_grad": vmem(ch_count, C, widths["attn"]),
                "sem_a": pltpu.SemaphoreType.DMA((4,)),
            })
        else:
            outs["spread_all"] = (whole((rows_here, 3 * C)), (rows_here, 3 * C), BF16)
            outs["attn_all"] = (whole((rows_here, C)), (rows_here, C), BF16)
        return call(
            functools.partial(
                backward_attention_kernel, plan=plan,
                earlier=0 if before is None else first * GROUP, need_grad=need_grad,
            ),
            f"attention_backward{l}_{first}", count, ins, outs, scratch,
            2 * attn_flops * count // groups,
        )

    x1, y1 = chain_of(last, "x", "up", "head"), chain_of(last, "y", "down")
    if regular:
        start(x1, y1)
    back1 = attention_backward(1, last["grad_mid"], mlp0["result"], saved1, 0, groups)
    a1 = chain_of(back1, "a", "attn")
    grad = back1["grad"]
    if regular:
        grad = meet(grad, x1, y1)
        x1, y1 = combine([[x1], [y1]], me, "sum1")
        grad = after(grad, x1, y1)
        start(x1, y1, a1)

    plan = Plan(widths, 0, layers)
    ins = {
        "me": (SCALARS, me),
        "w_down": (whole((C, HID)), mlp0["down_out"]),
        "w_up": (whole((C, HID)), mlp0["up_out"]),
    }
    ins["grad"] = given(wide, grad)
    ins.update(rows_of("middle", middle0))
    ins["mlp_in"] = given(thin, mlp0["mlp_in"])
    ins["active"] = given(hidden, mlp0["active"])
    ins["slope"] = given(hidden, mlp0["slope"])
    ins["vec"] = (whole(vectors.shape), vectors)
    first = call(
        functools.partial(backward_mlp_kernel, plan=plan), "mlp_backward0", groups, ins,
        {"grad_mid": wide, **up_sums, **grad_outputs(plan, x=["up"], y=["down"])},
        dict(mlp_rows), 2 * mlp_flops,
    )
    x0, y0 = chain_of(first, "x", "up"), chain_of(first, "y", "down")
    grad_mid = first["grad_mid"]
    if regular:
        grad_mid = meet(grad_mid, x1, y1, a1)
        x1, y1, a1 = combine([[x1], [y1], [a1]], me, "sum2")
        grad_mid = after(grad_mid, x1, y1, a1)
        start(x1, y1, a1, x0, y0)
    before0 = attention_backward(0, grad_mid, padded, early0, 0, groups - 1, store=False)
    if regular:
        before0["row_sums"] = meet(before0["row_sums"], a1, x0, y0, x1, y1)
        a1, x0, y0, z1 = combine([[a1], [x0], [y0], [x1, y1]], me, "sum3")
        grad_mid = after(grad_mid, a1, x0, y0, z1)
        start(a1, x0, y0, z1)
    small_parts = None
    if regular:
        small_parts = {
            "mlp_rows0": first["row_sums"], "up_rows0": first["up_rows"],
            "row_sums1": back1["row_sums"], "qkv_rows1": back1["qkv_rows"],
            "mlp_rows1": last["row_sums"], "up_rows1": last["up_rows"],
            "bias_grad1": back1["bias_grad"], "final_rows": last["final_rows"],
            "head_rows": last["head_rows"], "loss": last["loss"],
        }
    back0 = attention_backward(
        0, grad_mid, padded, saved0, groups - 1, 1, before0, early0, collect=small_parts
    )
    a0 = chain_of(back0, "a", "attn")
    if regular:
        b0 = chain_of(back0, "b", pair_at=widths["attn"] - widths["attn"] * 2 // 3)
        waiting = (a1, x0, y0, z1)
        a0.send, b0.send, *got = tie(a0.send, b0.send, *[chain.received for chain in waiting])
        for chain, array in zip(waiting, got):
            chain.received = array

    if regular:
        start(a0, b0)
        z1, x0, y0 = combine([[z1], [x0], [y0]], me, "sum5")
        start(z1, x0, y0)
        a0.received, b0.received, x0.keep = tie(a0.received, b0.received, x0.keep)
        a0, b0 = combine([[a0], [b0]], me, "sum6")
        start(a0, b0)
        x0.received, y0.received, z1.received = tie(x0.received, y0.received, z1.received)
        (z0,) = combine([[x0, y0, a1]], me, "sum7")
        start(z0)
        a0, b0 = combine([[a0], [b0]], me, "sum8")
        start(a0, b0)
        (z0,) = combine([[z0]], me, "sum9")
        start(z0)
        own1, square1 = finish(z1, "own1")
        (a0,) = combine([[a0, b0]], me, "sum10")
        start(a0)
        own0, square0 = finish(z0, "own0")
        (a0,) = combine([[a0]], me, "sum11")
        start(a0)
        own_attn, message = finish_pair(a0, [square0, square1], device_count, share, "own_attn")
    else:
        square, own_parts = jnp.zeros((1, 128), F32), []
        for chain in (a0, x0, y0, a1, x1, y1):
            start(chain)
            while chain.steps:
                (chain,) = combine([[chain]], me, "sum")
                start(chain)
            part, part_square = finish(chain, "own")
            square = square + part_square
            own_parts.append(part)
        own_attn = own_parts[0]
        own0, own1 = jnp.concatenate(own_parts[1:4], 1), jnp.concatenate(own_parts[4:], 1)
        (rows_all,) = small_call(
            lambda *refs: collect_rows(
                layers, head_real, share - 1, refs[:-2], refs[-2], refs[-1]
            ),
            "collect",
            [part[name] for part in ((first, back0), (last, back1))
             for part, name in (
                 (part[1], "row_sums"), (part[1], "qkv_rows"), (part[0], "row_sums"),
                 (part[0], "up_rows"), (part[1], "bias_grad"))]
            + [last["final_rows"], last["head_rows"], last["loss"]],
            [((device_count, share), F32)],
            stream=True,
            scratch=[pltpu.VMEM((HEADS * SLOT, 128), F32)],
        )
        rows_all = lax.all_to_all(rows_all, ("win", "ch"), 0, 0, tiled=True)
        message = jnp.concatenate([jnp.sum(rows_all, 0, keepdims=True), square], 1)
        message = jnp.broadcast_to(message, (device_count, share + 128))
    message = lax.all_to_all(message, ("win", "ch"), 0, 0, tiled=True)
    starts = [
        {"attn": (1, 0), "up": (2, 0), "down": (2, widths["up"])},
        {
            "attn": (2, widths["up"] + widths["down"]), "up": (0, 0), "head": (0, widths["up"]),
            "down": (0, widths["up"] + widths["head"]),
        },
    ]
    arrays = [
        [w_qkv, m_qkv, v_qkv], [w_proj, m_proj, v_proj], [w_fc1, m_fc1, v_fc1],
        [w_fc2, m_fc2, v_fc2], [w_head, m_head, v_head], [vectors, m_vec, v_vec],
        [rel_table, m_rel, v_rel],
    ]
    turns = {3: (0, 2, 1), 6: (2, 0, 1)}
    turned = [
        a.transpose(turns[n]) if n in turns else a for n, group in enumerate(arrays) for a in group
    ]
    results = small_call(
        functools.partial(
            update_kernel, starts, widths,
            (vectors.shape[0], layers * HEADS, offsets, share, share - 1),
        ),
        "update",
        [own1, own_attn, own0, message] + turned,
        [((1, 1), F32)] * 2 + [(a.shape, F32) for a in turned],
        stream=True,
    )
    loss_total, grad_norm, *results = results
    outs = [loss_total[0, 0], grad_norm[0, 0]]
    for n in range(0, len(results), 3):
        back = {3: (0, 2, 1), 6: (1, 2, 0)}.get(n // 3)
        outs += [r if back is None else r.transpose(back) for r in results[n : n + 3]]
    return tuple(outs)


def solution(mesh):
    cut = P(None, "win", "ch")
    down = P(None, "ch", "win")
    head = P("win", "ch")
    rows = P(None, ("win", "ch"))
    in_specs = (
        (P(None, ("win", "ch"), None, None),) + (rows,) * 4 + (P(),)
        + (cut,) * 9 + (down,) * 3 + (head,) * 3 + (P(),) * 6
    )
    out_specs = (P(),) * 2 + (cut,) * 9 + (down,) * 3 + (head,) * 3 + (P(),) * 6
    return jax.shard_map(
        per_device, mesh=mesh, in_specs=in_specs, out_specs=out_specs, check_vma=False
    )
```

```python
import functools

import jax
import jax.numpy as jnp
import numpy as np
from jax import lax
from jax.experimental import pallas as pl
from jax.experimental.pallas import tpu as pltpu
from jax.sharding import PartitionSpec as P

C = 384
HID = 1536
CLASSES = 1000
CLASS_PAD = 1024
WSIDE = 7
GRID = 14
STEP = 10
HEADS = 12
PER_LAYER = 8 + HID // C
DEPTH = 32
CELLS = GRID * GRID
ROWS = 208
AREA = WSIDE * WSIDE
SLOT = 64
NWIN = 4
NGRP = 3
PACK = 4
WROWS = NWIN * SLOT
LANES = PACK * SLOT

NORM_EPS = 1e-05
CLIP_NORM = 0.05
LEARN_RATE = 0.04
SMALL_RATE = 0.2
DECAY_RATE = 0.05
ADAM_EPS = 1e-08
MASKED = -1e30
SCALE = DEPTH ** (-0.5)
F32 = jnp.float32
BF16 = jnp.bfloat16
NN = (((1,), (0,)), ((), ()))
NT = (((1,), (1,)), ((), ()))
TN = (((0,), (0,)), ((), ()))
VMEM_LIMIT = 24 * 1024 * 1024
GROUP = 2
CHUNK = 512


def dot(a, b, dims=NN):
    return lax.dot_general(a, b, dims, preferred_element_type=F32)


@functools.lru_cache(None)
def window_tables(shifted):
    perm = np.zeros((WROWS, ROWS), np.float32)
    row_limit = np.full((NWIN, SLOT, 2 * SLOT), 99, np.int32)
    col_limit = np.full((NWIN, SLOT, 2 * SLOT), 99, np.int32)
    shift = WSIDE // 2 if shifted else 0

    def band(v):
        return 0 if v < GRID - WSIDE else (1 if v < GRID - WSIDE // 2 else 2)

    for window in range(NWIN):
        wr, wc = divmod(window, GRID // WSIDE)
        place = []
        for j in range(AREA):
            r, c = wr * WSIDE + j // WSIDE, wc * WSIDE + j % WSIDE
            region = 3 * band(r) + band(c) if shifted else 0
            source = ((r + shift) % GRID, (c + shift) % GRID)
            place.append((region, source))
            perm[window * SLOT + j, source[0] * GRID + source[1]] = 1
        for j in range(SLOT):
            for i in range(SLOT):
                if i == j:
                    pair = (-1, -1)
                elif i < AREA and j < AREA and place[i][0] == place[j][0]:
                    pair = place[j][1]
                else:
                    pair = (99, 99)
                row_limit[window, j, i::SLOT] = pair[0]
                col_limit[window, j, i::SLOT] = pair[1]
    return perm, row_limit, col_limit


@functools.lru_cache(None)
def relative_onehot():
    span = 2 * WSIDE - 1
    onehot = np.zeros((span * span, SLOT, SLOT), np.float32)
    for i in range(AREA):
        for j in range(AREA):
            row, col = i // WSIDE - j // WSIDE, i % WSIDE - j % WSIDE
            onehot[(row + WSIDE - 1) * span + col + WSIDE - 1, j, i] = 1
    return onehot.reshape(span * span, SLOT * SLOT)


def norm_parts(field):
    average = jnp.mean(field, -1, keepdims=True)
    centered = field - average
    spread = jnp.mean(centered * centered, -1, keepdims=True)
    rate = lax.rsqrt(spread + NORM_EPS)
    return centered * rate, rate


def norm_back(grad, hat, rate, gain):
    scaled = grad * gain
    return rate * (
        scaled
        - jnp.mean(scaled, -1, keepdims=True)
        - hat * jnp.mean(scaled * hat, -1, keepdims=True)
    )


def col_sum(field):
    return jnp.sum(field, 0, keepdims=True)


def head_masks(dtype):
    lane = lax.broadcasted_iota(jnp.int32, (SLOT, 128), 1)
    return [((lane // DEPTH) == h).astype(F32).astype(dtype) for h in range(PACK)]


def spread_heads(block, masks):
    return jnp.concatenate([block * m for m in masks], 0)


def relative_owners(bits):
    owners = []
    for index in range(1 << len(bits)):
        offset = 0
        for n, (_, bit) in enumerate(bits):
            offset |= ((index >> (len(bits) - 1 - n)) & 1) << bit
        owners.append(offset)
    return owners


def owner_part(ref, owner, width, start, size):
    if len(ref.shape) == 3:
        return ref.at[owner, :, start : start + size]
    return ref.at[:, pl.ds(pl.multiple_of(owner * width + start, 128), size)]


def load_blocks(pieces, target, width, sem, me_ref):
    for ref, owners, cut in pieces:
        if owners is None:
            pltpu.make_async_copy(ref, target, sem).start()
            continue
        source, size, start = cut
        for n, owner in enumerate(owners):
            pltpu.make_async_copy(
                ref.at[n, :, source : source + size],
                owner_part(target, me_ref[1] ^ owner, width, start, size),
                sem,
            ).start()


def wait_all(ref, sem):
    pltpu.make_async_copy(ref, ref, sem).wait()


def store_blocks(source, outs, width, sems, me_ref):
    for number, (ref, owners, start, source_start, size) in enumerate(outs):
        if owners is None:
            copy = pltpu.make_async_copy(source, ref, sems.at[number])
            copy.start()
            copy.wait()
            continue
        for n, owner in enumerate(owners):
            pltpu.make_async_copy(
                owner_part(source, me_ref[1] ^ owner, width, source_start, size),
                ref.at[n, :, start : start + size],
                sems.at[number],
            ).start()


def wait_blocks(outs, sems):
    for number, (ref, owners, *_) in enumerate(outs):
        if owners is not None:
            wait_all(ref, sems.at[number])


def join_attention(stage, w_qkv, w_proj):
    owners = stage.shape[0]
    wide, narrow = 3 * C // owners, C // owners
    w_qkv[...] = jnp.concatenate([stage[n, :, :wide] for n in range(owners)], 1)
    w_proj[...] = jnp.concatenate([stage[n, :, wide : wide + narrow] for n in range(owners)], 1)


def pick_heads(first, second):
    lane = lax.broadcasted_iota(jnp.int32, (DEPTH, 128), 1)
    parts = []
    for h in range(PACK):
        at = (slice(h * DEPTH, (h + 1) * DEPTH), slice(h // 2 * 128, (h // 2 + 1) * 128))
        one, two = first[at], second[at]
        if h % 2:
            one = pltpu.roll(one, SLOT, 1)
        else:
            two = pltpu.roll(two, SLOT, 1)
        parts.append(jnp.where(lane < SLOT, one, two))
    return jnp.concatenate(parts, 0)


def apply_pair(rows_ref, cut, eye, first, second):
    turned = dot(eye, rows_ref[cut], NT).astype(BF16)
    empty = jnp.zeros_like(first)
    full = dot(
        turned,
        jnp.concatenate(
            [jnp.concatenate([first, empty], 1), jnp.concatenate([empty, second], 1)], 0
        ),
    )
    return pick_heads(full[:, :LANES], full[:, LANES:])


def identity():
    shape = (128, 128)
    same = lax.broadcasted_iota(jnp.int32, shape, 0) == lax.broadcasted_iota(jnp.int32, shape, 1)
    return same.astype(F32).astype(BF16)


def pipelined(units, first, second, third):
    ones, twos = {}, {}
    count = len(units)
    for n in range(count + 2):
        if n < count:
            ones[n] = first(*units[n])
        if 1 <= n <= count:
            twos[n - 1] = second(*units[n - 1], ones.pop(n - 1))
        if n >= 2:
            third(*units[n - 2], twos.pop(n - 2))


def each_image(images, body, unrolled):
    lax.fori_loop(0, images, body, 0, unroll=images if unrolled else 1)


def forward_attention(
    field, sizes, w_qkv, w_proj, perm, perm_t, row_limit, col_limit, bias, small, qkv_bias,
    qkv_ref, prob_ref, windowed_ref, mixed_ref, attended_ref, unrolled,
):
    hat, _ = norm_parts(field)
    normed = (hat * small[0:1] + small[1:2]).astype(BF16)
    images = len(sizes)
    for b in range(images):
        windowed_ref[b] = dot(perm[...], normed[b * ROWS : (b + 1) * ROWS]).astype(BF16)
    flat = windowed_ref[...].reshape(images * WROWS, C)
    qkv = (dot(flat, w_qkv[...]) + qkv_bias).astype(BF16)
    qkv_ref[...] = qkv.reshape(images, WROWS, 3 * C)
    low_masks = head_masks(BF16)
    eye = identity()
    def one_image(b, carry):
        rows, cols = sizes[0]
        for n in range(1, images):
            rows = jnp.where(b == n, sizes[n][0], rows)
            cols = jnp.where(b == n, sizes[n][1], cols)
        blocks = {}
        for w in range(NWIN):
            allowed = (row_limit[w] < rows) & (col_limit[w] < cols)
            blocks[w] = jnp.where(allowed, 0.0, MASKED).astype(F32)
        attend(b, blocks)
        return carry

    def attend(b, blocks):
        units = [(b, pair, g, blocks) for pair in range(NWIN // 2) for g in range(NGRP)]
        pipelined(units, raw_scores, softmax, apply)

    def raw_scores(b, pair, g, blocks):
        results = []
        for w in (2 * pair, 2 * pair + 1):
            at = slice(w * SLOT, (w + 1) * SLOT)
            query = qkv_ref[b, at, g * 128 : (g + 1) * 128]
            key = qkv_ref[b, at, C + g * 128 : C + (g + 1) * 128]
            results.append(dot(key, spread_heads(query, low_masks), NT))
        return results

    def softmax(b, pair, g, blocks, raw):
        probs = []
        for n, score in enumerate(raw):
            w = 2 * pair + n
            block = jnp.concatenate([blocks[w]] * 2, 1)
            score = score * SCALE + (bias[g] + block)
            top = jnp.max(score, 0, keepdims=True)
            expo = jnp.exp(score - top)
            prob = (expo * (1.0 / jnp.sum(expo, 0, keepdims=True))).astype(BF16)
            prob_ref[b, w, g] = prob
            probs.append(prob)
        return probs

    def apply(b, pair, g, blocks, probs):
        both = slice(pair * 2 * SLOT, (pair + 1) * 2 * SLOT)
        value = (b, both, slice(2 * C + g * 128, 2 * C + (g + 1) * 128))
        mixed_ref[b, g * 128 : (g + 1) * 128, both] = apply_pair(qkv_ref, value, eye, *probs).astype(BF16)

    each_image(images, one_image, unrolled)
    for b in range(images):
        attended_ref[b] = dot(perm_t[...], mixed_ref[b], NT).astype(BF16)
    attended = attended_ref[...].reshape(images * ROWS, C)
    middle = field + dot(attended, w_proj[...]) + small[4:5]
    return normed, middle


def forward_mlp(middle, w_up, w_down, small, up_bias, active_ref, slope_ref):
    hat, _ = norm_parts(middle)
    mlp_in = (hat * small[5:6] + small[6:7]).astype(BF16)
    branch = jnp.zeros(middle.shape, F32)
    width = CHUNK
    for part in range(HID // width):
        at = slice(part * width, (part + 1) * width)
        pre = dot(mlp_in, w_up[:, at]) + up_bias[:, at]
        half = 0.5 * (1.0 + lax.erf(pre * (0.5**0.5)))
        active = (pre * half).astype(BF16)
        slope = half + pre * (jnp.exp(-0.5 * pre * pre) * ((2.0 * np.pi) ** -0.5))
        active_ref[..., at] = active.reshape(active_ref.shape[:-1] + (width,))
        slope_ref[..., at] = slope.astype(BF16).reshape(slope_ref.shape[:-1] + (width,))
        branch = branch + dot(active, w_down[:, at], NT)
    return mlp_in, middle + branch + small[7:8]


def backward_mlp(
    grad, middle, slope_ref, w_up, w_down, small, low_ref, pre_ref, rows_ref, up_rows_ref, place
):
    low = grad.astype(BF16)
    low_ref[place, :] = low
    rows_ref[7:8, :] += col_sum(low.astype(F32))
    normed_grad = jnp.zeros(grad.shape, F32)
    width = CHUNK
    for part in range(HID // width):
        at = slice(part * width, (part + 1) * width)
        slope = slope_ref[..., at].reshape(-1, width).astype(F32)
        pre = (dot(low, w_down[:, at]) * slope).astype(BF16)
        pre_ref[place, at] = pre
        up_rows_ref[:, at] += col_sum(pre.astype(F32))
        normed_grad = normed_grad + dot(pre, w_up[:, at], NT)
    hat, rate = norm_parts(middle)
    rows_ref[5:6, :] += col_sum(normed_grad * hat)
    rows_ref[6:7, :] += col_sum(normed_grad)
    return norm_back(normed_grad, hat, rate, small[5:6]) + grad


def backward_attention(
    grad_mid, field, qkv_ref, prob_ref, w_qkv, w_proj, perm, perm_t, small,
    spread_ref, dq_ref, dkv_ref, attn_ref, joined_ref, rows_ref, qkv_rows_ref, bias_grad_ref, start,
    need_grad, unrolled,
):
    images = qkv_ref.shape[0]
    place = pl.ds(start, images * ROWS)
    attn = grad_mid.astype(BF16)
    attn_ref[place, :] = attn
    rows_ref[4:5, :] += col_sum(attn.astype(F32))
    joined = dot(attn, w_proj[...], NT).astype(BF16)
    for b in range(images):
        joined_ref[b] = dot(perm[...], joined[b * ROWS : (b + 1) * ROWS]).astype(BF16)
    low_masks = head_masks(BF16)
    eye = identity()

    def cut(n, g):
        return slice(n * C + g * 128, n * C + (g + 1) * 128)

    def prob_grads(b, pair, g):
        results = []
        for w in (2 * pair, 2 * pair + 1):
            at = slice(w * SLOT, (w + 1) * SLOT)
            out = spread_heads(joined_ref[b, at, cut(0, g)], low_masks)
            results.append(dot(qkv_ref[b, at, cut(2, g)], out, NT))
            dkv_ref[b, at, cut(1, g)] = dot(prob_ref[b, 2 * pair + len(results) - 1, g], out).astype(BF16)
        return results

    def score_grads(b, pair, g, grads):
        results = []
        for n, prob_grad in enumerate(grads):
            wide = prob_ref[b, 2 * pair + n, g].astype(F32)
            weighted = wide * prob_grad
            score = weighted - wide * jnp.sum(weighted, 0, keepdims=True)
            bias_grad_ref[g] += score
            results.append(score.astype(BF16))
        return results

    def products(b, pair, g, scores):
        both = slice(pair * 2 * SLOT, (pair + 1) * 2 * SLOT)
        for n, score in enumerate(scores):
            w = 2 * pair + n
            at = slice(w * SLOT, (w + 1) * SLOT)
            query = spread_heads(qkv_ref[b, at, cut(0, g)], low_masks)
            dkv_ref[b, at, cut(0, g)] = (dot(score, query) * SCALE).astype(BF16)
        dq_ref[b, cut(0, g), both] = (
            apply_pair(qkv_ref, (b, both, cut(1, g)), eye, *scores) * SCALE
        ).astype(BF16)

    def one_image(b, carry):
        units = [(b, pair, g) for pair in range(NWIN // 2) for g in range(NGRP)]
        pipelined(units, prob_grads, score_grads, products)
        return carry

    each_image(images, one_image, unrolled)
    for b in range(images):
        rows = pl.ds(pl.multiple_of(start + b * ROWS, 16), ROWS)
        spread_ref[rows, :C] = dot(perm_t[...], dq_ref[b], NT).astype(BF16)
        spread_ref[rows, C:] = dot(perm_t[...], dkv_ref[b]).astype(BF16)
    back = spread_ref[place, :]
    qkv_rows_ref[:, :C] += col_sum(back[:, :C].astype(F32))
    qkv_rows_ref[:, 2 * C :] += col_sum(back[:, 2 * C :].astype(F32))
    normed_grad = dot(back, w_qkv[...], NT)
    hat, rate = norm_parts(field)
    rows_ref[0:1, :] += col_sum(normed_grad * hat)
    rows_ref[1:2, :] += col_sum(normed_grad)
    if not need_grad:
        return None
    return norm_back(normed_grad, hat, rate, small[0:1]) + grad_mid


def image_place():
    return pl.ds(pl.multiple_of(pl.program_id(0) * GROUP * ROWS, 16), GROUP * ROWS)


def flat(ref):
    return ref[...].reshape(-1, ref.shape[-1])


def rows_in(k, name):
    if hasattr(k, name):
        return flat(getattr(k, name))
    rows = flat(getattr(k, name + "0"))
    number = 1
    while hasattr(k, f"{name}{number}"):
        rows = jnp.where(pl.program_id(0) == number, flat(getattr(k, f"{name}{number}")), rows)
        number += 1
    return rows


def put_rows(ref, value):
    ref[...] = value.reshape(ref.shape)


def is_first():
    return pl.program_id(0) == 0


def is_last():
    return pl.program_id(0) == pl.num_programs(0) - 1


def clear(*refs):
    @pl.when(is_first())
    def _():
        for ref in refs:
            ref[...] = jnp.zeros(ref.shape, ref.dtype)


class Names:
    def __init__(self, **refs):
        self.__dict__.update(refs)


def fetch_attention(k, plan):
    if not plan.sources:
        return

    @pl.when(is_first())
    def _():
        load_blocks(plan.pieces(k, "attn"), k.stage, plan.widths["attn"], k.load_sem.at[0], k.me)
        wait_all(k.stage, k.load_sem.at[0])
        join_attention(k.stage, k.w_qkv, k.w_proj)
        for n, (source, target) in enumerate(((k.w_qkv, k.qkv_out), (k.w_proj, k.proj_out))):
            pltpu.make_async_copy(source, target, k.out_sem.at[n]).start()


def fetch_mlp(k, plan):
    @pl.when(is_first())
    def _():
        load_blocks(plan.pieces(k, "down"), k.w_down, plan.widths["down"], k.load_sem.at[1], k.me)
        load_blocks(plan.pieces(k, "up"), k.w_up, plan.widths["up"], k.load_sem.at[2], k.me)
        wait_all(k.w_down, k.load_sem.at[1])
        wait_all(k.w_up, k.load_sem.at[2])


def group_images(k, group=0):
    images = k.rows.shape[1]
    first = (pl.program_id(0) + group) * GROUP
    return [((first + b) // images, (first + b) % images) for b in range(GROUP)]


def group_sizes(k, group=0):
    return [(k.rows[m, n], k.cols[m, n]) for m, n in group_images(k, group)]


def small_rows(k, plan):
    return k.vec[plan.layer * PER_LAYER : plan.layer * PER_LAYER + 8]


def joined_rows(k, start, end):
    return jnp.concatenate([k.vec[n : n + 1] for n in range(start, end)], 1)


def up_bias_row(k, plan):
    return joined_rows(k, plan.layer * PER_LAYER + 8, (plan.layer + 1) * PER_LAYER)


def attention_forward_kernel(k, plan):
    fetch_attention(k, plan)
    small = small_rows(k, plan)
    qkv_bias = jnp.concatenate([small[2:3], jnp.zeros((1, C), F32), small[3:4]], 1)
    normed, middle = forward_attention(
        flat(k.field).astype(F32), group_sizes(k, plan.group), k.w_qkv, k.w_proj, k.perm, k.perm_t,
        k.row_limit, k.col_limit, k.bias, small, qkv_bias, k.qkv, k.prob, k.windowed,
        k.mixed, k.attended, False,
    )
    put_rows(k.normed, normed)
    put_rows(k.middle, middle)
    if not plan.sources:
        return

    @pl.when(is_last())
    def _():
        wait_all(k.w_qkv, k.out_sem.at[0])
        wait_all(k.w_proj, k.out_sem.at[1])


def first_mlp_kernel(k, plan):
    fetch_mlp(k, plan)

    @pl.when(is_first())
    def _():
        for n, (source, target) in enumerate(((k.w_down, k.down_out), (k.w_up, k.up_out))):
            pltpu.make_async_copy(source, target, k.out_sem.at[n]).start()

    mlp_in, result = forward_mlp(
        rows_in(k, "middle"), k.w_up, k.w_down, small_rows(k, plan), up_bias_row(k, plan), k.active,
        k.slope,
    )
    put_rows(k.mlp_in, mlp_in)
    put_rows(k.result, result)

    @pl.when(is_last())
    def _():
        wait_all(k.w_down, k.out_sem.at[0])
        wait_all(k.w_up, k.out_sem.at[1])


def store_mlp_grads(k, plan):
    for at in range(0, HID, CHUNK):
        k.up_grad[:, at : at + CHUNK] = dot(k.mlp_all[...], k.pre_all[:, at : at + CHUNK], TN).astype(BF16)
    store_blocks(k.up_grad, plan.outs(k, "up"), plan.widths["up"], k.sem_x, k.me)
    for at in range(0, HID, CHUNK):
        k.down_grad[:, at : at + CHUNK] = dot(k.low_all[...], k.active_all[:, at : at + CHUNK], TN).astype(BF16)
    store_blocks(k.down_grad, plan.outs(k, "down"), plan.widths["down"], k.sem_y, k.me)


def wait_mlp_grads(k, plan):
    wait_blocks(plan.outs(k, "up"), k.sem_x)
    wait_blocks(plan.outs(k, "down"), k.sem_y)


def head_pass(k, plan, result, sizes, total_images):
    first = pl.program_id(0) * GROUP
    base = plan.layers * PER_LAYER
    gain = k.vec[base : base + 1]
    hat, rate = norm_parts(result)
    final = hat * gain + k.vec[base + 1 : base + 2]
    places = group_images(k)
    owners, _, width = k.w_head.shape
    row = lax.broadcasted_iota(jnp.int32, (16, 1), 0)
    pooled = jnp.zeros((16, C), F32)
    own = other = jnp.full((16, 1), -1, jnp.int32)
    mixing = jnp.zeros((16, 1), F32)
    shares = []
    for b, (rows, cols) in enumerate(sizes):
        inside = ((k.cell_row[...] < rows) & (k.cell_col[...] < cols)).astype(F32)
        count = (rows * cols).astype(F32)
        mean = col_sum(final[b * ROWS : (b + 1) * ROWS] * inside) / count
        shares.append(inside / count)
        pooled = jnp.where(row == b, mean, pooled)
        m, n = places[b]
        mine = (k.me[0] * owners + k.me[1]) * k.rows.shape[1] + n
        own = jnp.where(row == b, k.labels[m, mine], own)
        other = jnp.where(row == b, k.labels[m, k.partner[m, n]], other)
        mixing = jnp.where(row == b, k.mix[m, n].astype(F32) / 16.0, mixing)
    pooled = pooled.astype(BF16)
    classes = owners * width
    real = CLASSES // owners
    bias = joined_rows(k, base + 2, base + 2 - (-CLASSES // C))
    empty = jnp.full((1, width - real), MASKED, F32)
    bias = jnp.concatenate(
        [part for n in range(owners) for part in (bias[:, n * real : (n + 1) * real], empty)], 1
    )
    logits = jnp.concatenate([dot(pooled, k.w_head[n]) for n in range(owners)], 1)
    logits = logits + bias
    top = jnp.max(logits, -1, keepdims=True)
    expo = jnp.exp(logits - top)
    log_probs = logits - top - jnp.log(jnp.sum(expo, -1, keepdims=True))
    lane = lax.broadcasted_iota(jnp.int32, (16, classes), 1)
    label = lane // width * real + lane % width
    label = jnp.where(lane % width < real, label, -2)
    target = jnp.where(label == own, mixing, 0.0)
    target = target + jnp.where(label == other, 1.0 - mixing, 0.0)
    loss = jnp.where(target > 0.0, target * log_probs, 0.0)
    loss = jnp.sum(jnp.sum(loss, -1, keepdims=True), 0, keepdims=True)
    k.loss[...] -= jnp.broadcast_to(loss, k.loss.shape)
    logit_grad = jnp.where(row < GROUP, (jnp.exp(log_probs) - target) / total_images, 0.0)
    logit_low = logit_grad.astype(BF16)
    wide = logit_low.astype(F32)
    k.head_rows[...] += col_sum(wide)
    for b in range(GROUP):
        k.pooled_all[pl.ds(first + b, 1), :] = pooled[b : b + 1].astype(F32)
        k.logit_all[pl.ds(first + b, 1), :] = wide[b : b + 1]
    pooled_grad = jnp.zeros((16, C), F32)
    for n in range(owners):
        pooled_grad += dot(logit_low[:, n * width : (n + 1) * width], k.w_head[n], NT)
    final_grad = jnp.concatenate(
        [pooled_grad[b : b + 1] * share for b, share in enumerate(shares)], 0
    )
    k.final_rows[0:1, :] += col_sum(final_grad * hat)
    k.final_rows[1:2, :] += col_sum(final_grad)
    return norm_back(final_grad, hat, rate, gain)


def last_mlp_kernel(k, plan, total_images):
    place = image_place()

    @pl.when(is_first())
    def _():
        load_blocks(plan.pieces(k, "head"), k.w_head, plan.widths["head"], k.load_sem.at[3], k.me)

    fetch_mlp(k, plan)

    @pl.when(is_first())
    def _():
        wait_all(k.w_head, k.load_sem.at[3])

    clear(k.row_sums, k.up_rows, k.final_rows, k.head_rows, k.loss, k.pooled_all, k.logit_all)
    middle = rows_in(k, "middle")
    mlp_in, result = forward_mlp(
        middle, k.w_up, k.w_down, small_rows(k, plan), up_bias_row(k, plan), k.active_all.at[place], k.slope
    )
    k.mlp_all[place, :] = mlp_in
    grad = head_pass(k, plan, result, group_sizes(k), total_images)
    put_rows(k.grad_mid, backward_mlp(
        grad, rows_in(k, "middle"), k.slope, k.w_up, k.w_down, small_rows(k, plan), k.low_all, k.pre_all,
        k.row_sums, k.up_rows, place,
    ))

    @pl.when(is_last())
    def _():
        store_mlp_grads(k, plan)
        total = dot(k.pooled_all[...].astype(BF16), k.logit_all[...].astype(BF16), TN).astype(BF16)
        owners, _, width = k.head_grad.shape
        for n in range(owners):
            k.head_grad[n] = total[:, n * width : (n + 1) * width]
        store_blocks(k.head_grad, plan.outs(k, "head"), plan.widths["head"], k.sem_x, k.me)
        wait_mlp_grads(k, plan)


def backward_mlp_kernel(k, plan):
    clear(k.row_sums, k.up_rows)
    place = image_place()
    k.mlp_all[place, :] = flat(k.mlp_in)
    k.active_all[place, :] = flat(k.active)
    put_rows(k.grad_mid, backward_mlp(
        rows_in(k, "grad"), rows_in(k, "middle"), k.slope, k.w_up, k.w_down, small_rows(k, plan), k.low_all, k.pre_all,
        k.row_sums, k.up_rows, place,
    ))

    @pl.when(is_last())
    def _():
        store_mlp_grads(k, plan)
        wait_mlp_grads(k, plan)


def backward_attention_kernel(k, plan, earlier, need_grad):
    sums = ("row_sums", "qkv_rows", "bias_grad")
    if earlier:
        @pl.when(is_first())
        def _():
            for name in sums:
                getattr(k, name)[...] = getattr(k, name + "_in")[...]
    else:
        clear(*[getattr(k, name) for name in sums])
    start = pl.multiple_of(earlier * ROWS + pl.program_id(0) * GROUP * ROWS, 16)
    grad = backward_attention(
        flat(k.grad_mid), flat(k.field).astype(F32), k.qkv, k.prob, k.w_qkv, k.w_proj, k.perm,
        k.perm_t, small_rows(k, plan), k.spread_all, k.dq, k.dkv, k.attn_all, k.joined, k.row_sums,
        k.qkv_rows, k.bias_grad, start, need_grad, True,
    )
    if need_grad:
        put_rows(k.grad, grad)
    if "attn" not in plan.targets:
        return
    place = pl.ds(start, GROUP * ROWS)
    k.normed_all[place, :] = flat(k.normed)
    k.attended_all[place, :] = flat(k.attended)

    @pl.when(is_last())
    def _():
        if earlier:
            before = slice(0, earlier * ROWS)
            k.normed_all[before, :] = flat(k.normed_in)
            k.attended_all[before, :] = flat(k.attended_in)
            k.spread_all[before, :] = k.spread_in[...]
            k.attn_all[before, :] = k.attn_in[...]
        owners, _, _ = k.attn_grad.shape
        wide, narrow = 3 * C // owners, C // owners
        if plan.collect is not None:
            layers, head_real, loss_at, near = plan.collect
            own = [k.row_sums, k.qkv_rows, k.mlp_rows0, k.up_rows0, k.bias_grad]
            collect_rows(
                layers, head_real, loss_at,
                own + [k.row_sums1, k.qkv_rows1, k.mlp_rows1, k.up_rows1, k.bias_grad1]
                + [k.final_rows, k.head_rows, k.loss],
                k.small_rows, k.spread_table,
            )
            pair_rows(k.small_rows, owners, near, k.me, k.pairs)
            for flip, (ref, *_) in enumerate(plan.outs(k, "attn")[2:]):
                width = ref.shape[2]
                pltpu.make_async_copy(
                    k.pairs.at[flip], ref.at[:, :, width - 128 : width], k.sem_a.at[2 + flip]
                ).start()
        total = dot(k.normed_all[...], k.spread_all[...], TN).astype(BF16)
        for n in range(owners):
            k.attn_grad[n, :, :wide] = total[:, n * wide : (n + 1) * wide]
        total = dot(k.attended_all[...], k.attn_all[...], TN).astype(BF16)
        for n in range(owners):
            k.attn_grad[n, :, wide:] = total[:, n * narrow : (n + 1) * narrow]
        store_blocks(k.attn_grad, plan.outs(k, "attn"), plan.widths["attn"], k.sem_a, k.me)
        wait_blocks(plan.outs(k, "attn"), k.sem_a)


class Plan:
    def __init__(self, widths, layer, layers):
        self.widths, self.layer, self.layers = widths, layer, layers
        self.sources = {}
        self.targets = {}
        self.collect = None
        self.group = 0

    def pieces(self, k, name):
        return [(getattr(k, ref), owners, cut) for ref, owners, cut in self.sources[name]]

    def outs(self, k, name):
        return [(getattr(k, ref), *rest) for ref, *rest in self.targets[name]]


def whole(shape):
    return pl.BlockSpec(shape, lambda i: (0,) * len(shape))


def per_image(*shape, first=0):
    return pl.BlockSpec((GROUP,) + shape, lambda i: (i + first,) + (0,) * len(shape))


SCALARS = pl.BlockSpec(memory_space=pltpu.SMEM)
FAR = pl.BlockSpec(memory_space=pl.ANY)
NEAR = pl.BlockSpec(memory_space=pltpu.VMEM)


def call(body, name, groups, ins, outs, scratch, flops):
    def kernel(*refs):
        body(Names(**dict(zip(list(ins) + list(outs) + list(scratch), refs))))

    moved = sum(a.size * a.dtype.itemsize for _, a in ins.values())
    results = pl.pallas_call(
        kernel,
        grid=(groups,),
        in_specs=[spec for spec, _ in ins.values()],
        out_specs=[spec for spec, _, _ in outs.values()],
        out_shape=[jax.ShapeDtypeStruct(dims, dtype) for _, dims, dtype in outs.values()],
        scratch_shapes=list(scratch.values()),
        compiler_params=pltpu.CompilerParams(
            dimension_semantics=("arbitrary",), vmem_limit_bytes=VMEM_LIMIT
        ),
        cost_estimate=pl.CostEstimate(flops=int(8 * flops), bytes_accessed=int(moved), transcendentals=0),
        name=name,
    )(*[array for _, array in ins.values()])
    return dict(zip(outs, results))


def exchange(array, step):
    axis, bit = step
    size = lax.axis_size(axis)
    return lax.ppermute(array, axis, [(i, i ^ (1 << bit)) for i in range(size)])


class Held:
    def __init__(self, array, dims=()):
        self.array, self.dims = array, list(dims)


def stack_blocks(parts, me, name, cuts=None):
    cuts = cuts or [None] * len(parts)
    args, outs, results = [], [], []
    for (held, received, step), cut in zip(parts, cuts):
        count, rows, columns = held.array.shape
        args += [held.array, received]
        axis, bit = step
        place = sum(d[0] == "win" and d[1] < bit for d in held.dims) if axis == "win" else len(held.dims)
        at = len(held.dims) - place
        dims = held.dims[:at] + [step] + held.dims[at:]
        bounds = [0, *(cut or ()), columns]
        pieces = list(zip(bounds, bounds[1:]))
        outs += [((2 * count, rows, end - start), BF16) for start, end in pieces]
        results.append((place, axis, bit, pieces, dims))

    def kernel(me_ref, *refs):
        ins, targets = list(refs[: len(args)]), list(refs[len(args) :])
        for place, axis, bit, pieces, _ in results:
            held, received = ins.pop(0), ins.pop(0)
            mine = (me_ref[0] >> bit) & 1 if axis == "win" else 0
            for start, end in pieces:
                out = targets.pop(0)
                for n in range(held.shape[0]):
                    base = (n >> place << (place + 1)) + (n & ((1 << place) - 1))
                    out[base + (mine << place)] = held[n, :, start:end]
                    out[base + ((1 - mine) << place)] = received[n, :, start:end]

    arrays = list(small_call(kernel, name, [me] + args, outs, scalars=1))
    return [
        [Held(arrays.pop(0), dims) for _ in pieces] for _, _, _, pieces, dims in results
    ]


def tie(*values):
    return lax.optimization_barrier(values)


def small_call(kernel, name, args, outs, stream=False, scratch=(), scalars=0, limit=24):
    def spec(dims):
        return whole(dims) if stream else pl.BlockSpec(memory_space=pltpu.VMEM)

    return pl.pallas_call(
        kernel,
        grid=(1,) if stream else (),
        out_shape=[jax.ShapeDtypeStruct(dims, dtype) for dims, dtype in outs],
        in_specs=[SCALARS] * scalars + [spec(a.shape) for a in args[scalars:]],
        out_specs=[spec(dims) for dims, _ in outs],
        scratch_shapes=list(scratch),
        compiler_params=pltpu.CompilerParams(
            vmem_limit_bytes=limit * 1024 * 1024
        ),
        cost_estimate=pl.CostEstimate(flops=1, bytes_accessed=1, transcendentals=0),
        name=name,
    )(*args)


class Chain:
    def __init__(self, keep, send, dims, steps, pair_at=None):
        self.keep, self.send, self.dims, self.steps = keep, send, list(dims), list(steps)
        self.pair_at = pair_at

    def start(self):
        self.received = exchange(self.send, self.steps.pop(0))


def add_blocks(keep, received, pair_at):
    total = keep.astype(F32) + received.astype(F32)
    if pair_at is None:
        return total.astype(BF16)
    pair = total[:16, pair_at:] + total[16:32, pair_at:]
    high = pair.astype(BF16)
    tail = jnp.zeros((total.shape[0] - 32, pair.shape[1]), BF16)
    parts = [jnp.concatenate([high, (pair - high.astype(F32)).astype(BF16), tail], 0)]
    if pair_at:
        parts = [total[:, :pair_at].astype(BF16)] + parts
    return jnp.concatenate(parts, 1)


def combine(groups, me, name):
    args, outs = [], []
    for group in groups:
        for chain in group:
            args += [chain.keep, chain.received]
        count, rows, _ = group[0].keep.shape
        width = sum(chain.keep.shape[2] for chain in group)
        outs += [((count // 2, rows, width), BF16)] * 2

    def kernel(me_ref, *refs):
        ins, results = list(refs[: len(args)]), list(refs[len(args) :])
        for group in groups:
            keep_out, send_out = results.pop(0), results.pop(0)
            start = 0
            for chain in group:
                keep, received = ins.pop(0), ins.pop(0)
                width = keep.shape[2]
                axis, bit = chain.steps[0]
                place = len(chain.dims) - 1 - chain.dims.index((axis, bit))
                mine = (me_ref[0] >> bit) & 1 if axis == "win" else 0
                for n in range(keep_out.shape[0]):
                    base = (n >> place << (place + 1)) + (n & ((1 << place) - 1))
                    for out, at in (
                        (keep_out, base + (mine << place)), (send_out, base + ((1 - mine) << place))
                    ):
                        out[n, :, start : start + width] = add_blocks(
                            keep[at], received[at], chain.pair_at
                        )
                start += width

    results = small_call(kernel, name, [me] + args, outs, scalars=1)
    chains = []
    for n, group in enumerate(groups):
        step = group[0].steps[0]
        at, pair_at = 0, None
        for chain in group:
            if chain.pair_at is not None:
                pair_at = at + chain.pair_at
            at += chain.keep.shape[2]
        dims = [d for d in group[0].dims if d != step]
        chains.append(Chain(results[2 * n], results[2 * n + 1], dims, group[0].steps, pair_at))
    return chains


def finish(chain, name):
    _, rows, width = chain.keep.shape

    def kernel(keep, received, own, square):
        total = keep[0].astype(F32) + received[0].astype(F32)
        own[...] = total
        square[...] = jnp.broadcast_to(jnp.sum(total * total), (1, 128))

    return small_call(
        kernel, name, [chain.keep, chain.received], [((rows, width), F32), ((1, 128), F32)]
    )


def finish_pair(chain, squares, devices, share, name):
    _, rows, width = chain.keep.shape
    at = chain.pair_at

    def kernel(keep, received, *refs):
        total = keep[0].astype(F32) + received[0].astype(F32)
        own, message = refs[-2:]
        own[...] = total[:, :at]
        pair = total[:16, at:] + total[16:32, at:]
        square = jnp.sum(total[:, :at] * total[:, :at])
        square = jnp.broadcast_to(square, (1, 128))
        for ref in refs[:-2]:
            square = square + ref[...]
        row = [pair[n : n + 1] for n in range(share // 128)] + [square]
        message[...] = jnp.broadcast_to(jnp.concatenate(row, 1), message.shape)

    return small_call(
        kernel, name, [chain.keep, chain.received] + squares,
        [((rows, at), F32), ((devices, share + 128), F32)],
    )


def adam_step(weight, grad, first, second, rate):
    new_first = 0.5 * first + 0.5 * grad
    new_second = 0.5 * second + 0.5 * grad * grad
    fix = 1.0 - 0.5**STEP
    update = new_first / fix / (jnp.sqrt(new_second / fix) + ADAM_EPS)
    return (new_first, new_second, weight - rate * (update + DECAY_RATE * weight))


def update_kernel(starts, widths, layout, *refs):
    own, message, rest = refs[:3], refs[3], list(refs[4:])
    groups = [rest[3 * n : 3 * n + 3] for n in range(7)]
    loss_ref, norm_ref = rest[21], rest[22]
    outs = [rest[23 + 3 * n : 26 + 3 * n] for n in range(7)]
    vector_rows, table_rows, offsets, square_at, loss_at = layout
    vector_grad = message[:vector_rows, :C]
    table_grad = message[:table_rows, C : C + offsets]
    total = (
        jnp.sum(message[:, square_at : square_at + 1])
        + jnp.sum(vector_grad * vector_grad)
        + jnp.sum(table_grad * table_grad)
    )
    norm = jnp.sqrt(jnp.broadcast_to(total, (1, 1)))
    factor = CLIP_NORM / jnp.maximum(norm, CLIP_NORM)
    norm_ref[...] = norm
    loss_ref[...] = message[0:1, loss_at : loss_at + 1]

    def put(number, layer, grad, rate):
        weight, first, second = groups[number]
        index = (Ellipsis,) if layer is None else (layer, Ellipsis)
        if number == 6:
            index = (slice(None), layer, slice(None))
        results = adam_step(weight[index], factor * grad, first[index], second[index], rate)
        for ref, value in zip(outs[number], results):
            ref[index] = value

    layers = len(starts)
    for l in range(layers):
        qkv_width = outs[0][0].shape[2]
        part, at = starts[l]["attn"]
        put(0, l, own[part][:, at : at + qkv_width], LEARN_RATE)
        put(1, l, own[part][:, at + qkv_width : at + widths["attn"]], LEARN_RATE)
        part, at = starts[l]["up"]
        put(2, l, own[part][:, at : at + widths["up"]], LEARN_RATE)
        part, at = starts[l]["down"]
        put(3, l, own[part][:, at : at + widths["down"]], LEARN_RATE)
        heads = table_rows // layers
        put(6, l, table_grad[l * heads : (l + 1) * heads], SMALL_RATE)
    part, at = starts[-1]["head"]
    put(4, None, own[part][:, at : at + outs[4][0].shape[1]], LEARN_RATE)
    put(5, None, vector_grad, SMALL_RATE)


def collect_rows(layers, head_real, loss_at, ins, out, spread):
    out[...] = jnp.zeros(out.shape, F32)
    row_of_slot = lax.broadcasted_iota(jnp.int32, (SLOT, 128), 0)
    lane = lax.broadcasted_iota(jnp.int32, (SLOT, 128), 1)
    target = row_of_slot // WSIDE * (2 * WSIDE - 1) + row_of_slot % WSIDE
    spreader = ((lane == target) & (row_of_slot < AREA)).astype(F32).astype(BF16)
    row = 0
    for l in range(layers):
        attn_rows, qkv_rows, mlp_rows, up_rows, bias_grad = ins[5 * l : 5 * l + 5]
        parts = [
            attn_rows[0:2], qkv_rows[:, :C], qkv_rows[:, 2 * C :], attn_rows[4:5], mlp_rows[5:8],
        ] + [up_rows[:, n * C : (n + 1) * C] for n in range(HID // C)]
        for part in parts:
            out[row : row + part.shape[0], :C] = part
            row += part.shape[0]
        for head in range(HEADS):
            g, h = divmod(head, PACK)
            left = bias_grad[g, :, h * SLOT : (h + 1) * SLOT]
            total = jnp.zeros((SLOT, 128), F32)
            for _ in range(3):
                low = left.astype(BF16)
                total = total + dot(low, spreader)
                left = left - low.astype(F32)
            spread[head * SLOT : (head + 1) * SLOT, :] = total
        table = jnp.zeros((HEADS, 256), F32)
        span = 2 * WSIDE - 1
        for j in range(AREA):
            wide = jnp.concatenate(
                [spread[pl.ds(j, HEADS, stride=SLOT), :], jnp.zeros((HEADS, 128), F32)], 1
            )
            shift = (WSIDE - 1 - j // WSIDE) * span + WSIDE - 1 - j % WSIDE
            table = table + (pltpu.roll(wide, shift, 1) if shift else wide)
        width = out.shape[1] - C
        out[l * HEADS : (l + 1) * HEADS, C:] = table[:, :width]
    final_rows, head_rows, loss = ins[5 * layers :]
    out[row : row + 2, :C] = final_rows[...]
    row += 2
    cuts = CLASSES // head_real
    width = head_rows.shape[1] // cuts
    classes = jnp.concatenate(
        [head_rows[:, n * width : n * width + head_real] for n in range(cuts)]
        + [jnp.zeros((1, -CLASSES % C), F32)], 1
    )
    for n in range(classes.shape[1] // C):
        out[row + n : row + n + 1, :C] = classes[:, n * C : (n + 1) * C]
    out[0:1, loss_at : loss_at + 1] = loss[:, 0:1]


def pair_rows(rows, ch_count, owners, me_ref, pairs):
    count = rows.shape[1] // 128
    wins = rows.shape[0] // ch_count
    high_rows = pairs.shape[2] // wins
    for flip in range(2):
        for n, owner in enumerate(owners):
            for win in range(wins):
                values = rows[pl.ds(win * ch_count + (me_ref[1] ^ (owner ^ flip)), 1), :]
                values = jnp.concatenate(
                    [values[:, m * 128 : (m + 1) * 128] for m in range(count)]
                    + [jnp.zeros((16 - count, 128), F32)], 0
                )
                high = values.astype(BF16)
                at = win * high_rows
                pairs[flip, n, at : at + 16] = high
                pairs[flip, n, at + 16 : at + 32] = (values - high.astype(F32)).astype(BF16)
                pairs[flip, n, at + 32 : at + high_rows] = jnp.zeros((high_rows - 32, 128), BF16)


def pack_kernel(head_width, qkv, proj, down, up, head, attn0, mlp0, all1):
    attn0[...] = jnp.concatenate([qkv[0], proj[0]], 1).astype(BF16)
    mlp0[...] = jnp.concatenate([down[0], up[0]], 1).astype(BF16)
    parts = [qkv[1], proj[1], down[1], up[1], head[...]]
    pad = head_width - head.shape[1]
    if pad:
        parts.append(jnp.zeros((head.shape[0], pad), F32))
    all1[...] = jnp.concatenate(parts, 1).astype(BF16)


def per_device(
    tokens, valid_rows, valid_cols, partner, mix_level, labels,
    w_qkv, m_qkv, v_qkv, w_proj, m_proj, v_proj, w_fc1, m_fc1, v_fc1, w_fc2, m_fc2, v_fc2,
    w_head, m_head, v_head, vectors, m_vec, v_vec, rel_table, m_rel, v_rel,
):
    micro, images, cells, chans = tokens.shape
    layers = rel_table.shape[0]
    per_layer = 8 + HID // C
    base = layers * per_layer
    head_rows = vectors.shape[0] - base - 2
    all_images = labels.shape[1]
    total_images = micro * all_images
    local = micro * images
    groups = local // GROUP
    sizes = {axis: lax.axis_size(axis) for axis in ("win", "ch")}
    win_count, ch_count = sizes["win"], sizes["ch"]
    device_count = win_count * ch_count
    win_index, ch_index = lax.axis_index("win"), lax.axis_index("ch")
    me = jnp.stack([win_index, ch_index]).astype(jnp.int32)
    block_rows = C // win_count
    widths = {"attn": 4 * C // ch_count, "down": HID // ch_count, "up": HID // ch_count}
    head_real = CLASSES // ch_count
    widths["head"] = -(-head_real // 128) * 128
    head_classes = widths["head"] * ch_count
    direct = block_rows % 16 == 0 and block_rows >= 32 and all(w % 128 == 0 for w in widths.values())

    core = ("ch", 0)
    ch_high = [("ch", b) for b in range(1, ch_count.bit_length() - 1)]
    win_low = [("win", 0)]
    win_high = [("win", b) for b in range(1, win_count.bit_length() - 1)]

    def low(v):
        return v.astype(BF16)

    packed = small_call(
        functools.partial(pack_kernel, widths["head"]), "pack",
        [w_qkv, w_proj, w_fc2.transpose(0, 2, 1), w_fc1, w_head],
        [((block_rows, sum(widths[n] for n in names)), BF16) for names in (
            ("attn",), ("down", "up"), ("attn", "down", "up", "head"))],
        stream=True,
        limit=56,
    )
    names = [["attn", "down", "up"], ["attn", "down", "up", "head"]]
    onehot = jnp.asarray(relative_onehot(), BF16)
    offsets = rel_table.shape[1]
    table_width = -(-(offsets + 1) // 128) * 128
    share = C + table_width
    tables = [window_tables(l % 2 == 1) for l in range(layers)]
    perms = [jnp.asarray(t[0], BF16) for t in tables]
    perms_t = [jnp.asarray(t[0].T, BF16) for t in tables]
    row_limits = [jnp.asarray(t[1]) for t in tables]
    col_limits = [jnp.asarray(t[2]) for t in tables]

    def bias_of(table):
        table = table.transpose(0, 2, 1).reshape(layers * HEADS, offsets)
        table_parts = []
        for _ in range(3):
            table_parts.append(low(table))
            table = table - table_parts[-1].astype(F32)
        bias = dot(jnp.concatenate(table_parts, 0), onehot).reshape(3, layers, HEADS, SLOT * SLOT)
        bias = (bias[0] + bias[1]) + bias[2]
        return (
            bias.reshape(layers, NGRP, PACK, SLOT, SLOT)
            .transpose(0, 1, 3, 2, 4)
            .reshape(layers, NGRP, SLOT, LANES)
        )

    padded = jnp.pad(tokens.reshape(local, cells, chans), ((0, 0), (0, ROWS - cells), (0, 0)))

    def stage(number, *moves, cuts=None, more=()):
        received = [exchange(part.array, step) for part, step in moves]
        tied = tie(*received, *more)
        received, more = tied[: len(moves)], tied[len(moves) :]
        stacked = stack_blocks(
            [(part, got, step) for (part, step), got in zip(moves, received)],
            me, f"stack{number}", cuts,
        )
        return (stacked, *more)

    def wait_for(value, *parts):
        value, *arrays = tie(value, *[part.array for part in parts])
        for part, array in zip(parts, arrays):
            part.array = array
        return value

    far = [Held(block[None]) for block in packed]
    edges = [
        [0, widths["attn"] * 2 // 3, widths["attn"], widths["attn"] + widths["down"],
         widths["attn"] + widths["down"] + widths["up"]],
        [0, widths["attn"], widths["attn"] + widths["down"] + widths["up"] * 2 // 3,
         sum(widths[name] for name in ("attn", "down", "up", "head"))],
    ]
    staged = win_count == 8 and ch_count == 4
    if staged:
        zh, zl, y, x = ("win", 2), ("win", 1), ("win", 0), ("ch", 1)
        ((attn,),), mlp, padded = stage(0, (far[0], zh), more=(far[1].array, padded))
        (attn, (mlp,)), all1, bias = stage(
            1, (attn, zl), (Held(mlp), zh), cuts=[edges[0][1:2], None],
            more=(packed[2], bias_of(rel_table)),
        )
        floating = exchange(all1[None], zh)
        ((one,), (two,), mlp), = stage(
            2, (attn[0], y), (attn[1], x), (mlp, zl), cuts=[None, None, [widths["down"]]]
        )
        (((all1,),),) = [stack_blocks([(Held(all1[None]), floating, zh)], me, "stack10")]
        mlp[0].array, mlp[1].array, all1.array = tie(mlp[0].array, mlp[1].array, all1.array)
        near = [(one, x), (two, y), (mlp[0], x), (mlp[1], y)]
        received = [exchange(part.array, step) for part, step in near]
        floating = exchange(all1.array, zl)
        *received, floating = tie(*received, floating)
        ((one,), (two,), (down,), (up,)) = stack_blocks(
            [(part, got, step) for (part, step), got in zip(near, received)], me, "stack3"
        )
        held = [[one, two]]
        *got, floating = tie(*[exchange(part.array, core) for part in held[0]], floating)
        other = [got]
        (parts1,) = stack_blocks([(all1, floating, zl)], me, "stack11", [edges[1][1:-1]])
        padded = wait_for(padded, *parts1)
    else:
        bias = bias_of(rel_table)
        bits = win_high[::-1] + win_low + ch_high[::-1]
        held, other = [[], []], []
        for number, part in enumerate(far):
            for n, step in enumerate(bits):
                ((part,),), = stage(10 * number + n, (part, step))
            layer = number // 2
            base = 0 if number != 1 else widths["attn"]
            for start, end in zip(edges[layer], edges[layer][1:]):
                if start >= base and end - base <= part.array.shape[-1]:
                    held[layer].append(Held(part.array[..., start - base : end - base], part.dims))
        other.append([exchange(part.array, core) for part in held[0]])

    def weight_inputs(layer, wanted):
        plan = Plan(widths, layer, layers)
        ins = {}
        starts, at = {}, 0
        for name in names[layer]:
            starts[name] = at
            at += widths[name]
        bounds = list(zip(edges[layer], edges[layer][1:]))
        blocks = []
        for group, part in enumerate(held[layer]):
            if group >= len(other[layer]):
                break
            owners = relative_owners([d for d in part.dims if d[0] == "ch"])
            for number, array in enumerate((part.array, other[layer][group])):
                flat_array = array.reshape(-1, C, array.shape[-1])
                blocks.append((group, [owner ^ number for owner in owners], flat_array))
        for name in wanted:
            plan.sources[name] = []
            columns = []
            for number, (group, owners, array) in enumerate(blocks):
                begin = max(starts[name], bounds[group][0])
                end = min(starts[name] + widths[name], bounds[group][1])
                if begin >= end:
                    continue
                cut = (begin - bounds[group][0], end - begin, begin - starts[name])
                if direct:
                    ref = f"blocks{number}"
                    ins[ref] = (FAR, array)
                    plan.sources[name].append((ref, owners, cut))
                elif number % 2 == 0:
                    table = np.argsort(np.asarray(owners + blocks[number + 1][1]))
                    both = jnp.concatenate([array, blocks[number + 1][2]])
                    index = jnp.asarray(table)[jnp.arange(ch_count) ^ ch_index]
                    columns.append(jnp.take(both, index, axis=0)[..., cut[0] : cut[0] + cut[1]])
            if not direct:
                full = jnp.concatenate(columns, -1)
                if name in ("up", "down"):
                    full = full.transpose(1, 0, 2).reshape(C, -1)
                ins[f"staged_{name}"] = (FAR, full)
                plan.sources[name] = [(f"staged_{name}", None, None)]
        ins["me"] = (SCALARS, me)
        return ins, plan

    orders = {
        "x": ch_high + win_low + win_high, "a": ch_high + win_low + win_high,
        "y": win_low + ch_high + win_high, "b": win_low + ch_high + win_high,
    }
    block_dims = ch_high + [("win", b) for b in reversed(range(win_count.bit_length() - 1))]
    owners = relative_owners(ch_high)
    regular = direct and len(ch_high) == 1

    def grad_outputs(plan, **members):
        outs = {}
        for group, wanted in members.items():
            if not direct:
                for name in wanted:
                    plan.targets[name] = [(f"full_{name}", None, 0, 0, widths[name])]
                    dims = (C, HID) if name in ("up", "down") else (ch_count, C, widths[name])
                    outs[f"full_{name}"] = (FAR, dims, BF16)
                continue
            starts = np.cumsum([0] + [widths[name] for name in wanted])
            refs = [
                (f"keep_{group}", owners), (f"send_{group}", [owner ^ 1 for owner in owners])
            ]
            for ref, _ in refs:
                outs[ref] = (FAR, (len(owners), C, int(starts[-1])), BF16)
            for name, start in zip(wanted, starts):
                plan.targets[name] = [(ref, at, int(start), 0, widths[name]) for ref, at in refs]
        return outs

    def cut_attention_outputs(plan):
        cut = widths["attn"] * 2 // 3
        outs, plan.targets["attn"] = {}, []
        for group, start, size, extra in (("a", 0, cut, 0), ("b", cut, widths["attn"] - cut, 128)):
            for kind, flip in (("keep", 0), ("send", 1)):
                ref = f"{kind}_{group}"
                outs[ref] = (NEAR, (len(owners), C, size + extra), BF16)
                plan.targets["attn"].append(
                    (ref, [owner ^ flip for owner in owners], 0, start, size)
                )
        return outs

    def chain_of(results, group, *members, pair_at=None):
        if direct:
            keep, send = results[f"keep_{group}"], results[f"send_{group}"]
        else:
            full = []
            for name in members:
                part = results[f"full_{name}"]
                if name in ("up", "down"):
                    part = part.reshape(C, ch_count, -1).transpose(1, 0, 2)
                full.append(part)
            full = jnp.concatenate(full, -1)
            keep, send = [
                jnp.take(full, np.asarray(owners) ^ flip ^ ch_index, axis=0) for flip in (0, 1)
            ]
        dims = (-1, block_rows, keep.shape[-1])
        return Chain(
            keep.reshape(dims), send.reshape(dims), block_dims, [core] + orders[group], pair_at
        )

    def start(*chains):
        for chain in chains:
            chain.start()

    def meet(value, *chains):
        value, *got = tie(value, *[chain.received for chain in chains])
        for chain, array in zip(chains, got):
            chain.received = array
        return value

    def after(value, *chains):
        held_back = [array for chain in chains for array in (chain.keep, chain.send)]
        value, *held_back = tie(value, *held_back)
        for n, chain in enumerate(chains):
            chain.keep, chain.send = held_back[2 * n], held_back[2 * n + 1]
        return value

    def attention_consts(l, forward):
        ins = {
            "perm": (whole((WROWS, ROWS)), perms[l]),
            "perm_t": (whole((ROWS, WROWS)), perms_t[l]),
            "vec": (whole(vectors.shape), vectors),
        }
        if forward:
            ins["rows"] = (SCALARS, valid_rows)
            ins["cols"] = (SCALARS, valid_cols)
            ins["row_limit"] = (whole((NWIN, SLOT, 128)), row_limits[l])
            ins["col_limit"] = (whole((NWIN, SLOT, 128)), col_limits[l])
            ins["bias"] = (
                pl.BlockSpec((None, NGRP, SLOT, LANES), lambda i, l=l: (l, 0, 0, 0)), bias
            )
        return ins

    def vmem(*dims, dtype=BF16):
        return pltpu.VMEM(dims, dtype)

    attn_weights = {
        "stage": vmem(ch_count, C, widths["attn"]),
        "w_qkv": vmem(C, 3 * C),
        "w_proj": vmem(C, C),
        "load_sem": pltpu.SemaphoreType.DMA((4,)),
    }
    mlp_weights = {
        "w_down": vmem(C, HID),
        "w_up": vmem(C, HID),
        "load_sem": pltpu.SemaphoreType.DMA((4,)),
    }
    all_rows = local * ROWS
    mlp_rows = {
        "mlp_all": vmem(all_rows, C), "active_all": vmem(all_rows, HID),
        "pre_all": vmem(all_rows, HID), "low_all": vmem(all_rows, C),
        "up_grad": vmem(C, HID), "down_grad": vmem(C, HID),
        "sem_x": pltpu.SemaphoreType.DMA((2,)), "sem_y": pltpu.SemaphoreType.DMA((2,)),
    }
    wide = (per_image(ROWS, C), (local, ROWS, C), F32)
    thin = (per_image(ROWS, C), (local, ROWS, C), BF16)
    hidden = (per_image(ROWS, HID), (local, ROWS, HID), BF16)
    attn_saved = {
        "normed": thin,
        "qkv": (per_image(WROWS, 3 * C), (local, WROWS, 3 * C), BF16),
        "prob": (per_image(NWIN, NGRP, SLOT, LANES), (local, NWIN, NGRP, SLOT, LANES), BF16),
        "attended": thin,
    }
    sums = {"row_sums": (whole((8, C)), (8, C), F32)}
    up_sums = {**sums, "up_rows": (whole((1, HID)), (1, HID), F32)}
    attn_sums = {
        **sums,
        "qkv_rows": (whole((1, 3 * C)), (1, 3 * C), F32),
        "bias_grad": (whole((NGRP, SLOT, LANES)), (NGRP, SLOT, LANES), F32),
    }

    def given(spec, array):
        return (spec[0], array)

    mlp_flops = 2 * all_rows * C * HID * 2
    attn_flops = 2 * all_rows * C * C * 8

    def attention_forward(l, field, first=0, count=groups, before=None):
        ins, plan = weight_inputs(l, ["attn"]) if before is None else ({}, Plan(widths, l, layers))
        plan.group = first
        ins["field"] = (per_image(*field.shape[1:], first=first), field)
        ins.update(attention_consts(l, True))
        outs = {
            name: (spec, (count * GROUP,) + dims[1:], dtype)
            for name, (spec, dims, dtype) in {"middle": wide, **attn_saved}.items()
        }
        scratch = {"mixed": vmem(GROUP, C, WROWS), "windowed": vmem(GROUP, WROWS, C)}
        if before is None:
            outs["qkv_out"] = (FAR, (C, 3 * C), BF16)
            outs["proj_out"] = (FAR, (C, C), BF16)
            scratch.update(attn_weights)
            scratch["out_sem"] = pltpu.SemaphoreType.DMA((2,))
        else:
            ins["w_qkv"] = (whole((C, 3 * C)), before["qkv_out"])
            ins["w_proj"] = (whole((C, C)), before["proj_out"])
        results = call(
            functools.partial(attention_forward_kernel, plan=plan), f"attention_forward{l}_{first}",
            count, ins, outs, scratch, attn_flops * count // groups,
        )
        return results if before is None else {**before, **results}

    def rows_of(name, arrays):
        if len(arrays) == 1:
            return {name: given(wide, arrays[0])}
        return {f"{name}{n}": (whole(array.shape), array) for n, array in enumerate(arrays)}

    def begin(*moves):
        return [(part, step, exchange(part.array, step)) for part, step in moves]

    def arrive(number, value, moves):
        value, *received = tie(value, *[got for _, _, got in moves])
        stacked = stack_blocks(
            [(part, got, step) for (part, step, _), got in zip(moves, received)], me, f"stack{number}"
        )
        return value, [parts[0] for parts in stacked]

    if staged:
        moves = begin((down, y), (up, x), (parts1[0], y), (parts1[1], x), (parts1[2], y))
        early0 = attention_forward(0, padded, 0, groups - 1)
        early0["proj_out"], (down, up, *parts1) = arrive(4, early0["proj_out"], moves)
        early0["proj_out"] = wait_for(early0["proj_out"], down, up, *parts1)
        held[0] += [down, up]
        got = [exchange(part.array, core) for part in (down, up)]
        moves = begin((parts1[0], x), (parts1[1], y), (parts1[2], x))
        saved0 = attention_forward(0, padded, groups - 1, 1, early0)
        saved0["middle"], *got = tie(saved0["middle"], *got)
        other[0] = list(other[0]) + got
        saved0["middle"], parts1 = arrive(5, saved0["middle"], moves[:1])
        middle0 = [early0["middle"], wait_for(saved0["middle"], *parts1)]
        held.append(parts1)
    else:
        saved0 = early0 = attention_forward(0, padded)
        middle0 = [saved0["middle"]]
    ins, plan = weight_inputs(0, ["down", "up"])
    ins.update(rows_of("middle", middle0))
    ins["vec"] = (whole(vectors.shape), vectors)
    mlp0 = call(
        functools.partial(first_mlp_kernel, plan=plan), "first_mlp", groups, ins,
        {
            "result": wide, "mlp_in": thin, "active": hidden, "slope": hidden,
            "down_out": (FAR, (C, HID), BF16),
            "up_out": (FAR, (C, HID), BF16),
        },
        {**mlp_weights, "out_sem": pltpu.SemaphoreType.DMA((2,))},
        mlp_flops,
    )
    result0 = mlp0["result"]
    got = [exchange(part.array, core) for part in held[1]]
    result0, *got = tie(result0, *got)
    other.append(got)

    if staged:
        early1 = attention_forward(1, result0, 0, groups - 1)
        early1["proj_out"], late1 = arrive(6, early1["proj_out"], moves[1:])
        early1["proj_out"] = wait_for(early1["proj_out"], *late1)
        got = [exchange(part.array, core) for part in late1]
        saved1 = attention_forward(1, result0, groups - 1, 1, early1)
        saved1["middle"], *got = tie(saved1["middle"], *got)
        held[1] = held[1] + late1
        other[1] = other[1] + got
        middle1 = [early1["middle"], saved1["middle"]]
    else:
        saved1 = early1 = attention_forward(1, result0)
        middle1 = [saved1["middle"]]
    ins, plan = weight_inputs(1, ["down", "up", "head"])
    ins.update(rows_of("middle", middle1))
    ins["vec"] = (whole(vectors.shape), vectors)
    ins["rows"] = (SCALARS, valid_rows)
    ins["cols"] = (SCALARS, valid_cols)
    ins["labels"] = (SCALARS, labels)
    ins["partner"] = (SCALARS, partner)
    ins["mix"] = (SCALARS, mix_level)
    cell = np.arange(ROWS)
    for name, place in (("cell_row", cell // GRID), ("cell_col", cell % GRID)):
        place = np.where(cell < CELLS, place, 99)[:, None].astype(np.int32)
        ins[name] = (whole((ROWS, 1)), jnp.asarray(place))
    outs = {
        "grad_mid": wide, **up_sums,
        "final_rows": (whole((2, C)), (2, C), F32),
        "head_rows": (whole((1, head_classes)), (1, head_classes), F32),
        "loss": (whole((1, 128)), (1, 128), F32),
        **grad_outputs(plan, x=["up", "head"], y=["down"]),
    }
    last = call(
        functools.partial(last_mlp_kernel, plan=plan, total_images=float(total_images)),
        "last_mlp", groups, ins, outs,
        {
            "slope": vmem(GROUP * ROWS, HID), "w_head": vmem(ch_count, C, widths["head"]),
            **mlp_weights, **mlp_rows,
            "pooled_all": vmem(16, C, dtype=F32), "logit_all": vmem(16, head_classes, dtype=F32),
            "head_grad": vmem(ch_count, C, widths["head"]),
        },
        3 * mlp_flops,
    )

    def attention_backward(l, grad_mid, field, saved, first, count, before=None, before_saved=None, store=True, collect=None):
        plan = Plan(widths, l, layers)
        ins = {
            "me": (SCALARS, me), "w_qkv": (whole((C, 3 * C)), saved["qkv_out"]),
            "w_proj": (whole((C, C)), saved["proj_out"]),
        }
        ins.update(attention_consts(l, False))
        wanted = ["qkv", "prob"] + (["normed", "attended"] if store else [])
        for name, array in [("grad_mid", grad_mid), ("field", field)] + [
            (name, saved[name]) for name in wanted
        ]:
            skip = first if array.shape[0] == local else 0
            ins[name] = (per_image(*array.shape[1:], first=skip), array)
        if before is not None:
            for name, (spec, _, _) in attn_sums.items():
                ins[name + "_in"] = (spec, before[name])
            for name in ("normed", "attended"):
                ins[name + "_in"] = (whole((first * GROUP, ROWS, C)), before_saved[name])
            for name in ("spread", "attn"):
                array = before[name + "_all"]
                ins[name + "_in"] = (whole(array.shape), array)
        rows_here = count * GROUP * ROWS
        outs = dict(attn_sums)
        scratch = {
            "dq": vmem(GROUP, C, WROWS), "dkv": vmem(GROUP, WROWS, 2 * C),
            "joined": vmem(GROUP, WROWS, C),
        }
        need_grad = l > 0
        if need_grad:
            outs["grad"] = (wide[0], (count * GROUP, ROWS, C), F32)
        if store:
            if collect is None:
                outs.update(grad_outputs(plan, a=["attn"]))
            else:
                outs.update(cut_attention_outputs(plan))
                plan.collect = (layers, head_real, share - 1, owners)
                ins.update({name: (whole(array.shape), array) for name, array in collect.items()})
                scratch["small_rows"] = vmem(device_count, share, dtype=F32)
                scratch["spread_table"] = vmem(HEADS * SLOT, 128, dtype=F32)
                scratch["pairs"] = vmem(2, len(owners), C, 128)
            scratch.update({
                "normed_all": vmem(all_rows, C), "attended_all": vmem(all_rows, C),
                "spread_all": vmem(all_rows, 3 * C), "attn_all": vmem(all_rows, C),
                "attn_grad": vmem(ch_count, C, widths["attn"]),
                "sem_a": pltpu.SemaphoreType.DMA((4,)),
            })
        else:
            outs["spread_all"] = (whole((rows_here, 3 * C)), (rows_here, 3 * C), BF16)
            outs["attn_all"] = (whole((rows_here, C)), (rows_here, C), BF16)
        return call(
            functools.partial(
                backward_attention_kernel, plan=plan,
                earlier=0 if before is None else first * GROUP, need_grad=need_grad,
            ),
            f"attention_backward{l}_{first}", count, ins, outs, scratch,
            2 * attn_flops * count // groups,
        )

    x1, y1 = chain_of(last, "x", "up", "head"), chain_of(last, "y", "down")
    if regular:
        start(x1, y1)
    grad_mid = last["grad_mid"]
    before1 = attention_backward(1, grad_mid, mlp0["result"], early1, 0, groups - 1, store=False)
    if regular:
        before1["row_sums"] = meet(before1["row_sums"], x1, y1)
        x1, y1 = combine([[x1], [y1]], me, "sum0")
        grad_mid = after(grad_mid, x1, y1)
        start(x1, y1)
    back1 = attention_backward(
        1, grad_mid, mlp0["result"], saved1, groups - 1, 1, before1, early1
    )
    a1 = chain_of(back1, "a", "attn")
    grad = back1["grad"]
    if regular:
        grad = meet(grad, x1, y1)
        x1, y1 = combine([[x1], [y1]], me, "sum1")
        grad = after(grad, x1, y1)
        start(x1, y1, a1)

    plan = Plan(widths, 0, layers)
    ins = {
        "me": (SCALARS, me),
        "w_down": (whole((C, HID)), mlp0["down_out"]),
        "w_up": (whole((C, HID)), mlp0["up_out"]),
    }
    ins.update(rows_of("grad", [before1["grad"], grad]))
    ins.update(rows_of("middle", middle0))
    ins["mlp_in"] = given(thin, mlp0["mlp_in"])
    ins["active"] = given(hidden, mlp0["active"])
    ins["slope"] = given(hidden, mlp0["slope"])
    ins["vec"] = (whole(vectors.shape), vectors)
    first = call(
        functools.partial(backward_mlp_kernel, plan=plan), "mlp_backward0", groups, ins,
        {"grad_mid": wide, **up_sums, **grad_outputs(plan, x=["up"], y=["down"])},
        dict(mlp_rows), 2 * mlp_flops,
    )
    x0, y0 = chain_of(first, "x", "up"), chain_of(first, "y", "down")
    grad_mid = first["grad_mid"]
    if regular:
        grad_mid = meet(grad_mid, x1, y1, a1)
        a1, z1 = combine([[a1], [x1, y1]], me, "sum2")
        grad_mid = after(grad_mid, a1, z1)
        start(a1, z1, x0, y0)
    before0 = attention_backward(0, grad_mid, padded, early0, 0, groups - 1, store=False)
    if regular:
        before0["row_sums"] = meet(before0["row_sums"], a1, x0, y0, z1)
        a1, x0, y0, z1 = combine([[a1], [x0], [y0], [z1]], me, "sum3")
        grad_mid = after(grad_mid, a1, x0, y0, z1)
        start(a1, x0, y0, z1)
    small_parts = None
    if regular:
        small_parts = {
            "mlp_rows0": first["row_sums"], "up_rows0": first["up_rows"],
            "row_sums1": back1["row_sums"], "qkv_rows1": back1["qkv_rows"],
            "mlp_rows1": last["row_sums"], "up_rows1": last["up_rows"],
            "bias_grad1": back1["bias_grad"], "final_rows": last["final_rows"],
            "head_rows": last["head_rows"], "loss": last["loss"],
        }
    back0 = attention_backward(
        0, grad_mid, padded, saved0, groups - 1, 1, before0, early0, collect=small_parts
    )
    a0 = chain_of(back0, "a", "attn")
    if regular:
        b0 = chain_of(back0, "b", pair_at=widths["attn"] - widths["attn"] * 2 // 3)
        waiting = (a1, x0, y0, z1)
        a0.send, b0.send, *got = tie(a0.send, b0.send, *[chain.received for chain in waiting])
        for chain, array in zip(waiting, got):
            chain.received = array

    if regular:
        start(a0, b0)
        x0, y0 = combine([[x0], [y0]], me, "sum5")
        start(x0, y0)
        a0.received, b0.received, x0.keep = tie(a0.received, b0.received, x0.keep)
        a0, b0 = combine([[a0], [b0]], me, "sum6")
        start(a0, b0)
        (z0,) = combine([[x0, y0, a1]], me, "sum7")
        start(z0)
        a0, b0 = combine([[a0], [b0]], me, "sum8")
        start(a0, b0)
        (z0,) = combine([[z0]], me, "sum9")
        start(z0)
        own1, square1 = finish(z1, "own1")
        (a0,) = combine([[a0, b0]], me, "sum10")
        start(a0)
        own0, square0 = finish(z0, "own0")
        (a0,) = combine([[a0]], me, "sum11")
        start(a0)
        own_attn, message = finish_pair(a0, [square0, square1], device_count, share, "own_attn")
    else:
        square, own_parts = jnp.zeros((1, 128), F32), []
        for chain in (a0, x0, y0, a1, x1, y1):
            start(chain)
            while chain.steps:
                (chain,) = combine([[chain]], me, "sum")
                start(chain)
            part, part_square = finish(chain, "own")
            square = square + part_square
            own_parts.append(part)
        own_attn = own_parts[0]
        own0, own1 = jnp.concatenate(own_parts[1:4], 1), jnp.concatenate(own_parts[4:], 1)
        (rows_all,) = small_call(
            lambda *refs: collect_rows(
                layers, head_real, share - 1, refs[:-2], refs[-2], refs[-1]
            ),
            "collect",
            [part[name] for part in ((first, back0), (last, back1))
             for part, name in (
                 (part[1], "row_sums"), (part[1], "qkv_rows"), (part[0], "row_sums"),
                 (part[0], "up_rows"), (part[1], "bias_grad"))]
            + [last["final_rows"], last["head_rows"], last["loss"]],
            [((device_count, share), F32)],
            stream=True,
            scratch=[pltpu.VMEM((HEADS * SLOT, 128), F32)],
        )
        rows_all = lax.all_to_all(rows_all, ("win", "ch"), 0, 0, tiled=True)
        message = jnp.concatenate([jnp.sum(rows_all, 0, keepdims=True), square], 1)
        message = jnp.broadcast_to(message, (device_count, share + 128))
    message = lax.all_to_all(message, ("win", "ch"), 0, 0, tiled=True)
    starts = [
        {"attn": (1, 0), "up": (2, 0), "down": (2, widths["up"])},
        {
            "attn": (2, widths["up"] + widths["down"]), "up": (0, 0), "head": (0, widths["up"]),
            "down": (0, widths["up"] + widths["head"]),
        },
    ]
    arrays = [
        [w_qkv, m_qkv, v_qkv], [w_proj, m_proj, v_proj], [w_fc1, m_fc1, v_fc1],
        [w_fc2, m_fc2, v_fc2], [w_head, m_head, v_head], [vectors, m_vec, v_vec],
        [rel_table, m_rel, v_rel],
    ]
    turns = {3: (0, 2, 1), 6: (2, 0, 1)}
    turned = [
        a.transpose(turns[n]) if n in turns else a for n, group in enumerate(arrays) for a in group
    ]
    results = small_call(
        functools.partial(
            update_kernel, starts, widths,
            (vectors.shape[0], layers * HEADS, offsets, share, share - 1),
        ),
        "update",
        [own1, own_attn, own0, message] + turned,
        [((1, 1), F32)] * 2 + [(a.shape, F32) for a in turned],
        stream=True,
    )
    loss_total, grad_norm, *results = results
    outs = [loss_total[0, 0], grad_norm[0, 0]]
    for n in range(0, len(results), 3):
        back = {3: (0, 2, 1), 6: (1, 2, 0)}.get(n // 3)
        outs += [r if back is None else r.transpose(back) for r in results[n : n + 3]]
    return tuple(outs)


def solution(mesh):
    cut = P(None, "win", "ch")
    down = P(None, "ch", "win")
    head = P("win", "ch")
    rows = P(None, ("win", "ch"))
    in_specs = (
        (P(None, ("win", "ch"), None, None),) + (rows,) * 4 + (P(),)
        + (cut,) * 9 + (down,) * 3 + (head,) * 3 + (P(),) * 6
    )
    out_specs = (P(),) * 2 + (cut,) * 9 + (down,) * 3 + (head,) * 3 + (P(),) * 6
    return jax.shard_map(
        per_device, mesh=mesh, in_specs=in_specs, out_specs=out_specs, check_vma=False
    )
```

```python
import functools

import jax
import jax.numpy as jnp
import numpy as np
from jax import lax
from jax.experimental import pallas as pl
from jax.experimental.pallas import tpu as pltpu
from jax.sharding import PartitionSpec as P

C = 384
HID = 1536
CLASSES = 1000
CLASS_PAD = 1024
WSIDE = 7
GRID = 14
STEP = 10
HEADS = 12
PER_LAYER = 8 + HID // C
DEPTH = 32
CELLS = GRID * GRID
ROWS = 208
AREA = WSIDE * WSIDE
SLOT = 64
NWIN = 4
NGRP = 3
PACK = 4
WROWS = NWIN * SLOT
LANES = PACK * SLOT

NORM_EPS = 1e-05
CLIP_NORM = 0.05
LEARN_RATE = 0.04
SMALL_RATE = 0.2
DECAY_RATE = 0.05
ADAM_EPS = 1e-08
MASKED = -1e30
SCALE = DEPTH ** (-0.5)
F32 = jnp.float32
BF16 = jnp.bfloat16
NN = (((1,), (0,)), ((), ()))
NT = (((1,), (1,)), ((), ()))
TN = (((0,), (0,)), ((), ()))
VMEM_LIMIT = 24 * 1024 * 1024
GROUP = 2
CHUNK = 512


def dot(a, b, dims=NN):
    return lax.dot_general(a, b, dims, preferred_element_type=F32)


@functools.lru_cache(None)
def window_tables(shifted):
    perm = np.zeros((WROWS, ROWS), np.float32)
    row_limit = np.full((NWIN, SLOT, 2 * SLOT), 99, np.int32)
    col_limit = np.full((NWIN, SLOT, 2 * SLOT), 99, np.int32)
    shift = WSIDE // 2 if shifted else 0

    def band(v):
        return 0 if v < GRID - WSIDE else (1 if v < GRID - WSIDE // 2 else 2)

    for window in range(NWIN):
        wr, wc = divmod(window, GRID // WSIDE)
        place = []
        for j in range(AREA):
            r, c = wr * WSIDE + j // WSIDE, wc * WSIDE + j % WSIDE
            region = 3 * band(r) + band(c) if shifted else 0
            source = ((r + shift) % GRID, (c + shift) % GRID)
            place.append((region, source))
            perm[window * SLOT + j, source[0] * GRID + source[1]] = 1
        for j in range(SLOT):
            for i in range(SLOT):
                if i == j:
                    pair = (-1, -1)
                elif i < AREA and j < AREA and place[i][0] == place[j][0]:
                    pair = place[j][1]
                else:
                    pair = (99, 99)
                row_limit[window, j, i::SLOT] = pair[0]
                col_limit[window, j, i::SLOT] = pair[1]
    return perm, row_limit, col_limit


@functools.lru_cache(None)
def relative_onehot():
    span = 2 * WSIDE - 1
    onehot = np.zeros((span * span, SLOT, SLOT), np.float32)
    for i in range(AREA):
        for j in range(AREA):
            row, col = i // WSIDE - j // WSIDE, i % WSIDE - j % WSIDE
            onehot[(row + WSIDE - 1) * span + col + WSIDE - 1, j, i] = 1
    return onehot.reshape(span * span, SLOT * SLOT)


def norm_parts(field):
    average = jnp.mean(field, -1, keepdims=True)
    centered = field - average
    spread = jnp.mean(centered * centered, -1, keepdims=True)
    rate = lax.rsqrt(spread + NORM_EPS)
    return centered * rate, rate


def norm_back(grad, hat, rate, gain):
    scaled = grad * gain
    return rate * (
        scaled
        - jnp.mean(scaled, -1, keepdims=True)
        - hat * jnp.mean(scaled * hat, -1, keepdims=True)
    )


def col_sum(field):
    return jnp.sum(field, 0, keepdims=True)


def head_masks(dtype):
    lane = lax.broadcasted_iota(jnp.int32, (SLOT, 128), 1)
    return [((lane // DEPTH) == h).astype(F32).astype(dtype) for h in range(PACK)]


def spread_heads(block, masks):
    return jnp.concatenate([block * m for m in masks], 0)


def relative_owners(bits):
    owners = []
    for index in range(1 << len(bits)):
        offset = 0
        for n, (_, bit) in enumerate(bits):
            offset |= ((index >> (len(bits) - 1 - n)) & 1) << bit
        owners.append(offset)
    return owners


def owner_part(ref, owner, width, start, size):
    if len(ref.shape) == 3:
        return ref.at[owner, :, start : start + size]
    return ref.at[:, pl.ds(pl.multiple_of(owner * width + start, 128), size)]


def load_blocks(pieces, target, width, sem, me_ref):
    for ref, owners, cut in pieces:
        if owners is None:
            pltpu.make_async_copy(ref, target, sem).start()
            continue
        source, size, start = cut
        for n, owner in enumerate(owners):
            pltpu.make_async_copy(
                ref.at[n, :, source : source + size],
                owner_part(target, me_ref[1] ^ owner, width, start, size),
                sem,
            ).start()


def wait_all(ref, sem):
    pltpu.make_async_copy(ref, ref, sem).wait()


def sem_of(sems, number):
    return sems[number] if isinstance(sems, list) else sems.at[number]


def store_blocks(source, outs, width, sems, me_ref):
    for number, (ref, owners, start, source_start, size) in enumerate(outs):
        if owners is None:
            copy = pltpu.make_async_copy(source, ref, sem_of(sems, number))
            copy.start()
            copy.wait()
            continue
        for n, owner in enumerate(owners):
            pltpu.make_async_copy(
                owner_part(source, me_ref[1] ^ owner, width, source_start, size),
                ref.at[n, :, start : start + size],
                sem_of(sems, number),
            ).start()


def wait_blocks(outs, sems):
    for number, (ref, owners, *_) in enumerate(outs):
        if owners is not None:
            wait_all(ref, sems.at[number])


def join_attention(stage, w_qkv, w_proj):
    owners = stage.shape[0]
    wide, narrow = 3 * C // owners, C // owners
    w_qkv[...] = jnp.concatenate([stage[n, :, :wide] for n in range(owners)], 1)
    w_proj[...] = jnp.concatenate([stage[n, :, wide : wide + narrow] for n in range(owners)], 1)


def pick_heads(first, second):
    lane = lax.broadcasted_iota(jnp.int32, (DEPTH, 128), 1)
    parts = []
    for h in range(PACK):
        at = (slice(h * DEPTH, (h + 1) * DEPTH), slice(h // 2 * 128, (h // 2 + 1) * 128))
        one, two = first[at], second[at]
        if h % 2:
            one = pltpu.roll(one, SLOT, 1)
        else:
            two = pltpu.roll(two, SLOT, 1)
        parts.append(jnp.where(lane < SLOT, one, two))
    return jnp.concatenate(parts, 0)


def apply_pair(rows_ref, cut, eye, first, second):
    turned = dot(eye, rows_ref[cut], NT).astype(BF16)
    empty = jnp.zeros_like(first)
    full = dot(
        turned,
        jnp.concatenate(
            [jnp.concatenate([first, empty], 1), jnp.concatenate([empty, second], 1)], 0
        ),
    )
    return pick_heads(full[:, :LANES], full[:, LANES:])


def identity():
    shape = (128, 128)
    same = lax.broadcasted_iota(jnp.int32, shape, 0) == lax.broadcasted_iota(jnp.int32, shape, 1)
    return same.astype(F32).astype(BF16)


def pipelined(units, first, second, third):
    ones, twos = {}, {}
    count = len(units)
    for n in range(count + 2):
        if n < count:
            ones[n] = first(*units[n])
        if 1 <= n <= count:
            twos[n - 1] = second(*units[n - 1], ones.pop(n - 1))
        if n >= 2:
            third(*units[n - 2], twos.pop(n - 2))


def each_image(images, body, unrolled):
    lax.fori_loop(0, images, body, 0, unroll=images if unrolled else 1)


def forward_attention(
    field, sizes, w_qkv, w_proj, perm, perm_t, row_limit, col_limit, bias, small, qkv_bias,
    qkv_ref, prob_ref, windowed_ref, mixed_ref, attended_ref, unrolled,
):
    hat, _ = norm_parts(field)
    normed = (hat * small[0:1] + small[1:2]).astype(BF16)
    images = len(sizes)
    for b in range(images):
        windowed_ref[b] = dot(perm[...], normed[b * ROWS : (b + 1) * ROWS]).astype(BF16)
    flat = windowed_ref[...].reshape(images * WROWS, C)
    qkv = (dot(flat, w_qkv[...]) + qkv_bias).astype(BF16)
    qkv_ref[...] = qkv.reshape(images, WROWS, 3 * C)
    low_masks = head_masks(BF16)
    eye = identity()
    def one_image(b, carry):
        rows, cols = sizes[0]
        for n in range(1, images):
            rows = jnp.where(b == n, sizes[n][0], rows)
            cols = jnp.where(b == n, sizes[n][1], cols)
        blocks = {}
        for w in range(NWIN):
            allowed = (row_limit[w] < rows) & (col_limit[w] < cols)
            blocks[w] = jnp.where(allowed, 0.0, MASKED).astype(F32)
        attend(b, blocks)
        return carry

    def attend(b, blocks):
        units = [(b, pair, g, blocks) for pair in range(NWIN // 2) for g in range(NGRP)]
        pipelined(units, raw_scores, softmax, apply)

    def raw_scores(b, pair, g, blocks):
        results = []
        for w in (2 * pair, 2 * pair + 1):
            at = slice(w * SLOT, (w + 1) * SLOT)
            query = qkv_ref[b, at, g * 128 : (g + 1) * 128]
            key = qkv_ref[b, at, C + g * 128 : C + (g + 1) * 128]
            results.append(dot(key, spread_heads(query, low_masks), NT))
        return results

    def softmax(b, pair, g, blocks, raw):
        probs = []
        for n, score in enumerate(raw):
            w = 2 * pair + n
            block = jnp.concatenate([blocks[w]] * 2, 1)
            score = score * SCALE + (bias[g] + block)
            top = jnp.max(score, 0, keepdims=True)
            expo = jnp.exp(score - top)
            prob = (expo * (1.0 / jnp.sum(expo, 0, keepdims=True))).astype(BF16)
            prob_ref[b, w, g] = prob
            probs.append(prob)
        return probs

    def apply(b, pair, g, blocks, probs):
        both = slice(pair * 2 * SLOT, (pair + 1) * 2 * SLOT)
        value = (b, both, slice(2 * C + g * 128, 2 * C + (g + 1) * 128))
        mixed_ref[b, g * 128 : (g + 1) * 128, both] = apply_pair(qkv_ref, value, eye, *probs).astype(BF16)

    each_image(images, one_image, unrolled)
    for b in range(images):
        attended_ref[b] = dot(perm_t[...], mixed_ref[b], NT).astype(BF16)
    attended = attended_ref[...].reshape(images * ROWS, C)
    middle = field + dot(attended, w_proj[...]) + small[4:5]
    return normed, middle


def forward_mlp(middle, w_up, w_down, small, up_bias, active_ref, slope_ref):
    hat, _ = norm_parts(middle)
    mlp_in = (hat * small[5:6] + small[6:7]).astype(BF16)
    branch = jnp.zeros(middle.shape, F32)
    width = CHUNK
    for part in range(HID // width):
        at = slice(part * width, (part + 1) * width)
        pre = dot(mlp_in, w_up[:, at]) + up_bias[:, at]
        half = 0.5 * (1.0 + lax.erf(pre * (0.5**0.5)))
        active = (pre * half).astype(BF16)
        slope = half + pre * (jnp.exp(-0.5 * pre * pre) * ((2.0 * np.pi) ** -0.5))
        active_ref[..., at] = active.reshape(active_ref.shape[:-1] + (width,))
        slope_ref[..., at] = slope.astype(BF16).reshape(slope_ref.shape[:-1] + (width,))
        branch = branch + dot(active, w_down[:, at], NT)
    return mlp_in, middle + branch + small[7:8]


def backward_mlp(
    grad, middle, slope_ref, w_up, w_down, small, low_ref, pre_ref, rows_ref, up_rows_ref, place
):
    low = grad.astype(BF16)
    low_ref[place, :] = low
    rows_ref[7:8, :] += col_sum(low.astype(F32))
    normed_grad = jnp.zeros(grad.shape, F32)
    width = CHUNK
    for part in range(HID // width):
        at = slice(part * width, (part + 1) * width)
        slope = slope_ref[..., at].reshape(-1, width).astype(F32)
        pre = (dot(low, w_down[:, at]) * slope).astype(BF16)
        pre_ref[place, at] = pre
        up_rows_ref[:, at] += col_sum(pre.astype(F32))
        normed_grad = normed_grad + dot(pre, w_up[:, at], NT)
    hat, rate = norm_parts(middle)
    rows_ref[5:6, :] += col_sum(normed_grad * hat)
    rows_ref[6:7, :] += col_sum(normed_grad)
    return norm_back(normed_grad, hat, rate, small[5:6]) + grad


def backward_attention(
    grad_mid, field, qkv_ref, prob_ref, w_qkv, w_proj, perm, perm_t, small,
    spread_ref, dq_ref, dkv_ref, attn_ref, joined_ref, rows_ref, qkv_rows_ref, bias_grad_ref, start,
    need_grad, unrolled,
):
    images = qkv_ref.shape[0]
    place = pl.ds(start, images * ROWS)
    attn = grad_mid.astype(BF16)
    attn_ref[place, :] = attn
    rows_ref[4:5, :] += col_sum(attn.astype(F32))
    joined = dot(attn, w_proj[...], NT).astype(BF16)
    for b in range(images):
        joined_ref[b] = dot(perm[...], joined[b * ROWS : (b + 1) * ROWS]).astype(BF16)
    low_masks = head_masks(BF16)
    eye = identity()

    def cut(n, g):
        return slice(n * C + g * 128, n * C + (g + 1) * 128)

    def prob_grads(b, pair, g):
        results = []
        for w in (2 * pair, 2 * pair + 1):
            at = slice(w * SLOT, (w + 1) * SLOT)
            out = spread_heads(joined_ref[b, at, cut(0, g)], low_masks)
            results.append(dot(qkv_ref[b, at, cut(2, g)], out, NT))
            dkv_ref[b, at, cut(1, g)] = dot(prob_ref[b, 2 * pair + len(results) - 1, g], out).astype(BF16)
        return results

    def score_grads(b, pair, g, grads):
        results = []
        for n, prob_grad in enumerate(grads):
            wide = prob_ref[b, 2 * pair + n, g].astype(F32)
            weighted = wide * prob_grad
            score = weighted - wide * jnp.sum(weighted, 0, keepdims=True)
            bias_grad_ref[g] += score
            results.append(score.astype(BF16))
        return results

    def products(b, pair, g, scores):
        both = slice(pair * 2 * SLOT, (pair + 1) * 2 * SLOT)
        for n, score in enumerate(scores):
            w = 2 * pair + n
            at = slice(w * SLOT, (w + 1) * SLOT)
            query = spread_heads(qkv_ref[b, at, cut(0, g)], low_masks)
            dkv_ref[b, at, cut(0, g)] = (dot(score, query) * SCALE).astype(BF16)
        dq_ref[b, cut(0, g), both] = (
            apply_pair(qkv_ref, (b, both, cut(1, g)), eye, *scores) * SCALE
        ).astype(BF16)

    def one_image(b, carry):
        units = [(b, pair, g) for pair in range(NWIN // 2) for g in range(NGRP)]
        pipelined(units, prob_grads, score_grads, products)
        return carry

    each_image(images, one_image, unrolled)
    for b in range(images):
        rows = pl.ds(pl.multiple_of(start + b * ROWS, 16), ROWS)
        spread_ref[rows, :C] = dot(perm_t[...], dq_ref[b], NT).astype(BF16)
        spread_ref[rows, C:] = dot(perm_t[...], dkv_ref[b]).astype(BF16)
    back = spread_ref[place, :]
    qkv_rows_ref[:, :C] += col_sum(back[:, :C].astype(F32))
    qkv_rows_ref[:, 2 * C :] += col_sum(back[:, 2 * C :].astype(F32))
    normed_grad = dot(back, w_qkv[...], NT)
    hat, rate = norm_parts(field)
    rows_ref[0:1, :] += col_sum(normed_grad * hat)
    rows_ref[1:2, :] += col_sum(normed_grad)
    if not need_grad:
        return None
    return norm_back(normed_grad, hat, rate, small[0:1]) + grad_mid


def image_place():
    return pl.ds(pl.multiple_of(pl.program_id(0) * GROUP * ROWS, 16), GROUP * ROWS)


def flat(ref):
    return ref[...].reshape(-1, ref.shape[-1])


def rows_in(k, name):
    if hasattr(k, name):
        return flat(getattr(k, name))
    rows = flat(getattr(k, name + "0"))
    number = 1
    while hasattr(k, f"{name}{number}"):
        rows = jnp.where(pl.program_id(0) == number, flat(getattr(k, f"{name}{number}")), rows)
        number += 1
    return rows


def put_rows(ref, value):
    ref[...] = value.reshape(ref.shape)


def is_first():
    return pl.program_id(0) == 0


def is_last():
    return pl.program_id(0) == pl.num_programs(0) - 1


def clear(*refs):
    @pl.when(is_first())
    def _():
        for ref in refs:
            ref[...] = jnp.zeros(ref.shape, ref.dtype)


class Names:
    def __init__(self, **refs):
        self.__dict__.update(refs)


def fetch_attention(k, plan):
    if not plan.sources:
        return

    @pl.when(is_first())
    def _():
        load_blocks(plan.pieces(k, "attn"), k.stage, plan.widths["attn"], k.load_sem.at[0], k.me)
        wait_all(k.stage, k.load_sem.at[0])
        join_attention(k.stage, k.w_qkv, k.w_proj)
        for n, (source, target) in enumerate(((k.w_qkv, k.qkv_out), (k.w_proj, k.proj_out))):
            pltpu.make_async_copy(source, target, k.out_sem.at[n]).start()


def fetch_mlp(k, plan):
    @pl.when(is_first())
    def _():
        load_blocks(plan.pieces(k, "down"), k.w_down, plan.widths["down"], k.load_sem.at[1], k.me)
        load_blocks(plan.pieces(k, "up"), k.w_up, plan.widths["up"], k.load_sem.at[2], k.me)
        wait_all(k.w_down, k.load_sem.at[1])
        wait_all(k.w_up, k.load_sem.at[2])


def group_images(k, group=0):
    images = k.rows.shape[1]
    first = (pl.program_id(0) + group) * GROUP
    return [((first + b) // images, (first + b) % images) for b in range(GROUP)]


def group_sizes(k, group=0):
    return [(k.rows[m, n], k.cols[m, n]) for m, n in group_images(k, group)]


def small_rows(k, plan):
    return k.vec[plan.layer * PER_LAYER : plan.layer * PER_LAYER + 8]


def joined_rows(k, start, end):
    return jnp.concatenate([k.vec[n : n + 1] for n in range(start, end)], 1)


def up_bias_row(k, plan):
    return joined_rows(k, plan.layer * PER_LAYER + 8, (plan.layer + 1) * PER_LAYER)


def attention_forward_kernel(k, plan):
    fetch_attention(k, plan)
    small = small_rows(k, plan)
    qkv_bias = jnp.concatenate([small[2:3], jnp.zeros((1, C), F32), small[3:4]], 1)
    normed, middle = forward_attention(
        flat(k.field).astype(F32), group_sizes(k, plan.group), k.w_qkv, k.w_proj, k.perm, k.perm_t,
        k.row_limit, k.col_limit, k.bias, small, qkv_bias, k.qkv, k.prob, k.windowed,
        k.mixed, k.attended, True,
    )
    put_rows(k.normed, normed)
    put_rows(k.middle, middle)
    if not plan.sources:
        return

    @pl.when(is_last())
    def _():
        wait_all(k.w_qkv, k.out_sem.at[0])
        wait_all(k.w_proj, k.out_sem.at[1])


def first_mlp_kernel(k, plan):
    fetch_mlp(k, plan)

    @pl.when(is_first())
    def _():
        for n, (source, target) in enumerate(((k.w_down, k.down_out), (k.w_up, k.up_out))):
            pltpu.make_async_copy(source, target, k.out_sem.at[n]).start()

    mlp_in, result = forward_mlp(
        rows_in(k, "middle"), k.w_up, k.w_down, small_rows(k, plan), up_bias_row(k, plan), k.active,
        k.slope,
    )
    put_rows(k.mlp_in, mlp_in)
    put_rows(k.result, result)

    @pl.when(is_last())
    def _():
        wait_all(k.w_down, k.out_sem.at[0])
        wait_all(k.w_up, k.out_sem.at[1])


def store_mlp_grads(k, plan):
    for at in range(0, HID, CHUNK):
        k.up_grad[:, at : at + CHUNK] = dot(k.mlp_all[...], k.pre_all[:, at : at + CHUNK], TN).astype(BF16)
    store_blocks(k.up_grad, plan.outs(k, "up"), plan.widths["up"], k.sem_x, k.me)
    for at in range(0, HID, CHUNK):
        k.down_grad[:, at : at + CHUNK] = dot(k.low_all[...], k.active_all[:, at : at + CHUNK], TN).astype(BF16)
    store_blocks(k.down_grad, plan.outs(k, "down"), plan.widths["down"], k.sem_y, k.me)


def wait_mlp_grads(k, plan):
    wait_blocks(plan.outs(k, "up"), k.sem_x)
    wait_blocks(plan.outs(k, "down"), k.sem_y)


def head_pass(k, plan, result, sizes, total_images):
    first = pl.program_id(0) * GROUP
    base = plan.layers * PER_LAYER
    gain = k.vec[base : base + 1]
    hat, rate = norm_parts(result)
    final = hat * gain + k.vec[base + 1 : base + 2]
    places = group_images(k)
    owners, _, width = k.w_head.shape
    row = lax.broadcasted_iota(jnp.int32, (16, 1), 0)
    pooled = jnp.zeros((16, C), F32)
    own = other = jnp.full((16, 1), -1, jnp.int32)
    mixing = jnp.zeros((16, 1), F32)
    shares = []
    for b, (rows, cols) in enumerate(sizes):
        inside = ((k.cell_row[...] < rows) & (k.cell_col[...] < cols)).astype(F32)
        count = (rows * cols).astype(F32)
        mean = col_sum(final[b * ROWS : (b + 1) * ROWS] * inside) / count
        shares.append(inside / count)
        pooled = jnp.where(row == b, mean, pooled)
        m, n = places[b]
        mine = (k.me[0] * owners + k.me[1]) * k.rows.shape[1] + n
        own = jnp.where(row == b, k.labels[m, mine], own)
        other = jnp.where(row == b, k.labels[m, k.partner[m, n]], other)
        mixing = jnp.where(row == b, k.mix[m, n].astype(F32) / 16.0, mixing)
    pooled = pooled.astype(BF16)
    classes = owners * width
    real = CLASSES // owners
    bias = joined_rows(k, base + 2, base + 2 - (-CLASSES // C))
    empty = jnp.full((1, width - real), MASKED, F32)
    bias = jnp.concatenate(
        [part for n in range(owners) for part in (bias[:, n * real : (n + 1) * real], empty)], 1
    )
    logits = jnp.concatenate([dot(pooled, k.w_head[n]) for n in range(owners)], 1)
    logits = logits + bias
    top = jnp.max(logits, -1, keepdims=True)
    expo = jnp.exp(logits - top)
    log_probs = logits - top - jnp.log(jnp.sum(expo, -1, keepdims=True))
    lane = lax.broadcasted_iota(jnp.int32, (16, classes), 1)
    label = lane // width * real + lane % width
    label = jnp.where(lane % width < real, label, -2)
    target = jnp.where(label == own, mixing, 0.0)
    target = target + jnp.where(label == other, 1.0 - mixing, 0.0)
    loss = jnp.where(target > 0.0, target * log_probs, 0.0)
    loss = jnp.sum(jnp.sum(loss, -1, keepdims=True), 0, keepdims=True)
    k.loss[...] -= jnp.broadcast_to(loss, k.loss.shape)
    logit_grad = jnp.where(row < GROUP, (jnp.exp(log_probs) - target) / total_images, 0.0)
    logit_low = logit_grad.astype(BF16)
    wide = logit_low.astype(F32)
    k.head_rows[...] += col_sum(wide)
    for b in range(GROUP):
        k.pooled_all[pl.ds(first + b, 1), :] = pooled[b : b + 1].astype(F32)
        k.logit_all[pl.ds(first + b, 1), :] = wide[b : b + 1]
    pooled_grad = jnp.zeros((16, C), F32)
    for n in range(owners):
        pooled_grad += dot(logit_low[:, n * width : (n + 1) * width], k.w_head[n], NT)
    final_grad = jnp.concatenate(
        [pooled_grad[b : b + 1] * share for b, share in enumerate(shares)], 0
    )
    k.final_rows[0:1, :] += col_sum(final_grad * hat)
    k.final_rows[1:2, :] += col_sum(final_grad)
    return norm_back(final_grad, hat, rate, gain)


def last_mlp_kernel(k, plan, total_images):
    place = image_place()

    @pl.when(is_first())
    def _():
        load_blocks(plan.pieces(k, "head"), k.w_head, plan.widths["head"], k.load_sem.at[3], k.me)

    fetch_mlp(k, plan)

    @pl.when(is_first())
    def _():
        wait_all(k.w_head, k.load_sem.at[3])

    clear(k.row_sums, k.up_rows, k.final_rows, k.head_rows, k.loss, k.pooled_all, k.logit_all)
    middle = rows_in(k, "middle")
    mlp_in, result = forward_mlp(
        middle, k.w_up, k.w_down, small_rows(k, plan), up_bias_row(k, plan), k.active_all.at[place], k.slope
    )
    k.mlp_all[place, :] = mlp_in
    grad = head_pass(k, plan, result, group_sizes(k), total_images)
    put_rows(k.grad_mid, backward_mlp(
        grad, rows_in(k, "middle"), k.slope, k.w_up, k.w_down, small_rows(k, plan), k.low_all, k.pre_all,
        k.row_sums, k.up_rows, place,
    ))

    @pl.when(is_last())
    def _():
        store_mlp_grads(k, plan)
        total = dot(k.pooled_all[...].astype(BF16), k.logit_all[...].astype(BF16), TN).astype(BF16)
        owners, _, width = k.head_grad.shape
        for n in range(owners):
            k.head_grad[n] = total[:, n * width : (n + 1) * width]
        store_blocks(
            k.head_grad, plan.outs(k, "head"), plan.widths["head"],
            [k.sem_x.at[0], k.sem_x.at[1], k.sem_y.at[0], k.sem_y.at[1]], k.me,
        )
        wait_mlp_grads(k, plan)


def backward_mlp_kernel(k, plan):
    clear(k.row_sums, k.up_rows)
    place = image_place()
    k.mlp_all[place, :] = flat(k.mlp_in)
    k.active_all[place, :] = flat(k.active)
    put_rows(k.grad_mid, backward_mlp(
        rows_in(k, "grad"), rows_in(k, "middle"), k.slope, k.w_up, k.w_down, small_rows(k, plan), k.low_all, k.pre_all,
        k.row_sums, k.up_rows, place,
    ))

    @pl.when(is_last())
    def _():
        store_mlp_grads(k, plan)
        wait_mlp_grads(k, plan)


def backward_attention_kernel(k, plan, earlier, need_grad):
    sums = ("row_sums", "qkv_rows", "bias_grad")
    if earlier:
        @pl.when(is_first())
        def _():
            for name in sums:
                getattr(k, name)[...] = getattr(k, name + "_in")[...]
    else:
        clear(*[getattr(k, name) for name in sums])
    start = pl.multiple_of(earlier * ROWS + pl.program_id(0) * GROUP * ROWS, 16)
    grad = backward_attention(
        flat(k.grad_mid), flat(k.field).astype(F32), k.qkv, k.prob, k.w_qkv, k.w_proj, k.perm,
        k.perm_t, small_rows(k, plan), k.spread_all, k.dq, k.dkv, k.attn_all, k.joined, k.row_sums,
        k.qkv_rows, k.bias_grad, start, need_grad, True,
    )
    if need_grad:
        put_rows(k.grad, grad)
    if "attn" not in plan.targets:
        return
    place = pl.ds(start, GROUP * ROWS)
    k.normed_all[place, :] = flat(k.normed)
    k.attended_all[place, :] = flat(k.attended)

    @pl.when(is_last())
    def _():
        if earlier:
            before = slice(0, earlier * ROWS)
            k.normed_all[before, :] = flat(k.normed_in)
            k.attended_all[before, :] = flat(k.attended_in)
            k.spread_all[before, :] = k.spread_in[...]
            k.attn_all[before, :] = k.attn_in[...]
        owners, _, _ = k.attn_grad.shape
        wide, narrow = 3 * C // owners, C // owners
        if plan.collect is not None:
            layers, head_real, loss_at, near = plan.collect
            own = [k.row_sums, k.qkv_rows, k.mlp_rows0, k.up_rows0, k.bias_grad]
            collect_rows(
                layers, head_real, loss_at,
                own + [k.row_sums1, k.qkv_rows1, k.mlp_rows1, k.up_rows1, k.bias_grad1]
                + [k.final_rows, k.head_rows, k.loss],
                k.small_rows, k.spread_table,
            )
            pair_rows(k.small_rows, owners, near, k.me, k.pairs)
            for flip, (ref, *_) in enumerate(plan.outs(k, "attn")[2:]):
                width = ref.shape[2]
                pltpu.make_async_copy(
                    k.pairs.at[flip], ref.at[:, :, width - 128 : width], k.sem_a.at[2 + flip]
                ).start()
        total = dot(k.normed_all[...], k.spread_all[...], TN).astype(BF16)
        for n in range(owners):
            k.attn_grad[n, :, :wide] = total[:, n * wide : (n + 1) * wide]
        total = dot(k.attended_all[...], k.attn_all[...], TN).astype(BF16)
        for n in range(owners):
            k.attn_grad[n, :, wide:] = total[:, n * narrow : (n + 1) * narrow]
        store_blocks(k.attn_grad, plan.outs(k, "attn"), plan.widths["attn"], k.sem_a, k.me)
        wait_blocks(plan.outs(k, "attn"), k.sem_a)


class Plan:
    def __init__(self, widths, layer, layers):
        self.widths, self.layer, self.layers = widths, layer, layers
        self.sources = {}
        self.targets = {}
        self.collect = None
        self.group = 0

    def pieces(self, k, name):
        return [(getattr(k, ref), owners, cut) for ref, owners, cut in self.sources[name]]

    def outs(self, k, name):
        return [(getattr(k, ref), *rest) for ref, *rest in self.targets[name]]


def whole(shape):
    return pl.BlockSpec(shape, lambda i: (0,) * len(shape))


def per_image(*shape, first=0):
    return pl.BlockSpec((GROUP,) + shape, lambda i: (i + first,) + (0,) * len(shape))


SCALARS = pl.BlockSpec(memory_space=pltpu.SMEM)
FAR = pl.BlockSpec(memory_space=pl.ANY)
NEAR = pl.BlockSpec(memory_space=pltpu.VMEM)


def call(body, name, groups, ins, outs, scratch, flops):
    def kernel(*refs):
        body(Names(**dict(zip(list(ins) + list(outs) + list(scratch), refs))))

    moved = sum(a.size * a.dtype.itemsize for _, a in ins.values())
    results = pl.pallas_call(
        kernel,
        grid=(groups,),
        in_specs=[spec for spec, _ in ins.values()],
        out_specs=[spec for spec, _, _ in outs.values()],
        out_shape=[jax.ShapeDtypeStruct(dims, dtype) for _, dims, dtype in outs.values()],
        scratch_shapes=list(scratch.values()),
        compiler_params=pltpu.CompilerParams(
            dimension_semantics=("arbitrary",), vmem_limit_bytes=VMEM_LIMIT
        ),
        cost_estimate=pl.CostEstimate(flops=int(8 * flops), bytes_accessed=int(moved), transcendentals=0),
        name=name,
    )(*[array for _, array in ins.values()])
    return dict(zip(outs, results))


def exchange(array, step):
    axis, bit = step
    size = lax.axis_size(axis)
    return lax.ppermute(array, axis, [(i, i ^ (1 << bit)) for i in range(size)])


class Held:
    def __init__(self, array, dims=()):
        self.array, self.dims = array, list(dims)


def stack_blocks(parts, me, name, cuts=None):
    cuts = cuts or [None] * len(parts)
    args, outs, results = [], [], []
    for (held, received, step), cut in zip(parts, cuts):
        count, rows, columns = held.array.shape
        args += [held.array, received]
        axis, bit = step
        place = sum(d[0] == "win" and d[1] < bit for d in held.dims) if axis == "win" else len(held.dims)
        at = len(held.dims) - place
        dims = held.dims[:at] + [step] + held.dims[at:]
        bounds = [0, *(cut or ()), columns]
        pieces = list(zip(bounds, bounds[1:]))
        outs += [((2 * count, rows, end - start), BF16) for start, end in pieces]
        results.append((place, axis, bit, pieces, dims))

    def kernel(me_ref, *refs):
        ins, targets = list(refs[: len(args)]), list(refs[len(args) :])
        for place, axis, bit, pieces, _ in results:
            held, received = ins.pop(0), ins.pop(0)
            mine = (me_ref[0] >> bit) & 1 if axis == "win" else 0
            for start, end in pieces:
                out = targets.pop(0)
                for n in range(held.shape[0]):
                    base = (n >> place << (place + 1)) + (n & ((1 << place) - 1))
                    out[base + (mine << place)] = held[n, :, start:end]
                    out[base + ((1 - mine) << place)] = received[n, :, start:end]

    arrays = list(small_call(kernel, name, [me] + args, outs, scalars=1))
    return [
        [Held(arrays.pop(0), dims) for _ in pieces] for _, _, _, pieces, dims in results
    ]


def tie(*values):
    return lax.optimization_barrier(values)


def small_call(kernel, name, args, outs, stream=False, scratch=(), scalars=0, limit=24):
    def spec(dims):
        return whole(dims) if stream else pl.BlockSpec(memory_space=pltpu.VMEM)

    return pl.pallas_call(
        kernel,
        grid=(1,) if stream else (),
        out_shape=[jax.ShapeDtypeStruct(dims, dtype) for dims, dtype in outs],
        in_specs=[SCALARS] * scalars + [spec(a.shape) for a in args[scalars:]],
        out_specs=[spec(dims) for dims, _ in outs],
        scratch_shapes=list(scratch),
        compiler_params=pltpu.CompilerParams(
            vmem_limit_bytes=limit * 1024 * 1024
        ),
        cost_estimate=pl.CostEstimate(flops=1, bytes_accessed=1, transcendentals=0),
        name=name,
    )(*args)


class Chain:
    def __init__(self, keep, send, dims, steps, pair_at=None):
        self.keep, self.send, self.dims, self.steps = keep, send, list(dims), list(steps)
        self.pair_at = pair_at

    def start(self):
        self.received = exchange(self.send, self.steps.pop(0))


def add_blocks(keep, received, pair_at):
    total = keep.astype(F32) + received.astype(F32)
    if pair_at is None:
        return total.astype(BF16)
    pair = total[:16, pair_at:] + total[16:32, pair_at:]
    high = pair.astype(BF16)
    tail = jnp.zeros((total.shape[0] - 32, pair.shape[1]), BF16)
    parts = [jnp.concatenate([high, (pair - high.astype(F32)).astype(BF16), tail], 0)]
    if pair_at:
        parts = [total[:, :pair_at].astype(BF16)] + parts
    return jnp.concatenate(parts, 1)


def combine(groups, me, name):
    args, outs = [], []
    for group in groups:
        for chain in group:
            args += [chain.keep, chain.received]
        count, rows, _ = group[0].keep.shape
        width = sum(chain.keep.shape[2] for chain in group)
        outs += [((count // 2, rows, width), BF16)] * 2

    def kernel(me_ref, *refs):
        ins, results = list(refs[: len(args)]), list(refs[len(args) :])
        for group in groups:
            keep_out, send_out = results.pop(0), results.pop(0)
            start = 0
            for chain in group:
                keep, received = ins.pop(0), ins.pop(0)
                width = keep.shape[2]
                axis, bit = chain.steps[0]
                place = len(chain.dims) - 1 - chain.dims.index((axis, bit))
                mine = (me_ref[0] >> bit) & 1 if axis == "win" else 0
                for n in range(keep_out.shape[0]):
                    base = (n >> place << (place + 1)) + (n & ((1 << place) - 1))
                    for out, at in (
                        (keep_out, base + (mine << place)), (send_out, base + ((1 - mine) << place))
                    ):
                        out[n, :, start : start + width] = add_blocks(
                            keep[at], received[at], chain.pair_at
                        )
                start += width

    results = small_call(kernel, name, [me] + args, outs, scalars=1)
    chains = []
    for n, group in enumerate(groups):
        step = group[0].steps[0]
        at, pair_at = 0, None
        for chain in group:
            if chain.pair_at is not None:
                pair_at = at + chain.pair_at
            at += chain.keep.shape[2]
        dims = [d for d in group[0].dims if d != step]
        chains.append(Chain(results[2 * n], results[2 * n + 1], dims, group[0].steps, pair_at))
    return chains


def finish(chain, name):
    _, rows, width = chain.keep.shape

    def kernel(keep, received, own, square):
        total = keep[0].astype(F32) + received[0].astype(F32)
        own[...] = total
        square[...] = jnp.broadcast_to(jnp.sum(total * total), (1, 128))

    return small_call(
        kernel, name, [chain.keep, chain.received], [((rows, width), F32), ((1, 128), F32)]
    )


def finish_pair(chain, squares, devices, share, name):
    _, rows, width = chain.keep.shape
    at = chain.pair_at

    def kernel(keep, received, *refs):
        total = keep[0].astype(F32) + received[0].astype(F32)
        own, message = refs[-2:]
        own[...] = total[:, :at]
        pair = total[:16, at:] + total[16:32, at:]
        square = jnp.sum(total[:, :at] * total[:, :at])
        square = jnp.broadcast_to(square, (1, 128))
        for ref in refs[:-2]:
            square = square + ref[...]
        row = [pair[n : n + 1] for n in range(share // 128)] + [square]
        message[...] = jnp.broadcast_to(jnp.concatenate(row, 1), message.shape)

    return small_call(
        kernel, name, [chain.keep, chain.received] + squares,
        [((rows, at), F32), ((devices, share + 128), F32)],
    )


def adam_step(weight, grad, first, second, rate):
    new_first = 0.5 * first + 0.5 * grad
    new_second = 0.5 * second + 0.5 * grad * grad
    fix = 1.0 - 0.5**STEP
    update = new_first / fix / (jnp.sqrt(new_second / fix) + ADAM_EPS)
    return (new_first, new_second, weight - rate * (update + DECAY_RATE * weight))


def update_kernel(starts, widths, layout, *refs):
    own, message, rest = refs[:3], refs[3], list(refs[4:])
    groups = [rest[3 * n : 3 * n + 3] for n in range(7)]
    loss_ref, norm_ref = rest[21], rest[22]
    outs = [rest[23 + 3 * n : 26 + 3 * n] for n in range(7)]
    vector_rows, table_rows, offsets, square_at, loss_at = layout
    vector_grad = message[:vector_rows, :C]
    table_grad = message[:table_rows, C : C + offsets]
    total = (
        jnp.sum(message[:, square_at : square_at + 1])
        + jnp.sum(vector_grad * vector_grad)
        + jnp.sum(table_grad * table_grad)
    )
    norm = jnp.sqrt(jnp.broadcast_to(total, (1, 1)))
    factor = CLIP_NORM / jnp.maximum(norm, CLIP_NORM)
    norm_ref[...] = norm
    loss_ref[...] = message[0:1, loss_at : loss_at + 1]

    def put(number, layer, grad, rate):
        weight, first, second = groups[number]
        index = (Ellipsis,) if layer is None else (layer, Ellipsis)
        if number == 6:
            index = (slice(None), layer, slice(None))
        results = adam_step(weight[index], factor * grad, first[index], second[index], rate)
        for ref, value in zip(outs[number], results):
            ref[index] = value

    layers = len(starts)
    for l in range(layers):
        qkv_width = outs[0][0].shape[2]
        part, at = starts[l]["attn"]
        put(0, l, own[part][:, at : at + qkv_width], LEARN_RATE)
        put(1, l, own[part][:, at + qkv_width : at + widths["attn"]], LEARN_RATE)
        part, at = starts[l]["up"]
        put(2, l, own[part][:, at : at + widths["up"]], LEARN_RATE)
        part, at = starts[l]["down"]
        put(3, l, own[part][:, at : at + widths["down"]], LEARN_RATE)
        heads = table_rows // layers
        put(6, l, table_grad[l * heads : (l + 1) * heads], SMALL_RATE)
    half = widths["head"] // 2
    head_grad = jnp.concatenate(
        [own[part][:, at : at + half] for part, at in starts[-1]["head"]], 1
    )
    put(4, None, head_grad[:, : outs[4][0].shape[1]], LEARN_RATE)
    put(5, None, vector_grad, SMALL_RATE)


def collect_rows(layers, head_real, loss_at, ins, out, spread):
    out[...] = jnp.zeros(out.shape, F32)
    row_of_slot = lax.broadcasted_iota(jnp.int32, (SLOT, 128), 0)
    lane = lax.broadcasted_iota(jnp.int32, (SLOT, 128), 1)
    target = row_of_slot // WSIDE * (2 * WSIDE - 1) + row_of_slot % WSIDE
    spreader = ((lane == target) & (row_of_slot < AREA)).astype(F32).astype(BF16)
    row = 0
    for l in range(layers):
        attn_rows, qkv_rows, mlp_rows, up_rows, bias_grad = ins[5 * l : 5 * l + 5]
        parts = [
            attn_rows[0:2], qkv_rows[:, :C], qkv_rows[:, 2 * C :], attn_rows[4:5], mlp_rows[5:8],
        ] + [up_rows[:, n * C : (n + 1) * C] for n in range(HID // C)]
        for part in parts:
            out[row : row + part.shape[0], :C] = part
            row += part.shape[0]
        for head in range(HEADS):
            g, h = divmod(head, PACK)
            left = bias_grad[g, :, h * SLOT : (h + 1) * SLOT]
            total = jnp.zeros((SLOT, 128), F32)
            for _ in range(3):
                low = left.astype(BF16)
                total = total + dot(low, spreader)
                left = left - low.astype(F32)
            spread[head * SLOT : (head + 1) * SLOT, :] = total
        table = jnp.zeros((HEADS, 256), F32)
        span = 2 * WSIDE - 1
        for j in range(AREA):
            wide = jnp.concatenate(
                [spread[pl.ds(j, HEADS, stride=SLOT), :], jnp.zeros((HEADS, 128), F32)], 1
            )
            shift = (WSIDE - 1 - j // WSIDE) * span + WSIDE - 1 - j % WSIDE
            table = table + (pltpu.roll(wide, shift, 1) if shift else wide)
        width = out.shape[1] - C
        out[l * HEADS : (l + 1) * HEADS, C:] = table[:, :width]
    final_rows, head_rows, loss = ins[5 * layers :]
    out[row : row + 2, :C] = final_rows[...]
    row += 2
    cuts = CLASSES // head_real
    width = head_rows.shape[1] // cuts
    classes = jnp.concatenate(
        [head_rows[:, n * width : n * width + head_real] for n in range(cuts)]
        + [jnp.zeros((1, -CLASSES % C), F32)], 1
    )
    for n in range(classes.shape[1] // C):
        out[row + n : row + n + 1, :C] = classes[:, n * C : (n + 1) * C]
    out[0:1, loss_at : loss_at + 1] = loss[:, 0:1]


def pair_rows(rows, ch_count, owners, me_ref, pairs):
    count = rows.shape[1] // 128
    wins = rows.shape[0] // ch_count
    high_rows = pairs.shape[2] // wins
    for flip in range(2):
        for n, owner in enumerate(owners):
            for win in range(wins):
                values = rows[pl.ds(win * ch_count + (me_ref[1] ^ (owner ^ flip)), 1), :]
                values = jnp.concatenate(
                    [values[:, m * 128 : (m + 1) * 128] for m in range(count)]
                    + [jnp.zeros((16 - count, 128), F32)], 0
                )
                high = values.astype(BF16)
                at = win * high_rows
                pairs[flip, n, at : at + 16] = high
                pairs[flip, n, at + 16 : at + 32] = (values - high.astype(F32)).astype(BF16)
                pairs[flip, n, at + 32 : at + high_rows] = jnp.zeros((high_rows - 32, 128), BF16)


def pack_kernel(head_width, qkv, proj, down, up, head, attn0, mlp0, all1):
    attn0[...] = jnp.concatenate([qkv[0], proj[0]], 1).astype(BF16)
    mlp0[...] = jnp.concatenate([down[0], up[0]], 1).astype(BF16)
    parts = [qkv[1], proj[1], down[1], up[1], head[...]]
    pad = head_width - head.shape[1]
    if pad:
        parts.append(jnp.zeros((head.shape[0], pad), F32))
    all1[...] = jnp.concatenate(parts, 1).astype(BF16)


def per_device(
    tokens, valid_rows, valid_cols, partner, mix_level, labels,
    w_qkv, m_qkv, v_qkv, w_proj, m_proj, v_proj, w_fc1, m_fc1, v_fc1, w_fc2, m_fc2, v_fc2,
    w_head, m_head, v_head, vectors, m_vec, v_vec, rel_table, m_rel, v_rel,
):
    micro, images, cells, chans = tokens.shape
    layers = rel_table.shape[0]
    per_layer = 8 + HID // C
    base = layers * per_layer
    head_rows = vectors.shape[0] - base - 2
    all_images = labels.shape[1]
    total_images = micro * all_images
    local = micro * images
    groups = local // GROUP
    sizes = {axis: lax.axis_size(axis) for axis in ("win", "ch")}
    win_count, ch_count = sizes["win"], sizes["ch"]
    device_count = win_count * ch_count
    win_index, ch_index = lax.axis_index("win"), lax.axis_index("ch")
    me = jnp.stack([win_index, ch_index]).astype(jnp.int32)
    block_rows = C // win_count
    widths = {"attn": 4 * C // ch_count, "down": HID // ch_count, "up": HID // ch_count}
    head_real = CLASSES // ch_count
    widths["head"] = -(-head_real // 128) * 128
    head_classes = widths["head"] * ch_count
    direct = block_rows % 16 == 0 and block_rows >= 32 and all(w % 128 == 0 for w in widths.values())

    core = ("ch", 0)
    ch_high = [("ch", b) for b in range(1, ch_count.bit_length() - 1)]
    win_low = [("win", 0)]
    win_high = [("win", b) for b in range(1, win_count.bit_length() - 1)]

    def low(v):
        return v.astype(BF16)

    packed = small_call(
        functools.partial(pack_kernel, widths["head"]), "pack",
        [w_qkv, w_proj, w_fc2.transpose(0, 2, 1), w_fc1, w_head],
        [((block_rows, sum(widths[n] for n in names)), BF16) for names in (
            ("attn",), ("down", "up"), ("attn", "down", "up", "head"))],
        stream=True,
        limit=56,
    )
    names = [["attn", "down", "up"], ["attn", "down", "up", "head"]]
    onehot = jnp.asarray(relative_onehot(), BF16)
    offsets = rel_table.shape[1]
    table_width = -(-(offsets + 1) // 128) * 128
    share = C + table_width
    tables = [window_tables(l % 2 == 1) for l in range(layers)]
    perms = [jnp.asarray(t[0], BF16) for t in tables]
    perms_t = [jnp.asarray(t[0].T, BF16) for t in tables]
    row_limits = [jnp.asarray(t[1]) for t in tables]
    col_limits = [jnp.asarray(t[2]) for t in tables]

    def bias_of(table):
        table = table.transpose(0, 2, 1).reshape(layers * HEADS, offsets)
        table_parts = []
        for _ in range(3):
            table_parts.append(low(table))
            table = table - table_parts[-1].astype(F32)
        bias = dot(jnp.concatenate(table_parts, 0), onehot).reshape(3, layers, HEADS, SLOT * SLOT)
        bias = (bias[0] + bias[1]) + bias[2]
        return (
            bias.reshape(layers, NGRP, PACK, SLOT, SLOT)
            .transpose(0, 1, 3, 2, 4)
            .reshape(layers, NGRP, SLOT, LANES)
        )

    padded = jnp.pad(tokens.reshape(local, cells, chans), ((0, 0), (0, ROWS - cells), (0, 0)))

    def stage(number, *moves, cuts=None, more=()):
        received = [exchange(part.array, step) for part, step in moves]
        tied = tie(*received, *more)
        received, more = tied[: len(moves)], tied[len(moves) :]
        stacked = stack_blocks(
            [(part, got, step) for (part, step), got in zip(moves, received)],
            me, f"stack{number}", cuts,
        )
        return (stacked, *more)

    def wait_for(value, *parts):
        value, *arrays = tie(value, *[part.array for part in parts])
        for part, array in zip(parts, arrays):
            part.array = array
        return value

    far = [Held(block[None]) for block in packed]
    edges = [
        [0, widths["attn"] * 2 // 3, widths["attn"], widths["attn"] + widths["down"],
         widths["attn"] + widths["down"] + widths["up"]],
        [0, widths["attn"], widths["attn"] + widths["down"] + widths["up"] * 2 // 3,
         sum(widths[name] for name in ("attn", "down", "up", "head"))],
    ]
    staged = win_count == 8 and ch_count == 4
    if staged:
        zh, zl, y, x = ("win", 2), ("win", 1), ("win", 0), ("ch", 1)
        ((attn,),), mlp, padded = stage(0, (far[0], zh), more=(far[1].array, padded))
        (attn, (mlp,)), all1, bias = stage(
            1, (attn, zl), (Held(mlp), zh), cuts=[edges[0][1:2], None],
            more=(packed[2], bias_of(rel_table)),
        )
        floating = exchange(all1[None], zh)
        ((one,), (two,), mlp), = stage(
            2, (attn[0], y), (attn[1], x), (mlp, zl), cuts=[None, None, [widths["down"]]]
        )
        (((all1,),),) = [stack_blocks([(Held(all1[None]), floating, zh)], me, "stack10")]
        mlp[0].array, mlp[1].array, all1.array = tie(mlp[0].array, mlp[1].array, all1.array)
        near = [(one, x), (two, y), (mlp[0], x), (mlp[1], y)]
        received = [exchange(part.array, step) for part, step in near]
        floating = exchange(all1.array, zl)
        *received, floating = tie(*received, floating)
        ((one,), (two,), (down,), (up,)) = stack_blocks(
            [(part, got, step) for (part, step), got in zip(near, received)], me, "stack3"
        )
        held = [[one, two]]
        *got, floating = tie(*[exchange(part.array, core) for part in held[0]], floating)
        other = [got]
        (parts1,) = stack_blocks([(all1, floating, zl)], me, "stack11", [edges[1][1:-1]])
        padded = wait_for(padded, *parts1)
    else:
        bias = bias_of(rel_table)
        bits = win_high[::-1] + win_low + ch_high[::-1]
        held, other = [[], []], []
        for number, part in enumerate(far):
            for n, step in enumerate(bits):
                ((part,),), = stage(10 * number + n, (part, step))
            layer = number // 2
            base = 0 if number != 1 else widths["attn"]
            for start, end in zip(edges[layer], edges[layer][1:]):
                if start >= base and end - base <= part.array.shape[-1]:
                    held[layer].append(Held(part.array[..., start - base : end - base], part.dims))
        other.append([exchange(part.array, core) for part in held[0]])

    def weight_inputs(layer, wanted):
        plan = Plan(widths, layer, layers)
        ins = {}
        starts, at = {}, 0
        for name in names[layer]:
            starts[name] = at
            at += widths[name]
        bounds = list(zip(edges[layer], edges[layer][1:]))
        blocks = []
        for group, part in enumerate(held[layer]):
            if group >= len(other[layer]):
                break
            owners = relative_owners([d for d in part.dims if d[0] == "ch"])
            for number, array in enumerate((part.array, other[layer][group])):
                flat_array = array.reshape(-1, C, array.shape[-1])
                blocks.append((group, [owner ^ number for owner in owners], flat_array))
        for name in wanted:
            plan.sources[name] = []
            columns = []
            for number, (group, owners, array) in enumerate(blocks):
                begin = max(starts[name], bounds[group][0])
                end = min(starts[name] + widths[name], bounds[group][1])
                if begin >= end:
                    continue
                cut = (begin - bounds[group][0], end - begin, begin - starts[name])
                if direct:
                    ref = f"blocks{number}"
                    ins[ref] = (FAR, array)
                    plan.sources[name].append((ref, owners, cut))
                elif number % 2 == 0:
                    table = np.argsort(np.asarray(owners + blocks[number + 1][1]))
                    both = jnp.concatenate([array, blocks[number + 1][2]])
                    index = jnp.asarray(table)[jnp.arange(ch_count) ^ ch_index]
                    columns.append(jnp.take(both, index, axis=0)[..., cut[0] : cut[0] + cut[1]])
            if not direct:
                full = jnp.concatenate(columns, -1)
                if name in ("up", "down"):
                    full = full.transpose(1, 0, 2).reshape(C, -1)
                ins[f"staged_{name}"] = (FAR, full)
                plan.sources[name] = [(f"staged_{name}", None, None)]
        ins["me"] = (SCALARS, me)
        return ins, plan

    orders = {
        "x": ch_high + win_low + win_high, "a": ch_high + win_low + win_high,
        "y": win_low + ch_high + win_high, "b": win_low + ch_high + win_high,
    }
    block_dims = ch_high + [("win", b) for b in reversed(range(win_count.bit_length() - 1))]
    owners = relative_owners(ch_high)
    regular = direct and len(ch_high) == 1

    def grad_outputs(plan, **members):
        outs = {}
        for group, wanted in members.items():
            if not direct:
                for name in wanted:
                    plan.targets[name] = [(f"full_{name}", None, 0, 0, widths[name])]
                    dims = (C, HID) if name in ("up", "down") else (ch_count, C, widths[name])
                    outs[f"full_{name}"] = (FAR, dims, BF16)
                continue
            starts = np.cumsum([0] + [widths[name] for name in wanted])
            refs = [
                (f"keep_{group}", owners), (f"send_{group}", [owner ^ 1 for owner in owners])
            ]
            for ref, _ in refs:
                outs[ref] = (FAR, (len(owners), C, int(starts[-1])), BF16)
            for name, start in zip(wanted, starts):
                plan.targets[name] = [(ref, at, int(start), 0, widths[name]) for ref, at in refs]
        return outs

    def cut_attention_outputs(plan):
        cut = widths["attn"] * 2 // 3
        outs, plan.targets["attn"] = {}, []
        for group, start, size, extra in (("a", 0, cut, 0), ("b", cut, widths["attn"] - cut, 128)):
            for kind, flip in (("keep", 0), ("send", 1)):
                ref = f"{kind}_{group}"
                outs[ref] = (NEAR, (len(owners), C, size + extra), BF16)
                plan.targets["attn"].append(
                    (ref, [owner ^ flip for owner in owners], 0, start, size)
                )
        return outs

    def halved_head_outputs(plan):
        half = widths["head"] // 2
        if not direct:
            return grad_outputs(plan, x=["up", "head"], y=["down"])
        outs, plan.targets["head"] = {}, []
        for group, name, at in (("x", "up", 0), ("y", "down", half)):
            plan.targets[name] = []
            for kind, flip in (("keep", 0), ("send", 1)):
                ref, places = f"{kind}_{group}", [owner ^ flip for owner in owners]
                outs[ref] = (FAR, (len(owners), C, widths[name] + half), BF16)
                plan.targets[name].append((ref, places, 0, 0, widths[name]))
                plan.targets["head"].append((ref, places, widths[name], at, half))
        return outs

    def chain_of(results, group, *members, pair_at=None):
        if direct:
            keep, send = results[f"keep_{group}"], results[f"send_{group}"]
        else:
            full = []
            for name in members:
                name, *cut = name if isinstance(name, tuple) else (name,)
                part = results[f"full_{name}"]
                if cut:
                    part = part[..., cut[0] : cut[1]]
                if name in ("up", "down"):
                    part = part.reshape(C, ch_count, -1).transpose(1, 0, 2)
                full.append(part)
            full = jnp.concatenate(full, -1)
            keep, send = [
                jnp.take(full, np.asarray(owners) ^ flip ^ ch_index, axis=0) for flip in (0, 1)
            ]
        dims = (-1, block_rows, keep.shape[-1])
        return Chain(
            keep.reshape(dims), send.reshape(dims), block_dims, [core] + orders[group], pair_at
        )

    def start(*chains):
        for chain in chains:
            chain.start()

    def meet(value, *chains):
        value, *got = tie(value, *[chain.received for chain in chains])
        for chain, array in zip(chains, got):
            chain.received = array
        return value

    def after(value, *chains):
        held_back = [array for chain in chains for array in (chain.keep, chain.send)]
        value, *held_back = tie(value, *held_back)
        for n, chain in enumerate(chains):
            chain.keep, chain.send = held_back[2 * n], held_back[2 * n + 1]
        return value

    def attention_consts(l, forward):
        ins = {
            "perm": (whole((WROWS, ROWS)), perms[l]),
            "perm_t": (whole((ROWS, WROWS)), perms_t[l]),
            "vec": (whole(vectors.shape), vectors),
        }
        if forward:
            ins["rows"] = (SCALARS, valid_rows)
            ins["cols"] = (SCALARS, valid_cols)
            ins["row_limit"] = (whole((NWIN, SLOT, 128)), row_limits[l])
            ins["col_limit"] = (whole((NWIN, SLOT, 128)), col_limits[l])
            ins["bias"] = (
                pl.BlockSpec((None, NGRP, SLOT, LANES), lambda i, l=l: (l, 0, 0, 0)), bias
            )
        return ins

    def vmem(*dims, dtype=BF16):
        return pltpu.VMEM(dims, dtype)

    attn_weights = {
        "stage": vmem(ch_count, C, widths["attn"]),
        "w_qkv": vmem(C, 3 * C),
        "w_proj": vmem(C, C),
        "load_sem": pltpu.SemaphoreType.DMA((4,)),
    }
    mlp_weights = {
        "w_down": vmem(C, HID),
        "w_up": vmem(C, HID),
        "load_sem": pltpu.SemaphoreType.DMA((4,)),
    }
    all_rows = local * ROWS
    mlp_rows = {
        "mlp_all": vmem(all_rows, C), "active_all": vmem(all_rows, HID),
        "pre_all": vmem(all_rows, HID), "low_all": vmem(all_rows, C),
        "up_grad": vmem(C, HID), "down_grad": vmem(C, HID),
        "sem_x": pltpu.SemaphoreType.DMA((2,)), "sem_y": pltpu.SemaphoreType.DMA((2,)),
    }
    wide = (per_image(ROWS, C), (local, ROWS, C), F32)
    thin = (per_image(ROWS, C), (local, ROWS, C), BF16)
    hidden = (per_image(ROWS, HID), (local, ROWS, HID), BF16)
    attn_saved = {
        "normed": thin,
        "qkv": (per_image(WROWS, 3 * C), (local, WROWS, 3 * C), BF16),
        "prob": (per_image(NWIN, NGRP, SLOT, LANES), (local, NWIN, NGRP, SLOT, LANES), BF16),
        "attended": thin,
    }
    sums = {"row_sums": (whole((8, C)), (8, C), F32)}
    up_sums = {**sums, "up_rows": (whole((1, HID)), (1, HID), F32)}
    attn_sums = {
        **sums,
        "qkv_rows": (whole((1, 3 * C)), (1, 3 * C), F32),
        "bias_grad": (whole((NGRP, SLOT, LANES)), (NGRP, SLOT, LANES), F32),
    }

    def given(spec, array):
        return (spec[0], array)

    mlp_flops = 2 * all_rows * C * HID * 2
    attn_flops = 2 * all_rows * C * C * 8

    def attention_forward(l, field, first=0, count=groups, before=None):
        ins, plan = weight_inputs(l, ["attn"]) if before is None else ({}, Plan(widths, l, layers))
        plan.group = first
        ins["field"] = (per_image(*field.shape[1:], first=first), field)
        ins.update(attention_consts(l, True))
        outs = {
            name: (spec, (count * GROUP,) + dims[1:], dtype)
            for name, (spec, dims, dtype) in {"middle": wide, **attn_saved}.items()
        }
        scratch = {"mixed": vmem(GROUP, C, WROWS), "windowed": vmem(GROUP, WROWS, C)}
        if before is None:
            outs["qkv_out"] = (FAR, (C, 3 * C), BF16)
            outs["proj_out"] = (FAR, (C, C), BF16)
            scratch.update(attn_weights)
            scratch["out_sem"] = pltpu.SemaphoreType.DMA((2,))
        else:
            ins["w_qkv"] = (whole((C, 3 * C)), before["qkv_out"])
            ins["w_proj"] = (whole((C, C)), before["proj_out"])
        results = call(
            functools.partial(attention_forward_kernel, plan=plan), f"attention_forward{l}_{first}",
            count, ins, outs, scratch, attn_flops * count // groups,
        )
        return results if before is None else {**before, **results}

    def rows_of(name, arrays):
        if len(arrays) == 1:
            return {name: given(wide, arrays[0])}
        return {f"{name}{n}": (whole(array.shape), array) for n, array in enumerate(arrays)}

    def begin(*moves):
        return [(part, step, exchange(part.array, step)) for part, step in moves]

    def arrive(number, value, moves):
        value, *received = tie(value, *[got for _, _, got in moves])
        stacked = stack_blocks(
            [(part, got, step) for (part, step, _), got in zip(moves, received)], me, f"stack{number}"
        )
        return value, [parts[0] for parts in stacked]

    if staged:
        moves = begin((down, y), (up, x), (parts1[0], y), (parts1[1], x), (parts1[2], y))
        early0 = attention_forward(0, padded, 0, groups - 1)
        early0["proj_out"], (down, up, *parts1) = arrive(4, early0["proj_out"], moves)
        early0["proj_out"] = wait_for(early0["proj_out"], down, up, *parts1)
        held[0] += [down, up]
        got = [exchange(part.array, core) for part in (down, up)]
        moves = begin((parts1[0], x), (parts1[1], y), (parts1[2], x))
        saved0 = attention_forward(0, padded, groups - 1, 1, early0)
        saved0["middle"], *got = tie(saved0["middle"], *got)
        other[0] = list(other[0]) + got
        saved0["middle"], parts1 = arrive(5, saved0["middle"], moves[:1])
        middle0 = [early0["middle"], wait_for(saved0["middle"], *parts1)]
        held.append(parts1)
    else:
        saved0 = early0 = attention_forward(0, padded)
        middle0 = [saved0["middle"]]
    ins, plan = weight_inputs(0, ["down", "up"])
    ins.update(rows_of("middle", middle0))
    ins["vec"] = (whole(vectors.shape), vectors)
    mlp0 = call(
        functools.partial(first_mlp_kernel, plan=plan), "first_mlp", groups, ins,
        {
            "result": wide, "mlp_in": thin, "active": hidden, "slope": hidden,
            "down_out": (FAR, (C, HID), BF16),
            "up_out": (FAR, (C, HID), BF16),
        },
        {**mlp_weights, "out_sem": pltpu.SemaphoreType.DMA((2,))},
        mlp_flops,
    )
    result0 = mlp0["result"]
    got = [exchange(part.array, core) for part in held[1]]
    result0, *got = tie(result0, *got)
    other.append(got)

    if staged:
        early1 = attention_forward(1, result0, 0, groups - 1)
        early1["proj_out"], late1 = arrive(6, early1["proj_out"], moves[1:])
        early1["proj_out"] = wait_for(early1["proj_out"], *late1)
        got = [exchange(part.array, core) for part in late1]
        saved1 = attention_forward(1, result0, groups - 1, 1, early1)
        saved1["middle"], *got = tie(saved1["middle"], *got)
        held[1] = held[1] + late1
        other[1] = other[1] + got
        middle1 = [early1["middle"], saved1["middle"]]
    else:
        saved1 = early1 = attention_forward(1, result0)
        middle1 = [saved1["middle"]]
    ins, plan = weight_inputs(1, ["down", "up", "head"])
    ins.update(rows_of("middle", middle1))
    ins["vec"] = (whole(vectors.shape), vectors)
    ins["rows"] = (SCALARS, valid_rows)
    ins["cols"] = (SCALARS, valid_cols)
    ins["labels"] = (SCALARS, labels)
    ins["partner"] = (SCALARS, partner)
    ins["mix"] = (SCALARS, mix_level)
    cell = np.arange(ROWS)
    for name, place in (("cell_row", cell // GRID), ("cell_col", cell % GRID)):
        place = np.where(cell < CELLS, place, 99)[:, None].astype(np.int32)
        ins[name] = (whole((ROWS, 1)), jnp.asarray(place))
    outs = {
        "grad_mid": wide, **up_sums,
        "final_rows": (whole((2, C)), (2, C), F32),
        "head_rows": (whole((1, head_classes)), (1, head_classes), F32),
        "loss": (whole((1, 128)), (1, 128), F32),
        **halved_head_outputs(plan),
    }
    last = call(
        functools.partial(last_mlp_kernel, plan=plan, total_images=float(total_images)),
        "last_mlp", groups, ins, outs,
        {
            "slope": vmem(GROUP * ROWS, HID), "w_head": vmem(ch_count, C, widths["head"]),
            **mlp_weights, **mlp_rows,
            "pooled_all": vmem(16, C, dtype=F32), "logit_all": vmem(16, head_classes, dtype=F32),
            "head_grad": vmem(ch_count, C, widths["head"]),
        },
        3 * mlp_flops,
    )

    def attention_backward(l, grad_mid, field, saved, first, count, before=None, before_saved=None, store=True, collect=None):
        plan = Plan(widths, l, layers)
        ins = {
            "me": (SCALARS, me), "w_qkv": (whole((C, 3 * C)), saved["qkv_out"]),
            "w_proj": (whole((C, C)), saved["proj_out"]),
        }
        ins.update(attention_consts(l, False))
        wanted = ["qkv", "prob"] + (["normed", "attended"] if store else [])
        for name, array in [("grad_mid", grad_mid), ("field", field)] + [
            (name, saved[name]) for name in wanted
        ]:
            skip = first if array.shape[0] == local else 0
            ins[name] = (per_image(*array.shape[1:], first=skip), array)
        if before is not None:
            for name, (spec, _, _) in attn_sums.items():
                ins[name + "_in"] = (spec, before[name])
            for name in ("normed", "attended"):
                ins[name + "_in"] = (whole((first * GROUP, ROWS, C)), before_saved[name])
            for name in ("spread", "attn"):
                array = before[name + "_all"]
                ins[name + "_in"] = (whole(array.shape), array)
        rows_here = count * GROUP * ROWS
        outs = dict(attn_sums)
        scratch = {
            "dq": vmem(GROUP, C, WROWS), "dkv": vmem(GROUP, WROWS, 2 * C),
            "joined": vmem(GROUP, WROWS, C),
        }
        need_grad = l > 0
        if need_grad:
            outs["grad"] = (wide[0], (count * GROUP, ROWS, C), F32)
        if store:
            if collect is None:
                outs.update(grad_outputs(plan, a=["attn"]))
            else:
                outs.update(cut_attention_outputs(plan))
                plan.collect = (layers, head_real, share - 1, owners)
                ins.update({name: (whole(array.shape), array) for name, array in collect.items()})
                scratch["small_rows"] = vmem(device_count, share, dtype=F32)
                scratch["spread_table"] = vmem(HEADS * SLOT, 128, dtype=F32)
                scratch["pairs"] = vmem(2, len(owners), C, 128)
            scratch.update({
                "normed_all": vmem(all_rows, C), "attended_all": vmem(all_rows, C),
                "spread_all": vmem(all_rows, 3 * C), "attn_all": vmem(all_rows, C),
                "attn_grad": vmem(ch_count, C, widths["attn"]),
                "sem_a": pltpu.SemaphoreType.DMA((4,)),
            })
        else:
            outs["spread_all"] = (whole((rows_here, 3 * C)), (rows_here, 3 * C), BF16)
            outs["attn_all"] = (whole((rows_here, C)), (rows_here, C), BF16)
        return call(
            functools.partial(
                backward_attention_kernel, plan=plan,
                earlier=0 if before is None else first * GROUP, need_grad=need_grad,
            ),
            f"attention_backward{l}_{first}", count, ins, outs, scratch,
            2 * attn_flops * count // groups,
        )

    half = widths["head"] // 2
    x1 = chain_of(last, "x", "up", ("head", 0, half))
    y1 = chain_of(last, "y", "down", ("head", half, 2 * half))
    if regular:
        start(x1, y1)
    grad_mid = last["grad_mid"]
    before1 = attention_backward(1, grad_mid, mlp0["result"], early1, 0, groups - 1, store=False)
    if regular:
        before1["row_sums"] = meet(before1["row_sums"], x1, y1)
        x1, y1 = combine([[x1], [y1]], me, "sum0")
        grad_mid = after(grad_mid, x1, y1)
        start(x1, y1)
    back1 = attention_backward(
        1, grad_mid, mlp0["result"], saved1, groups - 1, 1, before1, early1
    )
    a1 = chain_of(back1, "a", "attn")
    grad = back1["grad"]
    if regular:
        grad = meet(grad, x1, y1)
        x1, y1 = combine([[x1], [y1]], me, "sum1")
        grad = after(grad, x1, y1)
        start(x1, y1, a1)

    plan = Plan(widths, 0, layers)
    ins = {
        "me": (SCALARS, me),
        "w_down": (whole((C, HID)), mlp0["down_out"]),
        "w_up": (whole((C, HID)), mlp0["up_out"]),
    }
    ins.update(rows_of("grad", [before1["grad"], grad]))
    ins.update(rows_of("middle", middle0))
    ins["mlp_in"] = given(thin, mlp0["mlp_in"])
    ins["active"] = given(hidden, mlp0["active"])
    ins["slope"] = given(hidden, mlp0["slope"])
    ins["vec"] = (whole(vectors.shape), vectors)
    first = call(
        functools.partial(backward_mlp_kernel, plan=plan), "mlp_backward0", groups, ins,
        {"grad_mid": wide, **up_sums, **grad_outputs(plan, x=["up"], y=["down"])},
        dict(mlp_rows), 2 * mlp_flops,
    )
    x0, y0 = chain_of(first, "x", "up"), chain_of(first, "y", "down")
    grad_mid = first["grad_mid"]
    if regular:
        grad_mid = meet(grad_mid, x1, y1, a1)
        a1, z1 = combine([[a1], [x1, y1]], me, "sum2")
        grad_mid = after(grad_mid, a1, z1)
        start(a1, z1, x0, y0)
    before0 = attention_backward(0, grad_mid, padded, early0, 0, groups - 1, store=False)
    if regular:
        before0["row_sums"] = meet(before0["row_sums"], a1, x0, y0, z1)
        a1, x0, y0, z1 = combine([[a1], [x0], [y0], [z1]], me, "sum3")
        grad_mid = after(grad_mid, a1, x0, y0, z1)
        start(a1, x0, y0, z1)
    small_parts = None
    if regular:
        small_parts = {
            "mlp_rows0": first["row_sums"], "up_rows0": first["up_rows"],
            "row_sums1": back1["row_sums"], "qkv_rows1": back1["qkv_rows"],
            "mlp_rows1": last["row_sums"], "up_rows1": last["up_rows"],
            "bias_grad1": back1["bias_grad"], "final_rows": last["final_rows"],
            "head_rows": last["head_rows"], "loss": last["loss"],
        }
    back0 = attention_backward(
        0, grad_mid, padded, saved0, groups - 1, 1, before0, early0, collect=small_parts
    )
    a0 = chain_of(back0, "a", "attn")
    if regular:
        b0 = chain_of(back0, "b", pair_at=widths["attn"] - widths["attn"] * 2 // 3)
        waiting = (a1, x0, y0, z1)
        a0.send, b0.send, *got = tie(a0.send, b0.send, *[chain.received for chain in waiting])
        for chain, array in zip(waiting, got):
            chain.received = array

    if regular:
        start(a0, b0)
        x0, y0 = combine([[x0], [y0]], me, "sum5")
        start(x0, y0)
        a0.received, b0.received, x0.keep = tie(a0.received, b0.received, x0.keep)
        a0, b0 = combine([[a0], [b0]], me, "sum6")
        start(a0, b0)
        (z0,) = combine([[x0, y0, a1]], me, "sum7")
        start(z0)
        a0, b0 = combine([[a0], [b0]], me, "sum8")
        start(a0, b0)
        (z0,) = combine([[z0]], me, "sum9")
        start(z0)
        own1, square1 = finish(z1, "own1")
        (a0,) = combine([[a0, b0]], me, "sum10")
        start(a0)
        own0, square0 = finish(z0, "own0")
        (a0,) = combine([[a0]], me, "sum11")
        start(a0)
        own_attn, message = finish_pair(a0, [square0, square1], device_count, share, "own_attn")
    else:
        square, own_parts = jnp.zeros((1, 128), F32), []
        for chain in (a0, x0, y0, a1, x1, y1):
            start(chain)
            while chain.steps:
                (chain,) = combine([[chain]], me, "sum")
                start(chain)
            part, part_square = finish(chain, "own")
            square = square + part_square
            own_parts.append(part)
        own_attn = own_parts[0]
        own0, own1 = jnp.concatenate(own_parts[1:4], 1), jnp.concatenate(own_parts[4:], 1)
        (rows_all,) = small_call(
            lambda *refs: collect_rows(
                layers, head_real, share - 1, refs[:-2], refs[-2], refs[-1]
            ),
            "collect",
            [part[name] for part in ((first, back0), (last, back1))
             for part, name in (
                 (part[1], "row_sums"), (part[1], "qkv_rows"), (part[0], "row_sums"),
                 (part[0], "up_rows"), (part[1], "bias_grad"))]
            + [last["final_rows"], last["head_rows"], last["loss"]],
            [((device_count, share), F32)],
            stream=True,
            scratch=[pltpu.VMEM((HEADS * SLOT, 128), F32)],
        )
        rows_all = lax.all_to_all(rows_all, ("win", "ch"), 0, 0, tiled=True)
        message = jnp.concatenate([jnp.sum(rows_all, 0, keepdims=True), square], 1)
        message = jnp.broadcast_to(message, (device_count, share + 128))
    message = lax.all_to_all(message, ("win", "ch"), 0, 0, tiled=True)
    starts = [
        {"attn": (1, 0), "up": (2, 0), "down": (2, widths["up"])},
        {
            "attn": (2, widths["up"] + widths["down"]), "up": (0, 0),
            "down": (0, widths["up"] + half),
            "head": [(0, widths["up"]), (0, widths["up"] + half + widths["down"])],
        },
    ]
    arrays = [
        [w_qkv, m_qkv, v_qkv], [w_proj, m_proj, v_proj], [w_fc1, m_fc1, v_fc1],
        [w_fc2, m_fc2, v_fc2], [w_head, m_head, v_head], [vectors, m_vec, v_vec],
        [rel_table, m_rel, v_rel],
    ]
    turns = {3: (0, 2, 1), 6: (2, 0, 1)}
    turned = [
        a.transpose(turns[n]) if n in turns else a for n, group in enumerate(arrays) for a in group
    ]
    results = small_call(
        functools.partial(
            update_kernel, starts, widths,
            (vectors.shape[0], layers * HEADS, offsets, share, share - 1),
        ),
        "update",
        [own1, own_attn, own0, message] + turned,
        [((1, 1), F32)] * 2 + [(a.shape, F32) for a in turned],
        stream=True,
    )
    loss_total, grad_norm, *results = results
    outs = [loss_total[0, 0], grad_norm[0, 0]]
    for n in range(0, len(results), 3):
        back = {3: (0, 2, 1), 6: (1, 2, 0)}.get(n // 3)
        outs += [r if back is None else r.transpose(back) for r in results[n : n + 3]]
    return tuple(outs)


def solution(mesh):
    cut = P(None, "win", "ch")
    down = P(None, "ch", "win")
    head = P("win", "ch")
    rows = P(None, ("win", "ch"))
    in_specs = (
        (P(None, ("win", "ch"), None, None),) + (rows,) * 4 + (P(),)
        + (cut,) * 9 + (down,) * 3 + (head,) * 3 + (P(),) * 6
    )
    out_specs = (P(),) * 2 + (cut,) * 9 + (down,) * 3 + (head,) * 3 + (P(),) * 6
    return jax.shard_map(
        per_device, mesh=mesh, in_specs=in_specs, out_specs=out_specs, check_vma=False
    )
```

```python
import functools

import jax
import jax.numpy as jnp
import numpy as np
from jax import lax
from jax.experimental import pallas as pl
from jax.experimental.pallas import tpu as pltpu
from jax.sharding import PartitionSpec as P

C = 384
HID = 1536
CLASSES = 1000
CLASS_PAD = 1024
WSIDE = 7
GRID = 14
STEP = 10
HEADS = 12
PER_LAYER = 8 + HID // C
DEPTH = 32
CELLS = GRID * GRID
ROWS = 208
AREA = WSIDE * WSIDE
SLOT = 64
NWIN = 4
NGRP = 3
PACK = 4
WROWS = NWIN * SLOT
LANES = PACK * SLOT

NORM_EPS = 1e-05
CLIP_NORM = 0.05
LEARN_RATE = 0.04
SMALL_RATE = 0.2
DECAY_RATE = 0.05
ADAM_EPS = 1e-08
MASKED = -1e30
SCALE = DEPTH ** (-0.5)
F32 = jnp.float32
BF16 = jnp.bfloat16
NN = (((1,), (0,)), ((), ()))
NT = (((1,), (1,)), ((), ()))
TN = (((0,), (0,)), ((), ()))
VMEM_LIMIT = 24 * 1024 * 1024
GROUP = 2
CHUNK = 768


def dot(a, b, dims=NN):
    return lax.dot_general(a, b, dims, preferred_element_type=F32)


@functools.lru_cache(None)
def window_tables(shifted):
    perm = np.zeros((WROWS, ROWS), np.float32)
    row_limit = np.full((NWIN, SLOT, 2 * SLOT), 99, np.int32)
    col_limit = np.full((NWIN, SLOT, 2 * SLOT), 99, np.int32)
    shift = WSIDE // 2 if shifted else 0

    def band(v):
        return 0 if v < GRID - WSIDE else (1 if v < GRID - WSIDE // 2 else 2)

    for window in range(NWIN):
        wr, wc = divmod(window, GRID // WSIDE)
        place = []
        for j in range(AREA):
            r, c = wr * WSIDE + j // WSIDE, wc * WSIDE + j % WSIDE
            region = 3 * band(r) + band(c) if shifted else 0
            source = ((r + shift) % GRID, (c + shift) % GRID)
            place.append((region, source))
            perm[window * SLOT + j, source[0] * GRID + source[1]] = 1
        for j in range(SLOT):
            for i in range(SLOT):
                if i == j:
                    pair = (-1, -1)
                elif i < AREA and j < AREA and place[i][0] == place[j][0]:
                    pair = place[j][1]
                else:
                    pair = (99, 99)
                row_limit[window, j, i::SLOT] = pair[0]
                col_limit[window, j, i::SLOT] = pair[1]
    return perm, row_limit, col_limit


@functools.lru_cache(None)
def relative_onehot():
    span = 2 * WSIDE - 1
    onehot = np.zeros((span * span, SLOT, SLOT), np.float32)
    for i in range(AREA):
        for j in range(AREA):
            row, col = i // WSIDE - j // WSIDE, i % WSIDE - j % WSIDE
            onehot[(row + WSIDE - 1) * span + col + WSIDE - 1, j, i] = 1
    return onehot.reshape(span * span, SLOT * SLOT)


def norm_parts(field):
    average = jnp.mean(field, -1, keepdims=True)
    centered = field - average
    spread = jnp.mean(centered * centered, -1, keepdims=True)
    rate = lax.rsqrt(spread + NORM_EPS)
    return centered * rate, rate


def norm_back(grad, hat, rate, gain):
    scaled = grad * gain
    return rate * (
        scaled
        - jnp.mean(scaled, -1, keepdims=True)
        - hat * jnp.mean(scaled * hat, -1, keepdims=True)
    )


def col_sum(field):
    return jnp.sum(field, 0, keepdims=True)


def head_masks(dtype):
    lane = lax.broadcasted_iota(jnp.int32, (SLOT, 128), 1)
    return [((lane // DEPTH) == h).astype(F32).astype(dtype) for h in range(PACK)]


def spread_heads(block, masks):
    return jnp.concatenate([block * m for m in masks], 0)


def relative_owners(bits):
    owners = []
    for index in range(1 << len(bits)):
        offset = 0
        for n, (_, bit) in enumerate(bits):
            offset |= ((index >> (len(bits) - 1 - n)) & 1) << bit
        owners.append(offset)
    return owners


def owner_part(ref, owner, width, start, size):
    if len(ref.shape) == 3:
        return ref.at[owner, :, start : start + size]
    return ref.at[:, pl.ds(pl.multiple_of(owner * width + start, 128), size)]


def load_blocks(pieces, target, width, sem, me_ref):
    for ref, owners, cut in pieces:
        if owners is None:
            pltpu.make_async_copy(ref, target, sem).start()
            continue
        source, size, start = cut
        for n, owner in enumerate(owners):
            pltpu.make_async_copy(
                ref.at[n, :, source : source + size],
                owner_part(target, me_ref[1] ^ owner, width, start, size),
                sem,
            ).start()


def wait_all(ref, sem):
    pltpu.make_async_copy(ref, ref, sem).wait()


def sem_of(sems, number):
    return sems[number] if isinstance(sems, list) else sems.at[number]


def store_blocks(source, outs, width, sems, me_ref):
    for number, (ref, owners, start, source_start, size) in enumerate(outs):
        if owners is None:
            copy = pltpu.make_async_copy(source, ref, sem_of(sems, number))
            copy.start()
            copy.wait()
            continue
        for n, owner in enumerate(owners):
            pltpu.make_async_copy(
                owner_part(source, me_ref[1] ^ owner, width, source_start, size),
                ref.at[n, :, start : start + size],
                sem_of(sems, number),
            ).start()


def wait_blocks(outs, sems):
    for number, (ref, owners, *_) in enumerate(outs):
        if owners is not None:
            wait_all(ref, sems.at[number])


def join_attention(stage, w_qkv, w_proj):
    owners = stage.shape[0]
    wide, narrow = 3 * C // owners, C // owners
    w_qkv[...] = jnp.concatenate([stage[n, :, :wide] for n in range(owners)], 1)
    w_proj[...] = jnp.concatenate([stage[n, :, wide : wide + narrow] for n in range(owners)], 1)


def pick_heads(first, second):
    lane = lax.broadcasted_iota(jnp.int32, (DEPTH, 128), 1)
    parts = []
    for h in range(PACK):
        at = (slice(h * DEPTH, (h + 1) * DEPTH), slice(h // 2 * 128, (h // 2 + 1) * 128))
        one, two = first[at], second[at]
        if h % 2:
            one = pltpu.roll(one, SLOT, 1)
        else:
            two = pltpu.roll(two, SLOT, 1)
        parts.append(jnp.where(lane < SLOT, one, two))
    return jnp.concatenate(parts, 0)


def apply_pair(rows_ref, cut, eye, first, second):
    turned = dot(eye, rows_ref[cut], NT).astype(BF16)
    empty = jnp.zeros_like(first)
    full = dot(
        turned,
        jnp.concatenate(
            [jnp.concatenate([first, empty], 1), jnp.concatenate([empty, second], 1)], 0
        ),
    )
    return pick_heads(full[:, :LANES], full[:, LANES:])


def identity():
    shape = (128, 128)
    same = lax.broadcasted_iota(jnp.int32, shape, 0) == lax.broadcasted_iota(jnp.int32, shape, 1)
    return same.astype(F32).astype(BF16)


def pipelined(units, first, second, third):
    ones, twos = {}, {}
    count = len(units)
    for n in range(count + 2):
        if n < count:
            ones[n] = first(*units[n])
        if 1 <= n <= count:
            twos[n - 1] = second(*units[n - 1], ones.pop(n - 1))
        if n >= 2:
            third(*units[n - 2], twos.pop(n - 2))


def each_image(images, body, unrolled):
    lax.fori_loop(0, images, body, 0, unroll=images if unrolled else 1)


def forward_attention(
    field, sizes, w_qkv, w_proj, perm, perm_t, row_limit, col_limit, bias, small, qkv_bias,
    qkv_ref, prob_ref, windowed_ref, mixed_ref, attended_ref, unrolled,
):
    hat, _ = norm_parts(field)
    normed = (hat * small[0:1] + small[1:2]).astype(BF16)
    images = len(sizes)
    for b in range(images):
        windowed_ref[b] = dot(perm[...], normed[b * ROWS : (b + 1) * ROWS]).astype(BF16)
    flat = windowed_ref[...].reshape(images * WROWS, C)
    qkv = (dot(flat, w_qkv[...]) + qkv_bias).astype(BF16)
    qkv_ref[...] = qkv.reshape(images, WROWS, 3 * C)
    low_masks = head_masks(BF16)
    eye = identity()
    def one_image(b, carry):
        rows, cols = sizes[0]
        for n in range(1, images):
            rows = jnp.where(b == n, sizes[n][0], rows)
            cols = jnp.where(b == n, sizes[n][1], cols)
        blocks = {}
        for w in range(NWIN):
            allowed = (row_limit[w] < rows) & (col_limit[w] < cols)
            blocks[w] = jnp.where(allowed, 0.0, MASKED).astype(F32)
        attend(b, blocks)
        return carry

    def attend(b, blocks):
        units = [(b, pair, g, blocks) for pair in range(NWIN // 2) for g in range(NGRP)]
        pipelined(units, raw_scores, softmax, apply)

    def raw_scores(b, pair, g, blocks):
        results = []
        for w in (2 * pair, 2 * pair + 1):
            at = slice(w * SLOT, (w + 1) * SLOT)
            query = qkv_ref[b, at, g * 128 : (g + 1) * 128]
            key = qkv_ref[b, at, C + g * 128 : C + (g + 1) * 128]
            results.append(dot(key, spread_heads(query, low_masks), NT))
        return results

    def softmax(b, pair, g, blocks, raw):
        probs = []
        for n, score in enumerate(raw):
            w = 2 * pair + n
            block = jnp.concatenate([blocks[w]] * 2, 1)
            score = score * SCALE + (bias[g] + block)
            top = jnp.max(score, 0, keepdims=True)
            expo = jnp.exp(score - top)
            prob = (expo * (1.0 / jnp.sum(expo, 0, keepdims=True))).astype(BF16)
            prob_ref[b, w, g] = prob
            probs.append(prob)
        return probs

    def apply(b, pair, g, blocks, probs):
        both = slice(pair * 2 * SLOT, (pair + 1) * 2 * SLOT)
        value = (b, both, slice(2 * C + g * 128, 2 * C + (g + 1) * 128))
        mixed_ref[b, g * 128 : (g + 1) * 128, both] = apply_pair(qkv_ref, value, eye, *probs).astype(BF16)

    each_image(images, one_image, unrolled)
    for b in range(images):
        attended_ref[b] = dot(perm_t[...], mixed_ref[b], NT).astype(BF16)
    attended = attended_ref[...].reshape(images * ROWS, C)
    middle = field + dot(attended, w_proj[...]) + small[4:5]
    return normed, middle


def forward_mlp(middle, w_up, w_down, small, up_bias, active_ref, slope_ref):
    hat, _ = norm_parts(middle)
    mlp_in = (hat * small[5:6] + small[6:7]).astype(BF16)
    branch = jnp.zeros(middle.shape, F32)
    width = CHUNK
    for part in range(HID // width):
        at = slice(part * width, (part + 1) * width)
        pre = dot(mlp_in, w_up[:, at]) + up_bias[:, at]
        half = 0.5 * (1.0 + lax.erf(pre * (0.5**0.5)))
        active = (pre * half).astype(BF16)
        slope = half + pre * (jnp.exp(-0.5 * pre * pre) * ((2.0 * np.pi) ** -0.5))
        active_ref[..., at] = active.reshape(active_ref.shape[:-1] + (width,))
        slope_ref[..., at] = slope.astype(BF16).reshape(slope_ref.shape[:-1] + (width,))
        branch = branch + dot(active, w_down[:, at], NT)
    return mlp_in, middle + branch + small[7:8]


def backward_mlp(
    grad, middle, slope_ref, w_up, w_down, small, low_ref, pre_ref, rows_ref, up_rows_ref, place
):
    low = grad.astype(BF16)
    low_ref[place, :] = low
    rows_ref[7:8, :] += col_sum(low.astype(F32))
    normed_grad = jnp.zeros(grad.shape, F32)
    width = CHUNK
    for part in range(HID // width):
        at = slice(part * width, (part + 1) * width)
        slope = slope_ref[..., at].reshape(-1, width).astype(F32)
        pre = (dot(low, w_down[:, at]) * slope).astype(BF16)
        pre_ref[place, at] = pre
        up_rows_ref[:, at] += col_sum(pre.astype(F32))
        normed_grad = normed_grad + dot(pre, w_up[:, at], NT)
    hat, rate = norm_parts(middle)
    rows_ref[5:6, :] += col_sum(normed_grad * hat)
    rows_ref[6:7, :] += col_sum(normed_grad)
    return norm_back(normed_grad, hat, rate, small[5:6]) + grad


def backward_attention(
    grad_mid, field, qkv_ref, prob_ref, w_qkv, w_proj, perm, perm_t, small,
    spread_ref, dq_ref, dkv_ref, attn_ref, joined_ref, rows_ref, qkv_rows_ref, bias_grad_ref, start,
    need_grad, unrolled,
):
    images = qkv_ref.shape[0]
    place = pl.ds(start, images * ROWS)
    attn = grad_mid.astype(BF16)
    attn_ref[place, :] = attn
    rows_ref[4:5, :] += col_sum(attn.astype(F32))
    joined = dot(attn, w_proj[...], NT).astype(BF16)
    for b in range(images):
        joined_ref[b] = dot(perm[...], joined[b * ROWS : (b + 1) * ROWS]).astype(BF16)
    low_masks = head_masks(BF16)
    eye = identity()

    def cut(n, g):
        return slice(n * C + g * 128, n * C + (g + 1) * 128)

    def prob_grads(b, pair, g):
        results = []
        for w in (2 * pair, 2 * pair + 1):
            at = slice(w * SLOT, (w + 1) * SLOT)
            out = spread_heads(joined_ref[b, at, cut(0, g)], low_masks)
            results.append(dot(qkv_ref[b, at, cut(2, g)], out, NT))
            dkv_ref[b, at, cut(1, g)] = dot(prob_ref[b, 2 * pair + len(results) - 1, g], out).astype(BF16)
        return results

    def score_grads(b, pair, g, grads):
        results = []
        for n, prob_grad in enumerate(grads):
            wide = prob_ref[b, 2 * pair + n, g].astype(F32)
            weighted = wide * prob_grad
            score = weighted - wide * jnp.sum(weighted, 0, keepdims=True)
            bias_grad_ref[g] += score
            results.append(score.astype(BF16))
        return results

    def products(b, pair, g, scores):
        both = slice(pair * 2 * SLOT, (pair + 1) * 2 * SLOT)
        for n, score in enumerate(scores):
            w = 2 * pair + n
            at = slice(w * SLOT, (w + 1) * SLOT)
            query = spread_heads(qkv_ref[b, at, cut(0, g)], low_masks)
            dkv_ref[b, at, cut(0, g)] = (dot(score, query) * SCALE).astype(BF16)
        dq_ref[b, cut(0, g), both] = (
            apply_pair(qkv_ref, (b, both, cut(1, g)), eye, *scores) * SCALE
        ).astype(BF16)

    def one_image(b, carry):
        units = [(b, pair, g) for pair in range(NWIN // 2) for g in range(NGRP)]
        pipelined(units, prob_grads, score_grads, products)
        return carry

    each_image(images, one_image, unrolled)
    for b in range(images):
        rows = pl.ds(pl.multiple_of(start + b * ROWS, 16), ROWS)
        spread_ref[rows, :C] = dot(perm_t[...], dq_ref[b], NT).astype(BF16)
        spread_ref[rows, C:] = dot(perm_t[...], dkv_ref[b]).astype(BF16)
    back = spread_ref[place, :]
    qkv_rows_ref[:, :C] += col_sum(back[:, :C].astype(F32))
    qkv_rows_ref[:, 2 * C :] += col_sum(back[:, 2 * C :].astype(F32))
    normed_grad = dot(back, w_qkv[...], NT)
    hat, rate = norm_parts(field)
    rows_ref[0:1, :] += col_sum(normed_grad * hat)
    rows_ref[1:2, :] += col_sum(normed_grad)
    if not need_grad:
        return None
    return norm_back(normed_grad, hat, rate, small[0:1]) + grad_mid


def image_place():
    return pl.ds(pl.multiple_of(pl.program_id(0) * GROUP * ROWS, 16), GROUP * ROWS)


def flat(ref):
    return ref[...].reshape(-1, ref.shape[-1])


def rows_in(k, name):
    if hasattr(k, name):
        return flat(getattr(k, name))
    rows = flat(getattr(k, name + "0"))
    number = 1
    while hasattr(k, f"{name}{number}"):
        rows = jnp.where(pl.program_id(0) == number, flat(getattr(k, f"{name}{number}")), rows)
        number += 1
    return rows


def put_rows(ref, value):
    ref[...] = value.reshape(ref.shape)


def is_first():
    return pl.program_id(0) == 0


def is_last():
    return pl.program_id(0) == pl.num_programs(0) - 1


def clear(*refs):
    @pl.when(is_first())
    def _():
        for ref in refs:
            ref[...] = jnp.zeros(ref.shape, ref.dtype)


class Names:
    def __init__(self, **refs):
        self.__dict__.update(refs)


def fetch_attention(k, plan):
    if not plan.sources:
        return

    @pl.when(is_first())
    def _():
        load_blocks(plan.pieces(k, "attn"), k.stage, plan.widths["attn"], k.load_sem.at[0], k.me)
        wait_all(k.stage, k.load_sem.at[0])
        join_attention(k.stage, k.w_qkv, k.w_proj)
        for n, (source, target) in enumerate(((k.w_qkv, k.qkv_out), (k.w_proj, k.proj_out))):
            pltpu.make_async_copy(source, target, k.out_sem.at[n]).start()


def fetch_mlp(k, plan):
    @pl.when(is_first())
    def _():
        load_blocks(plan.pieces(k, "down"), k.w_down, plan.widths["down"], k.load_sem.at[1], k.me)
        load_blocks(plan.pieces(k, "up"), k.w_up, plan.widths["up"], k.load_sem.at[2], k.me)
        wait_all(k.w_down, k.load_sem.at[1])
        wait_all(k.w_up, k.load_sem.at[2])


def group_images(k, group=0):
    images = k.rows.shape[1]
    first = (pl.program_id(0) + group) * GROUP
    return [((first + b) // images, (first + b) % images) for b in range(GROUP)]


def group_sizes(k, group=0):
    return [(k.rows[m, n], k.cols[m, n]) for m, n in group_images(k, group)]


def small_rows(k, plan):
    return k.vec[plan.layer * PER_LAYER : plan.layer * PER_LAYER + 8]


def joined_rows(k, start, end):
    return jnp.concatenate([k.vec[n : n + 1] for n in range(start, end)], 1)


def up_bias_row(k, plan):
    return joined_rows(k, plan.layer * PER_LAYER + 8, (plan.layer + 1) * PER_LAYER)


def attention_forward_kernel(k, plan):
    fetch_attention(k, plan)
    small = small_rows(k, plan)
    qkv_bias = jnp.concatenate([small[2:3], jnp.zeros((1, C), F32), small[3:4]], 1)
    normed, middle = forward_attention(
        flat(k.field).astype(F32), group_sizes(k, plan.group), k.w_qkv, k.w_proj, k.perm, k.perm_t,
        k.row_limit, k.col_limit, k.bias, small, qkv_bias, k.qkv, k.prob, k.windowed,
        k.mixed, k.attended, True,
    )
    put_rows(k.normed, normed)
    put_rows(k.middle, middle)
    if not plan.sources:
        return

    @pl.when(is_last())
    def _():
        wait_all(k.w_qkv, k.out_sem.at[0])
        wait_all(k.w_proj, k.out_sem.at[1])


def first_mlp_kernel(k, plan):
    fetch_mlp(k, plan)

    @pl.when(is_first())
    def _():
        for n, (source, target) in enumerate(((k.w_down, k.down_out), (k.w_up, k.up_out))):
            pltpu.make_async_copy(source, target, k.out_sem.at[n]).start()

    mlp_in, result = forward_mlp(
        rows_in(k, "middle"), k.w_up, k.w_down, small_rows(k, plan), up_bias_row(k, plan), k.active,
        k.slope,
    )
    put_rows(k.mlp_in, mlp_in)
    put_rows(k.result, result)

    @pl.when(is_last())
    def _():
        wait_all(k.w_down, k.out_sem.at[0])
        wait_all(k.w_up, k.out_sem.at[1])


def store_mlp_grads(k, plan):
    for at in range(0, HID, CHUNK):
        k.up_grad[:, at : at + CHUNK] = dot(k.mlp_all[...], k.pre_all[:, at : at + CHUNK], TN).astype(BF16)
    store_blocks(k.up_grad, plan.outs(k, "up"), plan.widths["up"], k.sem_x, k.me)
    for at in range(0, HID, CHUNK):
        k.down_grad[:, at : at + CHUNK] = dot(k.low_all[...], k.active_all[:, at : at + CHUNK], TN).astype(BF16)
    store_blocks(k.down_grad, plan.outs(k, "down"), plan.widths["down"], k.sem_y, k.me)


def wait_mlp_grads(k, plan):
    wait_blocks(plan.outs(k, "up"), k.sem_x)
    wait_blocks(plan.outs(k, "down"), k.sem_y)


def head_pass(k, plan, result, sizes, total_images):
    first = pl.program_id(0) * GROUP
    base = plan.layers * PER_LAYER
    gain = k.vec[base : base + 1]
    hat, rate = norm_parts(result)
    final = hat * gain + k.vec[base + 1 : base + 2]
    places = group_images(k)
    owners, _, width = k.w_head.shape
    row = lax.broadcasted_iota(jnp.int32, (16, 1), 0)
    pooled = jnp.zeros((16, C), F32)
    own = other = jnp.full((16, 1), -1, jnp.int32)
    mixing = jnp.zeros((16, 1), F32)
    shares = []
    for b, (rows, cols) in enumerate(sizes):
        inside = ((k.cell_row[...] < rows) & (k.cell_col[...] < cols)).astype(F32)
        count = (rows * cols).astype(F32)
        mean = col_sum(final[b * ROWS : (b + 1) * ROWS] * inside) / count
        shares.append(inside / count)
        pooled = jnp.where(row == b, mean, pooled)
        m, n = places[b]
        mine = (k.me[0] * owners + k.me[1]) * k.rows.shape[1] + n
        own = jnp.where(row == b, k.labels[m, mine], own)
        other = jnp.where(row == b, k.labels[m, k.partner[m, n]], other)
        mixing = jnp.where(row == b, k.mix[m, n].astype(F32) / 16.0, mixing)
    pooled = pooled.astype(BF16)
    classes = owners * width
    real = CLASSES // owners
    bias = joined_rows(k, base + 2, base + 2 - (-CLASSES // C))
    empty = jnp.full((1, width - real), MASKED, F32)
    bias = jnp.concatenate(
        [part for n in range(owners) for part in (bias[:, n * real : (n + 1) * real], empty)], 1
    )
    logits = jnp.concatenate([dot(pooled, k.w_head[n]) for n in range(owners)], 1)
    logits = logits + bias
    top = jnp.max(logits, -1, keepdims=True)
    expo = jnp.exp(logits - top)
    log_probs = logits - top - jnp.log(jnp.sum(expo, -1, keepdims=True))
    lane = lax.broadcasted_iota(jnp.int32, (16, classes), 1)
    label = lane // width * real + lane % width
    label = jnp.where(lane % width < real, label, -2)
    target = jnp.where(label == own, mixing, 0.0)
    target = target + jnp.where(label == other, 1.0 - mixing, 0.0)
    loss = jnp.where(target > 0.0, target * log_probs, 0.0)
    loss = jnp.sum(jnp.sum(loss, -1, keepdims=True), 0, keepdims=True)
    k.loss[...] -= jnp.broadcast_to(loss, k.loss.shape)
    logit_grad = jnp.where(row < GROUP, (jnp.exp(log_probs) - target) / total_images, 0.0)
    logit_low = logit_grad.astype(BF16)
    wide = logit_low.astype(F32)
    k.head_rows[...] += col_sum(wide)
    for b in range(GROUP):
        k.pooled_all[pl.ds(first + b, 1), :] = pooled[b : b + 1].astype(F32)
        k.logit_all[pl.ds(first + b, 1), :] = wide[b : b + 1]
    pooled_grad = jnp.zeros((16, C), F32)
    for n in range(owners):
        pooled_grad += dot(logit_low[:, n * width : (n + 1) * width], k.w_head[n], NT)
    final_grad = jnp.concatenate(
        [pooled_grad[b : b + 1] * share for b, share in enumerate(shares)], 0
    )
    k.final_rows[0:1, :] += col_sum(final_grad * hat)
    k.final_rows[1:2, :] += col_sum(final_grad)
    return norm_back(final_grad, hat, rate, gain)


def last_mlp_kernel(k, plan, total_images):
    place = image_place()

    @pl.when(is_first())
    def _():
        load_blocks(plan.pieces(k, "head"), k.w_head, plan.widths["head"], k.load_sem.at[3], k.me)

    fetch_mlp(k, plan)

    @pl.when(is_first())
    def _():
        wait_all(k.w_head, k.load_sem.at[3])

    clear(k.row_sums, k.up_rows, k.final_rows, k.head_rows, k.loss, k.pooled_all, k.logit_all)
    middle = rows_in(k, "middle")
    mlp_in, result = forward_mlp(
        middle, k.w_up, k.w_down, small_rows(k, plan), up_bias_row(k, plan), k.active_all.at[place], k.slope
    )
    k.mlp_all[place, :] = mlp_in
    grad = head_pass(k, plan, result, group_sizes(k), total_images)
    put_rows(k.grad_mid, backward_mlp(
        grad, rows_in(k, "middle"), k.slope, k.w_up, k.w_down, small_rows(k, plan), k.low_all, k.pre_all,
        k.row_sums, k.up_rows, place,
    ))

    @pl.when(is_last())
    def _():
        store_mlp_grads(k, plan)
        total = dot(k.pooled_all[...].astype(BF16), k.logit_all[...].astype(BF16), TN).astype(BF16)
        owners, _, width = k.head_grad.shape
        for n in range(owners):
            k.head_grad[n] = total[:, n * width : (n + 1) * width]
        store_blocks(
            k.head_grad, plan.outs(k, "head"), plan.widths["head"],
            [k.sem_x.at[0], k.sem_x.at[1], k.sem_y.at[0], k.sem_y.at[1]], k.me,
        )
        wait_mlp_grads(k, plan)


def backward_mlp_kernel(k, plan):
    clear(k.row_sums, k.up_rows)
    place = image_place()
    k.mlp_all[place, :] = flat(k.mlp_in)
    k.active_all[place, :] = flat(k.active)
    put_rows(k.grad_mid, backward_mlp(
        rows_in(k, "grad"), rows_in(k, "middle"), k.slope, k.w_up, k.w_down, small_rows(k, plan), k.low_all, k.pre_all,
        k.row_sums, k.up_rows, place,
    ))

    @pl.when(is_last())
    def _():
        store_mlp_grads(k, plan)
        wait_mlp_grads(k, plan)


def backward_attention_kernel(k, plan, earlier, need_grad):
    sums = ("row_sums", "qkv_rows", "bias_grad")
    if earlier:
        @pl.when(is_first())
        def _():
            for name in sums:
                getattr(k, name)[...] = getattr(k, name + "_in")[...]
    else:
        clear(*[getattr(k, name) for name in sums])
    start = pl.multiple_of(earlier * ROWS + pl.program_id(0) * GROUP * ROWS, 16)
    grad = backward_attention(
        flat(k.grad_mid), flat(k.field).astype(F32), k.qkv, k.prob, k.w_qkv, k.w_proj, k.perm,
        k.perm_t, small_rows(k, plan), k.spread_all, k.dq, k.dkv, k.attn_all, k.joined, k.row_sums,
        k.qkv_rows, k.bias_grad, start, need_grad, True,
    )
    if need_grad:
        put_rows(k.grad, grad)
    if "attn" not in plan.targets:
        return
    place = pl.ds(start, GROUP * ROWS)
    k.normed_all[place, :] = flat(k.normed)
    k.attended_all[place, :] = flat(k.attended)

    @pl.when(is_last())
    def _():
        if earlier:
            before = slice(0, earlier * ROWS)
            k.normed_all[before, :] = flat(k.normed_in)
            k.attended_all[before, :] = flat(k.attended_in)
            k.spread_all[before, :] = k.spread_in[...]
            k.attn_all[before, :] = k.attn_in[...]
        owners, _, _ = k.attn_grad.shape
        wide, narrow = 3 * C // owners, C // owners
        if plan.collect is not None:
            layers, head_real, loss_at, near = plan.collect
            own = [k.row_sums, k.qkv_rows, k.mlp_rows0, k.up_rows0, k.bias_grad]
            collect_rows(
                layers, head_real, loss_at,
                own + [k.row_sums1, k.qkv_rows1, k.mlp_rows1, k.up_rows1, k.bias_grad1]
                + [k.final_rows, k.head_rows, k.loss],
                k.small_rows, k.spread_table,
            )
            pair_rows(k.small_rows, owners, near, k.me, k.pairs)
            for flip, (ref, *_) in enumerate(plan.outs(k, "attn")[2:]):
                width = ref.shape[2]
                pltpu.make_async_copy(
                    k.pairs.at[flip], ref.at[:, :, width - 128 : width], k.sem_a.at[2 + flip]
                ).start()
        total = dot(k.normed_all[...], k.spread_all[...], TN).astype(BF16)
        for n in range(owners):
            k.attn_grad[n, :, :wide] = total[:, n * wide : (n + 1) * wide]
        total = dot(k.attended_all[...], k.attn_all[...], TN).astype(BF16)
        for n in range(owners):
            k.attn_grad[n, :, wide:] = total[:, n * narrow : (n + 1) * narrow]
        store_blocks(k.attn_grad, plan.outs(k, "attn"), plan.widths["attn"], k.sem_a, k.me)
        wait_blocks(plan.outs(k, "attn"), k.sem_a)


class Plan:
    def __init__(self, widths, layer, layers):
        self.widths, self.layer, self.layers = widths, layer, layers
        self.sources = {}
        self.targets = {}
        self.collect = None
        self.group = 0

    def pieces(self, k, name):
        return [(getattr(k, ref), owners, cut) for ref, owners, cut in self.sources[name]]

    def outs(self, k, name):
        return [(getattr(k, ref), *rest) for ref, *rest in self.targets[name]]


def whole(shape):
    return pl.BlockSpec(shape, lambda i: (0,) * len(shape))


def per_image(*shape, first=0):
    return pl.BlockSpec((GROUP,) + shape, lambda i: (i + first,) + (0,) * len(shape))


SCALARS = pl.BlockSpec(memory_space=pltpu.SMEM)
FAR = pl.BlockSpec(memory_space=pl.ANY)
NEAR = pl.BlockSpec(memory_space=pltpu.VMEM)


def call(body, name, groups, ins, outs, scratch, flops):
    def kernel(*refs):
        body(Names(**dict(zip(list(ins) + list(outs) + list(scratch), refs))))

    moved = sum(a.size * a.dtype.itemsize for _, a in ins.values())
    results = pl.pallas_call(
        kernel,
        grid=(groups,),
        in_specs=[spec for spec, _ in ins.values()],
        out_specs=[spec for spec, _, _ in outs.values()],
        out_shape=[jax.ShapeDtypeStruct(dims, dtype) for _, dims, dtype in outs.values()],
        scratch_shapes=list(scratch.values()),
        compiler_params=pltpu.CompilerParams(
            dimension_semantics=("arbitrary",), vmem_limit_bytes=VMEM_LIMIT
        ),
        cost_estimate=pl.CostEstimate(flops=int(8 * flops), bytes_accessed=int(moved), transcendentals=0),
        name=name,
    )(*[array for _, array in ins.values()])
    return dict(zip(outs, results))


def exchange(array, step):
    axis, bit = step
    size = lax.axis_size(axis)
    return lax.ppermute(array, axis, [(i, i ^ (1 << bit)) for i in range(size)])


class Held:
    def __init__(self, array, dims=()):
        self.array, self.dims = array, list(dims)


def stack_blocks(parts, me, name, cuts=None):
    cuts = cuts or [None] * len(parts)
    args, outs, results = [], [], []
    for (held, received, step), cut in zip(parts, cuts):
        count, rows, columns = held.array.shape
        args += [held.array, received]
        axis, bit = step
        place = sum(d[0] == "win" and d[1] < bit for d in held.dims) if axis == "win" else len(held.dims)
        at = len(held.dims) - place
        dims = held.dims[:at] + [step] + held.dims[at:]
        bounds = [0, *(cut or ()), columns]
        pieces = list(zip(bounds, bounds[1:]))
        outs += [((2 * count, rows, end - start), BF16) for start, end in pieces]
        results.append((place, axis, bit, pieces, dims))

    def kernel(me_ref, *refs):
        ins, targets = list(refs[: len(args)]), list(refs[len(args) :])
        for place, axis, bit, pieces, _ in results:
            held, received = ins.pop(0), ins.pop(0)
            mine = (me_ref[0] >> bit) & 1 if axis == "win" else 0
            for start, end in pieces:
                out = targets.pop(0)
                for n in range(held.shape[0]):
                    base = (n >> place << (place + 1)) + (n & ((1 << place) - 1))
                    out[base + (mine << place)] = held[n, :, start:end]
                    out[base + ((1 - mine) << place)] = received[n, :, start:end]

    arrays = list(small_call(kernel, name, [me] + args, outs, scalars=1))
    return [
        [Held(arrays.pop(0), dims) for _ in pieces] for _, _, _, pieces, dims in results
    ]


def tie(*values):
    return lax.optimization_barrier(values)


def small_call(kernel, name, args, outs, stream=False, scratch=(), scalars=0, limit=24):
    def spec(dims):
        return whole(dims) if stream else pl.BlockSpec(memory_space=pltpu.VMEM)

    return pl.pallas_call(
        kernel,
        grid=(1,) if stream else (),
        out_shape=[jax.ShapeDtypeStruct(dims, dtype) for dims, dtype in outs],
        in_specs=[SCALARS] * scalars + [spec(a.shape) for a in args[scalars:]],
        out_specs=[spec(dims) for dims, _ in outs],
        scratch_shapes=list(scratch),
        compiler_params=pltpu.CompilerParams(
            vmem_limit_bytes=limit * 1024 * 1024
        ),
        cost_estimate=pl.CostEstimate(flops=1, bytes_accessed=1, transcendentals=0),
        name=name,
    )(*args)


class Chain:
    def __init__(self, keep, send, dims, steps, pair_at=None):
        self.keep, self.send, self.dims, self.steps = keep, send, list(dims), list(steps)
        self.pair_at = pair_at

    def start(self):
        self.received = exchange(self.send, self.steps.pop(0))


def add_blocks(keep, received, pair_at):
    total = keep.astype(F32) + received.astype(F32)
    if pair_at is None:
        return total.astype(BF16)
    pair = total[:16, pair_at:] + total[16:32, pair_at:]
    high = pair.astype(BF16)
    tail = jnp.zeros((total.shape[0] - 32, pair.shape[1]), BF16)
    parts = [jnp.concatenate([high, (pair - high.astype(F32)).astype(BF16), tail], 0)]
    if pair_at:
        parts = [total[:, :pair_at].astype(BF16)] + parts
    return jnp.concatenate(parts, 1)


def combine(groups, me, name):
    args, outs = [], []
    for group in groups:
        for chain in group:
            args += [chain.keep, chain.received]
        count, rows, _ = group[0].keep.shape
        width = sum(chain.keep.shape[2] for chain in group)
        outs += [((count // 2, rows, width), BF16)] * 2

    def kernel(me_ref, *refs):
        ins, results = list(refs[: len(args)]), list(refs[len(args) :])
        for group in groups:
            keep_out, send_out = results.pop(0), results.pop(0)
            start = 0
            for chain in group:
                keep, received = ins.pop(0), ins.pop(0)
                width = keep.shape[2]
                axis, bit = chain.steps[0]
                place = len(chain.dims) - 1 - chain.dims.index((axis, bit))
                mine = (me_ref[0] >> bit) & 1 if axis == "win" else 0
                for n in range(keep_out.shape[0]):
                    base = (n >> place << (place + 1)) + (n & ((1 << place) - 1))
                    for out, at in (
                        (keep_out, base + (mine << place)), (send_out, base + ((1 - mine) << place))
                    ):
                        out[n, :, start : start + width] = add_blocks(
                            keep[at], received[at], chain.pair_at
                        )
                start += width

    results = small_call(kernel, name, [me] + args, outs, scalars=1)
    chains = []
    for n, group in enumerate(groups):
        step = group[0].steps[0]
        at, pair_at = 0, None
        for chain in group:
            if chain.pair_at is not None:
                pair_at = at + chain.pair_at
            at += chain.keep.shape[2]
        dims = [d for d in group[0].dims if d != step]
        chains.append(Chain(results[2 * n], results[2 * n + 1], dims, group[0].steps, pair_at))
    return chains


def finish(chain, name):
    _, rows, width = chain.keep.shape

    def kernel(keep, received, own, square):
        total = keep[0].astype(F32) + received[0].astype(F32)
        own[...] = total
        square[...] = jnp.broadcast_to(jnp.sum(total * total), (1, 128))

    return small_call(
        kernel, name, [chain.keep, chain.received], [((rows, width), F32), ((1, 128), F32)]
    )


def finish_pair(chain, squares, devices, share, name):
    _, rows, width = chain.keep.shape
    at = chain.pair_at

    def kernel(keep, received, *refs):
        total = keep[0].astype(F32) + received[0].astype(F32)
        own, message = refs[-2:]
        own[...] = total[:, :at]
        pair = total[:16, at:] + total[16:32, at:]
        square = jnp.sum(total[:, :at] * total[:, :at])
        square = jnp.broadcast_to(square, (1, 128))
        for ref in refs[:-2]:
            square = square + ref[...]
        row = [pair[n : n + 1] for n in range(share // 128)] + [square]
        message[...] = jnp.broadcast_to(jnp.concatenate(row, 1), message.shape)

    return small_call(
        kernel, name, [chain.keep, chain.received] + squares,
        [((rows, at), F32), ((devices, share + 128), F32)],
    )


def adam_step(weight, grad, first, second, rate):
    new_first = 0.5 * first + 0.5 * grad
    new_second = 0.5 * second + 0.5 * grad * grad
    fix = 1.0 - 0.5**STEP
    update = new_first / fix / (jnp.sqrt(new_second / fix) + ADAM_EPS)
    return (new_first, new_second, weight - rate * (update + DECAY_RATE * weight))


def update_kernel(starts, widths, layout, *refs):
    own, message, rest = refs[:3], refs[3], list(refs[4:])
    groups = [rest[3 * n : 3 * n + 3] for n in range(7)]
    loss_ref, norm_ref = rest[21], rest[22]
    outs = [rest[23 + 3 * n : 26 + 3 * n] for n in range(7)]
    vector_rows, table_rows, offsets, square_at, loss_at = layout
    vector_grad = message[:vector_rows, :C]
    table_grad = message[:table_rows, C : C + offsets]
    total = (
        jnp.sum(message[:, square_at : square_at + 1])
        + jnp.sum(vector_grad * vector_grad)
        + jnp.sum(table_grad * table_grad)
    )
    norm = jnp.sqrt(jnp.broadcast_to(total, (1, 1)))
    factor = CLIP_NORM / jnp.maximum(norm, CLIP_NORM)
    norm_ref[...] = norm
    loss_ref[...] = message[0:1, loss_at : loss_at + 1]

    def put(number, layer, grad, rate):
        weight, first, second = groups[number]
        index = (Ellipsis,) if layer is None else (layer, Ellipsis)
        if number == 6:
            index = (slice(None), layer, slice(None))
        results = adam_step(weight[index], factor * grad, first[index], second[index], rate)
        for ref, value in zip(outs[number], results):
            ref[index] = value

    layers = len(starts)
    for l in range(layers):
        qkv_width = outs[0][0].shape[2]
        part, at = starts[l]["attn"]
        put(0, l, own[part][:, at : at + qkv_width], LEARN_RATE)
        put(1, l, own[part][:, at + qkv_width : at + widths["attn"]], LEARN_RATE)
        part, at = starts[l]["up"]
        put(2, l, own[part][:, at : at + widths["up"]], LEARN_RATE)
        part, at = starts[l]["down"]
        put(3, l, own[part][:, at : at + widths["down"]], LEARN_RATE)
        heads = table_rows // layers
        put(6, l, table_grad[l * heads : (l + 1) * heads], SMALL_RATE)
    half = widths["head"] // 2
    head_grad = jnp.concatenate(
        [own[part][:, at : at + half] for part, at in starts[-1]["head"]], 1
    )
    put(4, None, head_grad[:, : outs[4][0].shape[1]], LEARN_RATE)
    put(5, None, vector_grad, SMALL_RATE)


def collect_rows(layers, head_real, loss_at, ins, out, spread):
    out[...] = jnp.zeros(out.shape, F32)
    row_of_slot = lax.broadcasted_iota(jnp.int32, (SLOT, 128), 0)
    lane = lax.broadcasted_iota(jnp.int32, (SLOT, 128), 1)
    target = row_of_slot // WSIDE * (2 * WSIDE - 1) + row_of_slot % WSIDE
    spreader = ((lane == target) & (row_of_slot < AREA)).astype(F32).astype(BF16)
    row = 0
    for l in range(layers):
        attn_rows, qkv_rows, mlp_rows, up_rows, bias_grad = ins[5 * l : 5 * l + 5]
        parts = [
            attn_rows[0:2], qkv_rows[:, :C], qkv_rows[:, 2 * C :], attn_rows[4:5], mlp_rows[5:8],
        ] + [up_rows[:, n * C : (n + 1) * C] for n in range(HID // C)]
        for part in parts:
            out[row : row + part.shape[0], :C] = part
            row += part.shape[0]
        for head in range(HEADS):
            g, h = divmod(head, PACK)
            left = bias_grad[g, :, h * SLOT : (h + 1) * SLOT]
            total = jnp.zeros((SLOT, 128), F32)
            for _ in range(3):
                low = left.astype(BF16)
                total = total + dot(low, spreader)
                left = left - low.astype(F32)
            spread[head * SLOT : (head + 1) * SLOT, :] = total
        table = jnp.zeros((HEADS, 256), F32)
        span = 2 * WSIDE - 1
        for j in range(AREA):
            wide = jnp.concatenate(
                [spread[pl.ds(j, HEADS, stride=SLOT), :], jnp.zeros((HEADS, 128), F32)], 1
            )
            shift = (WSIDE - 1 - j // WSIDE) * span + WSIDE - 1 - j % WSIDE
            table = table + (pltpu.roll(wide, shift, 1) if shift else wide)
        width = out.shape[1] - C
        out[l * HEADS : (l + 1) * HEADS, C:] = table[:, :width]
    final_rows, head_rows, loss = ins[5 * layers :]
    out[row : row + 2, :C] = final_rows[...]
    row += 2
    cuts = CLASSES // head_real
    width = head_rows.shape[1] // cuts
    classes = jnp.concatenate(
        [head_rows[:, n * width : n * width + head_real] for n in range(cuts)]
        + [jnp.zeros((1, -CLASSES % C), F32)], 1
    )
    for n in range(classes.shape[1] // C):
        out[row + n : row + n + 1, :C] = classes[:, n * C : (n + 1) * C]
    out[0:1, loss_at : loss_at + 1] = loss[:, 0:1]


def pair_rows(rows, ch_count, owners, me_ref, pairs):
    count = rows.shape[1] // 128
    wins = rows.shape[0] // ch_count
    high_rows = pairs.shape[2] // wins
    for flip in range(2):
        for n, owner in enumerate(owners):
            for win in range(wins):
                values = rows[pl.ds(win * ch_count + (me_ref[1] ^ (owner ^ flip)), 1), :]
                values = jnp.concatenate(
                    [values[:, m * 128 : (m + 1) * 128] for m in range(count)]
                    + [jnp.zeros((16 - count, 128), F32)], 0
                )
                high = values.astype(BF16)
                at = win * high_rows
                pairs[flip, n, at : at + 16] = high
                pairs[flip, n, at + 16 : at + 32] = (values - high.astype(F32)).astype(BF16)
                pairs[flip, n, at + 32 : at + high_rows] = jnp.zeros((high_rows - 32, 128), BF16)


def pack_kernel(head_width, qkv, proj, down, up, head, attn0, mlp0, all1):
    attn0[...] = jnp.concatenate([qkv[0], proj[0]], 1).astype(BF16)
    mlp0[...] = jnp.concatenate([down[0], up[0]], 1).astype(BF16)
    parts = [qkv[1], proj[1], down[1], up[1], head[...]]
    pad = head_width - head.shape[1]
    if pad:
        parts.append(jnp.zeros((head.shape[0], pad), F32))
    all1[...] = jnp.concatenate(parts, 1).astype(BF16)


def per_device(
    tokens, valid_rows, valid_cols, partner, mix_level, labels,
    w_qkv, m_qkv, v_qkv, w_proj, m_proj, v_proj, w_fc1, m_fc1, v_fc1, w_fc2, m_fc2, v_fc2,
    w_head, m_head, v_head, vectors, m_vec, v_vec, rel_table, m_rel, v_rel,
):
    micro, images, cells, chans = tokens.shape
    layers = rel_table.shape[0]
    per_layer = 8 + HID // C
    base = layers * per_layer
    head_rows = vectors.shape[0] - base - 2
    all_images = labels.shape[1]
    total_images = micro * all_images
    local = micro * images
    groups = local // GROUP
    sizes = {axis: lax.axis_size(axis) for axis in ("win", "ch")}
    win_count, ch_count = sizes["win"], sizes["ch"]
    device_count = win_count * ch_count
    win_index, ch_index = lax.axis_index("win"), lax.axis_index("ch")
    me = jnp.stack([win_index, ch_index]).astype(jnp.int32)
    block_rows = C // win_count
    widths = {"attn": 4 * C // ch_count, "down": HID // ch_count, "up": HID // ch_count}
    head_real = CLASSES // ch_count
    widths["head"] = -(-head_real // 128) * 128
    head_classes = widths["head"] * ch_count
    direct = block_rows % 16 == 0 and block_rows >= 32 and all(w % 128 == 0 for w in widths.values())

    core = ("ch", 0)
    ch_high = [("ch", b) for b in range(1, ch_count.bit_length() - 1)]
    win_low = [("win", 0)]
    win_high = [("win", b) for b in range(1, win_count.bit_length() - 1)]

    def low(v):
        return v.astype(BF16)

    packed = small_call(
        functools.partial(pack_kernel, widths["head"]), "pack",
        [w_qkv, w_proj, w_fc2.transpose(0, 2, 1), w_fc1, w_head],
        [((block_rows, sum(widths[n] for n in names)), BF16) for names in (
            ("attn",), ("down", "up"), ("attn", "down", "up", "head"))],
        stream=True,
        limit=56,
    )
    names = [["attn", "down", "up"], ["attn", "down", "up", "head"]]
    onehot = jnp.asarray(relative_onehot(), BF16)
    offsets = rel_table.shape[1]
    table_width = -(-(offsets + 1) // 128) * 128
    share = C + table_width
    tables = [window_tables(l % 2 == 1) for l in range(layers)]
    perms = [jnp.asarray(t[0], BF16) for t in tables]
    perms_t = [jnp.asarray(t[0].T, BF16) for t in tables]
    row_limits = [jnp.asarray(t[1]) for t in tables]
    col_limits = [jnp.asarray(t[2]) for t in tables]

    def bias_of(table):
        table = table.transpose(0, 2, 1).reshape(layers * HEADS, offsets)
        table_parts = []
        for _ in range(3):
            table_parts.append(low(table))
            table = table - table_parts[-1].astype(F32)
        bias = dot(jnp.concatenate(table_parts, 0), onehot).reshape(3, layers, HEADS, SLOT * SLOT)
        bias = (bias[0] + bias[1]) + bias[2]
        return (
            bias.reshape(layers, NGRP, PACK, SLOT, SLOT)
            .transpose(0, 1, 3, 2, 4)
            .reshape(layers, NGRP, SLOT, LANES)
        )

    padded = jnp.pad(tokens.reshape(local, cells, chans), ((0, 0), (0, ROWS - cells), (0, 0)))

    def stage(number, *moves, cuts=None, more=()):
        received = [exchange(part.array, step) for part, step in moves]
        tied = tie(*received, *more)
        received, more = tied[: len(moves)], tied[len(moves) :]
        stacked = stack_blocks(
            [(part, got, step) for (part, step), got in zip(moves, received)],
            me, f"stack{number}", cuts,
        )
        return (stacked, *more)

    def wait_for(value, *parts):
        value, *arrays = tie(value, *[part.array for part in parts])
        for part, array in zip(parts, arrays):
            part.array = array
        return value

    far = [Held(block[None]) for block in packed]
    edges = [
        [0, widths["attn"] * 2 // 3, widths["attn"], widths["attn"] + widths["down"],
         widths["attn"] + widths["down"] + widths["up"]],
        [0, widths["attn"], widths["attn"] + widths["down"] + widths["up"] * 2 // 3,
         sum(widths[name] for name in ("attn", "down", "up", "head"))],
    ]
    staged = win_count == 8 and ch_count == 4
    if staged:
        zh, zl, y, x = ("win", 2), ("win", 1), ("win", 0), ("ch", 1)
        ((attn,),), mlp, padded = stage(0, (far[0], zh), more=(far[1].array, padded))
        (attn, (mlp,)), all1, bias = stage(
            1, (attn, zl), (Held(mlp), zh), cuts=[edges[0][1:2], None],
            more=(packed[2], bias_of(rel_table)),
        )
        floating = exchange(all1[None], zh)
        ((one,), (two,), mlp), = stage(
            2, (attn[0], y), (attn[1], x), (mlp, zl), cuts=[None, None, [widths["down"]]]
        )
        (((all1,),),) = [stack_blocks([(Held(all1[None]), floating, zh)], me, "stack10")]
        mlp[0].array, mlp[1].array, all1.array = tie(mlp[0].array, mlp[1].array, all1.array)
        near = [(one, x), (two, y), (mlp[0], x), (mlp[1], y)]
        received = [exchange(part.array, step) for part, step in near]
        floating = exchange(all1.array, zl)
        *received, floating = tie(*received, floating)
        ((one,), (two,), (down,), (up,)) = stack_blocks(
            [(part, got, step) for (part, step), got in zip(near, received)], me, "stack3"
        )
        held = [[one, two]]
        *got, floating = tie(*[exchange(part.array, core) for part in held[0]], floating)
        other = [got]
        (parts1,) = stack_blocks([(all1, floating, zl)], me, "stack11", [edges[1][1:-1]])
        padded = wait_for(padded, *parts1)
    else:
        bias = bias_of(rel_table)
        bits = win_high[::-1] + win_low + ch_high[::-1]
        held, other = [[], []], []
        for number, part in enumerate(far):
            for n, step in enumerate(bits):
                ((part,),), = stage(10 * number + n, (part, step))
            layer = number // 2
            base = 0 if number != 1 else widths["attn"]
            for start, end in zip(edges[layer], edges[layer][1:]):
                if start >= base and end - base <= part.array.shape[-1]:
                    held[layer].append(Held(part.array[..., start - base : end - base], part.dims))
        other.append([exchange(part.array, core) for part in held[0]])

    def weight_inputs(layer, wanted):
        plan = Plan(widths, layer, layers)
        ins = {}
        starts, at = {}, 0
        for name in names[layer]:
            starts[name] = at
            at += widths[name]
        bounds = list(zip(edges[layer], edges[layer][1:]))
        blocks = []
        for group, part in enumerate(held[layer]):
            if group >= len(other[layer]):
                break
            owners = relative_owners([d for d in part.dims if d[0] == "ch"])
            for number, array in enumerate((part.array, other[layer][group])):
                flat_array = array.reshape(-1, C, array.shape[-1])
                blocks.append((group, [owner ^ number for owner in owners], flat_array))
        for name in wanted:
            plan.sources[name] = []
            columns = []
            for number, (group, owners, array) in enumerate(blocks):
                begin = max(starts[name], bounds[group][0])
                end = min(starts[name] + widths[name], bounds[group][1])
                if begin >= end:
                    continue
                cut = (begin - bounds[group][0], end - begin, begin - starts[name])
                if direct:
                    ref = f"blocks{number}"
                    ins[ref] = (FAR, array)
                    plan.sources[name].append((ref, owners, cut))
                elif number % 2 == 0:
                    table = np.argsort(np.asarray(owners + blocks[number + 1][1]))
                    both = jnp.concatenate([array, blocks[number + 1][2]])
                    index = jnp.asarray(table)[jnp.arange(ch_count) ^ ch_index]
                    columns.append(jnp.take(both, index, axis=0)[..., cut[0] : cut[0] + cut[1]])
            if not direct:
                full = jnp.concatenate(columns, -1)
                if name in ("up", "down"):
                    full = full.transpose(1, 0, 2).reshape(C, -1)
                ins[f"staged_{name}"] = (FAR, full)
                plan.sources[name] = [(f"staged_{name}", None, None)]
        ins["me"] = (SCALARS, me)
        return ins, plan

    orders = {
        "x": ch_high + win_low + win_high, "a": ch_high + win_low + win_high,
        "y": win_low + ch_high + win_high, "b": win_low + ch_high + win_high,
    }
    block_dims = ch_high + [("win", b) for b in reversed(range(win_count.bit_length() - 1))]
    owners = relative_owners(ch_high)
    regular = direct and len(ch_high) == 1

    def grad_outputs(plan, **members):
        outs = {}
        for group, wanted in members.items():
            if not direct:
                for name in wanted:
                    plan.targets[name] = [(f"full_{name}", None, 0, 0, widths[name])]
                    dims = (C, HID) if name in ("up", "down") else (ch_count, C, widths[name])
                    outs[f"full_{name}"] = (FAR, dims, BF16)
                continue
            starts = np.cumsum([0] + [widths[name] for name in wanted])
            refs = [
                (f"keep_{group}", owners), (f"send_{group}", [owner ^ 1 for owner in owners])
            ]
            for ref, _ in refs:
                outs[ref] = (FAR, (len(owners), C, int(starts[-1])), BF16)
            for name, start in zip(wanted, starts):
                plan.targets[name] = [(ref, at, int(start), 0, widths[name]) for ref, at in refs]
        return outs

    def cut_attention_outputs(plan):
        cut = widths["attn"] * 2 // 3
        outs, plan.targets["attn"] = {}, []
        for group, start, size, extra in (("a", 0, cut, 0), ("b", cut, widths["attn"] - cut, 128)):
            for kind, flip in (("keep", 0), ("send", 1)):
                ref = f"{kind}_{group}"
                outs[ref] = (NEAR, (len(owners), C, size + extra), BF16)
                plan.targets["attn"].append(
                    (ref, [owner ^ flip for owner in owners], 0, start, size)
                )
        return outs

    def halved_head_outputs(plan):
        half = widths["head"] // 2
        if not direct:
            return grad_outputs(plan, x=["up", "head"], y=["down"])
        outs, plan.targets["head"] = {}, []
        for group, name, at in (("x", "up", 0), ("y", "down", half)):
            plan.targets[name] = []
            for kind, flip in (("keep", 0), ("send", 1)):
                ref, places = f"{kind}_{group}", [owner ^ flip for owner in owners]
                outs[ref] = (FAR, (len(owners), C, widths[name] + half), BF16)
                plan.targets[name].append((ref, places, 0, 0, widths[name]))
                plan.targets["head"].append((ref, places, widths[name], at, half))
        return outs

    def chain_of(results, group, *members, pair_at=None):
        if direct:
            keep, send = results[f"keep_{group}"], results[f"send_{group}"]
        else:
            full = []
            for name in members:
                name, *cut = name if isinstance(name, tuple) else (name,)
                part = results[f"full_{name}"]
                if cut:
                    part = part[..., cut[0] : cut[1]]
                if name in ("up", "down"):
                    part = part.reshape(C, ch_count, -1).transpose(1, 0, 2)
                full.append(part)
            full = jnp.concatenate(full, -1)
            keep, send = [
                jnp.take(full, np.asarray(owners) ^ flip ^ ch_index, axis=0) for flip in (0, 1)
            ]
        dims = (-1, block_rows, keep.shape[-1])
        return Chain(
            keep.reshape(dims), send.reshape(dims), block_dims, [core] + orders[group], pair_at
        )

    def start(*chains):
        for chain in chains:
            chain.start()

    def meet(value, *chains):
        value, *got = tie(value, *[chain.received for chain in chains])
        for chain, array in zip(chains, got):
            chain.received = array
        return value

    def after(value, *chains):
        held_back = [array for chain in chains for array in (chain.keep, chain.send)]
        value, *held_back = tie(value, *held_back)
        for n, chain in enumerate(chains):
            chain.keep, chain.send = held_back[2 * n], held_back[2 * n + 1]
        return value

    def attention_consts(l, forward):
        ins = {
            "perm": (whole((WROWS, ROWS)), perms[l]),
            "perm_t": (whole((ROWS, WROWS)), perms_t[l]),
            "vec": (whole(vectors.shape), vectors),
        }
        if forward:
            ins["rows"] = (SCALARS, valid_rows)
            ins["cols"] = (SCALARS, valid_cols)
            ins["row_limit"] = (whole((NWIN, SLOT, 128)), row_limits[l])
            ins["col_limit"] = (whole((NWIN, SLOT, 128)), col_limits[l])
            ins["bias"] = (
                pl.BlockSpec((None, NGRP, SLOT, LANES), lambda i, l=l: (l, 0, 0, 0)), bias
            )
        return ins

    def vmem(*dims, dtype=BF16):
        return pltpu.VMEM(dims, dtype)

    attn_weights = {
        "stage": vmem(ch_count, C, widths["attn"]),
        "w_qkv": vmem(C, 3 * C),
        "w_proj": vmem(C, C),
        "load_sem": pltpu.SemaphoreType.DMA((4,)),
    }
    mlp_weights = {
        "w_down": vmem(C, HID),
        "w_up": vmem(C, HID),
        "load_sem": pltpu.SemaphoreType.DMA((4,)),
    }
    all_rows = local * ROWS
    mlp_rows = {
        "mlp_all": vmem(all_rows, C), "active_all": vmem(all_rows, HID),
        "pre_all": vmem(all_rows, HID), "low_all": vmem(all_rows, C),
        "up_grad": vmem(C, HID), "down_grad": vmem(C, HID),
        "sem_x": pltpu.SemaphoreType.DMA((2,)), "sem_y": pltpu.SemaphoreType.DMA((2,)),
    }
    wide = (per_image(ROWS, C), (local, ROWS, C), F32)
    thin = (per_image(ROWS, C), (local, ROWS, C), BF16)
    hidden = (per_image(ROWS, HID), (local, ROWS, HID), BF16)
    attn_saved = {
        "normed": thin,
        "qkv": (per_image(WROWS, 3 * C), (local, WROWS, 3 * C), BF16),
        "prob": (per_image(NWIN, NGRP, SLOT, LANES), (local, NWIN, NGRP, SLOT, LANES), BF16),
        "attended": thin,
    }
    sums = {"row_sums": (whole((8, C)), (8, C), F32)}
    up_sums = {**sums, "up_rows": (whole((1, HID)), (1, HID), F32)}
    attn_sums = {
        **sums,
        "qkv_rows": (whole((1, 3 * C)), (1, 3 * C), F32),
        "bias_grad": (whole((NGRP, SLOT, LANES)), (NGRP, SLOT, LANES), F32),
    }

    def given(spec, array):
        return (spec[0], array)

    mlp_flops = 2 * all_rows * C * HID * 2
    attn_flops = 2 * all_rows * C * C * 8

    def attention_forward(l, field, first=0, count=groups, before=None):
        ins, plan = weight_inputs(l, ["attn"]) if before is None else ({}, Plan(widths, l, layers))
        plan.group = first
        ins["field"] = (per_image(*field.shape[1:], first=first), field)
        ins.update(attention_consts(l, True))
        outs = {
            name: (spec, (count * GROUP,) + dims[1:], dtype)
            for name, (spec, dims, dtype) in {"middle": wide, **attn_saved}.items()
        }
        scratch = {"mixed": vmem(GROUP, C, WROWS), "windowed": vmem(GROUP, WROWS, C)}
        if before is None:
            outs["qkv_out"] = (FAR, (C, 3 * C), BF16)
            outs["proj_out"] = (FAR, (C, C), BF16)
            scratch.update(attn_weights)
            scratch["out_sem"] = pltpu.SemaphoreType.DMA((2,))
        else:
            ins["w_qkv"] = (whole((C, 3 * C)), before["qkv_out"])
            ins["w_proj"] = (whole((C, C)), before["proj_out"])
        results = call(
            functools.partial(attention_forward_kernel, plan=plan), f"attention_forward{l}_{first}",
            count, ins, outs, scratch, attn_flops * count // groups,
        )
        return results if before is None else {**before, **results}

    def rows_of(name, arrays):
        if len(arrays) == 1:
            return {name: given(wide, arrays[0])}
        return {f"{name}{n}": (whole(array.shape), array) for n, array in enumerate(arrays)}

    def begin(*moves):
        return [(part, step, exchange(part.array, step)) for part, step in moves]

    def arrive(number, value, moves):
        value, *received = tie(value, *[got for _, _, got in moves])
        stacked = stack_blocks(
            [(part, got, step) for (part, step, _), got in zip(moves, received)], me, f"stack{number}"
        )
        return value, [parts[0] for parts in stacked]

    if staged:
        moves = begin((down, y), (up, x), (parts1[0], y), (parts1[1], x), (parts1[2], y))
        early0 = attention_forward(0, padded, 0, groups - 1)
        early0["proj_out"], (down, up, *parts1) = arrive(4, early0["proj_out"], moves)
        early0["proj_out"] = wait_for(early0["proj_out"], down, up, *parts1)
        held[0] += [down, up]
        got = [exchange(part.array, core) for part in (down, up)]
        moves = begin((parts1[0], x), (parts1[1], y), (parts1[2], x))
        saved0 = attention_forward(0, padded, groups - 1, 1, early0)
        saved0["middle"], *got = tie(saved0["middle"], *got)
        other[0] = list(other[0]) + got
        saved0["middle"], parts1 = arrive(5, saved0["middle"], moves[:1])
        middle0 = [early0["middle"], wait_for(saved0["middle"], *parts1)]
        held.append(parts1)
    else:
        saved0 = early0 = attention_forward(0, padded)
        middle0 = [saved0["middle"]]
    ins, plan = weight_inputs(0, ["down", "up"])
    ins.update(rows_of("middle", middle0))
    ins["vec"] = (whole(vectors.shape), vectors)
    mlp0 = call(
        functools.partial(first_mlp_kernel, plan=plan), "first_mlp", groups, ins,
        {
            "result": wide, "mlp_in": thin, "active": hidden, "slope": hidden,
            "down_out": (FAR, (C, HID), BF16),
            "up_out": (FAR, (C, HID), BF16),
        },
        {**mlp_weights, "out_sem": pltpu.SemaphoreType.DMA((2,))},
        mlp_flops,
    )
    result0 = mlp0["result"]
    got = [exchange(part.array, core) for part in held[1]]
    result0, *got = tie(result0, *got)
    other.append(got)

    if staged:
        early1 = attention_forward(1, result0, 0, groups - 1)
        early1["proj_out"], late1 = arrive(6, early1["proj_out"], moves[1:])
        early1["proj_out"] = wait_for(early1["proj_out"], *late1)
        got = [exchange(part.array, core) for part in late1]
        saved1 = attention_forward(1, result0, groups - 1, 1, early1)
        saved1["middle"], *got = tie(saved1["middle"], *got)
        held[1] = held[1] + late1
        other[1] = other[1] + got
        middle1 = [early1["middle"], saved1["middle"]]
    else:
        saved1 = early1 = attention_forward(1, result0)
        middle1 = [saved1["middle"]]
    ins, plan = weight_inputs(1, ["down", "up", "head"])
    ins.update(rows_of("middle", middle1))
    ins["vec"] = (whole(vectors.shape), vectors)
    ins["rows"] = (SCALARS, valid_rows)
    ins["cols"] = (SCALARS, valid_cols)
    ins["labels"] = (SCALARS, labels)
    ins["partner"] = (SCALARS, partner)
    ins["mix"] = (SCALARS, mix_level)
    cell = np.arange(ROWS)
    for name, place in (("cell_row", cell // GRID), ("cell_col", cell % GRID)):
        place = np.where(cell < CELLS, place, 99)[:, None].astype(np.int32)
        ins[name] = (whole((ROWS, 1)), jnp.asarray(place))
    outs = {
        "grad_mid": wide, **up_sums,
        "final_rows": (whole((2, C)), (2, C), F32),
        "head_rows": (whole((1, head_classes)), (1, head_classes), F32),
        "loss": (whole((1, 128)), (1, 128), F32),
        **halved_head_outputs(plan),
    }
    last = call(
        functools.partial(last_mlp_kernel, plan=plan, total_images=float(total_images)),
        "last_mlp", groups, ins, outs,
        {
            "slope": vmem(GROUP * ROWS, HID), "w_head": vmem(ch_count, C, widths["head"]),
            **mlp_weights, **mlp_rows,
            "pooled_all": vmem(16, C, dtype=F32), "logit_all": vmem(16, head_classes, dtype=F32),
            "head_grad": vmem(ch_count, C, widths["head"]),
        },
        3 * mlp_flops,
    )

    def attention_backward(l, grad_mid, field, saved, first, count, before=None, before_saved=None, store=True, collect=None):
        plan = Plan(widths, l, layers)
        ins = {
            "me": (SCALARS, me), "w_qkv": (whole((C, 3 * C)), saved["qkv_out"]),
            "w_proj": (whole((C, C)), saved["proj_out"]),
        }
        ins.update(attention_consts(l, False))
        wanted = ["qkv", "prob"] + (["normed", "attended"] if store else [])
        for name, array in [("grad_mid", grad_mid), ("field", field)] + [
            (name, saved[name]) for name in wanted
        ]:
            skip = first if array.shape[0] == local else 0
            ins[name] = (per_image(*array.shape[1:], first=skip), array)
        if before is not None:
            for name, (spec, _, _) in attn_sums.items():
                ins[name + "_in"] = (spec, before[name])
            for name in ("normed", "attended"):
                ins[name + "_in"] = (whole((first * GROUP, ROWS, C)), before_saved[name])
            for name in ("spread", "attn"):
                array = before[name + "_all"]
                ins[name + "_in"] = (whole(array.shape), array)
        rows_here = count * GROUP * ROWS
        outs = dict(attn_sums)
        scratch = {
            "dq": vmem(GROUP, C, WROWS), "dkv": vmem(GROUP, WROWS, 2 * C),
            "joined": vmem(GROUP, WROWS, C),
        }
        need_grad = l > 0
        if need_grad:
            outs["grad"] = (wide[0], (count * GROUP, ROWS, C), F32)
        if store:
            if collect is None:
                outs.update(grad_outputs(plan, a=["attn"]))
            else:
                outs.update(cut_attention_outputs(plan))
                plan.collect = (layers, head_real, share - 1, owners)
                ins.update({name: (whole(array.shape), array) for name, array in collect.items()})
                scratch["small_rows"] = vmem(device_count, share, dtype=F32)
                scratch["spread_table"] = vmem(HEADS * SLOT, 128, dtype=F32)
                scratch["pairs"] = vmem(2, len(owners), C, 128)
            scratch.update({
                "normed_all": vmem(all_rows, C), "attended_all": vmem(all_rows, C),
                "spread_all": vmem(all_rows, 3 * C), "attn_all": vmem(all_rows, C),
                "attn_grad": vmem(ch_count, C, widths["attn"]),
                "sem_a": pltpu.SemaphoreType.DMA((4,)),
            })
        else:
            outs["spread_all"] = (whole((rows_here, 3 * C)), (rows_here, 3 * C), BF16)
            outs["attn_all"] = (whole((rows_here, C)), (rows_here, C), BF16)
        return call(
            functools.partial(
                backward_attention_kernel, plan=plan,
                earlier=0 if before is None else first * GROUP, need_grad=need_grad,
            ),
            f"attention_backward{l}_{first}", count, ins, outs, scratch,
            2 * attn_flops * count // groups,
        )

    half = widths["head"] // 2
    x1 = chain_of(last, "x", "up", ("head", 0, half))
    y1 = chain_of(last, "y", "down", ("head", half, 2 * half))
    if regular:
        start(x1, y1)
    grad_mid = last["grad_mid"]
    before1 = attention_backward(1, grad_mid, mlp0["result"], early1, 0, groups - 1, store=False)
    if regular:
        before1["row_sums"] = meet(before1["row_sums"], x1, y1)
        x1, y1 = combine([[x1], [y1]], me, "sum0")
        grad_mid = after(grad_mid, x1, y1)
        start(x1, y1)
    back1 = attention_backward(
        1, grad_mid, mlp0["result"], saved1, groups - 1, 1, before1, early1
    )
    a1 = chain_of(back1, "a", "attn")
    grad = back1["grad"]
    if regular:
        grad = meet(grad, x1, y1)
        x1, y1 = combine([[x1], [y1]], me, "sum1")
        grad = after(grad, x1, y1)
        start(x1, y1, a1)

    plan = Plan(widths, 0, layers)
    ins = {
        "me": (SCALARS, me),
        "w_down": (whole((C, HID)), mlp0["down_out"]),
        "w_up": (whole((C, HID)), mlp0["up_out"]),
    }
    ins.update(rows_of("grad", [before1["grad"], grad]))
    ins.update(rows_of("middle", middle0))
    ins["mlp_in"] = given(thin, mlp0["mlp_in"])
    ins["active"] = given(hidden, mlp0["active"])
    ins["slope"] = given(hidden, mlp0["slope"])
    ins["vec"] = (whole(vectors.shape), vectors)
    first = call(
        functools.partial(backward_mlp_kernel, plan=plan), "mlp_backward0", groups, ins,
        {"grad_mid": wide, **up_sums, **grad_outputs(plan, x=["up"], y=["down"])},
        dict(mlp_rows), 2 * mlp_flops,
    )
    x0, y0 = chain_of(first, "x", "up"), chain_of(first, "y", "down")
    grad_mid = first["grad_mid"]
    if regular:
        grad_mid = meet(grad_mid, x1, y1, a1)
        a1, z1 = combine([[a1], [x1, y1]], me, "sum2")
        grad_mid = after(grad_mid, a1, z1)
        start(a1, z1, x0, y0)
    before0 = attention_backward(0, grad_mid, padded, early0, 0, groups - 1, store=False)
    if regular:
        before0["row_sums"] = meet(before0["row_sums"], a1, x0, y0, z1)
        a1, x0, y0, z1 = combine([[a1], [x0], [y0], [z1]], me, "sum3")
        grad_mid = after(grad_mid, a1, x0, y0, z1)
        start(a1, x0, y0, z1)
    small_parts = None
    if regular:
        small_parts = {
            "mlp_rows0": first["row_sums"], "up_rows0": first["up_rows"],
            "row_sums1": back1["row_sums"], "qkv_rows1": back1["qkv_rows"],
            "mlp_rows1": last["row_sums"], "up_rows1": last["up_rows"],
            "bias_grad1": back1["bias_grad"], "final_rows": last["final_rows"],
            "head_rows": last["head_rows"], "loss": last["loss"],
        }
    back0 = attention_backward(
        0, grad_mid, padded, saved0, groups - 1, 1, before0, early0, collect=small_parts
    )
    a0 = chain_of(back0, "a", "attn")
    if regular:
        b0 = chain_of(back0, "b", pair_at=widths["attn"] - widths["attn"] * 2 // 3)
        waiting = (a1, x0, y0, z1)
        a0.send, b0.send, *got = tie(a0.send, b0.send, *[chain.received for chain in waiting])
        for chain, array in zip(waiting, got):
            chain.received = array

    if regular:
        start(a0, b0)
        x0, y0 = combine([[x0], [y0]], me, "sum5")
        start(x0, y0)
        a0.received, b0.received, x0.keep = tie(a0.received, b0.received, x0.keep)
        a0, b0 = combine([[a0], [b0]], me, "sum6")
        start(a0, b0)
        (z0,) = combine([[x0, y0, a1]], me, "sum7")
        start(z0)
        a0, b0 = combine([[a0], [b0]], me, "sum8")
        start(a0, b0)
        (z0,) = combine([[z0]], me, "sum9")
        start(z0)
        own1, square1 = finish(z1, "own1")
        (a0,) = combine([[a0, b0]], me, "sum10")
        start(a0)
        own0, square0 = finish(z0, "own0")
        (a0,) = combine([[a0]], me, "sum11")
        start(a0)
        own_attn, message = finish_pair(a0, [square0, square1], device_count, share, "own_attn")
    else:
        square, own_parts = jnp.zeros((1, 128), F32), []
        for chain in (a0, x0, y0, a1, x1, y1):
            start(chain)
            while chain.steps:
                (chain,) = combine([[chain]], me, "sum")
                start(chain)
            part, part_square = finish(chain, "own")
            square = square + part_square
            own_parts.append(part)
        own_attn = own_parts[0]
        own0, own1 = jnp.concatenate(own_parts[1:4], 1), jnp.concatenate(own_parts[4:], 1)
        (rows_all,) = small_call(
            lambda *refs: collect_rows(
                layers, head_real, share - 1, refs[:-2], refs[-2], refs[-1]
            ),
            "collect",
            [part[name] for part in ((first, back0), (last, back1))
             for part, name in (
                 (part[1], "row_sums"), (part[1], "qkv_rows"), (part[0], "row_sums"),
                 (part[0], "up_rows"), (part[1], "bias_grad"))]
            + [last["final_rows"], last["head_rows"], last["loss"]],
            [((device_count, share), F32)],
            stream=True,
            scratch=[pltpu.VMEM((HEADS * SLOT, 128), F32)],
        )
        rows_all = lax.all_to_all(rows_all, ("win", "ch"), 0, 0, tiled=True)
        message = jnp.concatenate([jnp.sum(rows_all, 0, keepdims=True), square], 1)
        message = jnp.broadcast_to(message, (device_count, share + 128))
    message = lax.all_to_all(message, ("win", "ch"), 0, 0, tiled=True)
    starts = [
        {"attn": (1, 0), "up": (2, 0), "down": (2, widths["up"])},
        {
            "attn": (2, widths["up"] + widths["down"]), "up": (0, 0),
            "down": (0, widths["up"] + half),
            "head": [(0, widths["up"]), (0, widths["up"] + half + widths["down"])],
        },
    ]
    arrays = [
        [w_qkv, m_qkv, v_qkv], [w_proj, m_proj, v_proj], [w_fc1, m_fc1, v_fc1],
        [w_fc2, m_fc2, v_fc2], [w_head, m_head, v_head], [vectors, m_vec, v_vec],
        [rel_table, m_rel, v_rel],
    ]
    turns = {3: (0, 2, 1), 6: (2, 0, 1)}
    turned = [
        a.transpose(turns[n]) if n in turns else a for n, group in enumerate(arrays) for a in group
    ]
    results = small_call(
        functools.partial(
            update_kernel, starts, widths,
            (vectors.shape[0], layers * HEADS, offsets, share, share - 1),
        ),
        "update",
        [own1, own_attn, own0, message] + turned,
        [((1, 1), F32)] * 2 + [(a.shape, F32) for a in turned],
        stream=True,
    )
    loss_total, grad_norm, *results = results
    outs = [loss_total[0, 0], grad_norm[0, 0]]
    for n in range(0, len(results), 3):
        back = {3: (0, 2, 1), 6: (1, 2, 0)}.get(n // 3)
        outs += [r if back is None else r.transpose(back) for r in results[n : n + 3]]
    return tuple(outs)


def solution(mesh):
    cut = P(None, "win", "ch")
    down = P(None, "ch", "win")
    head = P("win", "ch")
    rows = P(None, ("win", "ch"))
    in_specs = (
        (P(None, ("win", "ch"), None, None),) + (rows,) * 4 + (P(),)
        + (cut,) * 9 + (down,) * 3 + (head,) * 3 + (P(),) * 6
    )
    out_specs = (P(),) * 2 + (cut,) * 9 + (down,) * 3 + (head,) * 3 + (P(),) * 6
    return jax.shard_map(
        per_device, mesh=mesh, in_specs=in_specs, out_specs=out_specs, check_vma=False
    )
```
